32 devices in a mesh: batch: 4 (over y, core), space: 8 (over z, x).
Axes of the slice: x: 2, y: 2, z: 4, core: 2. Of those that a mesh axis runs over, the one named last changes fastest.
Arguments:
- small_in: bfloat16 [1280, 32, 1024], P('batch', 'space'), may hold values from -45 to 45
- large_in: bfloat16 [320, 64, 2048], P('batch', 'space'), may hold values from -45 to 45
- small_teacher: bfloat16 [1280, 32, 4096], P('batch', 'space'), may hold values from -6 to 6
- large_teacher: bfloat16 [320, 64, 8192], P('batch', 'space'), may hold values from -6 to 6
- small_groups: int32 [1280], P('batch'), may hold values from 0 to 1
- large_groups: int32 [320], P('batch'), may hold values from 0 to 1
- small_cot: bfloat16 [1280, 16, 1024], P(('batch', 'space')), may hold values from -6 to 6
- large_cot: bfloat16 [320, 32, 2048], P(('batch', 'space')), may hold values from -6 to 6
- teacher_gains: float32 [2, 128], replicated, may hold values from 0.5 to 1.5
- teacher_first: bfloat16 [3, 3, 128, 256], replicated, may hold values from -0.1875 to 0.1875
- teacher_inner: float32 [2, 256], replicated, may hold values from 0.5 to 1.5
- teacher_second: bfloat16 [3, 3, 256, 256], replicated, may hold values from -0.125 to 0.125
- teacher_bypass: bfloat16 [128, 256], replicated, may hold values from -0.5 to 0.5
- entry_norm: float32 [2, 32], replicated, may hold values from 0.5 to 1.5
- first_conv: float32 [3, 3, 32, 64], replicated, may hold values from -0.375 to 0.375
- inner_norm: float32 [2, 64], replicated, may hold values from 0.5 to 1.5
- second_conv: float32 [3, 3, 64, 64], replicated, may hold values from -0.25 to 0.25
- shortcut: float32 [32, 64], replicated, may hold values from -1 to 1
- momentum_entry: float32 [2, 32], replicated, may hold values from -3072 to 3072
- momentum_first: float32 [3, 3, 32, 64], replicated, may hold values from -1536 to 1536
- momentum_inner: float32 [2, 64], replicated, may hold values from -1536 to 1536
- momentum_second: float32 [3, 3, 64, 64], replicated, may hold values from -1536 to 1536
- momentum_shortcut: float32 [32, 64], replicated, may hold values from -1536 to 1536
- average_entry: float32 [2, 32], replicated, may hold values from 0.5 to 1.5
- average_first: float32 [3, 3, 32, 64], replicated, may hold values from -0.375 to 0.375
- average_inner: float32 [2, 64], replicated, may hold values from 0.5 to 1.5
- average_second: float32 [3, 3, 64, 64], replicated, may hold values from -0.25 to 0.25
- average_shortcut: float32 [32, 64], replicated, may hold values from -1 to 1
Outputs:
- small_out: bfloat16 [1280, 16, 1024], P(('batch', 'space'))
- large_out: bfloat16 [320, 32, 2048], P(('batch', 'space'))
- small_grad: float32 [1280, 32, 1024], P('batch', 'space')
- large_grad: float32 [320, 64, 2048], P('batch', 'space')
- transfer_loss: float32 [], replicated
- entry_grads: float32 [2, 32], replicated
- entry_velocity: float32 [2, 32], replicated
- entry_average: float32 [2, 32], replicated
- entry_updated: float32 [2, 32], replicated
- first_grads: float32 [3, 3, 32, 64], replicated
- first_velocity: float32 [3, 3, 32, 64], replicated
- first_average: float32 [3, 3, 32, 64], replicated
- first_updated: float32 [3, 3, 32, 64], replicated
- first_copy: bfloat16 [3, 3, 32, 64], replicated
- inner_grads: float32 [2, 64], replicated
- inner_velocity: float32 [2, 64], replicated
- inner_average: float32 [2, 64], replicated
- inner_updated: float32 [2, 64], replicated
- second_grads: float32 [3, 3, 64, 64], replicated
- second_velocity: float32 [3, 3, 64, 64], replicated
- second_average: float32 [3, 3, 64, 64], replicated
- second_updated: float32 [3, 3, 64, 64], replicated
- second_copy: bfloat16 [3, 3, 64, 64], replicated
- shortcut_grads: float32 [32, 64], replicated
- shortcut_velocity: float32 [32, 64], replicated
- shortcut_average: float32 [32, 64], replicated
- shortcut_updated: float32 [32, 64], replicated
- shortcut_copy: bfloat16 [32, 64], replicated
The draws below stay inside these ranges and needn't reach their ends.
All inputs are finite; a program needn't handle non-finite values.
Results may differ from the reference program's by a relative error of at most 0.0025.
The reference program's roundings to bfloat16 on the way count: a program that leaves them out, or rounds other values in their place, can miss the bound.
Values may be sent and summed in bfloat16 or wider, within the bound.
A program may use at most 384 MiB of HBM per device.

```python
import math
import jax
import jax.numpy as jnp
from jax import lax

CS_IN = 32
CS_OUT = 64
CT_IN = 128
CT_OUT = 256
SIDE = 32
GROUPS = 2
OUT_SIDE = 16
IMAGES_S = 1280
IMAGES_L = 320
POSITIONS = 655360


def rising_factor(rising, image_count, image_side):
    image_place = jnp.arange(image_count, dtype=jnp.float32) / max(image_count - 1, 1)
    row_place = jnp.arange(image_side, dtype=jnp.float32) / (image_side - 1)
    return jnp.exp(rising * image_place)[:, None, None] * jnp.exp(rising * row_place)[None, :, None]


def draw_small_in(key, part):
    key = jax.random.fold_in(key, 11)
    shape = (IMAGES_S, SIDE, SIDE * CS_IN)
    base = jnp.clip(jax.random.normal(key, shape, jnp.float32), -4.0, 4.0)
    rising = math.log(3.0)
    return (base * rising_factor(rising, IMAGES_S, SIDE)).astype(jnp.bfloat16)


def draw_large_in(key, part):
    key = jax.random.fold_in(key, 13)
    shape = (IMAGES_L, 2 * SIDE, 2 * SIDE * CS_IN)
    base = jnp.clip(jax.random.normal(key, shape, jnp.float32), -4.0, 4.0)
    rising = math.log(3.0)
    return (base * rising_factor(rising, IMAGES_L, 2 * SIDE)).astype(jnp.bfloat16)


def place_ends(values, key, smallest, high):
    longest = values.shape.index(max(values.shape))
    spots = []
    for shift in (0, 1):
        where = [jax.random.randint(jax.random.fold_in(key, axis), (), 0, length) for axis, length in enumerate(values.shape)]
        where[longest] = (where[longest] + shift) % values.shape[longest]
        spots.append(tuple(where))
    return values.at[spots[0]].set(smallest).at[spots[1]].set(high)


def steps_of(rng, extent, cuts, low, top_value):
    factor_of = 1.0
    for axis_at, shards_of in cuts:
        draws = jax.random.uniform(jax.random.fold_in(jax.random.fold_in(rng, 6), axis_at), (shards_of,), jnp.float32, low / len(cuts), top_value / len(cuts))
        factor_of = factor_of * jnp.repeat(jnp.exp(draws), extent[axis_at] // shards_of).reshape((-1,) + (1,) * (len(extent) - 1 - axis_at))
    return factor_of


def normal_values(stream_key, dims, deviation, reach, pieces=(), held_as=jnp.bfloat16):
    entries = jax.random.normal(stream_key, dims, jnp.float32) * deviation
    if len(pieces) > 0:
        entries = steps_of(stream_key, dims, pieces, -0.22, 0.18) * entries
    return jnp.clip(entries, min=-reach, max=reach).astype(held_as)


def setup_inputs(seed: int = 0) -> dict:
    key_list = jax.random.split(jax.random.key(seed), 29)
    small_in = draw_small_in(jax.random.fold_in(key_list[28], 71), 0)
    large_in = draw_large_in(jax.random.fold_in(key_list[28], 71), 0)
    small_teacher = normal_values(key_list[2], (IMAGES_S, SIDE, SIDE * CT_IN), 1.0, 6.0, ((0, 4), (1, 8)))
    large_teacher = normal_values(key_list[3], (IMAGES_L, 2 * SIDE, 2 * SIDE * CT_IN), 1.0, 6.0, ((0, 4), (1, 8)))
    small_groups = place_ends(jax.random.randint(key_list[4], (IMAGES_S,), 0, GROUPS), jax.random.fold_in(key_list[4], 1), 0, GROUPS - 1).astype(jnp.int32)
    large_groups = place_ends(jax.random.randint(key_list[5], (IMAGES_L,), 0, GROUPS), jax.random.fold_in(key_list[5], 1), 0, GROUPS - 1).astype(jnp.int32)
    small_cot = normal_values(key_list[6], (IMAGES_S, OUT_SIDE, OUT_SIDE * CS_OUT), 1.0, 6.0, ((0, 32),))
    large_cot = normal_values(key_list[7], (IMAGES_L, 2 * OUT_SIDE, 2 * OUT_SIDE * CS_OUT), 1.0, 6.0, ((0, 32),))
    teacher_gains = jnp.clip(1.0 + 0.1 * jax.random.normal(key_list[8], (2, CT_IN), jnp.float32), 0.5, 1.5)
    teacher_first = normal_values(key_list[9], (3, 3, CT_IN, CT_OUT), (9 * CT_IN) ** -0.5, 0.1875)
    teacher_inner = jnp.clip(1.0 + 0.1 * jax.random.normal(key_list[10], (2, CT_OUT), jnp.float32), 0.5, 1.5)
    teacher_second = normal_values(key_list[11], (3, 3, CT_OUT, CT_OUT), (9 * CT_OUT) ** -0.5, 0.125)
    teacher_bypass = normal_values(key_list[12], (CT_IN, CT_OUT), CT_IN ** -0.5, 0.5)
    entry_norm = jnp.clip(1.0 + 0.1 * jax.random.normal(key_list[13], (2, CS_IN), jnp.float32), 0.5, 1.5)
    first_conv = normal_values(key_list[14], (3, 3, CS_IN, CS_OUT), (9 * CS_IN) ** -0.5, 0.375, (), jnp.float32)
    inner_norm = jnp.clip(1.0 + 0.1 * jax.random.normal(key_list[15], (2, CS_OUT), jnp.float32), 0.5, 1.5)
    second_conv = normal_values(key_list[16], (3, 3, CS_OUT, CS_OUT), (9 * CS_OUT) ** -0.5, 0.25, (), jnp.float32)
    shortcut = normal_values(key_list[17], (CS_IN, CS_OUT), CS_IN ** -0.5, 1.0, (), jnp.float32)
    momentum_entry = normal_values(key_list[18], (2, CS_IN), (0.3 * (4 * POSITIONS) ** 0.5), 3072.0, (), jnp.float32)
    momentum_first = normal_values(key_list[19], (3, 3, CS_IN, CS_OUT), (0.3 * POSITIONS ** 0.5), 1536.0, (), jnp.float32)
    momentum_inner = normal_values(key_list[20], (2, CS_OUT), (0.3 * POSITIONS ** 0.5), 1536.0, (), jnp.float32)
    momentum_second = normal_values(key_list[21], (3, 3, CS_OUT, CS_OUT), (0.3 * POSITIONS ** 0.5), 1536.0, (), jnp.float32)
    momentum_shortcut = normal_values(key_list[22], (CS_IN, CS_OUT), (0.3 * POSITIONS ** 0.5), 1536.0, (), jnp.float32)
    average_entry = jnp.clip(1.0 + 0.1 * jax.random.normal(key_list[23], (2, CS_IN), jnp.float32), 0.5, 1.5)
    average_first = normal_values(key_list[24], (3, 3, CS_IN, CS_OUT), (9 * CS_IN) ** -0.5, 0.375, (), jnp.float32)
    average_inner = jnp.clip(1.0 + 0.1 * jax.random.normal(key_list[25], (2, CS_OUT), jnp.float32), 0.5, 1.5)
    average_second = normal_values(key_list[26], (3, 3, CS_OUT, CS_OUT), (9 * CS_OUT) ** -0.5, 0.25, (), jnp.float32)
    average_shortcut = normal_values(key_list[27], (CS_IN, CS_OUT), CS_IN ** -0.5, 1.0, (), jnp.float32)
    return dict(small_in=small_in, large_in=large_in, small_teacher=small_teacher, large_teacher=large_teacher, small_groups=small_groups, large_groups=large_groups, small_cot=small_cot, large_cot=large_cot, teacher_gains=teacher_gains, teacher_first=teacher_first, teacher_inner=teacher_inner, teacher_second=teacher_second, teacher_bypass=teacher_bypass, entry_norm=entry_norm, first_conv=first_conv, inner_norm=inner_norm, second_conv=second_conv, shortcut=shortcut, momentum_entry=momentum_entry, momentum_first=momentum_first, momentum_inner=momentum_inner, momentum_second=momentum_second, momentum_shortcut=momentum_shortcut, average_entry=average_entry, average_first=average_first, average_inner=average_inner, average_second=average_second, average_shortcut=average_shortcut)


@jax.custom_vjp
def low(v):
    return lax.optimization_barrier(v.astype(jnp.bfloat16)).astype(jnp.float32)

@jax.custom_vjp
def low_back(v):
    return v

def low_keep(v):
    return (low(v), None)

def low_pass(kept, grad):
    return (grad,)

def back_keep(v):
    return (v, None)

def back_low(kept, grad):
    return (low(grad),)
low.defvjp(low_keep, low_pass)
low_back.defvjp(back_keep, back_low)
HIGHEST = lax.Precision.HIGHEST
EPSILON = 1e-05
TRANSFER_WEIGHT = 1000.0
MOMENTUM = 0.9
WEIGHT_DECAY = 0.0005
AVERAGING = 0.7
CONV_RATE = 0.06
NORM_RATE = 0.3

def convolve(inputs, kernel, stride):
    return lax.conv_general_dilated(inputs, kernel, (stride, stride), ((1, 1), (1, 1)), dimension_numbers=('NHWC', 'HWIO', 'NHWC'), precision=HIGHEST)

def batch_norm(small_part, large_part, small_table, large_table):
    group_counts = lax.optimization_barrier(jnp.sum(small_table, axis=0)) * (small_part.shape[1] * small_part.shape[2]) + lax.optimization_barrier(jnp.sum(large_table, axis=0)) * (large_part.shape[1] * large_part.shape[2])
    group_totals = jnp.einsum('ng,nhwc->gc', small_table, small_part, precision=HIGHEST) + jnp.einsum('ng,nhwc->gc', large_table, large_part, precision=HIGHEST)
    group_squares = jnp.einsum('ng,nhwc->gc', small_table, small_part * small_part, precision=HIGHEST) + jnp.einsum('ng,nhwc->gc', large_table, large_part * large_part, precision=HIGHEST)
    group_means = group_totals / group_counts[:, None]
    group_scales = lax.rsqrt(group_squares / group_counts[:, None] - group_means * group_means + EPSILON)

    def normalize(values, indicator):
        image_means = jnp.dot(indicator, group_means, precision=HIGHEST)
        image_scales = jnp.dot(indicator, group_scales, precision=HIGHEST)
        return (values - image_means[:, None, None, :]) * image_scales[:, None, None, :]
    return (normalize(small_part, small_table), normalize(large_part, large_table))

def attention_map(block_sum):
    energy = lax.optimization_barrier(jnp.mean(block_sum * block_sum, axis=-1)).reshape(block_sum.shape[0], -1)
    return energy * lax.rsqrt(lax.optimization_barrier(jnp.sum(energy * energy, axis=-1, keepdims=True)) + 1e-12)

def teacher_maps(teacher_in, image_side, block_images, teacher_gains, teacher_first, teacher_inner, teacher_second, teacher_bypass):
    first_kernel = teacher_first.astype(jnp.float32)
    second_kernel = teacher_second.astype(jnp.float32)
    bypass_kernel = teacher_bypass.astype(jnp.float32)
    image_count = teacher_in.shape[0]

    def teacher_block(images):
        raw_input = images.astype(jnp.float32).reshape(images.shape[0], image_side, image_side, CT_IN)
        teacher_act = low(jax.nn.silu(teacher_gains[0] * raw_input + teacher_gains[1]))
        teacher_mid = low(jax.nn.silu(teacher_inner[0] * convolve(teacher_act, first_kernel, 2) + teacher_inner[1]))
        bypass = jnp.einsum('nhwc,co->nhwo', teacher_act[:, ::2, ::2, :], bypass_kernel, precision=HIGHEST)
        return attention_map(convolve(teacher_mid, second_kernel, 1) + bypass)
    blocks = teacher_in.reshape(image_count // block_images, block_images, image_side, image_side * CT_IN)
    return lax.map(teacher_block, blocks).reshape(image_count, image_side // 2 * (image_side // 2))

def student_block(small_pixels, large_pixels, entry_norm, first_conv, inner_norm, second_conv, shortcut, small_table, large_table, small_map, large_map):
    first_kernel = low(first_conv)
    second_kernel = low(second_conv)
    bypass_kernel = low(shortcut)
    normed_small, normed_large = batch_norm(small_pixels, large_pixels, small_table, large_table)
    act_small = low_back(low(jax.nn.silu(entry_norm[0] * normed_small + entry_norm[1])))
    act_large = low_back(low(jax.nn.silu(entry_norm[0] * normed_large + entry_norm[1])))
    first_small = low_back(convolve(act_small, first_kernel, 2))
    first_large = low_back(convolve(act_large, first_kernel, 2))
    mid_small, mid_large = batch_norm(first_small, first_large, small_table, large_table)
    inner_small = low(jax.nn.silu(inner_norm[0] * mid_small + inner_norm[1]))
    inner_large = low(jax.nn.silu(inner_norm[0] * mid_large + inner_norm[1]))
    sum_small = low_back(convolve(inner_small, second_kernel, 1) + jnp.einsum('nhwc,co->nhwo', act_small[:, ::2, ::2, :], bypass_kernel, precision=HIGHEST))
    sum_large = low_back(convolve(inner_large, second_kernel, 1) + jnp.einsum('nhwc,co->nhwo', act_large[:, ::2, ::2, :], bypass_kernel, precision=HIGHEST))
    diff_small = attention_map(sum_small) - small_map
    diff_large = attention_map(sum_large) - large_map
    objective = TRANSFER_WEIGHT / 2 * (jnp.sum(diff_small * diff_small) + jnp.sum(diff_large * diff_large))
    return (sum_small, sum_large, objective)

def renew(weights, gradient, moment, average, factor):
    descent = gradient + WEIGHT_DECAY * weights
    velocity = MOMENTUM * moment + descent
    updated = weights - factor * (descent + MOMENTUM * velocity)
    smoothed = AVERAGING * average + (1.0 - AVERAGING) * updated
    return (gradient, velocity, smoothed, updated)

def reference(small_in, large_in, small_teacher, large_teacher, small_groups, large_groups, small_cot, large_cot, teacher_gains, teacher_first, teacher_inner, teacher_second, teacher_bypass, entry_norm, first_conv, inner_norm, second_conv, shortcut, momentum_entry, momentum_first, momentum_inner, momentum_second, momentum_shortcut, average_entry, average_first, average_inner, average_second, average_shortcut):
    small_map = teacher_maps(small_teacher, SIDE, 32, teacher_gains, teacher_first, teacher_inner, teacher_second, teacher_bypass)
    large_map = teacher_maps(large_teacher, 2 * SIDE, 8, teacher_gains, teacher_first, teacher_inner, teacher_second, teacher_bypass)
    small_pixels = small_in.astype(jnp.float32).reshape(IMAGES_S, SIDE, SIDE, CS_IN)
    large_pixels = large_in.astype(jnp.float32).reshape(IMAGES_L, 2 * SIDE, 2 * SIDE, CS_IN)
    small_table = (small_groups[:, None] == jnp.arange(GROUPS, dtype=jnp.int32)[None, :]).astype(jnp.float32)
    large_table = (large_groups[:, None] == jnp.arange(GROUPS, dtype=jnp.int32)[None, :]).astype(jnp.float32)

    def forward(small_pixels, large_pixels, entry_norm, first_conv, inner_norm, second_conv, shortcut):
        return student_block(small_pixels, large_pixels, entry_norm, first_conv, inner_norm, second_conv, shortcut, small_table, large_table, small_map, large_map)
    (sum_small, sum_large, objective), pullback = jax.vjp(forward, small_pixels, large_pixels, entry_norm, first_conv, inner_norm, second_conv, shortcut)
    cot_small = small_cot.astype(jnp.float32).reshape(IMAGES_S, OUT_SIDE, OUT_SIDE, CS_OUT)
    cot_large = large_cot.astype(jnp.float32).reshape(IMAGES_L, 2 * OUT_SIDE, 2 * OUT_SIDE, CS_OUT)
    grad_small, grad_large, entry_grads, first_grads, inner_grads, second_grads, shortcut_grads = pullback((cot_small, cot_large, jnp.ones((), jnp.float32)))
    rate_scale = 1.0 / math.sqrt(POSITIONS)
    entry_state = renew(entry_norm, entry_grads, momentum_entry, average_entry, NORM_RATE * rate_scale)
    first_state = renew(first_conv, first_grads, momentum_first, average_first, CONV_RATE * rate_scale)
    inner_state = renew(inner_norm, inner_grads, momentum_inner, average_inner, NORM_RATE * rate_scale)
    second_state = renew(second_conv, second_grads, momentum_second, average_second, CONV_RATE * rate_scale)
    bypass_state = renew(shortcut, shortcut_grads, momentum_shortcut, average_shortcut, CONV_RATE * rate_scale)
    return (sum_small.astype(jnp.bfloat16).reshape(IMAGES_S, OUT_SIDE, OUT_SIDE * CS_OUT), sum_large.astype(jnp.bfloat16).reshape(IMAGES_L, 2 * OUT_SIDE, 2 * OUT_SIDE * CS_OUT), grad_small.reshape(IMAGES_S, SIDE, SIDE * CS_IN), grad_large.reshape(IMAGES_L, 2 * SIDE, 2 * SIDE * CS_IN), objective / POSITIONS, entry_state[0], entry_state[1], entry_state[2], entry_state[3], first_state[0], first_state[1], first_state[2], first_state[3], first_state[3].astype(jnp.bfloat16), inner_state[0], inner_state[1], inner_state[2], inner_state[3], second_state[0], second_state[1], second_state[2], second_state[3], second_state[3].astype(jnp.bfloat16), bypass_state[0], bypass_state[1], bypass_state[2], bypass_state[3], bypass_state[3].astype(jnp.bfloat16))
```

```python
import functools
import math

import jax
import jax.numpy as jnp
import numpy as np
from jax import lax
from jax.experimental import pallas as pl
from jax.experimental.pallas import tpu as pltpu
from jax.sharding import PartitionSpec as P

CS_IN = 32
CS_OUT = 64
CT_IN = 128
CT_OUT = 256
SIDE = 32
SLABS = 4

EPSILON = 1e-05
TRANSFER_WEIGHT = 1000.0
MOMENTUM = 0.9
WEIGHT_DECAY = 0.0005
AVERAGING = 0.7
CONV_RATE = 0.06
NORM_RATE = 0.3

F32 = jnp.float32
BF16 = jnp.bfloat16
MESH = pl.DeviceIdType.MESH
VMEM_LIMIT = 56 << 20


def sigmoid(z):
    return 0.5 * jnp.tanh(0.5 * z) + 0.5


def matmul(a, b):
    return jnp.dot(a, b, preferred_element_type=F32)


def fold(rows, width):
    shift = width
    while shift < 128:
        rows = rows + pltpu.roll(rows, shift, 1)
        shift *= 2
    return rows


def group_norms(totals, counts, width):
    folded = fold(totals, width)
    means, scales = [], []
    for g in range(2):
        mean = folded[g : g + 1] / counts[g]
        variance = folded[2 + g : 3 + g] / counts[g] - mean * mean
        means.append(mean)
        scales.append(lax.rsqrt(variance + EPSILON))
    return means, scales


def per_image(w0, w1, pair):
    return w0 * pair[0] + w1 * pair[1]


def twice(table):
    return jnp.concatenate([table, table], axis=1)


def grouped_rows(w0, w1, values):
    rows = []
    for v in values:
        rows.append(jnp.sum(v * w0, axis=0, keepdims=True))
        rows.append(jnp.sum(v * w1, axis=0, keepdims=True))
    rows.append(jnp.zeros((8 - len(rows), 128), F32))
    return jnp.concatenate(rows, axis=0)


def entry_counts(tot_ref):
    return [tot_ref[4:5], tot_ref[5:6]]


def inner_counts(tot_ref):
    return [tot_ref[4:5] * 0.25, tot_ref[5:6] * 0.25]


def stats_kernel(x_refs, w_refs, out_ref):
    step = pl.program_id(0)
    total = jnp.zeros((8, 128), F32)
    for x_ref, (w0_ref, w1_ref) in zip(x_refs, w_refs):
        rows, images, lanes = x_ref.shape
        s = jnp.zeros((images, 128), F32)
        q = jnp.zeros((images, 128), F32)
        for r in range(rows):
            for c in range(0, lanes, 128):
                v = x_ref[r, :, c : c + 128].astype(F32)
                s = s + v
                q = q + v * v
        w0, w1 = w0_ref[...], w1_ref[...]
        positions = jnp.full((images, 128), float(rows * lanes // CS_IN), F32)
        total = total + grouped_rows(w0, w1, [s, q, positions])

    @pl.when(step == 0)
    def _():
        out_ref[...] = total

    @pl.when(step > 0)
    def _():
        out_ref[...] += total


def input_stats(slabs, weights):
    steps = 4

    def kernel(xs, xl, a0, a1, b0, b1, out_ref):
        stats_kernel((xs, xl), ((a0, a1), (b0, b1)), out_ref)

    specs = [
        pl.BlockSpec((x.shape[0] // steps,) + x.shape[1:], lambda i: (i, 0, 0)) for x in slabs
    ]
    tables = [w for pair in weights for w in pair]
    specs += [pl.BlockSpec(w.shape, lambda i: (0, 0)) for w in tables]
    return pl.pallas_call(
        kernel,
        grid=(steps,),
        in_specs=specs,
        out_specs=pl.BlockSpec((8, 128), lambda i: (0, 0)),
        out_shape=jax.ShapeDtypeStruct((8, 128), F32),
        compiler_params=pltpu.CompilerParams(vmem_limit_bytes=VMEM_LIMIT),
    )(*slabs, *tables)


def greet(axes):
    barrier = pltpu.get_barrier_semaphore()
    expected = 0
    for name, size in axes:
        me = lax.axis_index(name)
        for d in range(1, size):
            pl.semaphore_signal(
                barrier,
                inc=1,
                device_id={name: lax.rem(me + d, size)},
                device_id_type=MESH,
            )
            expected += 1
    pl.semaphore_wait(barrier, expected)


def total_kernel(axes, count, *refs):
    parts = refs[:count]
    out_ref, held, boxes_a, boxes_b, send_a, recv_a, send_b, recv_b = refs[count:]
    value = parts[0][...]
    for part in parts[1:]:
        value = value + part[...]
    held[0] = value
    greet(axes)
    for level, ((name, size), boxes, send, recv) in enumerate(
        zip(axes, (boxes_a, boxes_b), (send_a, send_b), (recv_a, recv_b))
    ):
        me = lax.axis_index(name)
        copies = []
        for d in range(1, size):
            copy = pltpu.make_async_remote_copy(
                src_ref=held.at[level],
                dst_ref=boxes.at[d],
                send_sem=send.at[d],
                recv_sem=recv.at[d],
                device_id={name: lax.rem(me + d, size)},
                device_id_type=MESH,
            )
            copy.start()
            copies.append(copy)
        for copy in copies:
            copy.wait_recv()
        value = jnp.zeros(value.shape, F32)
        for source in range(size):
            back = lax.rem(me - source + size, size)
            value = value + jnp.where(
                back == 0, held[level], boxes[jnp.maximum(back, 1)]
            )
        for copy in copies:
            copy.wait_send()
        if level == 0:
            held[1] = value
        else:
            out_ref[...] = value


def total_over_devices(parts, axes, collective_id):
    shape = parts[0].shape
    return pl.pallas_call(
        functools.partial(total_kernel, axes, len(parts)),
        out_shape=jax.ShapeDtypeStruct(shape, F32),
        in_specs=[pl.BlockSpec(memory_space=pltpu.VMEM)] * len(parts),
        out_specs=pl.BlockSpec(memory_space=pltpu.VMEM),
        scratch_shapes=[
            pltpu.VMEM((2,) + shape, F32),
            pltpu.VMEM((axes[0][1],) + shape, F32),
            pltpu.VMEM((axes[1][1],) + shape, F32),
            pltpu.SemaphoreType.DMA((axes[0][1],)),
            pltpu.SemaphoreType.DMA((axes[0][1],)),
            pltpu.SemaphoreType.DMA((axes[1][1],)),
            pltpu.SemaphoreType.DMA((axes[1][1],)),
        ],
        compiler_params=pltpu.CompilerParams(collective_id=collective_id, has_side_effects=True),
    )(*parts)


def spread_sum_kernel(axes, x_ref, out_ref, boxes_a, boxes_b, held, *sems):
    send_a, recv_a, send_b, recv_b, send_c, recv_c = sems
    (name_a, size_a), (name_b, size_b) = axes
    me_a, me_b = lax.axis_index(name_a), lax.axis_index(name_b)
    piece = x_ref.shape[0] // size_a
    greet(axes)

    def rows(index):
        return pl.ds(pl.multiple_of(index * piece, 8), piece)

    copies = []
    for d in range(1, size_a):
        peer = lax.rem(me_a + d, size_a)
        copy = pltpu.make_async_remote_copy(
            src_ref=x_ref.at[rows(peer)],
            dst_ref=boxes_a.at[d],
            send_sem=send_a.at[d],
            recv_sem=recv_a.at[d],
            device_id={name_a: peer},
            device_id_type=MESH,
        )
        copy.start()
        copies.append(copy)
    value = x_ref[rows(me_a)]
    for d in range(1, size_a):
        copies[d - 1].wait_recv()
        value = value + boxes_a[d]
    held[0] = value
    for copy in copies:
        copy.wait_send()
    copies = []
    for d in range(1, size_b):
        copy = pltpu.make_async_remote_copy(
            src_ref=held.at[0],
            dst_ref=boxes_b.at[d],
            send_sem=send_b.at[d],
            recv_sem=recv_b.at[d],
            device_id={name_b: lax.rem(me_b + d, size_b)},
            device_id_type=MESH,
        )
        copy.start()
        copies.append(copy)
    for copy in copies:
        copy.wait_recv()
    value = jnp.zeros(value.shape, F32)
    for source in range(size_b):
        back = lax.rem(me_b - source + size_b, size_b)
        value = value + jnp.where(back == 0, held[0], boxes_b[jnp.maximum(back, 1)])
    held[1] = value
    out_ref[rows(me_a)] = value
    for copy in copies:
        copy.wait_send()
    copies = []
    for d in range(1, size_a):
        copy = pltpu.make_async_remote_copy(
            src_ref=held.at[1],
            dst_ref=out_ref.at[rows(me_a)],
            send_sem=send_c.at[d],
            recv_sem=recv_c.at[d],
            device_id={name_a: lax.rem(me_a + d, size_a)},
            device_id_type=MESH,
        )
        copy.start()
        copies.append(copy)
    for copy in copies:
        copy.wait()


def spread_sum(x, axes, collective_id):
    (_, size_a), (_, size_b) = axes
    rows = x.shape[0]
    padded = -(-rows // (8 * size_a)) * 8 * size_a
    x = jnp.pad(x, ((0, padded - rows), (0, 0)))
    piece = padded // size_a
    sems = []
    for size in (size_a, size_b, size_a):
        sems += [pltpu.SemaphoreType.DMA((size,))] * 2
    total = pl.pallas_call(
        functools.partial(spread_sum_kernel, axes),
        out_shape=jax.ShapeDtypeStruct(x.shape, F32),
        in_specs=[pl.BlockSpec(memory_space=pltpu.VMEM)],
        out_specs=pl.BlockSpec(memory_space=pltpu.VMEM),
        scratch_shapes=[
            pltpu.VMEM((size_a, piece, 128), F32),
            pltpu.VMEM((size_b, piece, 128), F32),
            pltpu.VMEM((2, piece, 128), F32),
        ]
        + sems,
        compiler_params=pltpu.CompilerParams(collective_id=collective_id, has_side_effects=True),
    )(x)
    return total[:rows]


def teacher_kernel(
    p_rows, width, above, slab, below, first, second, bypass, inner, mask, out_ref, even, odd, mid
):
    images = slab.shape[1]
    lanes = slab.shape[2]
    m_rows = p_rows + 2
    zero = jnp.zeros((images, 128), BF16)
    for r in range(-3, 2 * p_rows + 2):
        if r < 0:
            source, at = above, r + 3
        elif r < 2 * p_rows:
            source, at = slab, r
        else:
            source, at = below, r - 2 * p_rows
        target, index = (even, r // 2 + 1) if r % 2 == 0 else (odd, (r + 1) // 2 + 1)
        target[index, :, 128 : 128 + lanes] = source[at]
    for i in range(m_rows):
        even[i, :, 0:128] = zero
    for i in range(m_rows + 1):
        odd[i, :, 0:128] = zero
    wide_zero = jnp.zeros((images, CT_OUT), BF16)
    for i in range(m_rows):
        mid[i, :, 0:CT_OUT] = wide_zero
        mid[i, :, (width + 1) * CT_OUT : (width + 2) * CT_OUT] = wide_zero
    scale, shift = inner[0:1], inner[1:2]
    top, bottom = mask[0:1], mask[1:2]

    def first_step(q, carry):
        at = pl.multiple_of(q * 256, 256)
        window = pl.ds(at, 384)
        left = jnp.concatenate(
            [odd[0:m_rows, :, window], even[0:m_rows, :, window], odd[1 : m_rows + 1, :, window]],
            axis=2,
        ).reshape(m_rows * images, 9 * CT_IN)
        z = scale * matmul(left, first[...]) + shift
        act = (z * sigmoid(z)).reshape(m_rows, images, CT_OUT)
        here = pl.ds(pl.multiple_of(at + CT_OUT, 256), CT_OUT)
        mid[0, :, here] = (act[0] * top).astype(BF16)
        mid[1 : p_rows + 1, :, here] = act[1 : p_rows + 1].astype(BF16)
        mid[p_rows + 1, :, here] = (act[p_rows + 1] * bottom).astype(BF16)
        return carry

    lax.fori_loop(0, width, first_step, 0)
    out_ref[...] = jnp.zeros(out_ref.shape, F32)
    lane = lax.broadcasted_iota(jnp.int32, (images, 128), 1)

    def second_step(q, carry):
        at = pl.multiple_of(q * 256, 256)
        window = pl.ds(at, 3 * CT_OUT)
        corner = pl.ds(pl.multiple_of(at + 128, 128), 128)
        left = jnp.concatenate(
            [mid[0:p_rows, :, window], mid[1 : p_rows + 1, :, window], mid[2 : p_rows + 2, :, window]],
            axis=2,
        ).reshape(p_rows * images, 9 * CT_OUT)
        corner_act = even[1 : p_rows + 1, :, corner].reshape(p_rows * images, CT_IN)
        y = matmul(left, second[...]) + matmul(corner_act, bypass[...])
        square = y * y
        energy = jnp.sum(square[:, 0:128] + square[:, 128:256], axis=1, keepdims=True)
        energy = (energy * (1.0 / CT_OUT)).reshape(p_rows, images, 1)
        for p in range(p_rows):
            chunk, start = divmod((p + 1) * width, 128)
            where = slice(chunk * 128, chunk * 128 + 128)
            out_ref[:, where] = jnp.where(lane == start + q, energy[p], out_ref[:, where])
        return carry

    lax.fori_loop(0, width, second_step, 0)


def teacher_energies(above, slab, below, first, second, bypass, inner, mask, tile):
    rows, images, lanes = slab.shape
    p_rows, width = rows // 2, lanes // (2 * CT_IN)
    out_lanes = -(-(p_rows + 3) * width // 128) * 128
    m_rows = p_rows + 2
    whole = lambda a: pl.BlockSpec(a.shape, lambda i: (0,) * a.ndim)
    by_image = lambda a: pl.BlockSpec((a.shape[0], tile, a.shape[2]), lambda i: (0, i, 0))
    positions = images * p_rows * width
    return pl.pallas_call(
        functools.partial(teacher_kernel, p_rows, width),
        grid=(images // tile,),
        in_specs=[by_image(above), by_image(slab), by_image(below)]
        + [whole(a) for a in (first, second, bypass, inner, mask)],
        out_specs=pl.BlockSpec((tile, out_lanes), lambda i: (i, 0)),
        out_shape=jax.ShapeDtypeStruct((images, out_lanes), F32),
        scratch_shapes=[
            pltpu.VMEM((m_rows, tile, 128 + lanes), BF16),
            pltpu.VMEM((m_rows + 1, tile, 128 + lanes), BF16),
            pltpu.VMEM((m_rows, tile, (width + 2) * CT_OUT), BF16),
        ],
        compiler_params=pltpu.CompilerParams(vmem_limit_bytes=VMEM_LIMIT),
        cost_estimate=pl.CostEstimate(
            flops=positions * 2 * CT_OUT * (9 * CT_IN + 9 * CT_OUT + CT_IN),
            bytes_accessed=images * (rows + 5) * lanes * 2,
            transcendentals=positions * CT_OUT,
        ),
    )(above, slab, below, first, second, bypass, inner, mask)


def entry_tables(tot_ref, norm_ref, w0, w1):
    means, scales = group_norms(tot_ref[...], entry_counts(tot_ref), CS_IN)
    scale = per_image(w0, w1, scales)
    shift = per_image(w0, w1, [-m * s for m, s in zip(means, scales)])
    gain, bias = norm_ref[0:1], norm_ref[1:2]
    present = w0 + w1
    return gain * scale, gain * shift + bias * present, scale, shift


def inner_tables(tot_ref, inner_ref, norm_ref, w0, w1):
    means, scales = group_norms(inner_ref[...], inner_counts(tot_ref), CS_OUT)
    scale = per_image(w0, w1, scales)
    shift = per_image(w0, w1, [-m * s for m, s in zip(means, scales)])
    gain, bias = norm_ref[0:1], norm_ref[1:2]
    present = w0 + w1
    return gain * scale, gain * shift + bias * present, scale, shift


def add_rows(ref, value):
    first = pl.program_id(0) == 0

    @pl.when(first)
    def _():
        ref[...] = value

    @pl.when(jnp.logical_not(first))
    def _():
        ref[...] += value


def forward_kernel(
    p_rows, raw, w0_ref, w1_ref, tot, norm, mask, weights, even, odd, out_ref, stats
):
    images, lanes = raw.shape[1:]
    w0, w1 = w0_ref[...], w1_ref[...]
    gain, bias, _, _ = entry_tables(tot, norm, w0, w1)
    gain2, bias2 = twice(gain), twice(bias)
    zero = jnp.zeros((images, 128), BF16)

    def activate(row, target, index):
        keep = twice(mask[pl.ds(row, 1)])
        target[index, :, 0:128] = zero
        for c in range(0, lanes, 256):
            z = raw[row, :, c : c + 256].astype(F32) * gain2 + bias2
            target[index, :, 128 + c : 384 + c] = (z * sigmoid(z) * keep).astype(BF16)

    def pair(i, carry):
        activate(2 * i, even, i)
        activate(2 * i + 1, odd, i)
        return carry

    f_rows = p_rows + 5
    lax.fori_loop(0, f_rows, pair, 0)
    activate(2 * f_rows, even, f_rows)

    def convolve(j, sums):
        window = pl.ds(pl.multiple_of(j * 256, 256), 384)
        left = jnp.concatenate(
            [even[0:f_rows, :, window], odd[0:f_rows, :, window], even[1 : f_rows + 1, :, window]],
            axis=2,
        ).reshape(f_rows * images, 9 * 128)
        y = matmul(left, weights[...]).reshape(f_rows, images, 256)
        out_ref[:, :, pl.ds(pl.multiple_of(j * 256, 256), 256)] = y
        own = y[2 : 2 + p_rows]
        s = jnp.sum(own, axis=0)
        q = jnp.sum(own * own, axis=0)
        return (sums[0] + s[:, 0:128] + s[:, 128:256], sums[1] + q[:, 0:128] + q[:, 128:256])

    blank = jnp.zeros((images, 128), F32)
    s, q = lax.fori_loop(0, lanes // 256, convolve, (blank, blank))
    add_rows(stats, grouped_rows(w0, w1, [s, q]))


def whole_spec(a):
    return pl.BlockSpec(a.shape, lambda i: (0,) * a.ndim)


def image_spec(a, tile):
    return pl.BlockSpec((a.shape[0], tile) + a.shape[2:], lambda i: (0, i) + (0,) * (a.ndim - 2))


def table_spec(a, tile):
    return pl.BlockSpec((tile, a.shape[1]), lambda i: (i, 0))


def shape_of(shape, dtype):
    return jax.ShapeDtypeStruct(shape, dtype)


def student_forward(raw, w0, w1, tot, norm, mask, weights, tile):
    rows, images, lanes = raw.shape
    p_rows = (rows - 11) // 2
    outs = [
        shape_of((p_rows + 6, images, 128 + lanes), BF16),
        shape_of((p_rows + 5, images, 128 + lanes), BF16),
        shape_of((p_rows + 5, images, lanes), F32),
    ]
    return pl.pallas_call(
        functools.partial(forward_kernel, p_rows),
        grid=(images // tile,),
        in_specs=[image_spec(raw, tile), table_spec(w0, tile), table_spec(w1, tile)]
        + [whole_spec(a) for a in (tot, norm, mask, weights)],
        out_specs=[image_spec(o, tile) for o in outs] + [pl.BlockSpec((8, 128), lambda i: (0, 0))],
        out_shape=outs + [shape_of((8, 128), F32)],
        compiler_params=pltpu.CompilerParams(vmem_limit_bytes=VMEM_LIMIT),
    )(raw, w0, w1, tot, norm, mask, weights)


def split_bf16(value):
    high = value.astype(BF16)
    return high, (value - high.astype(F32)).astype(BF16)


def block_kernel(
    p_rows,
    first_ref,
    odd,
    w0_ref,
    w1_ref,
    tot,
    inner,
    norm,
    mask,
    weights,
    spread,
    act,
    sum_ref,
    low_ref,
    energy,
):
    images, lanes = first_ref.shape[1:]
    w0, w1 = w0_ref[...], w1_ref[...]
    gain, bias, _, _ = inner_tables(tot, inner, norm, w0, w1)
    gain2, bias2 = twice(gain), twice(bias)
    zero = jnp.zeros((images, 128), BF16)
    f_rows, b_rows = p_rows + 5, p_rows + 3

    def activate(f, carry):
        keep = twice(mask[pl.ds(f, 1)])
        act[f, :, 0:128] = zero
        act[f, :, 128 + lanes : 256 + lanes] = zero
        for c in range(0, lanes, 256):
            z = first_ref[f, :, c : c + 256] * gain2 + bias2
            act[f, :, 128 + c : 384 + c] = (z * sigmoid(z) * keep).astype(BF16)
        return carry

    lax.fori_loop(0, f_rows, activate, 0)

    def convolve(j, carry):
        at = pl.multiple_of(j * 256, 256)
        window = pl.ds(at, 512)
        here = pl.ds(pl.multiple_of(at + 128, 128), 256)
        left = jnp.concatenate(
            [
                act[0:b_rows, :, window],
                act[1 : b_rows + 1, :, window],
                act[2 : b_rows + 2, :, window],
                odd[1 : b_rows + 1, :, here],
            ],
            axis=2,
        ).reshape(b_rows * images, 1792)
        y = matmul(left, weights[...]).reshape(b_rows, images, 256)
        sum_ref[:, :, pl.ds(at, 256)] = y
        low_ref[:, :, pl.ds(at, 256)] = y[1 : p_rows + 1].astype(BF16)
        return carry

    lax.fori_loop(0, lanes // 256, convolve, 0)
    per_chunk = spread.shape[0]
    energy[...] = jnp.zeros(energy.shape, F32)

    def measure(b, carry):
        v = sum_ref[b]
        high, low = split_bf16(v * v)
        table = spread[lax.rem(b, per_chunk)]
        contract = (((1,), (1,)), ((), ()))
        e = lax.dot_general(high, table, contract, preferred_element_type=F32)
        e = e + lax.dot_general(low, table, contract, preferred_element_type=F32)
        chunk = pl.ds(pl.multiple_of(lax.div(b, per_chunk) * 128, 128), 128)
        energy[:, chunk] += e * (1.0 / CS_OUT)
        return carry

    lax.fori_loop(0, b_rows, measure, 0)


def student_block(first_out, odd, w0, w1, tot, inner, norm, mask, weights, spread, tile):
    rows, images, lanes = first_out.shape
    p_rows = rows - 5
    width = lanes // CS_OUT
    energy_lanes = -(-(p_rows + 3) * width // 128) * 128
    outs = [
        shape_of((p_rows + 5, images, 256 + lanes), BF16),
        shape_of((p_rows + 3, images, lanes), F32),
        shape_of((p_rows, images, lanes), BF16),
    ]
    energy = shape_of((images, energy_lanes), F32)
    return pl.pallas_call(
        functools.partial(block_kernel, p_rows),
        grid=(images // tile,),
        in_specs=[image_spec(first_out, tile), image_spec(odd, tile)]
        + [table_spec(w0, tile), table_spec(w1, tile)]
        + [whole_spec(a) for a in (tot, inner, norm, mask, weights, spread)],
        out_specs=[image_spec(o, tile) for o in outs] + [table_spec(energy, tile)],
        out_shape=outs + [energy],
        compiler_params=pltpu.CompilerParams(vmem_limit_bytes=VMEM_LIMIT),
    )(first_out, odd, w0, w1, tot, inner, norm, mask, weights, spread)


def map_kernel(slabs, group, widths, p_counts, *refs):
    student, teacher, present = refs[0:2], refs[2:4], refs[4:6]
    outs, loss_ref = refs[6:8], refs[8]
    sums, boxes = refs[9:11], refs[11:13]
    from_above, from_below = refs[13:15], refs[15:17]
    send, recv, send_halo, recv_halo = refs[17:21]
    me = lax.axis_index("space")
    z, x = lax.div(me, group), lax.rem(me, group)
    greet_barrier = pltpu.get_barrier_semaphore()
    for d in range(1, slabs):
        pl.semaphore_signal(
            greet_barrier,
            inc=1,
            device_id={"space": lax.rem(z + d, slabs) * group + x},
            device_id_type=MESH,
        )
    pl.semaphore_wait(greet_barrier, slabs - 1)

    def halo_copies(res, direction):
        width, p_rows = widths[res], p_counts[res]
        lane = (p_rows * width if direction == 0 else width) // 128 * 128
        target = (from_above, from_below)[direction][res]
        return pltpu.make_async_remote_copy(
            src_ref=teacher[res].at[:, pl.ds(lane, 128)],
            dst_ref=target,
            send_sem=send_halo.at[2 * res + direction],
            recv_sem=recv_halo.at[2 * res + direction],
            device_id={"space": me + (group if direction == 0 else -group)},
            device_id_type=MESH,
        )

    for res in range(2):
        from_above[res][...] = jnp.zeros(from_above[res].shape, F32)
        from_below[res][...] = jnp.zeros(from_below[res].shape, F32)

    ready = refs[21]

    @pl.when(z > 0)
    def _():
        pl.semaphore_signal(
            ready.at[0], inc=1, device_id={"space": me - group}, device_id_type=MESH
        )

    @pl.when(z < slabs - 1)
    def _():
        pl.semaphore_signal(
            ready.at[1], inc=1, device_id={"space": me + group}, device_id_type=MESH
        )
        pl.semaphore_wait(ready.at[0], 1)
        halo_copies(0, 0).start()
        halo_copies(1, 0).start()

    @pl.when(z > 0)
    def _():
        pl.semaphore_wait(ready.at[1], 1)
        halo_copies(0, 1).start()
        halo_copies(1, 1).start()

    copies = []
    for res in range(2):
        width, p_rows = widths[res], p_counts[res]
        images, lanes = student[res].shape
        lane = lax.broadcasted_iota(jnp.int32, (images, lanes), 1)
        own = jnp.logical_and(lane >= width, lane < (p_rows + 1) * width)
        es = jnp.where(own, student[res][...], 0.0)
        et = jnp.where(own, teacher[res][...], 0.0)
        columns = [
            jnp.sum(v, axis=1, keepdims=True) for v in (es * es, et * et, es * et)
        ]
        small_lane = lax.broadcasted_iota(jnp.int32, (images, 128), 1)
        packed = jnp.zeros((images, 128), F32)
        for k, column in enumerate(columns):
            packed = jnp.where(small_lane == k, column, packed)
        padded = sums[res].shape[1]
        packed = jnp.concatenate([packed, jnp.zeros((padded - images, 128), F32)], axis=0)
        sums[res][...] = packed.T[0:8]
        for d in range(1, slabs):
            copy = pltpu.make_async_remote_copy(
                src_ref=sums[res],
                dst_ref=boxes[res].at[d],
                send_sem=send.at[res * slabs + d],
                recv_sem=recv.at[res * slabs + d],
                device_id={"space": lax.rem(z + d, slabs) * group + x},
                device_id_type=MESH,
            )
            copy.start()
            copies.append(copy)
    for copy in copies:
        copy.wait()

    @pl.when(z < slabs - 1)
    def _():
        halo_copies(0, 0).wait_send()
        halo_copies(1, 0).wait_send()
        halo_copies(0, 1).wait_recv()
        halo_copies(1, 1).wait_recv()

    @pl.when(z > 0)
    def _():
        halo_copies(0, 1).wait_send()
        halo_copies(1, 1).wait_send()
        halo_copies(0, 0).wait_recv()
        halo_copies(1, 0).wait_recv()

    loss = jnp.zeros((1, 128), F32)
    for res in range(2):
        width, p_rows = widths[res], p_counts[res]
        images, lanes = student[res].shape
        total = sums[res][...]
        for d in range(1, slabs):
            total = total + boxes[res][d]
        padded = total.shape[1]
        total = jnp.concatenate([total, jnp.zeros((120, padded), F32)], axis=0).T[0:images]
        ss, tt, st = total[:, 0:1], total[:, 1:2], total[:, 2:3]
        scale_s = lax.rsqrt(ss + 1e-12)
        scale_t = lax.rsqrt(tt + 1e-12)
        pulled = TRANSFER_WEIGHT * scale_s * (scale_s * ss - scale_t * st)
        lane = lax.broadcasted_iota(jnp.int32, (images, lanes), 1)
        shift = p_rows * width
        chunks = lanes // 128
        first_rows = from_below[res][...]
        last_rows = from_above[res][...]
        if shift % 128:
            first_rows = pltpu.roll(first_rows, shift % 128, 1)
            last_rows = pltpu.roll(last_rows, 128 - shift % 128, 1)
        blank = jnp.zeros((images, 128), F32)
        before = [last_rows] + [blank] * (chunks - 1)
        after = [blank] * (chunks - 1) + [first_rows]
        before = jnp.concatenate(before, axis=1) if chunks > 1 else before[0]
        after = jnp.concatenate(after, axis=1) if chunks > 1 else after[0]
        et = jnp.where(lane < width, before, teacher[res][...])
        et = jnp.where(lane >= (p_rows + 1) * width, after, et)
        u = student[res][...] * scale_s
        difference = u - et * scale_t
        own = jnp.logical_and(lane >= width, lane < (p_rows + 1) * width)
        squares = jnp.where(own, difference * difference, 0.0)
        kept = present[res][...]
        for c in range(chunks):
            loss = loss + jnp.sum(squares[:, c * 128 : c * 128 + 128] * kept, axis=0, keepdims=True)
        outs[res][...] = (TRANSFER_WEIGHT * difference - u * pulled) * (scale_s * (2.0 / CS_OUT))
    loss_ref[...] = jnp.concatenate(
        [loss * (TRANSFER_WEIGHT / 2), jnp.zeros((7, 128), F32)], axis=0
    )


def attention_maps(student, teacher, present, widths, p_counts, slabs, group, collective_id):
    padded = [-(-s.shape[0] // 128) * 128 for s in student]
    images = [s.shape[0] for s in student]
    vmem = pl.BlockSpec(memory_space=pltpu.VMEM)
    return pl.pallas_call(
        functools.partial(map_kernel, slabs, group, widths, p_counts),
        out_shape=[shape_of(s.shape, F32) for s in student] + [shape_of((8, 128), F32)],
        in_specs=[vmem] * 6,
        out_specs=[vmem] * 3,
        scratch_shapes=[pltpu.VMEM((8, n), F32) for n in padded]
        + [pltpu.VMEM((slabs, 8, n), F32) for n in padded]
        + [pltpu.VMEM((n, 128), F32) for n in images] * 2
        + [pltpu.SemaphoreType.DMA((2 * slabs,))] * 2
        + [pltpu.SemaphoreType.DMA((4,))] * 2
        + [pltpu.SemaphoreType.REGULAR((2,))],
        compiler_params=pltpu.CompilerParams(collective_id=collective_id, has_side_effects=True),
    )(*student, *teacher, *present)


def back_kernel(
    p_rows,
    sum_ref,
    cot,
    factor,
    spread,
    first_ref,
    act,
    odd,
    w0_ref,
    w1_ref,
    tot,
    inner,
    norm,
    mask,
    weights,
    flow_ref,
    grad,
    kernel_ref,
    stats,
):
    images, lanes = sum_ref.shape[1:]
    w0, w1 = w0_ref[...], w1_ref[...]
    gain, bias, scale, shift = inner_tables(tot, inner, norm, w0, w1)
    gain2, bias2, scale2, shift2 = twice(gain), twice(bias), twice(scale), twice(shift)
    zero = jnp.zeros((images, 128), BF16)
    b_rows, k_rows = p_rows + 3, p_rows + 1
    per_chunk = spread.shape[0]

    def block_grad(b, carry):
        keep = twice(mask[pl.ds(b, 1)])
        chunk = pl.ds(pl.multiple_of(lax.div(b, per_chunk) * 128, 128), 128)
        high, low = split_bf16(factor[:, chunk])
        table = spread[lax.rem(b, per_chunk)]
        wide = matmul(high, table) + matmul(low, table)
        grad[b, :, 0:128] = zero
        grad[b, :, 128 + lanes : 256 + lanes] = zero
        for c in range(0, lanes, 256):
            v = cot[b, :, c : c + 256].astype(F32) + wide[:, c : c + 256] * sum_ref[b, :, c : c + 256]
            grad[b, :, 128 + c : 384 + c] = (v * keep).astype(BF16)
        return carry

    lax.fori_loop(0, b_rows, block_grad, 0)

    @pl.when(pl.program_id(0) == 0)
    def _():
        kernel_ref[...] = jnp.zeros(kernel_ref.shape, F32)

    def step(j, sums):
        at = pl.multiple_of(j * 256, 256)
        window = pl.ds(at, 512)
        here = pl.ds(pl.multiple_of(at + 128, 128), 256)
        left = jnp.concatenate(
            [
                grad[0:k_rows, :, window],
                grad[1 : k_rows + 1, :, window],
                grad[2 : k_rows + 2, :, window],
            ],
            axis=2,
        ).reshape(k_rows * images, 1536)
        y = matmul(left, weights[...]).reshape(k_rows, images, 256)
        ones, cross = sums
        for k in range(k_rows):
            x = first_ref[k + 2, :, pl.ds(at, 256)]
            z = x * gain2 + bias2
            s = sigmoid(z)
            flow = y[k] * (s * (1.0 + z * (1.0 - s)))
            flow_ref[k, :, pl.ds(at, 256)] = flow
            if k < p_rows:
                crossed = flow * (x * scale2 + shift2)
                ones = ones + flow[:, 0:128] + flow[:, 128:256]
                cross = cross + crossed[:, 0:128] + crossed[:, 128:256]
        right = jnp.concatenate(
            [
                act[1 : p_rows + 1, :, window],
                act[2 : p_rows + 2, :, window],
                act[3 : p_rows + 3, :, window],
                odd[2 : p_rows + 2, :, here],
            ],
            axis=2,
        ).reshape(p_rows * images, 1792)
        own = grad[1 : p_rows + 1, :, here].reshape(p_rows * images, 256)
        kernel_ref[...] += lax.dot_general(
            own, right, (((0,), (0,)), ((), ())), preferred_element_type=F32
        )
        return ones, cross

    blank = jnp.zeros((images, 128), F32)
    ones, cross = lax.fori_loop(0, lanes // 256, step, (blank, blank))
    add_rows(stats, grouped_rows(w0, w1, [ones, cross]))


def student_back(
    block_sum, cot, factor, spread, first_out, act, odd, w0, w1, tot, inner, norm, mask, weights, tile
):
    rows, images, lanes = block_sum.shape
    p_rows = rows - 3
    outs = [
        shape_of((p_rows + 1, images, lanes), F32),
        shape_of((p_rows + 3, images, 256 + lanes), BF16),
    ]
    kernels = shape_of((256, 1792), F32)
    stats = shape_of((8, 128), F32)
    return pl.pallas_call(
        functools.partial(back_kernel, p_rows),
        grid=(images // tile,),
        in_specs=[image_spec(block_sum, tile), image_spec(cot, tile), table_spec(factor, tile)]
        + [whole_spec(spread), image_spec(first_out, tile), image_spec(act, tile)]
        + [image_spec(odd, tile), table_spec(w0, tile), table_spec(w1, tile)]
        + [whole_spec(a) for a in (tot, inner, norm, mask, weights)],
        out_specs=[image_spec(o, tile) for o in outs] + [whole_spec(kernels), whole_spec(stats)],
        out_shape=outs + [kernels, stats],
        compiler_params=pltpu.CompilerParams(vmem_limit_bytes=VMEM_LIMIT),
    )(block_sum, cot, factor, spread, first_out, act, odd, w0, w1, tot, inner, norm, mask, weights)


def entry_kernel(
    p_rows,
    flow_ref,
    first_ref,
    grad,
    even,
    odd,
    raw,
    w0_ref,
    w1_ref,
    tot,
    inner,
    pulled,
    norm_in,
    norm,
    mask,
    weights_even,
    weights_odd,
    out_ref,
    kernel_ref,
    stats,
    first_grad,
):
    images, lanes = first_ref.shape[1:]
    w0, w1 = w0_ref[...], w1_ref[...]
    gain, _, scale, shift = inner_tables(tot, inner, norm, w0, w1)
    counts = inner_counts(tot)
    folded = fold(pulled[...], CS_OUT)
    ones_mean = per_image(w0, w1, [folded[g : g + 1] / counts[g] for g in range(2)])
    cross_mean = per_image(w0, w1, [folded[2 + g : 3 + g] / counts[g] for g in range(2)])
    gain2, scale2, shift2 = twice(gain), twice(scale), twice(shift)
    ones2, cross2 = twice(ones_mean), twice(cross_mean)
    zero = jnp.zeros((images, 128), BF16)

    def first_rows(k, carry):
        keep = twice(mask[pl.ds(k, 1)])
        first_grad[k, :, lanes : lanes + 128] = zero
        for c in range(0, lanes, 256):
            normed = first_ref[k + 2, :, c : c + 256] * scale2 + shift2
            v = gain2 * (flow_ref[k, :, c : c + 256] - ones2 - normed * cross2)
            first_grad[k, :, c : c + 256] = (v * keep).astype(BF16)
        return carry

    lax.fori_loop(0, p_rows + 1, first_rows, 0)

    @pl.when(pl.program_id(0) == 0)
    def _():
        kernel_ref[...] = jnp.zeros(kernel_ref.shape, F32)

    gain, bias, scale, shift = entry_tables(tot, norm_in, w0, w1)
    gain2, bias2, scale2, shift2 = twice(gain), twice(bias), twice(scale), twice(shift)

    def step(j, sums):
        at = pl.multiple_of(j * 256, 256)
        window = pl.ds(at, 384)
        here = pl.ds(at, 256)
        middle = pl.ds(pl.multiple_of(at + 128, 128), 256)
        upper = first_grad[0:p_rows, :, window].reshape(p_rows * images, 384)
        lower = first_grad[1 : p_rows + 1, :, window].reshape(p_rows * images, 384)
        block = grad[1 : p_rows + 1, :, middle].reshape(p_rows * images, 256)
        rows_even = matmul(jnp.concatenate([upper, block], axis=1), weights_even[...])
        rows_odd = matmul(jnp.concatenate([upper, lower], axis=1), weights_odd[...])
        ones, cross = sums
        for parity, rows in enumerate((rows_even, rows_odd)):
            low = rows.astype(BF16).reshape(p_rows, images, 256)
            for p in range(p_rows):
                out_ref[2 * p + parity, :, here] = low[p]
                x = raw[2 * p + parity + 5, :, here].astype(F32)
                z = x * gain2 + bias2
                s = sigmoid(z)
                flow = low[p].astype(F32) * (s * (1.0 + z * (1.0 - s)))
                crossed = flow * (x * scale2 + shift2)
                ones = ones + flow[:, 0:128] + flow[:, 128:256]
                cross = cross + crossed[:, 0:128] + crossed[:, 128:256]
        right = jnp.concatenate(
            [
                even[2 : p_rows + 2, :, window],
                odd[2 : p_rows + 2, :, window],
                even[3 : p_rows + 3, :, window],
            ],
            axis=2,
        ).reshape(p_rows * images, 1152)
        own = first_grad[0:p_rows, :, here].reshape(p_rows * images, 256)
        kernel_ref[...] += lax.dot_general(
            own, right, (((0,), (0,)), ((), ())), preferred_element_type=F32
        )
        return ones, cross

    blank = jnp.zeros((images, 128), F32)
    ones, cross = lax.fori_loop(0, lanes // 256, step, (blank, blank))
    add_rows(stats, grouped_rows(w0, w1, [ones, cross]))


def student_entry(
    flow, first_out, grad, even, odd, raw, w0, w1, tot, inner, pulled, norm_in, norm, mask,
    weights_even, weights_odd, tile,
):
    rows, images, lanes = flow.shape
    p_rows = rows - 1
    out = shape_of((2 * p_rows, images, lanes), BF16)
    kernels = shape_of((256, 1152), F32)
    stats = shape_of((8, 128), F32)
    big = (flow, first_out, grad, even, odd, raw)
    shared = (tot, inner, pulled, norm_in, norm, mask, weights_even, weights_odd)
    return pl.pallas_call(
        functools.partial(entry_kernel, p_rows),
        grid=(images // tile,),
        in_specs=[image_spec(a, tile) for a in big]
        + [table_spec(w0, tile), table_spec(w1, tile)]
        + [whole_spec(a) for a in shared],
        out_specs=[image_spec(out, tile), whole_spec(kernels), whole_spec(stats)],
        out_shape=[out, kernels, stats],
        scratch_shapes=[pltpu.VMEM((p_rows + 1, tile, 128 + lanes), BF16)],
        compiler_params=pltpu.CompilerParams(vmem_limit_bytes=VMEM_LIMIT),
    )(*big, w0, w1, *shared)


def select(entries, shape):
    table = np.zeros(shape, np.float32)
    for index in entries:
        table[index] = 1.0
    return jnp.asarray(table, BF16)


def banded(selection, taps):
    k, n, b = selection.shape
    _, r, c = taps.shape
    out = jnp.einsum("knb,brc->krnc", selection, taps, preferred_element_type=F32)
    return out.astype(BF16).reshape(k * r, n * c)


def first_bands(kernel):
    pick = select([(2 * q + b + 3, q, b) for q in range(4) for b in range(3)], (12, 4, 3))
    return jnp.concatenate([banded(pick, kernel[a]) for a in range(3)], axis=0)


def second_bands(kernel, shortcut):
    pick = select([(q + b + 1, q, b) for q in range(4) for b in range(3)], (8, 4, 3))
    corner = select([(2 * q, q, 0) for q in range(4)], (8, 4, 1))
    return jnp.concatenate(
        [banded(pick, kernel[a]) for a in range(3)] + [banded(corner, shortcut[None])], axis=0
    )


def second_back_bands(kernel):
    pick = select([(s - b + 3, s, b) for s in range(4) for b in range(3)], (8, 4, 3))
    turned = jnp.swapaxes(kernel, 2, 3)
    return jnp.concatenate([banded(pick, turned[2 - d]) for d in range(3)], axis=0)


def first_back_bands(kernel, shortcut):
    entries = []
    for q in range(6):
        for b in range(3):
            s = 2 * q + b - 1
            if 0 <= s < 8:
                entries.append((q, s, b))
    pick = select(entries, (6, 8, 3))
    corner = select([(q, 2 * q, 0) for q in range(4)], (4, 8, 1))
    turned = jnp.swapaxes(kernel, 2, 3)
    rows_even = jnp.concatenate(
        [banded(pick, turned[1]), banded(corner, jnp.swapaxes(shortcut, 0, 1)[None])], axis=0
    )
    rows_odd = jnp.concatenate([banded(pick, turned[2]), banded(pick, turned[0])], axis=0)
    return rows_even, rows_odd


def spread_table(width):
    lanes = width * CS_OUT
    count = min(128 // width, 8)
    lane = lax.broadcasted_iota(jnp.int32, (count, 128, lanes), 1)
    column = lax.broadcasted_iota(jnp.int32, (count, 128, lanes), 2) // CS_OUT
    row = lax.broadcasted_iota(jnp.int32, (count, 128, lanes), 0)
    return (lane == row * width + column).astype(BF16)


def second_from_products(products):
    main = products[:, 0:1536].reshape(4, CS_OUT, 3, 8, CS_OUT)
    taps = []
    for b in range(3):
        taps.append(sum(main[q, :, :, q + b + 1] for q in range(4)))
    second = jnp.transpose(jnp.stack(taps), (2, 0, 3, 1))
    side = products[:, 1536:].reshape(4, CS_OUT, 8, CS_IN)
    shortcut = jnp.transpose(sum(side[q, :, 2 * q] for q in range(4)))
    return second, shortcut


def first_from_products(products):
    main = products.reshape(4, CS_OUT, 3, 12, CS_IN)
    taps = []
    for b in range(3):
        taps.append(sum(main[q, :, :, 2 * q + b + 3] for q in range(4)))
    return jnp.transpose(jnp.stack(taps), (2, 0, 3, 1))


def renew(weights, gradient, moment, average, factor):
    descent = gradient + WEIGHT_DECAY * weights
    velocity = MOMENTUM * moment + descent
    updated = weights - factor * (descent + MOMENTUM * velocity)
    smoothed = AVERAGING * average + (1.0 - AVERAGING) * updated
    return (gradient, velocity, smoothed, updated)


def body(
    space,
    batch,
    small_in,
    large_in,
    small_teacher,
    large_teacher,
    small_groups,
    large_groups,
    small_cot,
    large_cot,
    teacher_gains,
    teacher_first,
    teacher_inner,
    teacher_second,
    teacher_bypass,
    entry_norm,
    first_conv,
    inner_norm,
    second_conv,
    shortcut,
    momentum_entry,
    momentum_first,
    momentum_inner,
    momentum_second,
    momentum_shortcut,
    average_entry,
    average_first,
    average_inner,
    average_second,
    average_shortcut,
):
    slabs = SLABS
    group = space // slabs
    axes = (("space", space), ("batch", batch))
    me = lax.axis_index("space")
    z, x = me // group, me % group
    total_positions = batch * (small_in.shape[0] * SIDE * SIDE // 4 + large_in.shape[0] * SIDE * SIDE)
    pixels = [small_in, large_in]
    teachers = [small_teacher, large_teacher]
    labels = [small_groups, large_groups]
    cots = [small_cot, large_cot]
    sides = [SIDE, 2 * SIDE]
    per_device = [p.shape[0] // space for p in pixels]
    local_rows = [p.shape[1] for p in pixels]
    images = [slabs * n for n in per_device]
    padded = [-(-n // 16) * 16 for n in images]
    tiles = [32 if padded[0] % 32 == 0 else 16, padded[1]]
    p_counts = [s // (2 * slabs) for s in sides]
    widths = [s // 2 for s in sides]

    def to_sub(d):
        return [(k, k // group * group + (k % group + d) % group) for k in range(space)]

    def to_slab(d):
        return [(k, (k // group + d) % slabs * group + k % group) for k in range(space)]

    def down():
        return [(k, k + group) for k in range(space - group)]

    def up():
        return [(k, k - group) for k in range(group, space)]

    def pick_images(array, res, sub):
        n, rows, lanes = array.shape
        parts = array.reshape(slabs, group, per_device[res], rows, lanes)
        part = lax.dynamic_index_in_dim(parts, sub, 1, False)
        return jnp.transpose(part.reshape(images[res], rows, lanes), (1, 0, 2))

    def gather_rows(pieces):
        if group == 1:
            return pieces[0]
        ordered = [lax.select_n((x - s) % group, *pieces) for s in range(group)]
        return jnp.concatenate(ordered, axis=0)

    def exchange_rows(array, res):
        pieces = [pick_images(array, res, x)]
        for d in range(1, group):
            pieces.append(
                lax.ppermute(pick_images(array, res, (x + d) % group), "space", to_sub(d))
            )
        return gather_rows(pieces)

    def pad_images(array, res):
        extra = padded[res] - images[res]
        return jnp.pad(array, ((0, 0), (0, extra), (0, 0))) if extra else array

    def halos(slab, res, above, below):
        return (
            lax.ppermute(slab[slab.shape[0] - above :], "space", down()),
            lax.ppermute(slab[:below], "space", up()),
        )

    weights = []
    for res in range(2):
        mine = lax.dynamic_index_in_dim(
            labels[res].reshape(slabs, group, per_device[res]), x, 1, False
        ).reshape(images[res])
        mine = jnp.pad(mine, (0, padded[res] - images[res]), constant_values=-1)
        weights.append(
            [
                jnp.broadcast_to((mine == g).astype(F32)[:, None], (padded[res], 128))
                for g in range(2)
            ]
        )
    present = [w[0] + w[1] for w in weights]

    top = (z > 0).astype(F32)
    bottom = (z < slabs - 1).astype(F32)

    def row_mask(first, count, inside):
        row = lax.broadcasted_iota(jnp.int32, (-(-count // 8) * 8, 128), 0) + first
        return jnp.where(row < 0, top, jnp.where(row >= inside, bottom, 1.0))

    tile_norm = lambda n: jnp.pad(jnp.tile(n, (1, 128 // n.shape[1])), ((0, 6), (0, 0)))
    norm_in, norm_mid = tile_norm(entry_norm), tile_norm(inner_norm)
    first_low = first_conv.astype(BF16)
    second_low = second_conv.astype(BF16)
    shortcut_low = shortcut.astype(BF16)
    bands_first = first_bands(first_low)
    bands_second = second_bands(second_low, shortcut_low)
    bands_second_back = second_back_bands(second_low)
    bands_even, bands_odd = first_back_bands(first_low, shortcut_low)
    spreads = [spread_table(w) for w in widths]

    slabs_in = [exchange_rows(pixels[res], res) for res in range(2)]
    raw = []
    for res in range(2):
        above, below = halos(slabs_in[res], res, 5, 6)
        raw.append(pad_images(jnp.concatenate([above, slabs_in[res], below], axis=0), res))
    unpadded = [[w[: images[res]] for w in weights[res]] for res in range(2)]
    entry_sums = input_stats(slabs_in, unpadded)
    entry_total = total_over_devices([entry_sums], axes, 0)

    cot_rows = []
    for res in range(2):
        c = jnp.pad(jnp.transpose(cots[res], (1, 0, 2)), ((1, 2), (0, 0), (0, 0)))
        count = p_counts[res] + 3
        pieces = []
        for d in range(slabs):
            part = lax.dynamic_slice_in_dim(c, (z + d) % slabs * p_counts[res], count, 0)
            pieces.append(lax.ppermute(part, "space", to_slab(d)) if d else part)
        ordered = [lax.select_n((z - s) % slabs, *pieces) for s in range(slabs)]
        cot_rows.append(pad_images(jnp.concatenate(ordered, axis=1), res))

    evens, odds, firsts, first_sums = [], [], [], []
    for res in range(2):
        even, odd, first, sums = student_forward(
            raw[res],
            *weights[res],
            entry_total,
            norm_in,
            row_mask(-5, 2 * p_counts[res] + 11, 2 * p_counts[res]),
            bands_first,
            tiles[res],
        )
        evens.append(even)
        odds.append(odd)
        firsts.append(first)
        first_sums.append(sums)
    inner_total = total_over_devices(first_sums, axes, 1)
    acts, sums_out, lows, energies = [], [], [], []
    for res in range(2):
        act, block_sum, low, energy = student_block(
            firsts[res],
            odds[res],
            *weights[res],
            entry_total,
            inner_total,
            norm_mid,
            row_mask(-2, p_counts[res] + 5, p_counts[res]),
            bands_second,
            spreads[res],
            tiles[res],
        )
        acts.append(act)
        sums_out.append(block_sum)
        lows.append(low)
        energies.append(energy)
    block_outs = []
    for res in range(2):
        low = lows[res][:, : images[res]]
        rows, _, lanes = low.shape
        low = low.reshape(rows, slabs, per_device[res], lanes)
        pieces = []
        for d in range(slabs):
            part = lax.dynamic_index_in_dim(low, (z + d) % slabs, 1, False)
            pieces.append(lax.ppermute(part, "space", to_slab(d)) if d else part)
        ordered = [lax.select_n((z - s) % slabs, *pieces) for s in range(slabs)]
        block_outs.append(jnp.transpose(jnp.concatenate(ordered, axis=0), (1, 0, 2)))

    mask_mid = jnp.zeros((8, CT_OUT), F32).at[0].set(top).at[1].set(bottom)
    first_t = teacher_first.reshape(9 * CT_IN, CT_OUT)
    second_t = teacher_second.reshape(9 * CT_OUT, CT_OUT)
    teacher_maps = []
    for res in range(2):
        lanes = teachers[res].shape[2]
        gain = jnp.tile(teacher_gains[0], lanes // CT_IN)
        bias = jnp.tile(teacher_gains[1], lanes // CT_IN)
        active = jax.nn.silu(gain * teachers[res].astype(F32) + bias).astype(BF16)
        slab = exchange_rows(active, res)
        above, below = halos(slab, res, 3, 2)
        args = [pad_images(a, res) for a in (above, slab, below)]
        teacher_maps.append(
            teacher_energies(
                *args,
                first_t,
                second_t,
                teacher_bypass,
                jnp.pad(teacher_inner, ((0, 6), (0, 0))),
                mask_mid,
                tiles[0] if res == 0 else 16,
            )
        )
    factors = attention_maps(
        energies, teacher_maps, present, widths, p_counts, slabs, group, 2
    )
    loss_sums = factors[2]

    flows, grads, products, flow_sums = [], [], [], []
    for res in range(2):
        flow, grad, product, sums = student_back(
            sums_out[res],
            cot_rows[res],
            factors[res],
            spreads[res],
            firsts[res],
            acts[res],
            odds[res],
            *weights[res],
            entry_total,
            inner_total,
            norm_mid,
            row_mask(-1, p_counts[res] + 3, p_counts[res]),
            bands_second_back,
            tiles[res],
        )
        flows.append(flow)
        grads.append(grad)
        products.append(product)
        flow_sums.append(sums)
    flow_total = total_over_devices(flow_sums, axes, 3)
    entry_rows, first_products, entry_flow_sums = [], [], []
    for res in range(2):
        rows, product, sums = student_entry(
            flows[res],
            firsts[res],
            grads[res],
            evens[res],
            odds[res],
            raw[res],
            *weights[res],
            entry_total,
            inner_total,
            flow_total,
            norm_in,
            norm_mid,
            row_mask(0, p_counts[res] + 1, p_counts[res]),
            bands_even,
            bands_odd,
            tiles[res],
        )
        first_products.append(product)
        entry_flow_sums.append(sums)
        rows = rows[:, : images[res]]
        pieces = []
        for d in range(group):
            part = lax.dynamic_slice_in_dim(
                rows, (x + d) % group * local_rows[res], local_rows[res], 0
            )
            pieces.append(lax.ppermute(part, "space", to_sub(d)) if d else part)
        ordered = [lax.select_n((x - s) % group, *pieces) for s in range(group)]
        count, _, lanes = ordered[0].shape
        arrived = jnp.stack(ordered).reshape(group, count, slabs, per_device[res], lanes)
        entry_rows.append(
            jnp.transpose(arrived, (2, 0, 3, 1, 4)).reshape(-1, count, lanes)
        )

    second_part, shortcut_part = second_from_products(products[0] + products[1])
    first_part = first_from_products(first_products[0] + first_products[1])
    packed = jnp.concatenate(
        [
            first_part.reshape(-1, 128),
            second_part.reshape(-1, 128),
            shortcut_part.reshape(-1, 128),
            entry_flow_sums[0] + entry_flow_sums[1],
            loss_sums,
        ],
        axis=0,
    )
    packed = spread_sum(packed, axes, 4)
    sizes = [9 * CS_IN * CS_OUT // 128, 9 * CS_OUT * CS_OUT // 128, CS_IN * CS_OUT // 128, 8, 8]
    ends = np.cumsum(sizes)
    first_grads = packed[: ends[0]].reshape(3, 3, CS_IN, CS_OUT)
    second_grads = packed[ends[0] : ends[1]].reshape(3, 3, CS_OUT, CS_OUT)
    shortcut_grads = packed[ends[1] : ends[2]].reshape(CS_IN, CS_OUT)
    entry_pulled = packed[ends[2] : ends[3]].reshape(8, 128 // CS_IN, CS_IN).sum(axis=1)
    total_loss = jnp.sum(packed[ends[3]])

    entry_counts_ = entry_total[4:6, 0:1]
    entry_folded = entry_total.reshape(8, 128 // CS_IN, CS_IN).sum(axis=1)
    mean_entry = entry_folded[0:2] / entry_counts_
    scale_entry = lax.rsqrt(entry_folded[2:4] / entry_counts_ - mean_entry * mean_entry + EPSILON)
    ones_entry, cross_entry = entry_pulled[0:2], entry_pulled[2:4]
    inner_folded = flow_total.reshape(8, 128 // CS_OUT, CS_OUT).sum(axis=1)
    ones_inner, cross_inner = inner_folded[0:2], inner_folded[2:4]

    input_grads = []
    for res in range(2):
        n, rows, lanes = pixels[res].shape
        repeat = lanes // CS_IN
        one = (labels[res] == 1)[:, None]

        def by_image(pair):
            return jnp.tile(jnp.where(one, pair[1][None], pair[0][None]), (1, repeat))[:, None, :]

        scale = by_image(scale_entry)
        shift = by_image(-mean_entry * scale_entry)
        gain_row = jnp.tile(entry_norm[0], repeat)
        bias_row = jnp.tile(entry_norm[1], repeat)
        normed = pixels[res].astype(F32) * scale + shift
        before = gain_row * normed + bias_row
        s = jax.nn.sigmoid(before)
        flow = entry_rows[res].astype(F32) * (s * (1.0 + before * (1.0 - s)))
        input_grads.append(
            gain_row
            * scale
            * (
                flow
                - by_image(ones_entry / entry_counts_)
                - normed * by_image(cross_entry / entry_counts_)
            )
        )

    entry_grads = jnp.stack([jnp.sum(cross_entry, axis=0), jnp.sum(ones_entry, axis=0)])
    inner_grads = jnp.stack([jnp.sum(cross_inner, axis=0), jnp.sum(ones_inner, axis=0)])
    rate_scale = 1.0 / math.sqrt(total_positions)
    entry_state = renew(entry_norm, entry_grads, momentum_entry, average_entry, NORM_RATE * rate_scale)
    first_state = renew(first_conv, first_grads, momentum_first, average_first, CONV_RATE * rate_scale)
    inner_state = renew(inner_norm, inner_grads, momentum_inner, average_inner, NORM_RATE * rate_scale)
    second_state = renew(
        second_conv, second_grads, momentum_second, average_second, CONV_RATE * rate_scale
    )
    bypass_state = renew(
        shortcut, shortcut_grads, momentum_shortcut, average_shortcut, CONV_RATE * rate_scale
    )
    return (
        block_outs[0],
        block_outs[1],
        input_grads[0],
        input_grads[1],
        total_loss / total_positions,
        *entry_state,
        *first_state,
        first_state[3].astype(BF16),
        *inner_state,
        *second_state,
        second_state[3].astype(BF16),
        *bypass_state,
        bypass_state[3].astype(BF16),
    )


def solution(mesh):
    rows = P("batch", "space", None)
    blocks = P(("batch", "space"), None, None)
    return jax.shard_map(
        functools.partial(body, mesh.shape["space"], mesh.shape["batch"]),
        mesh=mesh,
        in_specs=(rows,) * 4 + (P("batch"),) * 2 + (blocks,) * 2 + (P(),) * 20,
        out_specs=(blocks,) * 2 + (rows,) * 2 + (P(),) * 24,
        check_vma=False,
    )
```

```python
import functools
import math

import jax
import jax.numpy as jnp
import numpy as np
from jax import lax
from jax.experimental import pallas as pl
from jax.experimental.pallas import tpu as pltpu
from jax.sharding import PartitionSpec as P

CS_IN = 32
CS_OUT = 64
CT_IN = 128
CT_OUT = 256
SIDE = 32
SLABS = 4

EPSILON = 1e-05
TRANSFER_WEIGHT = 1000.0
MOMENTUM = 0.9
WEIGHT_DECAY = 0.0005
AVERAGING = 0.7
CONV_RATE = 0.06
NORM_RATE = 0.3

F32 = jnp.float32
BF16 = jnp.bfloat16
MESH = pl.DeviceIdType.MESH
VMEM_LIMIT = 56 << 20


def sigmoid(z):
    return 0.5 * jnp.tanh(0.5 * z) + 0.5


def matmul(a, b):
    return jnp.dot(a, b, preferred_element_type=F32)


def after(value, *others):
    return lax.optimization_barrier((value, others))[0]


def cost(microseconds):
    return pl.CostEstimate(
        flops=int(microseconds * 1e9), bytes_accessed=1 << 20, transcendentals=0
    )


def stacked(first, count, images, rows, parts):
    blocks = []
    for t in range(count):
        at = (first + t) * 256
        pieces = [ref[lo : lo + rows, :, at + off : at + off + size] for ref, lo, off, size in parts]
        block = jnp.concatenate(pieces, axis=2) if len(pieces) > 1 else pieces[0]
        blocks.append(block.reshape(rows * images, block.shape[2]))
    return jnp.concatenate(blocks, axis=0) if count > 1 else blocks[0]


def fold(rows, width):
    shift = width
    while shift < 128:
        rows = rows + pltpu.roll(rows, shift, 1)
        shift *= 2
    return rows


def group_norms(totals, counts, width):
    folded = fold(totals, width)
    means, scales = [], []
    for g in range(2):
        mean = folded[g : g + 1] / counts[g]
        variance = folded[2 + g : 3 + g] / counts[g] - mean * mean
        means.append(mean)
        scales.append(lax.rsqrt(variance + EPSILON))
    return means, scales


def per_image(w0, w1, pair):
    return w0 * pair[0] + w1 * pair[1]


def twice(table):
    return jnp.concatenate([table, table], axis=1)


def grouped_rows(w0, w1, values):
    rows = []
    for v in values:
        rows.append(jnp.sum(v * w0, axis=0, keepdims=True))
        rows.append(jnp.sum(v * w1, axis=0, keepdims=True))
    rows.append(jnp.zeros((8 - len(rows), 128), F32))
    return jnp.concatenate(rows, axis=0)


def entry_counts(tot_ref):
    return [tot_ref[4:5], tot_ref[5:6]]


def inner_counts(tot_ref):
    return [tot_ref[4:5] * 0.25, tot_ref[5:6] * 0.25]


def stats_kernel(x_refs, label_refs, out_ref):
    step = pl.program_id(0)
    total = jnp.zeros((8, 128), F32)
    for x_ref, label_ref in zip(x_refs, label_refs):
        rows, images, lanes = x_ref.shape
        s = jnp.zeros((images, 128), F32)
        q = jnp.zeros((images, 128), F32)
        for r in range(rows):
            for c in range(0, lanes, 128):
                v = x_ref[r, :, c : c + 128].astype(F32)
                s = s + v
                q = q + v * v
        w0, w1 = indicators(label_ref)
        positions = jnp.full((images, 128), float(rows * lanes // CS_IN), F32)
        total = total + grouped_rows(w0, w1, [s, q, positions])

    @pl.when(step == 0)
    def _():
        out_ref[...] = total

    @pl.when(step > 0)
    def _():
        out_ref[...] += total


def input_stats(pieces, tables):
    steps = min(4, min(x.shape[0] for x in pieces))
    count = len(pieces)

    def kernel(*refs):
        stats_kernel(refs[:count], refs[count:-1], refs[-1])

    specs = [
        pl.BlockSpec((x.shape[0] // steps,) + x.shape[1:], lambda i: (i, 0, 0)) for x in pieces
    ]
    specs += [pl.BlockSpec(w.shape, lambda i: (0, 0)) for w in tables]
    return pl.pallas_call(
        kernel,
        grid=(steps,),
        in_specs=specs,
        out_specs=pl.BlockSpec((8, 128), lambda i: (0, 0)),
        out_shape=jax.ShapeDtypeStruct((8, 128), F32),
        compiler_params=pltpu.CompilerParams(vmem_limit_bytes=VMEM_LIMIT),
        cost_estimate=cost(5),
    )(*pieces, *tables)


def greet(axes):
    barrier = pltpu.get_barrier_semaphore()
    expected = 0
    for name, size in axes:
        me = lax.axis_index(name)
        for d in range(1, size):
            pl.semaphore_signal(
                barrier,
                inc=1,
                device_id={name: lax.rem(me + d, size)},
                device_id_type=MESH,
            )
            expected += 1
    pl.semaphore_wait(barrier, expected)


def total_kernel(axes, count, *refs):
    parts = refs[:count]
    out_ref, held, boxes_a, boxes_b, send_a, recv_a, send_b, recv_b = refs[count:]
    value = parts[0][...]
    for part in parts[1:]:
        value = value + part[...]
    held[0] = value
    greet(axes)
    for level, ((name, size), boxes, send, recv) in enumerate(
        zip(axes, (boxes_a, boxes_b), (send_a, send_b), (recv_a, recv_b))
    ):
        me = lax.axis_index(name)
        copies = []
        for d in range(1, size):
            copy = pltpu.make_async_remote_copy(
                src_ref=held.at[level],
                dst_ref=boxes.at[d],
                send_sem=send.at[d],
                recv_sem=recv.at[d],
                device_id={name: lax.rem(me + d, size)},
                device_id_type=MESH,
            )
            copy.start()
            copies.append(copy)
        for copy in copies:
            copy.wait_recv()
        value = jnp.zeros(value.shape, F32)
        for source in range(size):
            back = lax.rem(me - source + size, size)
            value = value + jnp.where(
                back == 0, held[level], boxes[jnp.maximum(back, 1)]
            )
        for copy in copies:
            copy.wait_send()
        if level == 0:
            held[1] = value
        else:
            out_ref[...] = value


def total_over_devices(parts, axes, collective_id):
    shape = parts[0].shape
    return pl.pallas_call(
        functools.partial(total_kernel, axes, len(parts)),
        out_shape=jax.ShapeDtypeStruct(shape, F32),
        in_specs=[pl.BlockSpec(memory_space=pltpu.VMEM)] * len(parts),
        out_specs=pl.BlockSpec(memory_space=pltpu.VMEM),
        scratch_shapes=[
            pltpu.VMEM((2,) + shape, F32),
            pltpu.VMEM((axes[0][1],) + shape, F32),
            pltpu.VMEM((axes[1][1],) + shape, F32),
            pltpu.SemaphoreType.DMA((axes[0][1],)),
            pltpu.SemaphoreType.DMA((axes[0][1],)),
            pltpu.SemaphoreType.DMA((axes[1][1],)),
            pltpu.SemaphoreType.DMA((axes[1][1],)),
        ],
        compiler_params=pltpu.CompilerParams(collective_id=collective_id, has_side_effects=True),
        cost_estimate=cost(12),
    )(*parts)


def spread_sum_kernel(axes, layout, *refs):
    count = sum(len(parts) for parts in layout)
    inputs, out_ref, x_ref, boxes_a, boxes_b, held = refs[:count], *refs[count : count + 5]
    send_a, recv_a, send_b, recv_b, send_c, recv_c = refs[count + 5 :]
    at = 0
    for parts in layout:
        value = inputs[parts[0]][...]
        for k in parts[1:]:
            value = value + inputs[k][...]
        if value.shape[1] == 64:
            half = value.shape[0] // 2
            value = jnp.concatenate([value[:half], value[half:]], axis=1)
        x_ref[at : at + value.shape[0]] = value
        at += value.shape[0]
    if at < x_ref.shape[0]:
        x_ref[at:] = jnp.zeros((x_ref.shape[0] - at, 128), F32)
    (name_a, size_a), (name_b, size_b) = axes
    me_a, me_b = lax.axis_index(name_a), lax.axis_index(name_b)
    piece = x_ref.shape[0] // size_a
    greet(axes)

    def rows(index):
        return pl.ds(pl.multiple_of(index * piece, 8), piece)

    copies = []
    for d in range(1, size_a):
        peer = lax.rem(me_a + d, size_a)
        copy = pltpu.make_async_remote_copy(
            src_ref=x_ref.at[rows(peer)],
            dst_ref=boxes_a.at[d],
            send_sem=send_a.at[d],
            recv_sem=recv_a.at[d],
            device_id={name_a: peer},
            device_id_type=MESH,
        )
        copy.start()
        copies.append(copy)
    value = x_ref[rows(me_a)]
    for d in range(1, size_a):
        copies[d - 1].wait_recv()
        value = value + boxes_a[d]
    held[0] = value
    for copy in copies:
        copy.wait_send()
    copies = []
    for d in range(1, size_b):
        copy = pltpu.make_async_remote_copy(
            src_ref=held.at[0],
            dst_ref=boxes_b.at[d],
            send_sem=send_b.at[d],
            recv_sem=recv_b.at[d],
            device_id={name_b: lax.rem(me_b + d, size_b)},
            device_id_type=MESH,
        )
        copy.start()
        copies.append(copy)
    for copy in copies:
        copy.wait_recv()
    value = jnp.zeros(value.shape, F32)
    for source in range(size_b):
        back = lax.rem(me_b - source + size_b, size_b)
        value = value + jnp.where(back == 0, held[0], boxes_b[jnp.maximum(back, 1)])
    held[1] = value
    out_ref[rows(me_a)] = value
    for copy in copies:
        copy.wait_send()
    copies = []
    for d in range(1, size_a):
        copy = pltpu.make_async_remote_copy(
            src_ref=held.at[1],
            dst_ref=out_ref.at[rows(me_a)],
            send_sem=send_c.at[d],
            recv_sem=recv_c.at[d],
            device_id={name_a: lax.rem(me_a + d, size_a)},
            device_id_type=MESH,
        )
        copy.start()
        copies.append(copy)
    for copy in copies:
        copy.wait()


def spread_sum(groups, axes, collective_id):
    (_, size_a), (_, size_b) = axes
    arrays, layout, rows = [], [], []
    for members in groups:
        layout.append(tuple(range(len(arrays), len(arrays) + len(members))))
        arrays += members
        rows.append(members[0].shape[0] * members[0].shape[1] // 128)
    padded = -(-sum(rows) // (8 * size_a)) * 8 * size_a
    piece = padded // size_a
    sems = []
    for size in (size_a, size_b, size_a):
        sems += [pltpu.SemaphoreType.DMA((size,))] * 2
    total = pl.pallas_call(
        functools.partial(spread_sum_kernel, axes, tuple(layout)),
        out_shape=jax.ShapeDtypeStruct((padded, 128), F32),
        in_specs=[pl.BlockSpec(memory_space=pltpu.VMEM)] * len(arrays),
        out_specs=pl.BlockSpec(memory_space=pltpu.VMEM),
        scratch_shapes=[
            pltpu.VMEM((padded, 128), F32),
            pltpu.VMEM((size_a, piece, 128), F32),
            pltpu.VMEM((size_b, piece, 128), F32),
            pltpu.VMEM((2, piece, 128), F32),
        ]
        + sems,
        compiler_params=pltpu.CompilerParams(collective_id=collective_id, has_side_effects=True),
        cost_estimate=cost(20),
    )(*arrays)
    ends = np.cumsum(rows)
    return [total[e - n : e] for e, n in zip(ends, rows)]


def teacher_kernel(p_rows, width, group, columns, place, *refs):
    pieces, refs = refs[:group], refs[group:]
    above, below, first, second, bypass, inner, out_ref, even, odd, mid = refs
    local, lanes = pieces[0].shape[0], pieces[0].shape[-1]
    real, images = above.shape[1], even.shape[1]
    m_rows = p_rows + 2
    zero = jnp.zeros((images, 128), BF16)

    def put(row, source, at):
        if row % 2 == 0:
            even[row // 2 + 1, 0:real, 128 : 128 + lanes] = source[at]
        else:
            odd[(row + 1) // 2 + 1, 0:real, 128 : 128 + lanes] = source[at]

    for k in range(3):
        put(k - 3, above, k)
    for k in range(2):
        put(2 * p_rows + k, below, k)
    x = place[0]
    for s in range(group):
        distance = lax.rem(x - s + group, group)
        for d in range(group):

            @pl.when(distance == d)
            def _():
                for k in range(local):
                    at = (k, 0, 0) if len(pieces[d].shape) == 5 else k
                    put(s * local + k, pieces[d], at)

    for i in range(m_rows):
        even[i, :, 0:128] = zero
    for i in range(m_rows + 1):
        odd[i, :, 0:128] = zero
    wide_zero = jnp.zeros((images, CT_OUT), BF16)
    for i in range(m_rows):
        mid[i, :, 0:CT_OUT] = wide_zero
        mid[i, :, (width + 1) * CT_OUT : (width + 2) * CT_OUT] = wide_zero
    scale, shift = inner[0:1], inner[1:2]
    top, bottom = keep_row(place, -1, p_rows), keep_row(place, p_rows, p_rows)

    def first_step(g, carry):
        lefts = []
        for t in range(columns):
            window = pl.ds(pl.multiple_of((g * columns + t) * 256, 256), 384)
            parts = [odd[0:m_rows, :, window], even[0:m_rows, :, window]]
            parts.append(odd[1 : m_rows + 1, :, window])
            lefts.append(jnp.concatenate(parts, axis=2).reshape(m_rows * images, 9 * CT_IN))
        z = scale * matmul(jnp.concatenate(lefts, axis=0), first[...]) + shift
        act = (z * sigmoid(z)).reshape(columns, m_rows, images, CT_OUT)
        for t in range(columns):
            here = pl.ds(pl.multiple_of((g * columns + t + 1) * CT_OUT, 256), CT_OUT)
            mid[0, :, here] = (act[t, 0] * top).astype(BF16)
            mid[1 : p_rows + 1, :, here] = act[t, 1 : p_rows + 1].astype(BF16)
            mid[p_rows + 1, :, here] = (act[t, p_rows + 1] * bottom).astype(BF16)
        return carry

    lax.fori_loop(0, width // columns, first_step, 0)
    out_ref[...] = jnp.zeros(out_ref.shape, F32)
    lane = lax.broadcasted_iota(jnp.int32, (real, 128), 1)

    def second_step(g, carry):
        lefts, corners = [], []
        for t in range(columns):
            at = pl.multiple_of((g * columns + t) * 256, 256)
            window = pl.ds(at, 3 * CT_OUT)
            corner = pl.ds(pl.multiple_of(at + 128, 128), 128)
            parts = [mid[a : a + p_rows, :, window] for a in range(3)]
            lefts.append(jnp.concatenate(parts, axis=2).reshape(p_rows * images, 9 * CT_OUT))
            corners.append(even[1 : p_rows + 1, :, corner].reshape(p_rows * images, CT_IN))
        y = matmul(jnp.concatenate(lefts, axis=0), second[...])
        y = y + matmul(jnp.concatenate(corners, axis=0), bypass[...])
        square = y * y
        energy = jnp.sum(square[:, 0:128] + square[:, 128:256], axis=1, keepdims=True)
        energy = (energy * (1.0 / CT_OUT)).reshape(columns, p_rows, images, 1)
        for t in range(columns):
            for p in range(p_rows):
                chunk, start = divmod((p + 1) * width, 128)
                where = slice(chunk * 128, chunk * 128 + 128)
                here = lane == start + g * columns + t
                out_ref[:, where] = jnp.where(here, energy[t, p, 0:real], out_ref[:, where])
        return carry

    lax.fori_loop(0, width // columns, second_step, 0)


def teacher_energies(place, own, slab, received, above, below, shared, tile):
    group = len(received) + 1
    local, lanes = own.shape[0], own.shape[-1]
    images = above.shape[1]
    p_rows, width = group * local // 2, lanes // (2 * CT_IN)
    out_lanes = -(-(p_rows + 3) * width // 128) * 128
    m_rows = p_rows + 2
    space = -(-tile // 16) * 16
    if own.ndim == 5:
        own_spec = pl.BlockSpec(
            (local, 1, 1, tile, lanes), lambda i, place: (0, slab, place[0], i, 0)
        )
    else:
        own_spec = pl.BlockSpec((local, tile, lanes), lambda i, place: (0, i, 0))
    whole = lambda a: pl.BlockSpec(a.shape, lambda i, place: (0,) * a.ndim)
    by_image = lambda a: pl.BlockSpec((a.shape[0], tile, a.shape[2]), lambda i, place: (0, i, 0))
    grid_spec = pltpu.PrefetchScalarGridSpec(
        num_scalar_prefetch=1,
        grid=(images // tile,),
        in_specs=[own_spec]
        + [by_image(a) for a in received]
        + [by_image(above), by_image(below)]
        + [whole(a) for a in shared],
        out_specs=pl.BlockSpec((tile, out_lanes), lambda i, place: (i, 0)),
        scratch_shapes=[
            pltpu.VMEM((m_rows, space, 128 + lanes), BF16),
            pltpu.VMEM((m_rows + 1, space, 128 + lanes), BF16),
            pltpu.VMEM((m_rows, space, (width + 2) * CT_OUT), BF16),
        ],
    )
    return pl.pallas_call(
        functools.partial(teacher_kernel, p_rows, width, group, 4),
        grid_spec=grid_spec,
        out_shape=jax.ShapeDtypeStruct((images, out_lanes), F32),
        compiler_params=pltpu.CompilerParams(vmem_limit_bytes=VMEM_LIMIT),
        cost_estimate=cost(40 * images * p_rows * width / 10240),
    )(place, own, *received, above, below, *shared)


def entry_tables(tot_ref, norm_ref, w0, w1):
    means, scales = group_norms(tot_ref[...], entry_counts(tot_ref), CS_IN)
    scale = per_image(w0, w1, scales)
    shift = per_image(w0, w1, [-m * s for m, s in zip(means, scales)])
    gain, bias = norm_ref[0:1], norm_ref[1:2]
    present = w0 + w1
    return gain * scale, gain * shift + bias * present, scale, shift


def inner_tables(tot_ref, inner_ref, norm_ref, w0, w1):
    means, scales = group_norms(inner_ref[...], inner_counts(tot_ref), CS_OUT)
    scale = per_image(w0, w1, scales)
    shift = per_image(w0, w1, [-m * s for m, s in zip(means, scales)])
    gain, bias = norm_ref[0:1], norm_ref[1:2]
    present = w0 + w1
    return gain * scale, gain * shift + bias * present, scale, shift


def indicators(label_ref):
    label = label_ref[...]
    return (label == 0.0).astype(F32), (label == 1.0).astype(F32)


def keep_row(place, row, inside):
    z = place[1]
    outside = jnp.logical_or(
        jnp.logical_and(row < 0, z == 0), jnp.logical_and(row >= inside, z == SLABS - 1)
    )
    return jnp.where(outside, 0.0, 1.0)


def add_rows(ref, value):
    first = pl.program_id(0) == 0

    @pl.when(first)
    def _():
        ref[...] = value

    @pl.when(jnp.logical_not(first))
    def _():
        ref[...] += value


def forward_kernel(
    p_rows, group, blocks, place, *refs
):
    pieces, refs = refs[:group], refs[group:]
    above, below, label_ref, tot, norm, weights = refs[:6]
    raw, even, odd, out_ref, stats = refs[6:]
    images, lanes = raw.shape[1:]
    local = pieces[0].shape[0]
    w0, w1 = indicators(label_ref)
    gain, bias, _, _ = entry_tables(tot, norm, w0, w1)
    gain2, bias2 = twice(gain), twice(bias)
    zero = jnp.zeros((images, 128), BF16)
    raw[0:5] = above[...]
    raw[2 * p_rows + 5 : 2 * p_rows + 11] = below[...]
    x = place[0]
    for s in range(group):
        distance = lax.rem(x - s + group, group)
        for d in range(group):

            @pl.when(distance == d)
            def _():
                raw[5 + s * local : 5 + (s + 1) * local] = pieces[d][...]

    def activate(row, target, index):
        keep = keep_row(place, row - 5, 2 * p_rows)
        target[index, :, 0:128] = zero
        for c in range(0, lanes, 256):
            z = raw[row, :, c : c + 256].astype(F32) * gain2 + bias2
            target[index, :, 128 + c : 384 + c] = (z * sigmoid(z) * keep).astype(BF16)

    def pair(i, carry):
        activate(2 * i, even, i)
        activate(2 * i + 1, odd, i)
        return carry

    f_rows = p_rows + 5
    lax.fori_loop(0, f_rows, pair, 0)
    activate(2 * f_rows, even, f_rows)
    s = jnp.zeros((images, 128), F32)
    q = jnp.zeros((images, 128), F32)
    for j in range(0, lanes // 256, blocks):
        left = stacked(
            j, blocks, images, f_rows, [(even, 0, 0, 384), (odd, 0, 0, 384), (even, 1, 0, 384)]
        )
        y = matmul(left, weights[...]).reshape(blocks, f_rows, images, 256)
        for t in range(blocks):
            out_ref[:, :, (j + t) * 256 : (j + t + 1) * 256] = y[t]
            own = y[t, 2 : 2 + p_rows]
            u = jnp.sum(own, axis=0)
            v = jnp.sum(own * own, axis=0)
            s = s + u[:, 0:128] + u[:, 128:256]
            q = q + v[:, 0:128] + v[:, 128:256]
    add_rows(stats, grouped_rows(w0, w1, [s, q]))


def whole_spec(a):
    return pl.BlockSpec(a.shape, lambda i, *_: (0,) * len(a.shape))


def image_spec(a, tile):
    return pl.BlockSpec((a.shape[0], tile, a.shape[2]), lambda i, *_: (0, i, 0))


def table_spec(a, tile):
    return pl.BlockSpec((tile, a.shape[1]), lambda i, *_: (i, 0))


def shape_of(shape, dtype):
    return jax.ShapeDtypeStruct(shape, dtype)


def student_forward(place, pieces, above, below, label, tot, norm, weights, tile):
    group = len(pieces)
    local, images, lanes = pieces[0].shape
    p_rows = group * local // 2
    outs = [
        shape_of((2 * p_rows + 11, images, lanes), BF16),
        shape_of((p_rows + 6, images, 128 + lanes), BF16),
        shape_of((p_rows + 5, images, 128 + lanes), BF16),
        shape_of((p_rows + 5, images, lanes), F32),
    ]
    stats = shape_of((8, 128), F32)
    big = (*pieces, above, below)
    shared = (tot, norm, weights)
    grid_spec = pltpu.PrefetchScalarGridSpec(
        num_scalar_prefetch=1,
        grid=(images // tile,),
        in_specs=[image_spec(a, tile) for a in big]
        + [table_spec(label, tile)]
        + [whole_spec(a) for a in shared],
        out_specs=[image_spec(o, tile) for o in outs] + [whole_spec(stats)],
    )
    return pl.pallas_call(
        functools.partial(forward_kernel, p_rows, group, 4),
        grid_spec=grid_spec,
        out_shape=outs + [stats],
        compiler_params=pltpu.CompilerParams(vmem_limit_bytes=VMEM_LIMIT),
        cost_estimate=cost(15),
    )(place, *big, label, *shared)


def split_bf16(value):
    high = value.astype(BF16)
    return high, (value - high.astype(F32)).astype(BF16)


def block_kernel(
    p_rows,
    blocks,
    place,
    first_ref,
    odd,
    label_ref,
    tot,
    inner,
    norm,
    weights,
    spread,
    act,
    sum_ref,
    low_ref,
    energy,
):
    images, lanes = first_ref.shape[1:]
    w0, w1 = indicators(label_ref)
    gain, bias, _, _ = inner_tables(tot, inner, norm, w0, w1)
    gain2, bias2 = twice(gain), twice(bias)
    zero = jnp.zeros((images, 128), BF16)
    f_rows, b_rows = p_rows + 5, p_rows + 3

    def activate(f, carry):
        keep = keep_row(place, f - 2, p_rows)
        act[f, :, 0:128] = zero
        act[f, :, 128 + lanes : 256 + lanes] = zero
        for c in range(0, lanes, 256):
            z = first_ref[f, :, c : c + 256] * gain2 + bias2
            act[f, :, 128 + c : 384 + c] = (z * sigmoid(z) * keep).astype(BF16)
        return carry

    lax.fori_loop(0, f_rows, activate, 0)

    per_chunk = 128 // (lanes // CS_OUT)
    chunks = energy.shape[1] // 128
    measured = [jnp.zeros((images, 128), F32) for _ in range(chunks)]
    for j in range(0, lanes // 256, blocks):
        parts = [(act, a, 0, 512) for a in range(3)] + [(odd, 1, 128, 256)]
        left = stacked(j, blocks, images, b_rows, parts)
        flat = matmul(left, weights[...])
        y = flat.reshape(blocks, b_rows, images, 256)
        high, low = split_bf16(flat * flat)
        e = matmul(jnp.concatenate([high, low], axis=1), spread[...])
        e = e.reshape(blocks, b_rows, images, 128)
        for t in range(blocks):
            here = slice((j + t) * 256, (j + t + 1) * 256)
            sum_ref[:, :, here] = y[t]
            low_ref[:, :, here] = y[t, 1 : p_rows + 1].astype(BF16)
            for b in range(b_rows):
                shift = b % per_chunk * (128 // per_chunk) + 4 * (j + t)
                part = pltpu.roll(e[t, b], shift, 1) if shift else e[t, b]
                measured[b // per_chunk] = measured[b // per_chunk] + part
    for c in range(chunks):
        energy[:, c * 128 : c * 128 + 128] = measured[c]


def student_block(place, first_out, odd, label, tot, inner, norm, weights, spread, tile):
    rows, images, lanes = first_out.shape
    p_rows = rows - 5
    width = lanes // CS_OUT
    energy_lanes = -(-(p_rows + 3) * width // 128) * 128
    outs = [
        shape_of((p_rows + 5, images, 256 + lanes), BF16),
        shape_of((p_rows + 3, images, lanes), F32),
        shape_of((p_rows, images, lanes), BF16),
    ]
    energy = shape_of((images, energy_lanes), F32)
    return pl.pallas_call(
        functools.partial(block_kernel, p_rows, 4),
        grid_spec=pltpu.PrefetchScalarGridSpec(
            num_scalar_prefetch=1,
            grid=(images // tile,),
            in_specs=[image_spec(first_out, tile), image_spec(odd, tile), table_spec(label, tile)]
            + [whole_spec(a) for a in (tot, inner, norm, weights, spread)],
            out_specs=[image_spec(o, tile) for o in outs] + [table_spec(energy, tile)],
        ),
        out_shape=outs + [energy],
        compiler_params=pltpu.CompilerParams(vmem_limit_bytes=VMEM_LIMIT),
        cost_estimate=cost(18),
    )(place, first_out, odd, label, tot, inner, norm, weights, spread)


def map_kernel(slabs, group, widths, p_counts, pieces, *refs):
    student, present = refs[0:2], refs[2:4]
    given = refs[4 : 4 + sum(pieces)]
    refs = refs[4 + sum(pieces) :]
    outs, loss_ref = refs[0:2], refs[2]
    teacher, sums, boxes = refs[3:5], refs[5:7], refs[7:9]
    from_above, from_below = refs[9:11], refs[11:13]
    send, recv, send_halo, recv_halo, ready = refs[13:]
    for res in range(2):
        at = 0
        for part in given[res * pieces[0] : res * pieces[0] + pieces[res]]:
            teacher[res][at : at + part.shape[0]] = part[...]
            at += part.shape[0]
    me = lax.axis_index("space")
    z, x = lax.div(me, group), lax.rem(me, group)
    greet_barrier = pltpu.get_barrier_semaphore()
    for d in range(1, slabs):
        pl.semaphore_signal(
            greet_barrier,
            inc=1,
            device_id={"space": lax.rem(z + d, slabs) * group + x},
            device_id_type=MESH,
        )
    pl.semaphore_wait(greet_barrier, slabs - 1)

    def halo_copies(res, direction):
        width, p_rows = widths[res], p_counts[res]
        lane = (p_rows * width if direction == 0 else width) // 128 * 128
        target = (from_above, from_below)[direction][res]
        return pltpu.make_async_remote_copy(
            src_ref=teacher[res].at[:, pl.ds(lane, 128)],
            dst_ref=target,
            send_sem=send_halo.at[2 * res + direction],
            recv_sem=recv_halo.at[2 * res + direction],
            device_id={"space": me + (group if direction == 0 else -group)},
            device_id_type=MESH,
        )

    for res in range(2):
        from_above[res][...] = jnp.zeros(from_above[res].shape, F32)
        from_below[res][...] = jnp.zeros(from_below[res].shape, F32)

    @pl.when(z > 0)
    def _():
        pl.semaphore_signal(
            ready.at[0], inc=1, device_id={"space": me - group}, device_id_type=MESH
        )

    @pl.when(z < slabs - 1)
    def _():
        pl.semaphore_signal(
            ready.at[1], inc=1, device_id={"space": me + group}, device_id_type=MESH
        )
        pl.semaphore_wait(ready.at[0], 1)
        halo_copies(0, 0).start()
        halo_copies(1, 0).start()

    @pl.when(z > 0)
    def _():
        pl.semaphore_wait(ready.at[1], 1)
        halo_copies(0, 1).start()
        halo_copies(1, 1).start()

    copies = []
    for res in range(2):
        width, p_rows = widths[res], p_counts[res]
        images, lanes = student[res].shape
        lane = lax.broadcasted_iota(jnp.int32, (images, lanes), 1)
        own = jnp.logical_and(lane >= width, lane < (p_rows + 1) * width)
        es = jnp.where(own, student[res][...], 0.0)
        et = jnp.where(own, teacher[res][...], 0.0)
        columns = [
            jnp.sum(v, axis=1, keepdims=True) for v in (es * es, et * et, es * et)
        ]
        small_lane = lax.broadcasted_iota(jnp.int32, (images, 128), 1)
        packed = jnp.zeros((images, 128), F32)
        for k, column in enumerate(columns):
            packed = jnp.where(small_lane == k, column, packed)
        padded = sums[res].shape[1]
        packed = jnp.concatenate([packed, jnp.zeros((padded - images, 128), F32)], axis=0)
        sums[res][...] = packed.T[0:8]
        for d in range(1, slabs):
            copy = pltpu.make_async_remote_copy(
                src_ref=sums[res],
                dst_ref=boxes[res].at[d],
                send_sem=send.at[res * slabs + d],
                recv_sem=recv.at[res * slabs + d],
                device_id={"space": lax.rem(z + d, slabs) * group + x},
                device_id_type=MESH,
            )
            copy.start()
            copies.append(copy)
    for copy in copies:
        copy.wait()

    @pl.when(z < slabs - 1)
    def _():
        halo_copies(0, 0).wait_send()
        halo_copies(1, 0).wait_send()
        halo_copies(0, 1).wait_recv()
        halo_copies(1, 1).wait_recv()

    @pl.when(z > 0)
    def _():
        halo_copies(0, 1).wait_send()
        halo_copies(1, 1).wait_send()
        halo_copies(0, 0).wait_recv()
        halo_copies(1, 0).wait_recv()

    loss = jnp.zeros((1, 128), F32)
    for res in range(2):
        width, p_rows = widths[res], p_counts[res]
        images, lanes = student[res].shape
        total = sums[res][...]
        for d in range(1, slabs):
            total = total + boxes[res][d]
        padded = total.shape[1]
        total = jnp.concatenate([total, jnp.zeros((120, padded), F32)], axis=0).T[0:images]
        ss, tt, st = total[:, 0:1], total[:, 1:2], total[:, 2:3]
        scale_s = lax.rsqrt(ss + 1e-12)
        scale_t = lax.rsqrt(tt + 1e-12)
        pulled = TRANSFER_WEIGHT * scale_s * (scale_s * ss - scale_t * st)
        lane = lax.broadcasted_iota(jnp.int32, (images, lanes), 1)
        shift = p_rows * width
        chunks = lanes // 128
        first_rows = from_below[res][...]
        last_rows = from_above[res][...]
        if shift % 128:
            first_rows = pltpu.roll(first_rows, shift % 128, 1)
            last_rows = pltpu.roll(last_rows, 128 - shift % 128, 1)
        blank = jnp.zeros((images, 128), F32)
        before = [last_rows] + [blank] * (chunks - 1)
        after = [blank] * (chunks - 1) + [first_rows]
        before = jnp.concatenate(before, axis=1) if chunks > 1 else before[0]
        after = jnp.concatenate(after, axis=1) if chunks > 1 else after[0]
        et = jnp.where(lane < width, before, teacher[res][...])
        et = jnp.where(lane >= (p_rows + 1) * width, after, et)
        u = student[res][...] * scale_s
        difference = u - et * scale_t
        own = jnp.logical_and(lane >= width, lane < (p_rows + 1) * width)
        squares = jnp.where(own, difference * difference, 0.0)
        kept = (present[res][...] >= 0.0).astype(F32)
        for c in range(chunks):
            loss = loss + jnp.sum(squares[:, c * 128 : c * 128 + 128] * kept, axis=0, keepdims=True)
        factor = (TRANSFER_WEIGHT * difference - u * pulled) * (scale_s * (2.0 / CS_OUT))
        for c in range(chunks):
            here = slice(c * 128, c * 128 + 128)
            outs[res][:, here] = jnp.where(kept > 0.0, factor[:, here], 0.0)
    loss_ref[...] = jnp.concatenate(
        [loss * (TRANSFER_WEIGHT / 2), jnp.zeros((7, 128), F32)], axis=0
    )


def attention_maps(student, teacher, present, widths, p_counts, slabs, group, collective_id):
    padded = [-(-s.shape[0] // 128) * 128 for s in student]
    images = [s.shape[0] for s in student]
    vmem = pl.BlockSpec(memory_space=pltpu.VMEM)
    return pl.pallas_call(
        functools.partial(
            map_kernel, slabs, group, widths, p_counts, tuple(len(t) for t in teacher)
        ),
        out_shape=[shape_of(s.shape, F32) for s in student] + [shape_of((8, 128), F32)],
        in_specs=[vmem] * (4 + sum(len(t) for t in teacher)),
        out_specs=[vmem] * 3,
        scratch_shapes=[pltpu.VMEM(s.shape, F32) for s in student]
        + [pltpu.VMEM((8, n), F32) for n in padded]
        + [pltpu.VMEM((slabs, 8, n), F32) for n in padded]
        + [pltpu.VMEM((n, 128), F32) for n in images] * 2
        + [pltpu.SemaphoreType.DMA((2 * slabs,))] * 2
        + [pltpu.SemaphoreType.DMA((4,))] * 2
        + [pltpu.SemaphoreType.REGULAR((2,))],
        compiler_params=pltpu.CompilerParams(collective_id=collective_id, has_side_effects=True),
        cost_estimate=cost(11),
    )(*student, *present, *teacher[0], *teacher[1])


def back_kernel(
    p_rows,
    blocks,
    place,
    sum_ref,
    cot,
    factor,
    spread,
    first_ref,
    act,
    odd,
    label_ref,
    tot,
    inner,
    norm,
    weights,
    flow_ref,
    grad,
    stats,
    second_ref,
    shortcut_ref,
    kernel_ref,
):
    images, lanes = sum_ref.shape[1:]
    w0, w1 = indicators(label_ref)
    gain, bias, scale, shift = inner_tables(tot, inner, norm, w0, w1)
    gain2, bias2, scale2, shift2 = twice(gain), twice(bias), twice(scale), twice(shift)
    zero = jnp.zeros((images, 128), BF16)
    b_rows, k_rows = p_rows + 3, p_rows + 1
    width = lanes // CS_OUT
    per_chunk = 128 // width
    for b in range(b_rows):
        grad[b, :, 0:128] = zero
        grad[b, :, 128 + lanes : 256 + lanes] = zero
    halves = [split_bf16(factor[:, c * 128 : c * 128 + 128]) for c in range(factor.shape[1] // 128)]
    halves = [[h.astype(F32) for h in pair] for pair in halves]
    for j in range(0, lanes // 256, blocks):
        rows = []
        for t in range(blocks):
            for b in range(b_rows):
                shift = (128 - (b % per_chunk * width + 4 * (j + t))) % 128
                pair = halves[b // per_chunk]
                if shift:
                    pair = [pltpu.roll(h, shift, 1) for h in pair]
                rows.append(jnp.concatenate(pair, axis=1))
        wide = matmul(jnp.concatenate(rows, axis=0).astype(BF16), spread[...])
        wide = wide.reshape(blocks, b_rows, images, 256)
        for t in range(blocks):
            at = (j + t) * 256
            for b in range(b_rows):
                keep = keep_row(place, b - 1, p_rows)
                v = cot[b, :, at : at + 256].astype(F32) + wide[t, b] * sum_ref[b, :, at : at + 256]
                grad[b, :, 128 + at : 384 + at] = (v * keep).astype(BF16)

    @pl.when(pl.program_id(0) == 0)
    def _():
        kernel_ref[...] = jnp.zeros(kernel_ref.shape, F32)

    ones = jnp.zeros((images, 128), F32)
    cross = jnp.zeros((images, 128), F32)
    for j in range(0, lanes // 256, blocks):
        left = stacked(j, blocks, images, k_rows, [(grad, d, 0, 512) for d in range(3)])
        y = matmul(left, weights[...]).reshape(blocks, k_rows, images, 256)
        for t in range(blocks):
            here = slice((j + t) * 256, (j + t + 1) * 256)
            for k in range(k_rows):
                x = first_ref[k + 2, :, here]
                z = x * gain2 + bias2
                s = sigmoid(z)
                flow = y[t, k] * (s * (1.0 + z * (1.0 - s)))
                flow_ref[k, :, here] = flow
                if k < p_rows:
                    crossed = flow * (x * scale2 + shift2)
                    ones = ones + flow[:, 0:128] + flow[:, 128:256]
                    cross = cross + crossed[:, 0:128] + crossed[:, 128:256]
        right = stacked(
            j,
            blocks,
            images,
            p_rows,
            [(act, a, 0, 512) for a in range(1, 4)] + [(odd, 2, 128, 256)],
        )
        own = stacked(j, blocks, images, p_rows, [(grad, 1, 128, 256)])
        kernel_ref[...] += lax.dot_general(
            own, right, (((0,), (0,)), ((), ())), preferred_element_type=F32
        )
    add_rows(stats, grouped_rows(w0, w1, [ones, cross]))

    @pl.when(pl.program_id(0) == pl.num_programs(0) - 1)
    def _():
        turned = kernel_ref[...].T
        for a in range(3):
            for b in range(3):
                tap = jnp.zeros((CS_OUT, CS_OUT), F32)
                for q in range(4):
                    row = a * 512 + (q + b + 1) * CS_OUT
                    tap = tap + turned[row : row + CS_OUT, q * CS_OUT : (q + 1) * CS_OUT]
                row = (3 * a + b) * CS_OUT
                second_ref[row : row + CS_OUT] = tap
        tap = jnp.zeros((CS_IN, CS_OUT), F32)
        for q in range(4):
            row = 1536 + 2 * q * CS_IN
            tap = tap + turned[row : row + CS_IN, q * CS_OUT : (q + 1) * CS_OUT]
        shortcut_ref[...] = tap


def student_back(
    place, block_sum, cot, factor, spread, first_out, act, odd, label, tot, inner, norm, weights, tile
):
    rows, images, lanes = block_sum.shape
    p_rows = rows - 3
    outs = [
        shape_of((p_rows + 1, images, lanes), F32),
        shape_of((p_rows + 3, images, 256 + lanes), BF16),
    ]
    stats = shape_of((8, 128), F32)
    second = shape_of((9 * CS_OUT, CS_OUT), F32)
    shortcut = shape_of((CS_IN, CS_OUT), F32)
    return pl.pallas_call(
        functools.partial(back_kernel, p_rows, 4),
        grid_spec=pltpu.PrefetchScalarGridSpec(
            num_scalar_prefetch=1,
            grid=(images // tile,),
            in_specs=[image_spec(block_sum, tile), image_spec(cot, tile), table_spec(factor, tile)]
            + [whole_spec(spread), image_spec(first_out, tile), image_spec(act, tile)]
            + [image_spec(odd, tile), table_spec(label, tile)]
            + [whole_spec(a) for a in (tot, inner, norm, weights)],
            out_specs=[image_spec(o, tile) for o in outs]
            + [whole_spec(a) for a in (stats, second, shortcut)],
            scratch_shapes=[pltpu.VMEM((256, 1792), F32)],
        ),
        out_shape=outs + [stats, second, shortcut],
        compiler_params=pltpu.CompilerParams(vmem_limit_bytes=VMEM_LIMIT),
        cost_estimate=cost(18),
    )(place, block_sum, cot, factor, spread, first_out, act, odd, label, tot, inner, norm, weights)


def entry_kernel(
    p_rows,
    blocks,
    place,
    flow_ref,
    first_ref,
    grad,
    even,
    odd,
    raw,
    label_ref,
    tot,
    inner,
    pulled,
    norm_in,
    norm,
    weights_even,
    weights_odd,
    out_ref,
    taps_ref,
    stats,
    first_grad,
    kernel_ref,
):
    images, lanes = first_ref.shape[1:]
    w0, w1 = indicators(label_ref)
    gain, _, scale, shift = inner_tables(tot, inner, norm, w0, w1)
    counts = inner_counts(tot)
    folded = fold(pulled[...], CS_OUT)
    ones_mean = per_image(w0, w1, [folded[g : g + 1] / counts[g] for g in range(2)])
    cross_mean = per_image(w0, w1, [folded[2 + g : 3 + g] / counts[g] for g in range(2)])
    gain2, scale2, shift2 = twice(gain), twice(scale), twice(shift)
    ones2, cross2 = twice(ones_mean), twice(cross_mean)
    zero = jnp.zeros((images, 128), BF16)

    def first_rows(k, carry):
        keep = keep_row(place, k, p_rows)
        first_grad[k, :, lanes : lanes + 128] = zero
        for c in range(0, lanes, 256):
            normed = first_ref[k + 2, :, c : c + 256] * scale2 + shift2
            v = gain2 * (flow_ref[k, :, c : c + 256] - ones2 - normed * cross2)
            first_grad[k, :, c : c + 256] = (v * keep).astype(BF16)
        return carry

    lax.fori_loop(0, p_rows + 1, first_rows, 0)

    @pl.when(pl.program_id(0) == 0)
    def _():
        kernel_ref[...] = jnp.zeros(kernel_ref.shape, F32)

    gain, bias, scale, shift = entry_tables(tot, norm_in, w0, w1)
    gain2, bias2, scale2, shift2 = twice(gain), twice(bias), twice(scale), twice(shift)

    ones = jnp.zeros((images, 128), F32)
    cross = jnp.zeros((images, 128), F32)
    for j in range(0, lanes // 256, blocks):
        upper = (first_grad, 0, 0, 384)
        lower = (first_grad, 1, 0, 384)
        left = stacked(j, blocks, images, p_rows, [upper, (grad, 1, 128, 256)])
        rows_even = matmul(left, weights_even[...])
        rows_odd = matmul(stacked(j, blocks, images, p_rows, [upper, lower]), weights_odd[...])
        for parity, rows in enumerate((rows_even, rows_odd)):
            low = rows.astype(BF16).reshape(blocks, p_rows, images, 256)
            for t in range(blocks):
                here = slice((j + t) * 256, (j + t + 1) * 256)
                for p in range(p_rows):
                    out_ref[2 * p + parity, :, here] = low[t, p]
                    x = raw[2 * p + parity + 5, :, here].astype(F32)
                    z = x * gain2 + bias2
                    s = sigmoid(z)
                    flow = low[t, p].astype(F32) * (s * (1.0 + z * (1.0 - s)))
                    crossed = flow * (x * scale2 + shift2)
                    ones = ones + flow[:, 0:128] + flow[:, 128:256]
                    cross = cross + crossed[:, 0:128] + crossed[:, 128:256]
        right = stacked(
            j,
            blocks,
            images,
            p_rows,
            [(even, 2, 0, 384), (odd, 2, 0, 384), (even, 3, 0, 384)],
        )
        own = stacked(j, blocks, images, p_rows, [(first_grad, 0, 0, 256)])
        kernel_ref[...] += lax.dot_general(
            own, right, (((0,), (0,)), ((), ())), preferred_element_type=F32
        )
    add_rows(stats, grouped_rows(w0, w1, [ones, cross]))

    @pl.when(pl.program_id(0) == pl.num_programs(0) - 1)
    def _():
        turned = kernel_ref[...].T
        for a in range(3):
            for b in range(3):
                tap = jnp.zeros((CS_IN, CS_OUT), F32)
                for q in range(4):
                    row = a * 384 + (2 * q + b + 3) * CS_IN
                    tap = tap + turned[row : row + CS_IN, q * CS_OUT : (q + 1) * CS_OUT]
                row = (3 * a + b) * CS_IN
                taps_ref[row : row + CS_IN] = tap


def student_entry(
    place, flow, first_out, grad, even, odd, raw, label, tot, inner, pulled, norm_in, norm,
    weights_even, weights_odd, tile,
):
    rows, images, lanes = flow.shape
    p_rows = rows - 1
    out = shape_of((2 * p_rows, images, lanes), BF16)
    taps = shape_of((9 * CS_IN, CS_OUT), F32)
    stats = shape_of((8, 128), F32)
    big = (flow, first_out, grad, even, odd, raw)
    shared = (tot, inner, pulled, norm_in, norm, weights_even, weights_odd)
    return pl.pallas_call(
        functools.partial(entry_kernel, p_rows, 4),
        grid_spec=pltpu.PrefetchScalarGridSpec(
            num_scalar_prefetch=1,
            grid=(images // tile,),
            in_specs=[image_spec(a, tile) for a in big]
            + [table_spec(label, tile)]
            + [whole_spec(a) for a in shared],
            out_specs=[image_spec(out, tile), whole_spec(taps), whole_spec(stats)],
            scratch_shapes=[
                pltpu.VMEM((p_rows + 1, tile, 128 + lanes), BF16),
                pltpu.VMEM((256, 1152), F32),
            ],
        ),
        out_shape=[out, taps, stats],
        compiler_params=pltpu.CompilerParams(vmem_limit_bytes=VMEM_LIMIT),
        cost_estimate=cost(16),
    )(place, *big, label, *shared)


def bands_kernel(first, first_t, second, second_t, short, short_t, *outs):
    one, two, back, even, odd, gather, scatter, wide = outs

    def fill(out, entries):
        rows = out.shape[0]
        wide[0:rows] = jnp.zeros((rows, 256), F32)
        for row, lane, tap in entries:
            wide[row : row + tap.shape[0], lane : lane + tap.shape[1]] = tap
        out[...] = wide[0:rows].astype(BF16)

    def tap_of(ref, a, b):
        size = ref.shape[0] // 9
        return ref[(3 * a + b) * size : (3 * a + b + 1) * size]

    taps = [(a, b) for a in range(3) for b in range(3)]
    fill(
        one,
        [
            (a * 384 + (2 * q + b + 3) * CS_IN, q * CS_OUT, tap_of(first, a, b))
            for a, b in taps
            for q in range(4)
        ],
    )
    fill(
        two,
        [
            (a * 512 + (q + b + 1) * CS_OUT, q * CS_OUT, tap_of(second, a, b))
            for a, b in taps
            for q in range(4)
        ]
        + [(1536 + 2 * q * CS_IN, q * CS_OUT, short[...]) for q in range(4)],
    )
    fill(
        back,
        [
            ((2 - a) * 512 + (s - b + 3) * CS_OUT, s * CS_OUT, tap_of(second_t, a, b))
            for a, b in taps
            for s in range(4)
        ],
    )

    def backward(a, row):
        entries = []
        for q in range(6):
            for b in range(3):
                s = 2 * q + b - 1
                if 0 <= s < 8:
                    entries.append((row + q * CS_OUT, s * CS_IN, tap_of(first_t, a, b)))
        return entries

    corner = [(384 + q * CS_OUT, 2 * q * CS_IN, short_t[...]) for q in range(4)]
    fill(even, backward(1, 0) + corner)
    fill(odd, backward(2, 0) + backward(0, 384))
    channel = lax.rem(lax.broadcasted_iota(jnp.int32, gather.shape, 0), 256)
    lane = lax.broadcasted_iota(jnp.int32, gather.shape, 1)
    gather[...] = jnp.where(lax.div(channel, CS_OUT) == lane, 1.0 / CS_OUT, 0.0).astype(BF16)
    lane = lax.rem(lax.broadcasted_iota(jnp.int32, scatter.shape, 0), 128)
    channel = lax.broadcasted_iota(jnp.int32, scatter.shape, 1)
    scatter[...] = jnp.where(lax.div(channel, CS_OUT) == lane, 1.0, 0.0).astype(BF16)


def banded_kernels(first, second, shortcut):
    turn = lambda k: jnp.swapaxes(k, 2, 3).reshape(-1, k.shape[2])
    rounded = lambda k: k.astype(BF16).astype(F32)
    first, second, shortcut = rounded(first), rounded(second), rounded(shortcut)
    args = (
        first.reshape(-1, CS_OUT),
        turn(first),
        second.reshape(-1, CS_OUT),
        turn(second),
        shortcut,
        shortcut.T,
    )
    shapes = [(1152, 256), (1792, 256), (1536, 256), (640, 256), (768, 256), (512, 128), (256, 256)]
    return pl.pallas_call(
        bands_kernel,
        in_specs=[pl.BlockSpec(memory_space=pltpu.VMEM)] * 6,
        out_specs=[pl.BlockSpec(memory_space=pltpu.VMEM)] * len(shapes),
        out_shape=[shape_of(shape, BF16) for shape in shapes],
        scratch_shapes=[pltpu.VMEM((1792, 256), F32)],
        compiler_params=pltpu.CompilerParams(vmem_limit_bytes=VMEM_LIMIT),
        cost_estimate=cost(8),
    )(*args)


def renew(weights, gradient, moment, average, factor):
    descent = gradient + WEIGHT_DECAY * weights
    velocity = MOMENTUM * moment + descent
    updated = weights - factor * (descent + MOMENTUM * velocity)
    smoothed = AVERAGING * average + (1.0 - AVERAGING) * updated
    return (gradient, velocity, smoothed, updated)


def body(
    space,
    batch,
    small_in,
    large_in,
    small_teacher,
    large_teacher,
    small_groups,
    large_groups,
    small_cot,
    large_cot,
    teacher_gains,
    teacher_first,
    teacher_inner,
    teacher_second,
    teacher_bypass,
    entry_norm,
    first_conv,
    inner_norm,
    second_conv,
    shortcut,
    momentum_entry,
    momentum_first,
    momentum_inner,
    momentum_second,
    momentum_shortcut,
    average_entry,
    average_first,
    average_inner,
    average_second,
    average_shortcut,
):
    slabs = SLABS
    group = space // slabs
    axes = (("space", space), ("batch", batch))
    me = lax.axis_index("space")
    z, x = me // group, me % group
    place = jnp.stack([x, z]).astype(jnp.int32)
    total_positions = batch * (small_in.shape[0] * SIDE * SIDE // 4 + large_in.shape[0] * SIDE * SIDE)
    pixels = [small_in, large_in]
    teachers = [small_teacher, large_teacher]
    labels = [small_groups, large_groups]
    cots = [small_cot, large_cot]
    sides = [SIDE, 2 * SIDE]
    both = range(2)
    per_device = [p.shape[0] // space for p in pixels]
    local_rows = [p.shape[1] for p in pixels]
    images = [slabs * n for n in per_device]
    padded = [-(-n // 16) * 16 for n in images]
    tiles = [32 if padded[0] % 32 == 0 else 16, 16]
    p_counts = [s // (2 * slabs) for s in sides]
    widths = [s // 2 for s in sides]

    def to_sub(d):
        return [(k, k // group * group + (k % group + d) % group) for k in range(space)]

    def to_slab(d):
        return [(k, (k // group + d) % slabs * group + k % group) for k in range(space)]

    def send(array, pairs):
        return lax.ppermute(array, "space", pairs)

    down = [(k, k + group) for k in range(space - group)]
    up = [(k, k - group) for k in range(group, space)]

    def pick_images(array, res, sub):
        n, rows, lanes = array.shape
        parts = array.reshape(slabs, group, per_device[res], rows, lanes)
        part = lax.dynamic_index_in_dim(parts, sub, 1, False)
        return part.reshape(images[res], rows, lanes)

    def rows_first(array):
        return jnp.transpose(array, (1, 0, 2))

    def slab_rows(pieces, first, last):
        local = pieces[0].shape[0]
        out = []
        for s in range(first // local, (last - 1) // local + 1):
            lo, hi = max(first - s * local, 0), min(last - s * local, local)
            cut = [p[lo:hi] for p in pieces]
            out.append(lax.select_n((x - s) % group, *cut) if group > 1 else cut[0])
        return jnp.concatenate(out, axis=0) if len(out) > 1 else out[0]

    def edge_rows(pieces, above, below):
        rows = group * pieces[0].shape[0]
        return slab_rows(pieces, rows - above, rows), slab_rows(pieces, 0, below)

    def to_neighbours(rows):
        return send(rows[0], down), send(rows[1], up)

    def halos(pieces, above, below):
        return to_neighbours(edge_rows(pieces, above, below))

    def pad_to(array, size):
        extra = size - array.shape[1]
        return jnp.pad(array, ((0, 0), (0, extra), (0, 0))) if extra else array

    def pad_images(array, res):
        return pad_to(array, padded[res])

    def label_table(res, sub, size):
        mine = lax.dynamic_index_in_dim(
            labels[res].reshape(slabs, group, per_device[res]), sub, 1, False
        ).reshape(images[res])
        mine = jnp.pad(mine.astype(F32), (0, size - images[res]), constant_values=-1.0)
        return jnp.broadcast_to(mine[:, None], (size, 128))

    tables = [label_table(res, x, padded[res]) for res in both]
    norm_in = jnp.tile(entry_norm, (1, 128 // CS_IN))
    norm_mid = jnp.tile(inner_norm, (1, 128 // CS_OUT))
    by_slab = [[sub + group * k for k in range(slabs)] for sub in range(group)]

    def among_slabs(array, axis):
        if axis:
            array = jnp.moveaxis(array, axis, 0)
        return lax.all_to_all(array, "space", 0, 0, axis_index_groups=by_slab, tiled=True)

    subs = [(x + d) % group for d in range(group)]
    picked = [[rows_first(pick_images(pixels[res], res, sub)) for sub in subs] for res in both]
    arrived = [
        [picked[res][0]] + [send(picked[res][d], to_sub(d)) for d in range(1, group)]
        for res in both
    ]

    narrow = cots[0].shape[2]
    cot_stacks = []
    for res in both:
        c = jnp.pad(rows_first(cots[res]), ((1, 2), (0, 0), (0, 0)))
        count = p_counts[res]
        c = jnp.stack([c[k * count : (k + 1) * count + 3] for k in range(slabs)])
        if c.shape[3] > narrow:
            c = jnp.concatenate(
                [c[..., k : k + narrow] for k in range(0, c.shape[3], narrow)], axis=2
            )
        cot_stacks.append(c)
    flat = [c.reshape(slabs, -1, narrow) for c in cot_stacks]
    cot_flat = among_slabs(jnp.concatenate(flat, axis=1), 0)

    gains = jnp.tile(teacher_gains, (1, max(t.shape[2] for t in teachers) // CT_IN))

    def activated(array, size):
        lanes = array.shape[2]
        z_t = gains[0, :lanes] * array.astype(F32) + gains[1, :lanes]
        return pad_to(rows_first(jax.nn.silu(z_t).astype(BF16)), size)

    large_raw_in = after(large_teacher, [p[1:] for p in picked])
    own_large = pick_images(large_raw_in, 1, x)
    away_large = [pick_images(large_raw_in, 1, sub) for sub in subs[1:]]
    cut = min(16, images[1])
    sizes = [cut, -(-(images[1] - cut) // 16) * 16]
    ranges = [(0, cut), (cut, images[1])]

    def large_part(k, *others):
        lo, hi = ranges[k]
        return [
            send(after(away_large[d - 1][lo:hi], *others), to_sub(d)) for d in range(1, group)
        ]

    large_raw = [large_part(0)]

    stat_tables = [label_table(res, sub, images[res]) for res in both for sub in subs]
    entry_sums = input_stats(picked[0] + picked[1], stat_tables)
    entry_sums = after(entry_sums, [p[1:] for p in arrived], cot_flat, large_raw)
    entry_total = total_over_devices([entry_sums], axes, 0)

    raw_halos = [halos([after(p, entry_total) for p in arrived[res]], 5, 6) for res in both]
    large_raw.append(large_part(1, entry_total))
    large_own = [
        activated(after(own_large[lo:hi], large_raw_in), size)
        for (lo, hi), size in zip(ranges, sizes)
    ]
    large_pieces = [
        [own] + [activated(after(p, entry_total), size) for p in raw]
        for own, size, raw in zip(large_own, sizes, large_raw)
    ]

    def large_edges_of(k, *others):
        lo, hi = ranges[k]
        rows = [after(p[:, : hi - lo], *others) for p in large_pieces[k]]
        return [pad_to(h, sizes[k]) for h in halos(rows, 3, 2)]

    large_edges = [large_edges_of(0, raw_halos[1])]
    lanes = small_teacher.shape[2]
    z_t = after(small_teacher, large_raw_in).astype(F32) * gains[0, :lanes] + gains[1, :lanes]
    small_active = rows_first(jax.nn.silu(z_t).astype(BF16))
    small_active = small_active.reshape(local_rows[0], slabs, group, per_device[0], lanes)

    small_away = [
        [lax.dynamic_index_in_dim(small_active[:, k], sub, 1, False) for sub in subs[1:]]
        for k in range(slabs)
    ]
    cot_here = after(cot_flat, entry_total)
    cot_slabs = []
    at = 0
    for res, sent in zip(both, cot_stacks):
        size = sent.shape[1] * sent.shape[2]
        c = cot_here[:, at : at + size].reshape(sent.shape)
        at += size
        n = per_device[res]
        c = jnp.concatenate([c[:, :, k : k + n] for k in range(0, c.shape[2], n)], axis=3)
        c = jnp.moveaxis(c, 0, 1).reshape(c.shape[1], images[res], c.shape[3])
        cot_slabs.append(pad_images(c, res))

    bands = banded_kernels(*after((first_conv, second_conv, shortcut), large_raw_in))
    bands_first, bands_second, bands_second_back, bands_even, bands_odd, gather, scatter = bands
    raws, evens, odds, firsts, first_sums = [], [], [], [], []
    for res in both:
        raw, even, odd, first, sums = student_forward(
            place,
            [pad_images(p, res) for p in arrived[res]],
            *[pad_images(p, res) for p in raw_halos[res]],
            tables[res],
            entry_total,
            norm_in,
            bands_first,
            tiles[res],
        )
        raws.append(raw)
        evens.append(even)
        odds.append(odd)
        firsts.append(first)
        first_sums.append(sums)
    first_sums = after(first_sums, large_pieces, large_edges)
    inner_total = total_over_devices(first_sums, axes, 1)

    large_edges.append(large_edges_of(1, inner_total))
    order = list(range(slabs))[::-1]
    small_pieces = {}
    for k in order:
        waits = [inner_total]
        if k == order[-1]:
            waits.append(small_pieces[order[0]])
        small_pieces[k] = [
            send(after(p, *waits), to_sub(d + 1)) for d, p in enumerate(small_away[k])
        ]

    def small_rows(k, *others):
        own = lax.dynamic_index_in_dim(small_active[:, k], x, 1, False)
        return edge_rows([own] + after(small_pieces[k], *others), 3, 2)

    small_edge_rows = {order[0]: small_rows(order[0])}

    acts, sums_out, lows, energies = [], [], [], []
    for res in both:
        act, block_sum, low, energy = student_block(
            place,
            after(firsts[res], small_edge_rows[order[0]]) if res else firsts[res],
            odds[res],
            tables[res],
            entry_total,
            inner_total,
            norm_mid,
            bands_second,
            gather,
            tiles[res],
        )
        acts.append(act)
        sums_out.append(block_sum)
        lows.append(low)
        energies.append(energy)

    shared = (
        teacher_first.reshape(9 * CT_IN, CT_OUT),
        teacher_second.reshape(9 * CT_OUT, CT_OUT),
        teacher_bypass,
        teacher_inner,
    )
    def large_map(k, *others):
        pieces = large_pieces[k]
        own = after(pieces[0], *others)
        return teacher_energies(place, own, 0, pieces[1:], *large_edges[k], shared, tiles[1])

    def small_map(k, *others):
        edges = to_neighbours(small_edge_rows[k])
        pieces = after(small_pieces[k], *others)
        return teacher_energies(
            place, small_active, k, pieces, *edges, shared, per_device[0]
        )

    large_maps = [large_map(0, inner_total)]
    small_maps = {}
    small_edge_rows[order[1]] = small_rows(order[1], large_maps[0])
    large_maps.append(large_map(1, small_edge_rows[order[1]]))
    small_edge_rows[order[2]] = small_rows(order[2], large_maps[1])
    for k in order[:2]:
        small_maps[k] = small_map(k, small_edge_rows[order[2]])
    small_edge_rows[order[3]] = small_rows(order[3], small_maps[order[0]], small_maps[order[1]])
    for k in order[2:]:
        small_maps[k] = small_map(k, small_edge_rows[order[3]])
    small_maps = [small_maps[k] for k in range(slabs)]
    factors = attention_maps(
        energies, [small_maps, large_maps], tables, widths, p_counts, slabs, group, 2
    )
    loss_sums = factors[2]

    def to_owners(res, *others):
        low = after(lows[res][:, : images[res]], *others)
        rows, _, lanes = low.shape
        return among_slabs(low.reshape(rows, slabs, per_device[res], lanes), 1)

    out_parts = [to_owners(0, factors[2])]

    flows, grads, flow_sums, second_parts, shortcut_parts = [], [], [], [], []
    for res in both:
        flow, grad, sums, second_part, shortcut_part = student_back(
            place,
            sums_out[res],
            cot_slabs[res],
            factors[res],
            scatter,
            firsts[res],
            acts[res],
            odds[res],
            tables[res],
            entry_total,
            inner_total,
            norm_mid,
            bands_second_back,
            tiles[res],
        )
        flows.append(flow)
        grads.append(grad)
        flow_sums.append(sums)
        second_parts.append(second_part)
        shortcut_parts.append(shortcut_part)
    flow_total = total_over_devices(after(flow_sums, out_parts[0]), axes, 3)
    out_parts.append(to_owners(1, flow_total))

    entry_parts, first_parts, entry_flow_sums = [], [], []
    packed = None
    for res in both:
        rows, first_part, sums = student_entry(
            place,
            after(flows[res], entry_parts[0][0]) if res == 1 else flows[res],
            firsts[res],
            grads[res],
            evens[res],
            odds[res],
            raws[res],
            tables[res],
            entry_total,
            inner_total,
            flow_total,
            norm_in,
            norm_mid,
            bands_even,
            bands_odd,
            tiles[res],
        )
        first_parts.append(first_part)
        entry_flow_sums.append(sums)
        if res == 1:
            held = after(entry_flow_sums, entry_parts[0][1:], out_parts[1])
            packed = spread_sum(
                [first_parts, second_parts, shortcut_parts, held, [loss_sums]], axes, 4
            )
        rows = rows[:, : images[res]]
        parts = []
        for d in range(group):
            part = lax.dynamic_slice_in_dim(rows, subs[d] * local_rows[res], local_rows[res], 0)
            if d:
                part = send(after(part, packed) if res == 1 else part, to_sub(d))
            parts.append(part)
        entry_parts.append(parts)

    def unpack(pairs, shape):
        return jnp.concatenate([pairs[:, :64], pairs[:, 64:]], axis=0).reshape(shape)

    first_grads = unpack(packed[0], first_conv.shape)
    second_grads = unpack(packed[1], second_conv.shape)
    shortcut_grads = unpack(packed[2], shortcut.shape)
    entry_pulled = packed[3].reshape(8, 128 // CS_IN, CS_IN).sum(axis=1)
    total_loss = jnp.sum(packed[4])

    counts = entry_total[4:6, 0:1]
    entry_folded = entry_total.reshape(8, 128 // CS_IN, CS_IN).sum(axis=1)
    mean_entry = entry_folded[0:2] / counts
    scale_entry = lax.rsqrt(entry_folded[2:4] / counts - mean_entry * mean_entry + EPSILON)
    shift_entry = -mean_entry * scale_entry
    ones_entry, cross_entry = entry_pulled[0:2], entry_pulled[2:4]
    inner_folded = flow_total.reshape(8, 128 // CS_OUT, CS_OUT).sum(axis=1)
    ones_inner, cross_inner = inner_folded[0:2], inner_folded[2:4]

    gain_entry = entry_norm[0] * scale_entry
    bias_entry = entry_norm[0] * shift_entry + entry_norm[1]
    slope_entry = -gain_entry * (cross_entry / counts) * scale_entry
    level_entry = -gain_entry * ((ones_entry + cross_entry * shift_entry) / counts)
    block_outs = []
    for res in both:
        low = after(out_parts[res], packed)
        low = jnp.transpose(low, (2, 0, 1, 3))
        block_outs.append(low.reshape(low.shape[0], -1, low.shape[3]))
    entry_parts[0] = after(entry_parts[0], packed)
    input_grads = []
    for res in both:
        n, rows, lanes = pixels[res].shape
        ordered = [lax.select_n((x - s) % group, *entry_parts[res]) for s in range(group)]
        rows_in = jnp.stack(ordered).reshape(group, rows, slabs, per_device[res], lanes)
        rows_in = jnp.transpose(rows_in, (2, 0, 3, 1, 4)).reshape(n, rows, lanes)
        one = (labels[res] == 1)[:, None, None]

        def by_image(pair):
            wide = jnp.tile(pair, (1, lanes // CS_IN))
            return jnp.where(one, wide[1], wide[0])

        value = pixels[res].astype(F32)
        gain = by_image(gain_entry)
        before = value * gain + by_image(bias_entry)
        s = jax.nn.sigmoid(before)
        flow = rows_in.astype(F32) * (s * (1.0 + before * (1.0 - s)))
        input_grads.append(gain * flow + (value * by_image(slope_entry) + by_image(level_entry)))

    entry_grads = jnp.stack([jnp.sum(cross_entry, axis=0), jnp.sum(ones_entry, axis=0)])
    inner_grads = jnp.stack([jnp.sum(cross_inner, axis=0), jnp.sum(ones_inner, axis=0)])
    rate_scale = 1.0 / math.sqrt(total_positions)
    entry_state = renew(entry_norm, entry_grads, momentum_entry, average_entry, NORM_RATE * rate_scale)
    first_state = renew(first_conv, first_grads, momentum_first, average_first, CONV_RATE * rate_scale)
    inner_state = renew(inner_norm, inner_grads, momentum_inner, average_inner, NORM_RATE * rate_scale)
    second_state = renew(
        second_conv, second_grads, momentum_second, average_second, CONV_RATE * rate_scale
    )
    bypass_state = renew(
        shortcut, shortcut_grads, momentum_shortcut, average_shortcut, CONV_RATE * rate_scale
    )
    return (
        *block_outs,
        input_grads[0],
        input_grads[1],
        total_loss / total_positions,
        *entry_state,
        *first_state,
        first_state[3].astype(BF16),
        *inner_state,
        *second_state,
        second_state[3].astype(BF16),
        *bypass_state,
        bypass_state[3].astype(BF16),
    )


def solution(mesh):
    rows = P("batch", "space", None)
    blocks = P(("batch", "space"), None, None)
    return jax.shard_map(
        functools.partial(body, mesh.shape["space"], mesh.shape["batch"]),
        mesh=mesh,
        in_specs=(rows,) * 4 + (P("batch"),) * 2 + (blocks,) * 2 + (P(),) * 20,
        out_specs=(blocks,) * 2 + (rows,) * 2 + (P(),) * 24,
        check_vma=False,
    )
```

```python
import functools
import math

import jax
import jax.numpy as jnp
import numpy as np
from jax import lax
from jax.experimental import pallas as pl
from jax.experimental.pallas import tpu as pltpu
from jax.sharding import PartitionSpec as P

CS_IN = 32
CS_OUT = 64
CT_IN = 128
CT_OUT = 256
SIDE = 32
SLABS = 4

EPSILON = 1e-05
TRANSFER_WEIGHT = 1000.0
MOMENTUM = 0.9
WEIGHT_DECAY = 0.0005
AVERAGING = 0.7
CONV_RATE = 0.06
NORM_RATE = 0.3

F32 = jnp.float32
BF16 = jnp.bfloat16
MESH = pl.DeviceIdType.MESH
VMEM_LIMIT = 56 << 20


def sigmoid(z):
    return 0.5 * jnp.tanh(0.5 * z) + 0.5


def matmul(a, b):
    return jnp.dot(a, b, preferred_element_type=F32)


def after(value, *others):
    return lax.optimization_barrier((value, others))[0]


def cost(microseconds):
    return pl.CostEstimate(
        flops=int(microseconds * 1e9), bytes_accessed=1 << 20, transcendentals=0
    )


def stacked(first, count, images, rows, parts):
    blocks = []
    for t in range(count):
        at = (first + t) * 256
        pieces = [ref[lo : lo + rows, :, at + off : at + off + size] for ref, lo, off, size in parts]
        block = jnp.concatenate(pieces, axis=2) if len(pieces) > 1 else pieces[0]
        blocks.append(block.reshape(rows * images, block.shape[2]))
    return jnp.concatenate(blocks, axis=0) if count > 1 else blocks[0]


def fold(rows, width):
    shift = width
    while shift < 128:
        rows = rows + pltpu.roll(rows, shift, 1)
        shift *= 2
    return rows


def group_norms(totals, counts, width):
    folded = fold(totals, width)
    means, scales = [], []
    for g in range(2):
        mean = folded[g : g + 1] / counts[g]
        variance = folded[2 + g : 3 + g] / counts[g] - mean * mean
        means.append(mean)
        scales.append(lax.rsqrt(variance + EPSILON))
    return means, scales


def per_image(w0, w1, pair):
    return w0 * pair[0] + w1 * pair[1]


def twice(table):
    return jnp.concatenate([table, table], axis=1)


def grouped_rows(w0, w1, values):
    rows = []
    for v in values:
        rows.append(jnp.sum(v * w0, axis=0, keepdims=True))
        rows.append(jnp.sum(v * w1, axis=0, keepdims=True))
    rows.append(jnp.zeros((8 - len(rows), 128), F32))
    return jnp.concatenate(rows, axis=0)


def entry_counts(tot_ref):
    return [tot_ref[4:5], tot_ref[5:6]]


def inner_counts(tot_ref):
    return [tot_ref[4:5] * 0.25, tot_ref[5:6] * 0.25]


def renew(weights, gradient, moment, average, factor):
    descent = gradient + WEIGHT_DECAY * weights
    velocity = MOMENTUM * moment + descent
    updated = weights - factor * (descent + MOMENTUM * velocity)
    smoothed = AVERAGING * average + (1.0 - AVERAGING) * updated
    return (gradient, velocity, smoothed, updated)


def stats_kernel(x_refs, label_refs, out_ref):
    step = pl.program_id(0)
    total = jnp.zeros((8, 128), F32)
    for x_ref, label_ref in zip(x_refs, label_refs):
        rows, images, lanes = x_ref.shape
        s = jnp.zeros((images, 128), F32)
        q = jnp.zeros((images, 128), F32)
        for r in range(rows):
            for c in range(0, lanes, 128):
                v = x_ref[r, :, c : c + 128].astype(F32)
                s = s + v
                q = q + v * v
        w0, w1 = indicators(label_ref)
        positions = jnp.full((images, 128), float(rows * lanes // CS_IN), F32)
        total = total + grouped_rows(w0, w1, [s, q, positions])

    @pl.when(step == 0)
    def _():
        out_ref[...] = total

    @pl.when(step > 0)
    def _():
        out_ref[...] += total


def input_stats(pieces, tables):
    steps = min(4, min(x.shape[0] for x in pieces))
    count = len(pieces)

    def kernel(*refs):
        stats_kernel(refs[:count], refs[count:-1], refs[-1])

    specs = [
        pl.BlockSpec((x.shape[0] // steps,) + x.shape[1:], lambda i: (i, 0, 0)) for x in pieces
    ]
    specs += [pl.BlockSpec(w.shape, lambda i: (0, 0)) for w in tables]
    return pl.pallas_call(
        kernel,
        grid=(steps,),
        in_specs=specs,
        out_specs=pl.BlockSpec((8, 128), lambda i: (0, 0)),
        out_shape=jax.ShapeDtypeStruct((8, 128), F32),
        compiler_params=pltpu.CompilerParams(vmem_limit_bytes=VMEM_LIMIT),
        cost_estimate=cost(5),
    )(*pieces, *tables)


def greet(axes):
    barrier = pltpu.get_barrier_semaphore()
    expected = 0
    for name, size in axes:
        me = lax.axis_index(name)
        for d in range(1, size):
            pl.semaphore_signal(
                barrier,
                inc=1,
                device_id={name: lax.rem(me + d, size)},
                device_id_type=MESH,
            )
            expected += 1
    pl.semaphore_wait(barrier, expected)


def total_kernel(axes, count, *refs):
    parts = refs[:count]
    out_ref, held, boxes_a, boxes_b, send_a, recv_a, send_b, recv_b = refs[-8:]
    value = parts[0][...]
    for part in parts[1:]:
        value = value + part[...]
    held[0] = value
    greet(axes)
    for level, ((name, size), boxes, send, recv) in enumerate(
        zip(axes, (boxes_a, boxes_b), (send_a, send_b), (recv_a, recv_b))
    ):
        me = lax.axis_index(name)
        copies = []
        for d in range(1, size):
            copy = pltpu.make_async_remote_copy(
                src_ref=held.at[level],
                dst_ref=boxes.at[d],
                send_sem=send.at[d],
                recv_sem=recv.at[d],
                device_id={name: lax.rem(me + d, size)},
                device_id_type=MESH,
            )
            copy.start()
            copies.append(copy)
        for copy in copies:
            copy.wait_recv()
        value = jnp.zeros(value.shape, F32)
        for source in range(size):
            back = lax.rem(me - source + size, size)
            value = value + jnp.where(
                back == 0, held[level], boxes[jnp.maximum(back, 1)]
            )
        for copy in copies:
            copy.wait_send()
        if level == 0:
            held[1] = value
        else:
            out_ref[...] = value


def total_over_devices(parts, axes, collective_id, waits):
    waits = jax.tree.leaves(waits)
    shape = parts[0].shape
    return pl.pallas_call(
        functools.partial(total_kernel, axes, len(parts)),
        out_shape=jax.ShapeDtypeStruct(shape, F32),
        in_specs=[pl.BlockSpec(memory_space=pltpu.VMEM)] * len(parts)
        + [pl.BlockSpec(memory_space=pl.ANY)] * len(waits),
        out_specs=pl.BlockSpec(memory_space=pltpu.VMEM),
        scratch_shapes=[
            pltpu.VMEM((2,) + shape, F32),
            pltpu.VMEM((axes[0][1],) + shape, F32),
            pltpu.VMEM((axes[1][1],) + shape, F32),
            pltpu.SemaphoreType.DMA((axes[0][1],)),
            pltpu.SemaphoreType.DMA((axes[0][1],)),
            pltpu.SemaphoreType.DMA((axes[1][1],)),
            pltpu.SemaphoreType.DMA((axes[1][1],)),
        ],
        compiler_params=pltpu.CompilerParams(collective_id=collective_id, has_side_effects=True),
        cost_estimate=cost(12),
    )(*parts, *waits)


def finish_kernel(axes, layout, rates, waits, *refs):
    count = sum(len(parts) for parts in layout)
    inputs, states, entry = refs[:count], refs[count : count + 9], refs[count + 9 : count + 12]
    tot, norm = refs[count + 12 : count + 14]
    refs = refs[waits:]
    outs = refs[count + 14 : count + 35]
    out_ref, x_ref, boxes_a, boxes_b, held = refs[count + 35 : count + 40]
    send_a, recv_a, send_b, recv_b, send_c, recv_c = refs[count + 40 :]
    conv_rate, norm_rate, per_position = rates
    at = 0
    for parts in layout:
        value = inputs[parts[0]][...]
        for k in parts[1:]:
            value = value + inputs[k][...]
        if value.shape[1] == 64:
            half = value.shape[0] // 2
            value = jnp.concatenate([value[:half], value[half:]], axis=1)
        x_ref[at : at + value.shape[0]] = value
        at += value.shape[0]
    if at < x_ref.shape[0]:
        x_ref[at:] = jnp.zeros((x_ref.shape[0] - at, 128), F32)
    (name_a, size_a), (name_b, size_b) = axes
    me_a, me_b = lax.axis_index(name_a), lax.axis_index(name_b)
    piece = x_ref.shape[0] // size_a
    greet(axes)

    def rows(index):
        return pl.ds(pl.multiple_of(index * piece, 8), piece)

    copies = []
    for d in range(1, size_a):
        peer = lax.rem(me_a + d, size_a)
        copy = pltpu.make_async_remote_copy(
            src_ref=x_ref.at[rows(peer)],
            dst_ref=boxes_a.at[d],
            send_sem=send_a.at[d],
            recv_sem=recv_a.at[d],
            device_id={name_a: peer},
            device_id_type=MESH,
        )
        copy.start()
        copies.append(copy)
    value = x_ref[rows(me_a)]
    for d in range(1, size_a):
        copies[d - 1].wait_recv()
        value = value + boxes_a[d]
    held[0] = value
    for copy in copies:
        copy.wait_send()
    copies = []
    for d in range(1, size_b):
        copy = pltpu.make_async_remote_copy(
            src_ref=held.at[0],
            dst_ref=boxes_b.at[d],
            send_sem=send_b.at[d],
            recv_sem=recv_b.at[d],
            device_id={name_b: lax.rem(me_b + d, size_b)},
            device_id_type=MESH,
        )
        copy.start()
        copies.append(copy)
    for copy in copies:
        copy.wait_recv()
    value = jnp.zeros(value.shape, F32)
    for source in range(size_b):
        back = lax.rem(me_b - source + size_b, size_b)
        value = value + jnp.where(back == 0, held[0], boxes_b[jnp.maximum(back, 1)])
    held[1] = value
    out_ref[rows(me_a)] = value
    for copy in copies:
        copy.wait_send()
    copies = []
    for d in range(1, size_a):
        copy = pltpu.make_async_remote_copy(
            src_ref=held.at[1],
            dst_ref=out_ref.at[rows(me_a)],
            send_sem=send_c.at[d],
            recv_sem=recv_c.at[d],
            device_id={name_a: lax.rem(me_a + d, size_a)},
            device_id_type=MESH,
        )
        copy.start()
        copies.append(copy)
    for copy in copies:
        copy.wait()

    at = 0
    for k in range(3):
        weights, moment, average = [ref[...] for ref in states[3 * k : 3 * k + 3]]
        half = weights.shape[0] // 2
        pairs = out_ref[at : at + half]
        at += half
        gradient = jnp.concatenate([pairs[:, 0:64], pairs[:, 64:128]], axis=0)
        state = renew(weights, gradient, moment, average, conv_rate)
        for ref, value in zip(outs[5 * k : 5 * k + 4], state):
            ref[...] = value
        outs[5 * k + 4][...] = state[3].astype(BF16)
    pulled = fold(out_ref[at : at + 8], CS_IN)
    ones, cross = [pulled[0:1], pulled[1:2]], [pulled[2:3], pulled[3:4]]
    gradient = jnp.concatenate([cross[0] + cross[1], ones[0] + ones[1]], axis=0)[:, 0:CS_IN]
    state = renew(entry[0][...], gradient, entry[1][...], entry[2][...], norm_rate)
    for ref, value in zip(outs[15:19], state):
        ref[...] = value
    counts = entry_counts(tot)
    means, scales = group_norms(tot[...], counts, CS_IN)
    gains, biases, slopes, levels = [], [], [], []
    for g in range(2):
        shift = -means[g] * scales[g]
        gain = norm[0:1] * scales[g]
        gains.append(gain)
        biases.append(norm[0:1] * shift + norm[1:2])
        slopes.append(-gain * (cross[g] / counts[g]) * scales[g])
        levels.append(-gain * ((ones[g] + cross[g] * shift) / counts[g]))
    outs[19][...] = jnp.concatenate(gains + biases + slopes + levels, axis=0)
    losses = out_ref[at + 8 : at + 9]
    outs[20][...] = jnp.sum(losses, axis=1, keepdims=True) * per_position


def finish(groups, states, entry, tot, norm, rates, axes, collective_id, waits):
    (_, size_a), (_, size_b) = axes
    arrays, layout, rows = [], [], []
    for members in groups:
        layout.append(tuple(range(len(arrays), len(arrays) + len(members))))
        arrays += members
        rows.append(members[0].shape[0] * members[0].shape[1] // 128)
    padded = -(-sum(rows) // (8 * size_a)) * 8 * size_a
    piece = padded // size_a
    sems = []
    for size in (size_a, size_b, size_a):
        sems += [pltpu.SemaphoreType.DMA((size,))] * 2
    given = arrays + [a for state in states for a in state] + entry + [tot, norm]
    outs = []
    for state in states:
        outs += [shape_of(state[0].shape, F32)] * 4 + [shape_of(state[0].shape, BF16)]
    outs += [shape_of(entry[0].shape, F32)] * 4 + [shape_of((8, 128), F32), shape_of((1, 1), F32)]
    waits = jax.tree.leaves(waits)
    vmem = pl.BlockSpec(memory_space=pltpu.VMEM)
    got = pl.pallas_call(
        functools.partial(finish_kernel, axes, tuple(layout), rates, len(waits)),
        out_shape=outs,
        in_specs=[vmem] * len(given) + [pl.BlockSpec(memory_space=pl.ANY)] * len(waits),
        out_specs=[vmem] * len(outs),
        scratch_shapes=[
            pltpu.VMEM((padded, 128), F32),
            pltpu.VMEM((padded, 128), F32),
            pltpu.VMEM((size_a, piece, 128), F32),
            pltpu.VMEM((size_b, piece, 128), F32),
            pltpu.VMEM((2, piece, 128), F32),
        ]
        + sems,
        compiler_params=pltpu.CompilerParams(collective_id=collective_id, has_side_effects=True),
        cost_estimate=cost(20),
    )(*given, *waits)
    return got[0:5], got[5:10], got[10:15], got[15:19], got[19], got[20]


def teacher_kernel(p_rows, width, group, columns, place, *refs):
    pieces, refs = refs[:group], refs[group:]
    edge_a, edge_b, first, second, bypass, inner, out_ref, even, odd, mid = refs
    local, lanes = pieces[0].shape[0], pieces[0].shape[-1]
    real, images = edge_a.shape[1], even.shape[1]
    m_rows = p_rows + 2
    zero = jnp.zeros((images, 128), BF16)

    def put(row, source, at):
        if row % 2 == 0:
            even[row // 2 + 1, 0:real, 128 : 128 + lanes] = source[at]
        else:
            odd[(row + 1) // 2 + 1, 0:real, 128 : 128 + lanes] = source[at]

    def put_edges(above, below):
        for k in range(3):
            put(k - 3, above, k)
        for k in range(2):
            put(2 * p_rows + k, below, k)

    rows_of_neighbours(place, edge_a, edge_b, put_edges)
    nothing = jnp.zeros((1, real, lanes), BF16)

    @pl.when(place[1] == 0)
    def _():
        for k in range(3):
            put(k - 3, nothing, 0)

    @pl.when(place[1] == SLABS - 1)
    def _():
        for k in range(2):
            put(2 * p_rows + k, nothing, 0)

    x = place[0]
    for s in range(group):
        distance = lax.rem(x - s + group, group)
        for d in range(group):

            @pl.when(distance == d)
            def _():
                for k in range(local):
                    at = (k, 0, 0) if len(pieces[d].shape) == 5 else k
                    put(s * local + k, pieces[d], at)

    for i in range(m_rows):
        even[i, :, 0:128] = zero
    for i in range(m_rows + 1):
        odd[i, :, 0:128] = zero
    wide_zero = jnp.zeros((images, CT_OUT), BF16)
    for i in range(m_rows):
        mid[i, :, 0:CT_OUT] = wide_zero
        mid[i, :, (width + 1) * CT_OUT : (width + 2) * CT_OUT] = wide_zero
    scale, shift = inner[0:1], inner[1:2]
    top, bottom = keep_row(place, -1, p_rows), keep_row(place, p_rows, p_rows)

    def first_step(g, carry):
        lefts = []
        for t in range(columns):
            window = pl.ds(pl.multiple_of((g * columns + t) * 256, 256), 384)
            parts = [odd[0:m_rows, :, window], even[0:m_rows, :, window]]
            parts.append(odd[1 : m_rows + 1, :, window])
            lefts.append(jnp.concatenate(parts, axis=2).reshape(m_rows * images, 9 * CT_IN))
        z = scale * matmul(jnp.concatenate(lefts, axis=0), first[...]) + shift
        act = (z * sigmoid(z)).reshape(columns, m_rows, images, CT_OUT)
        for t in range(columns):
            here = pl.ds(pl.multiple_of((g * columns + t + 1) * CT_OUT, 256), CT_OUT)
            mid[0, :, here] = (act[t, 0] * top).astype(BF16)
            mid[1 : p_rows + 1, :, here] = act[t, 1 : p_rows + 1].astype(BF16)
            mid[p_rows + 1, :, here] = (act[t, p_rows + 1] * bottom).astype(BF16)
        return carry

    lax.fori_loop(0, width // columns, first_step, 0)
    out_ref[...] = jnp.zeros(out_ref.shape, F32)
    lane = lax.broadcasted_iota(jnp.int32, (real, 128), 1)

    def second_step(g, carry):
        lefts, corners = [], []
        for t in range(columns):
            at = pl.multiple_of((g * columns + t) * 256, 256)
            window = pl.ds(at, 3 * CT_OUT)
            corner = pl.ds(pl.multiple_of(at + 128, 128), 128)
            parts = [mid[a : a + p_rows, :, window] for a in range(3)]
            lefts.append(jnp.concatenate(parts, axis=2).reshape(p_rows * images, 9 * CT_OUT))
            corners.append(even[1 : p_rows + 1, :, corner].reshape(p_rows * images, CT_IN))
        y = matmul(jnp.concatenate(lefts, axis=0), second[...])
        y = y + matmul(jnp.concatenate(corners, axis=0), bypass[...])
        square = y * y
        energy = jnp.sum(square[:, 0:128] + square[:, 128:256], axis=1, keepdims=True)
        energy = (energy * (1.0 / CT_OUT)).reshape(columns, p_rows, images, 1)
        for t in range(columns):
            for p in range(p_rows):
                chunk, start = divmod((p + 1) * width, 128)
                where = slice(chunk * 128, chunk * 128 + 128)
                here = lane == start + g * columns + t
                out_ref[:, where] = jnp.where(here, energy[t, p, 0:real], out_ref[:, where])
        return carry

    lax.fori_loop(0, width // columns, second_step, 0)


def teacher_energies(place, own, slab, received, edge_a, edge_b, shared, tile):
    group = len(received) + 1
    local, lanes = own.shape[0], own.shape[-1]
    images = edge_a.shape[1]
    p_rows, width = group * local // 2, lanes // (2 * CT_IN)
    out_lanes = -(-(p_rows + 3) * width // 128) * 128
    m_rows = p_rows + 2
    space = -(-tile // 16) * 16
    if own.ndim == 5:
        own_spec = pl.BlockSpec(
            (local, 1, 1, tile, lanes), lambda i, place: (0, slab + i, place[0], 0, 0)
        )
    else:
        own_spec = pl.BlockSpec((local, tile, lanes), lambda i, place: (0, i, 0))
    whole = lambda a: pl.BlockSpec(a.shape, lambda i, place: (0,) * a.ndim)
    by_image = lambda a: pl.BlockSpec((a.shape[0], tile, a.shape[2]), lambda i, place: (0, i, 0))
    grid_spec = pltpu.PrefetchScalarGridSpec(
        num_scalar_prefetch=1,
        grid=(images // tile,),
        in_specs=[own_spec]
        + [by_image(a) for a in received]
        + [by_image(edge_a), by_image(edge_b)]
        + [whole(a) for a in shared],
        out_specs=pl.BlockSpec((tile, out_lanes), lambda i, place: (i, 0)),
        scratch_shapes=[
            pltpu.VMEM((m_rows, space, 128 + lanes), BF16),
            pltpu.VMEM((m_rows + 1, space, 128 + lanes), BF16),
            pltpu.VMEM((m_rows, space, (width + 2) * CT_OUT), BF16),
        ],
    )
    return pl.pallas_call(
        functools.partial(teacher_kernel, p_rows, width, group, 4),
        grid_spec=grid_spec,
        out_shape=jax.ShapeDtypeStruct((images, out_lanes), F32),
        compiler_params=pltpu.CompilerParams(vmem_limit_bytes=VMEM_LIMIT),
        cost_estimate=cost(40 * images * p_rows * width / 10240),
    )(place, own, *received, edge_a, edge_b, *shared)


def entry_tables(tot_ref, norm_ref, w0, w1):
    means, scales = group_norms(tot_ref[...], entry_counts(tot_ref), CS_IN)
    scale = per_image(w0, w1, scales)
    shift = per_image(w0, w1, [-m * s for m, s in zip(means, scales)])
    gain, bias = norm_ref[0:1], norm_ref[1:2]
    present = w0 + w1
    return gain * scale, gain * shift + bias * present, scale, shift


def inner_tables(tot_ref, inner_ref, norm_ref, w0, w1):
    means, scales = group_norms(inner_ref[...], inner_counts(tot_ref), CS_OUT)
    scale = per_image(w0, w1, scales)
    shift = per_image(w0, w1, [-m * s for m, s in zip(means, scales)])
    gain, bias = norm_ref[0:1], norm_ref[1:2]
    present = w0 + w1
    return gain * scale, gain * shift + bias * present, scale, shift


def indicators(label_ref):
    label = label_ref[...]
    return (label == 0.0).astype(F32), (label == 1.0).astype(F32)


def keep_row(place, row, inside):
    z = place[1]
    outside = jnp.logical_or(
        jnp.logical_and(row < 0, z == 0), jnp.logical_and(row >= inside, z == SLABS - 1)
    )
    return jnp.where(outside, 0.0, 1.0)


def rows_of_neighbours(place, first, second, use):
    even = lax.rem(place[1], 2) == 0

    @pl.when(even)
    def _():
        use(second, first)

    @pl.when(jnp.logical_not(even))
    def _():
        use(first, second)


def add_rows(ref, value):
    first = pl.program_id(0) == 0

    @pl.when(first)
    def _():
        ref[...] = value

    @pl.when(jnp.logical_not(first))
    def _():
        ref[...] += value


def forward_kernel(
    p_rows, group, blocks, place, *refs
):
    pieces, refs = refs[:group], refs[group:]
    first, second, label_ref, tot, norm, weights = refs[:6]
    raw_ref, even_ref, odd_ref, out_ref, stats, raw, even, odd = refs[6:]
    images, lanes = raw.shape[1:]
    local = pieces[0].shape[0]
    w0, w1 = indicators(label_ref)
    gain, bias, _, _ = entry_tables(tot, norm, w0, w1)
    gain2, bias2 = twice(gain), twice(bias)
    zero = jnp.zeros((images, 128), BF16)

    def put_edges(above, below):
        raw[0:5] = above[1:6]
        raw[2 * p_rows + 5 : 2 * p_rows + 11] = below[...]

    rows_of_neighbours(place, first, second, put_edges)
    x = place[0]
    for s in range(group):
        distance = lax.rem(x - s + group, group)
        for d in range(group):

            @pl.when(distance == d)
            def _():
                raw[5 + s * local : 5 + (s + 1) * local] = pieces[d][...]

    def activate(row, target, index):
        keep = keep_row(place, row - 5, 2 * p_rows)
        target[index, :, 0:128] = zero
        for c in range(0, lanes, 256):
            z = raw[row, :, c : c + 256].astype(F32) * gain2 + bias2
            target[index, :, 128 + c : 384 + c] = (z * sigmoid(z) * keep).astype(BF16)

    def pair(i, carry):
        activate(2 * i, even, i)
        activate(2 * i + 1, odd, i)
        return carry

    f_rows = p_rows + 5
    lax.fori_loop(0, f_rows, pair, 0)
    activate(2 * f_rows, even, f_rows)
    raw_ref[...] = raw[5 : 2 * p_rows + 5]
    even_ref[...] = even[2 : p_rows + 3]
    odd_ref[...] = odd[1 : p_rows + 4]
    s = jnp.zeros((images, 128), F32)
    q = jnp.zeros((images, 128), F32)
    for j in range(0, lanes // 256, blocks):
        left = stacked(
            j, blocks, images, f_rows, [(even, 0, 0, 384), (odd, 0, 0, 384), (even, 1, 0, 384)]
        )
        y = matmul(left, weights[...]).reshape(blocks, f_rows, images, 256)
        for t in range(blocks):
            out_ref[:, :, (j + t) * 256 : (j + t + 1) * 256] = y[t]
            own = y[t, 2 : 2 + p_rows]
            u = jnp.sum(own, axis=0)
            v = jnp.sum(own * own, axis=0)
            s = s + u[:, 0:128] + u[:, 128:256]
            q = q + v[:, 0:128] + v[:, 128:256]
    add_rows(stats, grouped_rows(w0, w1, [s, q]))


def whole_spec(a):
    return pl.BlockSpec(a.shape, lambda i, *_: (0,) * len(a.shape))


def image_spec(a, tile):
    return pl.BlockSpec((a.shape[0], tile, a.shape[2]), lambda i, *_: (0, i, 0))


def table_spec(a, tile):
    return pl.BlockSpec((tile, a.shape[1]), lambda i, *_: (i, 0))


def shape_of(shape, dtype):
    return jax.ShapeDtypeStruct(shape, dtype)


def student_forward(place, pieces, first, second, label, tot, norm, weights, tile):
    group = len(pieces)
    local, images, lanes = pieces[0].shape
    p_rows = group * local // 2
    outs = [
        shape_of((2 * p_rows, images, lanes), BF16),
        shape_of((p_rows + 1, images, 128 + lanes), BF16),
        shape_of((p_rows + 3, images, 128 + lanes), BF16),
        shape_of((p_rows + 5, images, lanes), F32),
    ]
    stats = shape_of((8, 128), F32)
    big = (*pieces, first, second)
    shared = (tot, norm, weights)
    grid_spec = pltpu.PrefetchScalarGridSpec(
        num_scalar_prefetch=1,
        grid=(images // tile,),
        in_specs=[image_spec(a, tile) for a in big]
        + [table_spec(label, tile)]
        + [whole_spec(a) for a in shared],
        out_specs=[image_spec(o, tile) for o in outs] + [whole_spec(stats)],
        scratch_shapes=[
            pltpu.VMEM((2 * p_rows + 11, tile, lanes), BF16),
            pltpu.VMEM((p_rows + 6, tile, 128 + lanes), BF16),
            pltpu.VMEM((p_rows + 5, tile, 128 + lanes), BF16),
        ],
    )
    return pl.pallas_call(
        functools.partial(forward_kernel, p_rows, group, 4),
        grid_spec=grid_spec,
        out_shape=outs + [stats],
        compiler_params=pltpu.CompilerParams(vmem_limit_bytes=VMEM_LIMIT),
        cost_estimate=cost(15),
    )(place, *big, label, *shared)


def split_bf16(value):
    high = value.astype(BF16)
    return high, (value - high.astype(F32)).astype(BF16)


def block_kernel(
    p_rows,
    blocks,
    place,
    first_ref,
    odd,
    label_ref,
    tot,
    inner,
    norm,
    weights,
    spread,
    act_ref,
    own_ref,
    sum_ref,
    low_ref,
    energy,
    act,
):
    images, lanes = first_ref.shape[1:]
    w0, w1 = indicators(label_ref)
    gain, bias, _, _ = inner_tables(tot, inner, norm, w0, w1)
    gain2, bias2 = twice(gain), twice(bias)
    zero = jnp.zeros((images, 128), BF16)
    f_rows, b_rows = p_rows + 5, p_rows + 3

    def activate(f, carry):
        keep = keep_row(place, f - 2, p_rows)
        act[f, :, 0:128] = zero
        act[f, :, 128 + lanes : 256 + lanes] = zero
        for c in range(0, lanes, 256):
            z = first_ref[f, :, c : c + 256] * gain2 + bias2
            act[f, :, 128 + c : 384 + c] = (z * sigmoid(z) * keep).astype(BF16)
        return carry

    lax.fori_loop(0, f_rows, activate, 0)
    act_ref[...] = act[1 : p_rows + 3]
    own_ref[...] = first_ref[2 : p_rows + 3]

    per_chunk = 128 // (lanes // CS_OUT)
    chunks = energy.shape[1] // 128
    measured = [jnp.zeros((images, 128), F32) for _ in range(chunks)]
    for j in range(0, lanes // 256, blocks):
        parts = [(act, a, 0, 512) for a in range(3)] + [(odd, 0, 128, 256)]
        left = stacked(j, blocks, images, b_rows, parts)
        flat = matmul(left, weights[...])
        y = flat.reshape(blocks, b_rows, images, 256)
        high, low = split_bf16(flat * flat)
        e = matmul(jnp.concatenate([high, low], axis=1), spread[...])
        e = e.reshape(blocks, b_rows, images, 128)
        for t in range(blocks):
            here = slice((j + t) * 256, (j + t + 1) * 256)
            sum_ref[:, :, here] = y[t]
            low_ref[:, :, here] = y[t, 1 : p_rows + 1].astype(BF16)
            for b in range(b_rows):
                shift = b % per_chunk * (128 // per_chunk) + 4 * (j + t)
                part = pltpu.roll(e[t, b], shift, 1) if shift else e[t, b]
                measured[b // per_chunk] = measured[b // per_chunk] + part
    for c in range(chunks):
        energy[:, c * 128 : c * 128 + 128] = measured[c]


def student_block(place, first_out, odd, label, tot, inner, norm, weights, spread, tile):
    rows, images, lanes = first_out.shape
    p_rows = rows - 5
    width = lanes // CS_OUT
    energy_lanes = -(-(p_rows + 3) * width // 128) * 128
    outs = [
        shape_of((p_rows + 2, images, 256 + lanes), BF16),
        shape_of((p_rows + 1, images, lanes), F32),
        shape_of((p_rows + 3, images, lanes), F32),
        shape_of((p_rows, images, lanes), BF16),
    ]
    energy = shape_of((images, energy_lanes), F32)
    return pl.pallas_call(
        functools.partial(block_kernel, p_rows, 4),
        grid_spec=pltpu.PrefetchScalarGridSpec(
            num_scalar_prefetch=1,
            grid=(images // tile,),
            in_specs=[image_spec(first_out, tile), image_spec(odd, tile), table_spec(label, tile)]
            + [whole_spec(a) for a in (tot, inner, norm, weights, spread)],
            out_specs=[image_spec(o, tile) for o in outs] + [table_spec(energy, tile)],
            scratch_shapes=[pltpu.VMEM((p_rows + 5, tile, 256 + lanes), BF16)],
        ),
        out_shape=outs + [energy],
        compiler_params=pltpu.CompilerParams(vmem_limit_bytes=VMEM_LIMIT),
        cost_estimate=cost(18),
    )(place, first_out, odd, label, tot, inner, norm, weights, spread)


def map_kernel(slabs, group, widths, p_counts, pieces, *refs):
    student, present = refs[0:2], refs[2:4]
    given = refs[4 : 4 + sum(pieces)]
    refs = refs[4 + sum(pieces) :]
    outs, loss_ref = refs[0:2], refs[2]
    teacher, sums, boxes = refs[3:5], refs[5:7], refs[7:9]
    from_above, from_below = refs[9:11], refs[11:13]
    send, recv, send_halo, recv_halo, ready = refs[13:]
    for res in range(2):
        at = 0
        for part in given[res * pieces[0] : res * pieces[0] + pieces[res]]:
            teacher[res][at : at + part.shape[0]] = part[...]
            at += part.shape[0]
    me = lax.axis_index("space")
    z, x = lax.div(me, group), lax.rem(me, group)
    greet_barrier = pltpu.get_barrier_semaphore()
    for d in range(1, slabs):
        pl.semaphore_signal(
            greet_barrier,
            inc=1,
            device_id={"space": lax.rem(z + d, slabs) * group + x},
            device_id_type=MESH,
        )
    pl.semaphore_wait(greet_barrier, slabs - 1)

    def halo_copies(res, direction):
        width, p_rows = widths[res], p_counts[res]
        lane = (p_rows * width if direction == 0 else width) // 128 * 128
        target = (from_above, from_below)[direction][res]
        return pltpu.make_async_remote_copy(
            src_ref=teacher[res].at[:, pl.ds(lane, 128)],
            dst_ref=target,
            send_sem=send_halo.at[2 * res + direction],
            recv_sem=recv_halo.at[2 * res + direction],
            device_id={"space": me + (group if direction == 0 else -group)},
            device_id_type=MESH,
        )

    for res in range(2):
        from_above[res][...] = jnp.zeros(from_above[res].shape, F32)
        from_below[res][...] = jnp.zeros(from_below[res].shape, F32)

    @pl.when(z > 0)
    def _():
        pl.semaphore_signal(
            ready.at[0], inc=1, device_id={"space": me - group}, device_id_type=MESH
        )

    @pl.when(z < slabs - 1)
    def _():
        pl.semaphore_signal(
            ready.at[1], inc=1, device_id={"space": me + group}, device_id_type=MESH
        )
        pl.semaphore_wait(ready.at[0], 1)
        halo_copies(0, 0).start()
        halo_copies(1, 0).start()

    @pl.when(z > 0)
    def _():
        pl.semaphore_wait(ready.at[1], 1)
        halo_copies(0, 1).start()
        halo_copies(1, 1).start()

    copies = []
    for res in range(2):
        width, p_rows = widths[res], p_counts[res]
        images, lanes = student[res].shape
        lane = lax.broadcasted_iota(jnp.int32, (images, lanes), 1)
        own = jnp.logical_and(lane >= width, lane < (p_rows + 1) * width)
        es = jnp.where(own, student[res][...], 0.0)
        et = jnp.where(own, teacher[res][...], 0.0)
        columns = [
            jnp.sum(v, axis=1, keepdims=True) for v in (es * es, et * et, es * et)
        ]
        small_lane = lax.broadcasted_iota(jnp.int32, (images, 128), 1)
        packed = jnp.zeros((images, 128), F32)
        for k, column in enumerate(columns):
            packed = jnp.where(small_lane == k, column, packed)
        padded = sums[res].shape[1]
        packed = jnp.concatenate([packed, jnp.zeros((padded - images, 128), F32)], axis=0)
        sums[res][...] = packed.T[0:8]
        for d in range(1, slabs):
            copy = pltpu.make_async_remote_copy(
                src_ref=sums[res],
                dst_ref=boxes[res].at[d],
                send_sem=send.at[res * slabs + d],
                recv_sem=recv.at[res * slabs + d],
                device_id={"space": lax.rem(z + d, slabs) * group + x},
                device_id_type=MESH,
            )
            copy.start()
            copies.append(copy)
    for copy in copies:
        copy.wait()

    @pl.when(z < slabs - 1)
    def _():
        halo_copies(0, 0).wait_send()
        halo_copies(1, 0).wait_send()
        halo_copies(0, 1).wait_recv()
        halo_copies(1, 1).wait_recv()

    @pl.when(z > 0)
    def _():
        halo_copies(0, 1).wait_send()
        halo_copies(1, 1).wait_send()
        halo_copies(0, 0).wait_recv()
        halo_copies(1, 0).wait_recv()

    loss = jnp.zeros((1, 128), F32)
    for res in range(2):
        width, p_rows = widths[res], p_counts[res]
        images, lanes = student[res].shape
        total = sums[res][...]
        for d in range(1, slabs):
            total = total + boxes[res][d]
        padded = total.shape[1]
        total = jnp.concatenate([total, jnp.zeros((120, padded), F32)], axis=0).T[0:images]
        ss, tt, st = total[:, 0:1], total[:, 1:2], total[:, 2:3]
        scale_s = lax.rsqrt(ss + 1e-12)
        scale_t = lax.rsqrt(tt + 1e-12)
        pulled = TRANSFER_WEIGHT * scale_s * (scale_s * ss - scale_t * st)
        lane = lax.broadcasted_iota(jnp.int32, (images, lanes), 1)
        shift = p_rows * width
        chunks = lanes // 128
        first_rows = from_below[res][...]
        last_rows = from_above[res][...]
        if shift % 128:
            first_rows = pltpu.roll(first_rows, shift % 128, 1)
            last_rows = pltpu.roll(last_rows, 128 - shift % 128, 1)
        blank = jnp.zeros((images, 128), F32)
        before = [last_rows] + [blank] * (chunks - 1)
        after = [blank] * (chunks - 1) + [first_rows]
        before = jnp.concatenate(before, axis=1) if chunks > 1 else before[0]
        after = jnp.concatenate(after, axis=1) if chunks > 1 else after[0]
        et = jnp.where(lane < width, before, teacher[res][...])
        et = jnp.where(lane >= (p_rows + 1) * width, after, et)
        u = student[res][...] * scale_s
        difference = u - et * scale_t
        own = jnp.logical_and(lane >= width, lane < (p_rows + 1) * width)
        squares = jnp.where(own, difference * difference, 0.0)
        kept = (present[res][...] >= 0.0).astype(F32)
        for c in range(chunks):
            loss = loss + jnp.sum(squares[:, c * 128 : c * 128 + 128] * kept, axis=0, keepdims=True)
        factor = (TRANSFER_WEIGHT * difference - u * pulled) * (scale_s * (2.0 / CS_OUT))
        for c in range(chunks):
            here = slice(c * 128, c * 128 + 128)
            outs[res][:, here] = jnp.where(kept > 0.0, factor[:, here], 0.0)
    loss_ref[...] = jnp.concatenate(
        [loss * (TRANSFER_WEIGHT / 2), jnp.zeros((7, 128), F32)], axis=0
    )


def attention_maps(student, teacher, present, widths, p_counts, slabs, group, collective_id):
    padded = [-(-s.shape[0] // 128) * 128 for s in student]
    images = [s.shape[0] for s in student]
    vmem = pl.BlockSpec(memory_space=pltpu.VMEM)
    return pl.pallas_call(
        functools.partial(
            map_kernel, slabs, group, widths, p_counts, tuple(len(t) for t in teacher)
        ),
        out_shape=[shape_of(s.shape, F32) for s in student] + [shape_of((8, 128), F32)],
        in_specs=[vmem] * (4 + sum(len(t) for t in teacher)),
        out_specs=[vmem] * 3,
        scratch_shapes=[pltpu.VMEM(s.shape, F32) for s in student]
        + [pltpu.VMEM((8, n), F32) for n in padded]
        + [pltpu.VMEM((slabs, 8, n), F32) for n in padded]
        + [pltpu.VMEM((n, 128), F32) for n in images] * 2
        + [pltpu.SemaphoreType.DMA((2 * slabs,))] * 2
        + [pltpu.SemaphoreType.DMA((4,))] * 2
        + [pltpu.SemaphoreType.REGULAR((2,))],
        compiler_params=pltpu.CompilerParams(collective_id=collective_id, has_side_effects=True),
        cost_estimate=cost(11),
    )(*student, *present, *teacher[0], *teacher[1])


def back_kernel(
    p_rows,
    blocks,
    place,
    sum_ref,
    cot,
    factor,
    spread,
    first_ref,
    act,
    odd,
    label_ref,
    tot,
    inner,
    norm,
    weights,
    flow_ref,
    grad_ref,
    stats,
    second_ref,
    shortcut_ref,
    kernel_ref,
    grad,
):
    images, lanes = sum_ref.shape[1:]
    w0, w1 = indicators(label_ref)
    gain, bias, scale, shift = inner_tables(tot, inner, norm, w0, w1)
    gain2, bias2, scale2, shift2 = twice(gain), twice(bias), twice(scale), twice(shift)
    zero = jnp.zeros((images, 128), BF16)
    b_rows, k_rows = p_rows + 3, p_rows + 1
    width = lanes // CS_OUT
    per_chunk = 128 // width
    for b in range(b_rows):
        grad[b, :, 0:128] = zero
        grad[b, :, 128 + lanes : 256 + lanes] = zero
    halves = [split_bf16(factor[:, c * 128 : c * 128 + 128]) for c in range(factor.shape[1] // 128)]
    halves = [[h.astype(F32) for h in pair] for pair in halves]
    for j in range(0, lanes // 256, blocks):
        rows = []
        for t in range(blocks):
            for b in range(b_rows):
                shift = (128 - (b % per_chunk * width + 4 * (j + t))) % 128
                pair = halves[b // per_chunk]
                if shift:
                    pair = [pltpu.roll(h, shift, 1) for h in pair]
                rows.append(jnp.concatenate(pair, axis=1))
        wide = matmul(jnp.concatenate(rows, axis=0).astype(BF16), spread[...])
        wide = wide.reshape(blocks, b_rows, images, 256)
        for t in range(blocks):
            at = (j + t) * 256
            for b in range(b_rows):
                keep = keep_row(place, b - 1, p_rows)
                v = cot[b, :, at : at + 256].astype(F32) + wide[t, b] * sum_ref[b, :, at : at + 256]
                grad[b, :, 128 + at : 384 + at] = (v * keep).astype(BF16)

    grad_ref[...] = grad[1 : p_rows + 1, :, 128 : 128 + lanes]

    @pl.when(pl.program_id(0) == 0)
    def _():
        kernel_ref[...] = jnp.zeros(kernel_ref.shape, F32)

    ones = jnp.zeros((images, 128), F32)
    cross = jnp.zeros((images, 128), F32)
    for j in range(0, lanes // 256, blocks):
        left = stacked(j, blocks, images, k_rows, [(grad, d, 0, 512) for d in range(3)])
        y = matmul(left, weights[...]).reshape(blocks, k_rows, images, 256)
        for t in range(blocks):
            here = slice((j + t) * 256, (j + t + 1) * 256)
            for k in range(k_rows):
                x = first_ref[k, :, here]
                z = x * gain2 + bias2
                s = sigmoid(z)
                flow = y[t, k] * (s * (1.0 + z * (1.0 - s)))
                flow_ref[k, :, here] = flow
                if k < p_rows:
                    crossed = flow * (x * scale2 + shift2)
                    ones = ones + flow[:, 0:128] + flow[:, 128:256]
                    cross = cross + crossed[:, 0:128] + crossed[:, 128:256]
        right = stacked(
            j,
            blocks,
            images,
            p_rows,
            [(act, a, 0, 512) for a in range(3)] + [(odd, 1, 128, 256)],
        )
        own = stacked(j, blocks, images, p_rows, [(grad, 1, 128, 256)])
        kernel_ref[...] += lax.dot_general(
            own, right, (((0,), (0,)), ((), ())), preferred_element_type=F32
        )
    add_rows(stats, grouped_rows(w0, w1, [ones, cross]))

    @pl.when(pl.program_id(0) == pl.num_programs(0) - 1)
    def _():
        turned = kernel_ref[...].T
        for a in range(3):
            for b in range(3):
                tap = jnp.zeros((CS_OUT, CS_OUT), F32)
                for q in range(4):
                    row = a * 512 + (q + b + 1) * CS_OUT
                    tap = tap + turned[row : row + CS_OUT, q * CS_OUT : (q + 1) * CS_OUT]
                row = (3 * a + b) * CS_OUT
                second_ref[row : row + CS_OUT] = tap
        tap = jnp.zeros((CS_IN, CS_OUT), F32)
        for q in range(4):
            row = 1536 + 2 * q * CS_IN
            tap = tap + turned[row : row + CS_IN, q * CS_OUT : (q + 1) * CS_OUT]
        shortcut_ref[...] = tap


def student_back(
    place, block_sum, cot, factor, spread, first_out, act, odd, label, tot, inner, norm, weights, tile
):
    rows, images, lanes = block_sum.shape
    p_rows = rows - 3
    outs = [
        shape_of((p_rows + 1, images, lanes), F32),
        shape_of((p_rows, images, lanes), BF16),
    ]
    stats = shape_of((8, 128), F32)
    second = shape_of((9 * CS_OUT, CS_OUT), F32)
    shortcut = shape_of((CS_IN, CS_OUT), F32)
    return pl.pallas_call(
        functools.partial(back_kernel, p_rows, 4),
        grid_spec=pltpu.PrefetchScalarGridSpec(
            num_scalar_prefetch=1,
            grid=(images // tile,),
            in_specs=[image_spec(block_sum, tile), image_spec(cot, tile), table_spec(factor, tile)]
            + [whole_spec(spread), image_spec(first_out, tile), image_spec(act, tile)]
            + [image_spec(odd, tile), table_spec(label, tile)]
            + [whole_spec(a) for a in (tot, inner, norm, weights)],
            out_specs=[image_spec(o, tile) for o in outs]
            + [whole_spec(a) for a in (stats, second, shortcut)],
            scratch_shapes=[
                pltpu.VMEM((256, 1792), F32),
                pltpu.VMEM((p_rows + 3, tile, 256 + lanes), BF16),
            ],
        ),
        out_shape=outs + [stats, second, shortcut],
        compiler_params=pltpu.CompilerParams(vmem_limit_bytes=VMEM_LIMIT),
        cost_estimate=cost(18),
    )(place, block_sum, cot, factor, spread, first_out, act, odd, label, tot, inner, norm, weights)


def entry_kernel(
    p_rows,
    blocks,
    place,
    flow_ref,
    first_ref,
    grad,
    even,
    odd,
    raw,
    label_ref,
    tot,
    inner,
    pulled,
    norm_in,
    norm,
    weights_even,
    weights_odd,
    *refs,
):
    outs, (taps_ref, stats, first_grad, kernel_ref, rows_ref) = refs[:-5], refs[-5:]
    images, lanes = first_ref.shape[1:]
    w0, w1 = indicators(label_ref)
    gain, _, scale, shift = inner_tables(tot, inner, norm, w0, w1)
    counts = inner_counts(tot)
    folded = fold(pulled[...], CS_OUT)
    ones_mean = per_image(w0, w1, [folded[g : g + 1] / counts[g] for g in range(2)])
    cross_mean = per_image(w0, w1, [folded[2 + g : 3 + g] / counts[g] for g in range(2)])
    gain2, scale2, shift2 = twice(gain), twice(scale), twice(shift)
    ones2, cross2 = twice(ones_mean), twice(cross_mean)
    zero = jnp.zeros((images, 128), BF16)

    def first_rows(k, carry):
        keep = keep_row(place, k, p_rows)
        first_grad[k, :, lanes : lanes + 128] = zero
        for c in range(0, lanes, 256):
            normed = first_ref[k, :, c : c + 256] * scale2 + shift2
            v = gain2 * (flow_ref[k, :, c : c + 256] - ones2 - normed * cross2)
            first_grad[k, :, c : c + 256] = (v * keep).astype(BF16)
        return carry

    lax.fori_loop(0, p_rows + 1, first_rows, 0)

    @pl.when(pl.program_id(0) == 0)
    def _():
        kernel_ref[...] = jnp.zeros(kernel_ref.shape, F32)

    gain, bias, scale, shift = entry_tables(tot, norm_in, w0, w1)
    gain2, bias2, scale2, shift2 = twice(gain), twice(bias), twice(scale), twice(shift)

    ones = jnp.zeros((images, 128), F32)
    cross = jnp.zeros((images, 128), F32)
    for j in range(0, lanes // 256, blocks):
        upper = (first_grad, 0, 0, 384)
        lower = (first_grad, 1, 0, 384)
        left = stacked(j, blocks, images, p_rows, [upper, (grad, 0, 0, 256)])
        rows_even = matmul(left, weights_even[...])
        rows_odd = matmul(stacked(j, blocks, images, p_rows, [upper, lower]), weights_odd[...])
        for parity, rows in enumerate((rows_even, rows_odd)):
            low = rows.astype(BF16).reshape(blocks, p_rows, images, 256)
            for t in range(blocks):
                here = slice((j + t) * 256, (j + t + 1) * 256)
                for p in range(p_rows):
                    rows_ref[2 * p + parity, :, here] = low[t, p]
                    x = raw[2 * p + parity, :, here].astype(F32)
                    z = x * gain2 + bias2
                    s = sigmoid(z)
                    flow = low[t, p].astype(F32) * (s * (1.0 + z * (1.0 - s)))
                    crossed = flow * (x * scale2 + shift2)
                    ones = ones + flow[:, 0:128] + flow[:, 128:256]
                    cross = cross + crossed[:, 0:128] + crossed[:, 128:256]
        right = stacked(
            j,
            blocks,
            images,
            p_rows,
            [(even, 0, 0, 384), (odd, 1, 0, 384), (even, 1, 0, 384)],
        )
        own = stacked(j, blocks, images, p_rows, [(first_grad, 0, 0, 256)])
        kernel_ref[...] += lax.dot_general(
            own, right, (((0,), (0,)), ((), ())), preferred_element_type=F32
        )
    group, local = len(outs), outs[0].shape[0]
    for s in range(group):
        distance = lax.rem(s - place[0] + group, group)
        for d in range(group):

            @pl.when(distance == d)
            def _():
                outs[d][...] = rows_ref[s * local : (s + 1) * local]

    add_rows(stats, grouped_rows(w0, w1, [ones, cross]))

    @pl.when(pl.program_id(0) == pl.num_programs(0) - 1)
    def _():
        turned = kernel_ref[...].T
        for a in range(3):
            for b in range(3):
                tap = jnp.zeros((CS_IN, CS_OUT), F32)
                for q in range(4):
                    row = a * 384 + (2 * q + b + 3) * CS_IN
                    tap = tap + turned[row : row + CS_IN, q * CS_OUT : (q + 1) * CS_OUT]
                row = (3 * a + b) * CS_IN
                taps_ref[row : row + CS_IN] = tap


def student_entry(
    place, flow, first_out, grad, even, odd, raw, label, tot, inner, pulled, norm_in, norm,
    weights_even, weights_odd, tile, group,
):
    rows, images, lanes = flow.shape
    p_rows = rows - 1
    outs = [shape_of((2 * p_rows // group, images, lanes), BF16)] * group
    taps = shape_of((9 * CS_IN, CS_OUT), F32)
    stats = shape_of((8, 128), F32)
    big = (flow, first_out, grad, even, odd, raw)
    shared = (tot, inner, pulled, norm_in, norm, weights_even, weights_odd)
    return pl.pallas_call(
        functools.partial(entry_kernel, p_rows, 4),
        grid_spec=pltpu.PrefetchScalarGridSpec(
            num_scalar_prefetch=1,
            grid=(images // tile,),
            in_specs=[image_spec(a, tile) for a in big]
            + [table_spec(label, tile)]
            + [whole_spec(a) for a in shared],
            out_specs=[image_spec(o, tile) for o in outs] + [whole_spec(taps), whole_spec(stats)],
            scratch_shapes=[
                pltpu.VMEM((p_rows + 1, tile, 128 + lanes), BF16),
                pltpu.VMEM((256, 1152), F32),
                pltpu.VMEM((2 * p_rows, tile, lanes), BF16),
            ],
        ),
        out_shape=outs + [taps, stats],
        compiler_params=pltpu.CompilerParams(vmem_limit_bytes=VMEM_LIMIT),
        cost_estimate=cost(16),
    )(place, *big, label, *shared)


def bands_kernel(first, first_t, second, second_t, short, short_t, *outs):
    one, two, back, even, odd, gather, scatter, wide = outs

    def fill(out, entries):
        rows = out.shape[0]
        wide[0:rows] = jnp.zeros((rows, 256), F32)
        for row, lane, tap in entries:
            wide[row : row + tap.shape[0], lane : lane + tap.shape[1]] = tap
        out[...] = wide[0:rows].astype(BF16)

    def tap_of(ref, a, b):
        size = ref.shape[0] // 9
        return ref[(3 * a + b) * size : (3 * a + b + 1) * size]

    taps = [(a, b) for a in range(3) for b in range(3)]
    fill(
        one,
        [
            (a * 384 + (2 * q + b + 3) * CS_IN, q * CS_OUT, tap_of(first, a, b))
            for a, b in taps
            for q in range(4)
        ],
    )
    fill(
        two,
        [
            (a * 512 + (q + b + 1) * CS_OUT, q * CS_OUT, tap_of(second, a, b))
            for a, b in taps
            for q in range(4)
        ]
        + [(1536 + 2 * q * CS_IN, q * CS_OUT, short[...]) for q in range(4)],
    )
    fill(
        back,
        [
            ((2 - a) * 512 + (s - b + 3) * CS_OUT, s * CS_OUT, tap_of(second_t, a, b))
            for a, b in taps
            for s in range(4)
        ],
    )

    def backward(a, row):
        entries = []
        for q in range(6):
            for b in range(3):
                s = 2 * q + b - 1
                if 0 <= s < 8:
                    entries.append((row + q * CS_OUT, s * CS_IN, tap_of(first_t, a, b)))
        return entries

    corner = [(384 + q * CS_OUT, 2 * q * CS_IN, short_t[...]) for q in range(4)]
    fill(even, backward(1, 0) + corner)
    fill(odd, backward(2, 0) + backward(0, 384))
    channel = lax.rem(lax.broadcasted_iota(jnp.int32, gather.shape, 0), 256)
    lane = lax.broadcasted_iota(jnp.int32, gather.shape, 1)
    gather[...] = jnp.where(lax.div(channel, CS_OUT) == lane, 1.0 / CS_OUT, 0.0).astype(BF16)
    lane = lax.rem(lax.broadcasted_iota(jnp.int32, scatter.shape, 0), 128)
    channel = lax.broadcasted_iota(jnp.int32, scatter.shape, 1)
    scatter[...] = jnp.where(lax.div(channel, CS_OUT) == lane, 1.0, 0.0).astype(BF16)


def banded_kernels(first, second, shortcut):
    turn = lambda k: jnp.swapaxes(k, 2, 3).reshape(-1, k.shape[2])
    rounded = lambda k: k.astype(BF16).astype(F32)
    first, second, shortcut = rounded(first), rounded(second), rounded(shortcut)
    args = (
        first.reshape(-1, CS_OUT),
        turn(first),
        second.reshape(-1, CS_OUT),
        turn(second),
        shortcut,
        shortcut.T,
    )
    shapes = [(1152, 256), (1792, 256), (1536, 256), (640, 256), (768, 256), (512, 128), (256, 256)]
    return pl.pallas_call(
        bands_kernel,
        in_specs=[pl.BlockSpec(memory_space=pltpu.VMEM)] * 6,
        out_specs=[pl.BlockSpec(memory_space=pltpu.VMEM)] * len(shapes),
        out_shape=[shape_of(shape, BF16) for shape in shapes],
        scratch_shapes=[pltpu.VMEM((1792, 256), F32)],
        compiler_params=pltpu.CompilerParams(vmem_limit_bytes=VMEM_LIMIT),
        cost_estimate=cost(8),
    )(*args)


def body(
    space,
    batch,
    small_in,
    large_in,
    small_teacher,
    large_teacher,
    small_groups,
    large_groups,
    small_cot,
    large_cot,
    teacher_gains,
    teacher_first,
    teacher_inner,
    teacher_second,
    teacher_bypass,
    entry_norm,
    first_conv,
    inner_norm,
    second_conv,
    shortcut,
    momentum_entry,
    momentum_first,
    momentum_inner,
    momentum_second,
    momentum_shortcut,
    average_entry,
    average_first,
    average_inner,
    average_second,
    average_shortcut,
):
    slabs = SLABS
    group = space // slabs
    axes = (("space", space), ("batch", batch))
    me = lax.axis_index("space")
    z, x = me // group, me % group
    place = jnp.stack([x, z]).astype(jnp.int32)
    total_positions = batch * (small_in.shape[0] * SIDE * SIDE // 4 + large_in.shape[0] * SIDE * SIDE)
    pixels = [small_in, large_in]
    teachers = [small_teacher, large_teacher]
    labels = [small_groups, large_groups]
    cots = [small_cot, large_cot]
    sides = [SIDE, 2 * SIDE]
    both = range(2)
    per_device = [p.shape[0] // space for p in pixels]
    local_rows = [p.shape[1] for p in pixels]
    images = [slabs * n for n in per_device]
    padded = [-(-n // 16) * 16 for n in images]
    tiles = [32 if padded[0] % 32 == 0 else 16, 16]
    p_counts = [s // (2 * slabs) for s in sides]
    widths = [s // 2 for s in sides]

    def to_sub(d):
        return [(k, k // group * group + (k % group + d) % group) for k in range(space)]

    def to_slab(d):
        return [(k, (k // group + d) % slabs * group + k % group) for k in range(space)]

    def send(array, pairs):
        return lax.ppermute(array, "space", pairs)

    def pick_images(array, res, sub):
        n, rows, lanes = array.shape
        parts = array.reshape(slabs, group, per_device[res], rows, lanes)
        part = lax.dynamic_index_in_dim(parts, sub, 1, False)
        return part.reshape(images[res], rows, lanes)

    def rows_first(array):
        return jnp.transpose(array, (1, 0, 2))

    def slab_rows(pieces, first, last):
        local = pieces[0].shape[0]
        out = []
        for s in range(first // local, (last - 1) // local + 1):
            lo, hi = max(first - s * local, 0), min(last - s * local, local)
            cut = [p[lo:hi] for p in pieces]
            out.append(lax.select_n((x - s) % group, *cut) if group > 1 else cut[0])
        return jnp.concatenate(out, axis=0) if len(out) > 1 else out[0]

    def partner(b, k, first):
        slab = k // group
        other = slab ^ 1 if first else ((slab + 1) ^ 1) - 1
        if 0 <= other < slabs:
            return b * space + other * group + k % group
        return (b ^ 1) * space + k

    pair_lists = [
        [(b * space + k, partner(b, k, first)) for b in range(batch) for k in range(space)]
        for first in (True, False)
    ]

    def edge_rows(pieces, count):
        rows = group * pieces[0].shape[0]
        last, first = slab_rows(pieces, rows - count, rows), slab_rows(pieces, 0, count)
        even = z % 2 == 0
        return lax.select(even, last, first), lax.select(even, first, last)

    def to_neighbours(rows):
        return [lax.ppermute(r, ("batch", "space"), pairs) for r, pairs in zip(rows, pair_lists)]

    def pad_to(array, size):
        extra = size - array.shape[1]
        return jnp.pad(array, ((0, 0), (0, extra), (0, 0))) if extra else array

    def pad_images(array, res):
        return pad_to(array, padded[res])

    def label_table(res, sub, size):
        mine = lax.dynamic_index_in_dim(
            labels[res].reshape(slabs, group, per_device[res]), sub, 1, False
        ).reshape(images[res])
        mine = jnp.pad(mine.astype(F32), (0, size - images[res]), constant_values=-1.0)
        return jnp.broadcast_to(mine[:, None], (size, 128))

    tables = [label_table(res, x, padded[res]) for res in both]
    norm_in = jnp.tile(entry_norm, (1, 128 // CS_IN))
    norm_mid = jnp.tile(inner_norm, (1, 128 // CS_OUT))
    by_slab = [[sub + group * k for k in range(slabs)] for sub in range(group)]

    def among_slabs(array, axis):
        if axis:
            array = jnp.moveaxis(array, axis, 0)
        return lax.all_to_all(array, "space", 0, 0, axis_index_groups=by_slab, tiled=True)

    subs = [(x + d) % group for d in range(group)]
    picked = [[rows_first(pick_images(pixels[res], res, sub)) for sub in subs] for res in both]
    arrived = [
        [picked[res][0]] + [send(picked[res][d], to_sub(d)) for d in range(1, group)]
        for res in both
    ]

    narrow = cots[0].shape[2]
    cot_stacks = []
    for res in both:
        c = jnp.pad(rows_first(cots[res]), ((1, 2), (0, 0), (0, 0)))
        count = p_counts[res]
        c = jnp.stack([c[k * count : (k + 1) * count + 3] for k in range(slabs)])
        if c.shape[3] > narrow:
            c = jnp.concatenate(
                [c[..., k : k + narrow] for k in range(0, c.shape[3], narrow)], axis=2
            )
        cot_stacks.append(c)
    flat = [c.reshape(slabs, -1, narrow) for c in cot_stacks]
    cot_flat = jnp.concatenate(flat, axis=1)
    cots_ready = cot_flat
    cot_flat = among_slabs(cot_flat, 0)

    gains = jnp.tile(teacher_gains, (1, max(t.shape[2] for t in teachers) // CT_IN))

    def activated(array, size):
        lanes = array.shape[2]
        z_t = gains[0, :lanes] * array.astype(F32) + gains[1, :lanes]
        return pad_to(rows_first(jax.nn.silu(z_t).astype(BF16)), size)

    large_raw_in = after(large_teacher, [p[1:] for p in picked], cots_ready)
    own_large = pick_images(large_raw_in, 1, x)
    away_large = [pick_images(large_raw_in, 1, sub) for sub in subs[1:]]
    cut = min(16, images[1])
    sizes = [cut, -(-(images[1] - cut) // 16) * 16]
    ranges = [(0, cut), (cut, images[1])]

    def large_part(k, *others):
        lo, hi = ranges[k]
        return [
            send(after(away_large[d - 1][lo:hi], *others), to_sub(d)) for d in range(1, group)
        ]

    large_raw = [large_part(0)]

    stat_tables = [label_table(res, sub, images[res]) for res in both for sub in subs]
    entry_sums = input_stats(picked[0] + picked[1], stat_tables)
    large_own = [activated(own_large[lo:hi], size) for (lo, hi), size in zip(ranges, sizes)]
    raw_edges = [edge_rows(arrived[res], 6) for res in both]
    corners = lambda parts: [p[:1, :, :128] for p in parts]
    waits = ([p[1:] for p in arrived], cot_flat, corners(large_raw[0]), large_own, raw_edges)
    entry_total = total_over_devices([entry_sums], axes, 0, waits)

    raw_halos = [to_neighbours(after(raw_edges[res], entry_total)) for res in both]
    large_raw.append(large_part(1, entry_total))
    large_pieces = [
        [own] + [activated(after(p, *others), size) for p in raw]
        for own, size, raw, others in zip(
            large_own, sizes, large_raw, ([entry_total], [])
        )
    ]

    def large_edges_of(k, *others):
        lo, hi = ranges[k]
        rows = [after(p[:, : hi - lo], *others) for p in large_pieces[k]]
        return to_neighbours(edge_rows(rows, 3))

    lanes = small_teacher.shape[2]
    z_t = after(small_teacher, large_raw_in).astype(F32) * gains[0, :lanes] + gains[1, :lanes]
    small_active = rows_first(jax.nn.silu(z_t).astype(BF16))
    small_active = small_active.reshape(local_rows[0], slabs, group, per_device[0], lanes)

    parts_of = [list(range(slabs // 2)), *([k] for k in range(slabs // 2, slabs))]

    def small_part(ks, sub):
        part = lax.dynamic_slice(
            small_active,
            (0, ks[0], sub, 0, 0),
            (local_rows[0], len(ks), 1, per_device[0], lanes),
        )
        return part.reshape(local_rows[0], len(ks) * per_device[0], lanes)

    small_away = [[small_part(ks, sub) for sub in subs[1:]] for ks in parts_of]
    bands = banded_kernels(*after((first_conv, second_conv, shortcut), large_raw_in))
    bands_first, bands_second, bands_second_back, bands_even, bands_odd, gather, scatter = bands
    raws, evens, odds, firsts, first_sums = ([None, None] for _ in range(5))
    for res in (1, 0):
        pieces = [pad_images(p, res) for p in arrived[res]]
        if res == 0:
            large_edges = [large_edges_of(0, sums)]
            cot_here = after(cot_flat, sums)
            cot_slabs = []
            at = 0
            for at_res, sent in zip(both, cot_stacks):
                size = sent.shape[1] * sent.shape[2]
                c = cot_here[:, at : at + size].reshape(sent.shape)
                at += size
                n = per_device[at_res]
                c = jnp.concatenate([c[:, :, k : k + n] for k in range(0, c.shape[2], n)], axis=3)
                c = jnp.moveaxis(c, 0, 1).reshape(c.shape[1], images[at_res], c.shape[3])
                cot_slabs.append(pad_images(c, at_res))
            pieces = after(pieces, cot_slabs)
        raw, even, odd, first, sums = student_forward(
            place,
            pieces,
            *[pad_images(p, res) for p in raw_halos[res]],
            tables[res],
            entry_total,
            norm_in,
            bands_first,
            tiles[res],
        )
        raws[res] = raw
        evens[res] = even
        odds[res] = odd
        firsts[res] = first
        first_sums[res] = sums
    inner_total = total_over_devices(first_sums, axes, 1, (corners(large_raw[1]), large_edges))

    large_edges.append(large_edges_of(1, inner_total))
    small_pieces = [
        [send(after(p, inner_total), to_sub(d + 1)) for d, p in enumerate(away)]
        for away in small_away[::-1]
    ][::-1]

    def small_rows(n, *others):
        own = small_part(parts_of[n], x)
        return edge_rows([own] + after(small_pieces[n], *others), 3)

    acts, own_firsts, sums_out, lows, energies = [], [], [], [], []
    for res in both:
        act, own_first, block_sum, low, energy = student_block(
            place,
            firsts[res],
            odds[res],
            tables[res],
            entry_total,
            inner_total,
            norm_mid,
            bands_second,
            gather,
            tiles[res],
        )
        acts.append(act)
        own_firsts.append(own_first)
        sums_out.append(block_sum)
        lows.append(low)
        energies.append(energy)

    shared = (
        teacher_first.reshape(9 * CT_IN, CT_OUT),
        teacher_second.reshape(9 * CT_OUT, CT_OUT),
        teacher_bypass,
        teacher_inner,
    )
    def large_map(k, *others):
        pieces = large_pieces[k]
        own = after(pieces[0], *others)
        edges = [pad_to(h, sizes[k]) for h in large_edges[k]]
        return teacher_energies(place, own, 0, pieces[1:], *edges, shared, tiles[1])

    def small_map(n, edges, *others):
        arrays = after((*small_pieces[n], *edges), *others)
        return [
            teacher_energies(
                place, small_active, parts_of[n][0], arrays[:-2], *arrays[-2:], shared, per_device[0]
            )
        ]

    large_maps = [large_map(0, inner_total)]
    rows = small_rows(0, large_maps[0], energies)
    edges = [to_neighbours(rows)]
    large_maps.append(large_map(1, rows))
    rows = small_rows(1, large_maps[1])
    edges.append(to_neighbours(rows))
    small_maps = small_map(0, edges[0], rows)
    for n in range(2, len(parts_of)):
        rows = small_rows(n, small_maps)
        edges.append(to_neighbours(rows))
        small_maps = small_maps + small_map(n - 1, edges[n - 1], rows)
    small_maps = small_maps + small_map(len(parts_of) - 1, edges[-1])
    factors = attention_maps(
        energies, [small_maps, large_maps], tables, widths, p_counts, slabs, group, 2
    )
    loss_sums = factors[2]

    def to_owners(res, *others):
        low = after(lows[res][:, : images[res]], *others)
        rows, _, lanes = low.shape
        return among_slabs(low.reshape(rows, slabs, per_device[res], lanes), 1)

    out_parts = [to_owners(0, factors[2])]

    flows, grads, flow_sums, second_parts, shortcut_parts = [], [], [], [], []
    for res in both:
        flow, grad, sums, second_part, shortcut_part = student_back(
            place,
            sums_out[res],
            cot_slabs[res],
            factors[res],
            scatter,
            own_firsts[res],
            acts[res],
            odds[res],
            tables[res],
            entry_total,
            inner_total,
            norm_mid,
            bands_second_back,
            tiles[res],
        )
        flows.append(flow)
        grads.append(grad)
        flow_sums.append(sums)
        second_parts.append(second_part)
        shortcut_parts.append(shortcut_part)
    flow_total = total_over_devices(flow_sums, axes, 3, out_parts)

    entry_parts, first_parts, entry_flow_sums = [], [], []
    held = None
    for res in both:
        flow = flows[res] if held is None else after(flows[res], held)
        *rows, first_part, sums = student_entry(
            place,
            flow,
            own_firsts[res],
            grads[res],
            evens[res],
            odds[res],
            raws[res],
            tables[res],
            entry_total,
            inner_total,
            flow_total,
            norm_in,
            norm_mid,
            bands_even,
            bands_odd,
            tiles[res],
            group,
        )
        if res == 0:
            held = rows[0]
        first_parts.append(first_part)
        entry_flow_sums.append(sums)
        rows = [r[:, : images[res]] for r in rows]
        if res == 0:
            rows[1:] = [send(r, to_sub(d + 1)) for d, r in enumerate(rows[1:])]
        entry_parts.append(rows)
    def native_rows(res):
        ordered = [lax.select_n((x - s) % group, *entry_parts[res]) for s in range(group)]
        n, rows, lanes = pixels[res].shape
        rows_in = jnp.stack(ordered).reshape(group, rows, slabs, per_device[res], lanes)
        return jnp.transpose(rows_in, (2, 0, 3, 1, 4)).reshape(n, rows, lanes)

    arrived_rows = [native_rows(0)]
    rate_scale = 1.0 / math.sqrt(total_positions)
    flat = lambda k: k.reshape(-1, k.shape[-1])
    kernel_states = [
        [flat(k) for k in (first_conv, momentum_first, average_first)],
        [flat(k) for k in (second_conv, momentum_second, average_second)],
        [shortcut, momentum_shortcut, average_shortcut],
    ]
    first_state, second_state, bypass_state, entry_state, image_tables, total_loss = finish(
        [first_parts, second_parts, shortcut_parts, entry_flow_sums, [loss_sums]],
        kernel_states,
        [entry_norm, momentum_entry, average_entry],
        entry_total,
        norm_in,
        (CONV_RATE * rate_scale, NORM_RATE * rate_scale, 1.0 / total_positions),
        axes,
        4,
        (entry_parts[0][1:], entry_parts[1]),
    )
    rows = entry_parts[1]
    rows[1:] = [send(after(r, image_tables), to_sub(d + 1)) for d, r in enumerate(rows[1:])]
    arrived_rows.append(native_rows(1))
    out_parts.append(to_owners(1, image_tables))
    first_state = [k.reshape(first_conv.shape) for k in first_state]
    second_state = [k.reshape(second_conv.shape) for k in second_state]
    inner_folded = flow_total.reshape(8, 128 // CS_OUT, CS_OUT).sum(axis=1)
    ones_inner, cross_inner = inner_folded[0:2], inner_folded[2:4]
    block_outs = []
    for res in both:
        low = jnp.transpose(out_parts[res], (2, 0, 1, 3))
        block_outs.append(low.reshape(low.shape[0], -1, low.shape[3]))

    input_grads = []
    for res in both:
        lanes = pixels[res].shape[2]
        one = (labels[res] == 1)[:, None, None]
        wide = jnp.tile(image_tables, (1, lanes // 128))
        gain, bias, slope, level = [
            jnp.where(one, wide[2 * k + 1], wide[2 * k]) for k in range(4)
        ]
        value = pixels[res].astype(F32)
        before = value * gain + bias
        s = jax.nn.sigmoid(before)
        flow = arrived_rows[res].astype(F32) * (s * (1.0 + before * (1.0 - s)))
        input_grads.append(gain * flow + (value * slope + level))

    inner_grads = jnp.stack([jnp.sum(cross_inner, axis=0), jnp.sum(ones_inner, axis=0)])
    inner_state = renew(inner_norm, inner_grads, momentum_inner, average_inner, NORM_RATE * rate_scale)
    return (
        *block_outs,
        input_grads[0],
        input_grads[1],
        total_loss.reshape(()),
        *entry_state,
        *first_state,
        *inner_state,
        *second_state,
        *bypass_state,
    )


def solution(mesh):
    rows = P("batch", "space", None)
    blocks = P(("batch", "space"), None, None)
    return jax.shard_map(
        functools.partial(body, mesh.shape["space"], mesh.shape["batch"]),
        mesh=mesh,
        in_specs=(rows,) * 4 + (P("batch"),) * 2 + (blocks,) * 2 + (P(),) * 20,
        out_specs=(blocks,) * 2 + (rows,) * 2 + (P(),) * 24,
        check_vma=False,
    )
```

```python
import functools
import math

import jax
import jax.numpy as jnp
import numpy as np
from jax import lax
from jax.experimental import pallas as pl
from jax.experimental.pallas import tpu as pltpu
from jax.sharding import PartitionSpec as P

CS_IN = 32
CS_OUT = 64
CT_IN = 128
CT_OUT = 256
SIDE = 32
SLABS = 4

EPSILON = 1e-05
TRANSFER_WEIGHT = 1000.0
MOMENTUM = 0.9
WEIGHT_DECAY = 0.0005
AVERAGING = 0.7
CONV_RATE = 0.06
NORM_RATE = 0.3

F32 = jnp.float32
BF16 = jnp.bfloat16
MESH = pl.DeviceIdType.MESH
VMEM_LIMIT = 56 << 20


def sigmoid(z):
    return 0.5 * jnp.tanh(0.5 * z) + 0.5


def matmul(a, b):
    return jnp.dot(a, b, preferred_element_type=F32)


def after(value, *others):
    return lax.optimization_barrier((value, others))[0]


def cost(microseconds):
    return pl.CostEstimate(
        flops=int(microseconds * 1e9), bytes_accessed=1 << 20, transcendentals=0
    )


def stacked(first, count, images, rows, parts):
    blocks = []
    for t in range(count):
        at = (first + t) * 256
        pieces = [ref[lo : lo + rows, :, at + off : at + off + size] for ref, lo, off, size in parts]
        block = jnp.concatenate(pieces, axis=2) if len(pieces) > 1 else pieces[0]
        blocks.append(block.reshape(rows * images, block.shape[2]))
    return jnp.concatenate(blocks, axis=0) if count > 1 else blocks[0]


def fold(rows, width):
    shift = width
    while shift < 128:
        rows = rows + pltpu.roll(rows, shift, 1)
        shift *= 2
    return rows


def group_norms(totals, counts, width):
    folded = fold(totals, width)
    means, scales = [], []
    for g in range(2):
        mean = folded[g : g + 1] / counts[g]
        variance = folded[2 + g : 3 + g] / counts[g] - mean * mean
        means.append(mean)
        scales.append(lax.rsqrt(variance + EPSILON))
    return means, scales


def per_image(w0, w1, pair):
    return w0 * pair[0] + w1 * pair[1]


def twice(table):
    return jnp.concatenate([table, table], axis=1)


def grouped_rows(w0, w1, values):
    rows = []
    for v in values:
        rows.append(jnp.sum(v * w0, axis=0, keepdims=True))
        rows.append(jnp.sum(v * w1, axis=0, keepdims=True))
    rows.append(jnp.zeros((8 - len(rows), 128), F32))
    return jnp.concatenate(rows, axis=0)


def entry_counts(tot_ref):
    return [tot_ref[4:5], tot_ref[5:6]]


def inner_counts(tot_ref):
    return [tot_ref[4:5] * 0.25, tot_ref[5:6] * 0.25]


def renew(weights, gradient, moment, average, factor):
    descent = gradient + WEIGHT_DECAY * weights
    velocity = MOMENTUM * moment + descent
    updated = weights - factor * (descent + MOMENTUM * velocity)
    smoothed = AVERAGING * average + (1.0 - AVERAGING) * updated
    return (gradient, velocity, smoothed, updated)


def stats_kernel(x_refs, label_refs, out_ref):
    step = pl.program_id(0)
    total = jnp.zeros((8, 128), F32)
    for x_ref, label_ref in zip(x_refs, label_refs):
        rows, images, lanes = x_ref.shape
        s = jnp.zeros((images, 128), F32)
        q = jnp.zeros((images, 128), F32)
        for r in range(rows):
            for c in range(0, lanes, 128):
                v = x_ref[r, :, c : c + 128].astype(F32)
                s = s + v
                q = q + v * v
        w0, w1 = indicators(label_ref)
        positions = jnp.full((images, 128), float(rows * lanes // CS_IN), F32)
        total = total + grouped_rows(w0, w1, [s, q, positions])

    @pl.when(step == 0)
    def _():
        out_ref[...] = total

    @pl.when(step > 0)
    def _():
        out_ref[...] += total


def input_stats(pieces, tables):
    steps = min(4, min(x.shape[0] for x in pieces))
    count = len(pieces)

    def kernel(*refs):
        stats_kernel(refs[:count], refs[count:-1], refs[-1])

    specs = [
        pl.BlockSpec((x.shape[0] // steps,) + x.shape[1:], lambda i: (i, 0, 0)) for x in pieces
    ]
    specs += [pl.BlockSpec(w.shape, lambda i: (0, 0)) for w in tables]
    return pl.pallas_call(
        kernel,
        grid=(steps,),
        in_specs=specs,
        out_specs=pl.BlockSpec((8, 128), lambda i: (0, 0)),
        out_shape=jax.ShapeDtypeStruct((8, 128), F32),
        compiler_params=pltpu.CompilerParams(vmem_limit_bytes=VMEM_LIMIT),
        cost_estimate=cost(5),
    )(*pieces, *tables)


def greet(axes):
    barrier = pltpu.get_barrier_semaphore()
    expected = 0
    for name, size in axes:
        me = lax.axis_index(name)
        for d in range(1, size):
            pl.semaphore_signal(
                barrier,
                inc=1,
                device_id={name: lax.rem(me + d, size)},
                device_id_type=MESH,
            )
            expected += 1
    pl.semaphore_wait(barrier, expected)


def total_kernel(axes, count, *refs):
    parts = refs[:count]
    out_ref, held, boxes_a, boxes_b, send_a, recv_a, send_b, recv_b = refs[-8:]
    value = parts[0][...]
    for part in parts[1:]:
        value = value + part[...]
    held[0] = value
    greet(axes)
    for level, ((name, size), boxes, send, recv) in enumerate(
        zip(axes, (boxes_a, boxes_b), (send_a, send_b), (recv_a, recv_b))
    ):
        me = lax.axis_index(name)
        copies = []
        for d in range(1, size):
            copy = pltpu.make_async_remote_copy(
                src_ref=held.at[level],
                dst_ref=boxes.at[d],
                send_sem=send.at[d],
                recv_sem=recv.at[d],
                device_id={name: lax.rem(me + d, size)},
                device_id_type=MESH,
            )
            copy.start()
            copies.append(copy)
        for copy in copies:
            copy.wait_recv()
        value = jnp.zeros(value.shape, F32)
        for source in range(size):
            back = lax.rem(me - source + size, size)
            value = value + jnp.where(
                back == 0, held[level], boxes[jnp.maximum(back, 1)]
            )
        for copy in copies:
            copy.wait_send()
        if level == 0:
            held[1] = value
        else:
            out_ref[...] = value


def total_over_devices(parts, axes, collective_id, waits):
    waits = jax.tree.leaves(waits)
    shape = parts[0].shape
    return pl.pallas_call(
        functools.partial(total_kernel, axes, len(parts)),
        out_shape=jax.ShapeDtypeStruct(shape, F32),
        in_specs=[pl.BlockSpec(memory_space=pltpu.VMEM)] * len(parts)
        + [pl.BlockSpec(memory_space=pl.ANY)] * len(waits),
        out_specs=pl.BlockSpec(memory_space=pltpu.VMEM),
        scratch_shapes=[
            pltpu.VMEM((2,) + shape, F32),
            pltpu.VMEM((axes[0][1],) + shape, F32),
            pltpu.VMEM((axes[1][1],) + shape, F32),
            pltpu.SemaphoreType.DMA((axes[0][1],)),
            pltpu.SemaphoreType.DMA((axes[0][1],)),
            pltpu.SemaphoreType.DMA((axes[1][1],)),
            pltpu.SemaphoreType.DMA((axes[1][1],)),
        ],
        compiler_params=pltpu.CompilerParams(collective_id=collective_id, has_side_effects=True),
        cost_estimate=cost(12),
    )(*parts, *waits)


def gradient_sum_kernel(axes, layout, waits, *refs):
    count = sum(len(parts) for parts in layout)
    inputs, refs = refs[:count], refs[count + waits :]
    out_ref, x_ref, boxes_a, boxes_b, held = refs[:5]
    send_a, recv_a, send_b, recv_b, send_c, recv_c = refs[5:]
    at = 0
    for parts in layout:
        value = inputs[parts[0]][...]
        for k in parts[1:]:
            value = value + inputs[k][...]
        parts = 128 // value.shape[1]
        if parts > 1:
            n = value.shape[0] // parts
            value = jnp.concatenate([value[k * n : k * n + n] for k in range(parts)], axis=1)
        x_ref[at : at + value.shape[0]] = value
        at += value.shape[0]
    if at < x_ref.shape[0]:
        x_ref[at:] = jnp.zeros((x_ref.shape[0] - at, 128), F32)
    (name_a, size_a), (name_b, size_b) = axes
    me_a, me_b = lax.axis_index(name_a), lax.axis_index(name_b)
    piece = x_ref.shape[0] // size_a
    greet(axes)

    def rows(index):
        return pl.ds(pl.multiple_of(index * piece, 8), piece)

    copies = []
    for d in range(1, size_a):
        peer = lax.rem(me_a + d, size_a)
        copy = pltpu.make_async_remote_copy(
            src_ref=x_ref.at[rows(peer)],
            dst_ref=boxes_a.at[d],
            send_sem=send_a.at[d],
            recv_sem=recv_a.at[d],
            device_id={name_a: peer},
            device_id_type=MESH,
        )
        copy.start()
        copies.append(copy)
    value = x_ref[rows(me_a)]
    for d in range(1, size_a):
        copies[d - 1].wait_recv()
        value = value + boxes_a[d]
    held[0] = value
    for copy in copies:
        copy.wait_send()
    copies = []
    for d in range(1, size_b):
        copy = pltpu.make_async_remote_copy(
            src_ref=held.at[0],
            dst_ref=boxes_b.at[d],
            send_sem=send_b.at[d],
            recv_sem=recv_b.at[d],
            device_id={name_b: lax.rem(me_b + d, size_b)},
            device_id_type=MESH,
        )
        copy.start()
        copies.append(copy)
    for copy in copies:
        copy.wait_recv()
    value = jnp.zeros(value.shape, F32)
    for source in range(size_b):
        back = lax.rem(me_b - source + size_b, size_b)
        value = value + jnp.where(back == 0, held[0], boxes_b[jnp.maximum(back, 1)])
    held[1] = value
    out_ref[rows(me_a)] = value
    for copy in copies:
        copy.wait_send()
    copies = []
    for d in range(1, size_a):
        copy = pltpu.make_async_remote_copy(
            src_ref=held.at[1],
            dst_ref=out_ref.at[rows(me_a)],
            send_sem=send_c.at[d],
            recv_sem=recv_c.at[d],
            device_id={name_a: lax.rem(me_a + d, size_a)},
            device_id_type=MESH,
        )
        copy.start()
        copies.append(copy)
    for copy in copies:
        copy.wait()


def update_kernel(rates, *refs):
    out_ref, tot, norm = refs[:3]
    states, entry, outs = refs[3:12], refs[12:15], refs[15:]
    conv_rate, norm_rate, per_position = rates
    at = 0
    for k in range(3):
        weights, moment, average = [ref[...] for ref in states[3 * k : 3 * k + 3]]
        width = (CS_IN, CS_OUT, CS_IN)[k]
        n = weights.shape[0] * weights.shape[1] // 128
        packed = out_ref[at : at + n]
        at += n
        parts = [packed[:, lane : lane + width] for lane in range(0, 128, width)]
        turned = jnp.concatenate(parts, axis=0)
        taps = turned.shape[0] // CS_OUT
        gradient = jnp.concatenate(
            [turned[t * CS_OUT : (t + 1) * CS_OUT].T for t in range(taps)], axis=0
        )
        state = renew(weights, gradient, moment, average, conv_rate)
        for ref, value in zip(outs[5 * k : 5 * k + 4], state):
            ref[...] = value
        outs[5 * k + 4][...] = state[3].astype(BF16)
    pulled = fold(out_ref[at : at + 8], CS_IN)
    ones, cross = [pulled[0:1], pulled[1:2]], [pulled[2:3], pulled[3:4]]
    gradient = jnp.concatenate([cross[0] + cross[1], ones[0] + ones[1]], axis=0)[:, 0:CS_IN]
    state = renew(entry[0][...], gradient, entry[1][...], entry[2][...], norm_rate)
    for ref, value in zip(outs[15:19], state):
        ref[...] = value
    counts = entry_counts(tot)
    means, scales = group_norms(tot[...], counts, CS_IN)
    gains, biases, slopes, levels = [], [], [], []
    for g in range(2):
        shift = -means[g] * scales[g]
        gain = norm[0:1] * scales[g]
        gains.append(gain)
        biases.append(norm[0:1] * shift + norm[1:2])
        slopes.append(-gain * (cross[g] / counts[g]) * scales[g])
        levels.append(-gain * ((ones[g] + cross[g] * shift) / counts[g]))
    outs[19][...] = jnp.concatenate(gains + biases + slopes + levels, axis=0)
    losses = out_ref[at + 8 : at + 9]
    outs[20][...] = jnp.sum(losses, axis=1, keepdims=True) * per_position


def gradient_sum(groups, axes, collective_id, waits):
    (_, size_a), (_, size_b) = axes
    arrays, layout, rows = [], [], []
    for members in groups:
        layout.append(tuple(range(len(arrays), len(arrays) + len(members))))
        arrays += members
        rows.append(members[0].shape[0] * members[0].shape[1] // 128)
    padded = -(-sum(rows) // (8 * size_a)) * 8 * size_a
    piece = padded // size_a
    sems = []
    for size in (size_a, size_b, size_a):
        sems += [pltpu.SemaphoreType.DMA((size,))] * 2
    waits = jax.tree.leaves(waits)
    vmem = pl.BlockSpec(memory_space=pltpu.VMEM)
    return pl.pallas_call(
        functools.partial(gradient_sum_kernel, axes, tuple(layout), len(waits)),
        out_shape=jax.ShapeDtypeStruct((padded, 128), F32),
        in_specs=[vmem] * len(arrays) + [pl.BlockSpec(memory_space=pl.ANY)] * len(waits),
        out_specs=vmem,
        scratch_shapes=[
            pltpu.VMEM((padded, 128), F32),
            pltpu.VMEM((size_a, piece, 128), F32),
            pltpu.VMEM((size_b, piece, 128), F32),
            pltpu.VMEM((2, piece, 128), F32),
        ]
        + sems,
        compiler_params=pltpu.CompilerParams(collective_id=collective_id, has_side_effects=True),
        cost_estimate=cost(20),
    )(*arrays, *waits)


def update(total, states, entry, tot, norm, rates):
    given = [total, tot, norm] + [a for state in states for a in state] + entry
    outs = []
    for state in states:
        outs += [shape_of(state[0].shape, F32)] * 4 + [shape_of(state[0].shape, BF16)]
    outs += [shape_of(entry[0].shape, F32)] * 4 + [shape_of((8, 128), F32), shape_of((1, 1), F32)]
    vmem = pl.BlockSpec(memory_space=pltpu.VMEM)
    got = pl.pallas_call(
        functools.partial(update_kernel, rates),
        out_shape=outs,
        in_specs=[vmem] * len(given),
        out_specs=[vmem] * len(outs),
        compiler_params=pltpu.CompilerParams(vmem_limit_bytes=VMEM_LIMIT),
        cost_estimate=cost(4),
    )(*given)
    return got[0:5], got[5:10], got[10:15], got[15:19], got[19], got[20]


def teacher_kernel(p_rows, width, group, columns, place, *refs):
    pieces, refs = refs[:group], refs[group:]
    edge_a, edge_b, first, second, bypass, inner, out_ref, even, odd, mid = refs
    local, lanes = pieces[0].shape[0], pieces[0].shape[-1]
    real, images = edge_a.shape[1], even.shape[1]
    m_rows = p_rows + 2
    zero = jnp.zeros((images, 128), BF16)

    def put(row, source, at):
        if row % 2 == 0:
            even[row // 2 + 1, 0:real, 128 : 128 + lanes] = source[at]
        else:
            odd[(row + 1) // 2 + 1, 0:real, 128 : 128 + lanes] = source[at]

    def put_edges(above, below):
        for k in range(3):
            put(k - 3, above, k)
        for k in range(2):
            put(2 * p_rows + k, below, k)

    rows_of_neighbours(place, edge_a, edge_b, put_edges)
    nothing = jnp.zeros((1, real, lanes), BF16)

    @pl.when(place[1] == 0)
    def _():
        for k in range(3):
            put(k - 3, nothing, 0)

    @pl.when(place[1] == SLABS - 1)
    def _():
        for k in range(2):
            put(2 * p_rows + k, nothing, 0)

    x = place[0]
    for s in range(group):
        distance = lax.rem(x - s + group, group)
        for d in range(group):

            @pl.when(distance == d)
            def _():
                for k in range(local):
                    at = (k, 0, 0) if len(pieces[d].shape) == 5 else k
                    put(s * local + k, pieces[d], at)

    for i in range(m_rows):
        even[i, :, 0:128] = zero
    for i in range(m_rows + 1):
        odd[i, :, 0:128] = zero
    wide_zero = jnp.zeros((images, CT_OUT), BF16)
    for i in range(m_rows):
        mid[i, :, 0:CT_OUT] = wide_zero
        mid[i, :, (width + 1) * CT_OUT : (width + 2) * CT_OUT] = wide_zero
    scale, shift = inner[0:1], inner[1:2]
    top, bottom = keep_row(place, -1, p_rows), keep_row(place, p_rows, p_rows)

    def first_step(g, carry):
        lefts = []
        for t in range(columns):
            window = pl.ds(pl.multiple_of((g * columns + t) * 256, 256), 384)
            parts = [odd[0:m_rows, :, window], even[0:m_rows, :, window]]
            parts.append(odd[1 : m_rows + 1, :, window])
            lefts.append(jnp.concatenate(parts, axis=2).reshape(m_rows * images, 9 * CT_IN))
        z = scale * matmul(jnp.concatenate(lefts, axis=0), first[...]) + shift
        act = (z * sigmoid(z)).reshape(columns, m_rows, images, CT_OUT)
        for t in range(columns):
            here = pl.ds(pl.multiple_of((g * columns + t + 1) * CT_OUT, 256), CT_OUT)
            mid[0, :, here] = (act[t, 0] * top).astype(BF16)
            mid[1 : p_rows + 1, :, here] = act[t, 1 : p_rows + 1].astype(BF16)
            mid[p_rows + 1, :, here] = (act[t, p_rows + 1] * bottom).astype(BF16)
        return carry

    lax.fori_loop(0, width // columns, first_step, 0)
    out_ref[...] = jnp.zeros(out_ref.shape, F32)
    lane = lax.broadcasted_iota(jnp.int32, (real, 128), 1)

    def second_step(g, carry):
        lefts, corners = [], []
        for t in range(columns):
            at = pl.multiple_of((g * columns + t) * 256, 256)
            window = pl.ds(at, 3 * CT_OUT)
            corner = pl.ds(pl.multiple_of(at + 128, 128), 128)
            parts = [mid[a : a + p_rows, :, window] for a in range(3)]
            lefts.append(jnp.concatenate(parts, axis=2).reshape(p_rows * images, 9 * CT_OUT))
            corners.append(even[1 : p_rows + 1, :, corner].reshape(p_rows * images, CT_IN))
        y = matmul(jnp.concatenate(lefts, axis=0), second[...])
        y = y + matmul(jnp.concatenate(corners, axis=0), bypass[...])
        square = y * y
        energy = jnp.sum(square[:, 0:128] + square[:, 128:256], axis=1, keepdims=True)
        energy = (energy * (1.0 / CT_OUT)).reshape(columns, p_rows, images, 1)
        for t in range(columns):
            for p in range(p_rows):
                chunk, start = divmod((p + 1) * width, 128)
                where = slice(chunk * 128, chunk * 128 + 128)
                here = lane == start + g * columns + t
                out_ref[:, where] = jnp.where(here, energy[t, p, 0:real], out_ref[:, where])
        return carry

    lax.fori_loop(0, width // columns, second_step, 0)


def teacher_energies(place, own, slab, received, edge_a, edge_b, shared, tile):
    group = len(received) + 1
    local, lanes = own.shape[0], own.shape[-1]
    images = edge_a.shape[1]
    p_rows, width = group * local // 2, lanes // (2 * CT_IN)
    out_lanes = -(-(p_rows + 3) * width // 128) * 128
    m_rows = p_rows + 2
    space = -(-tile // 16) * 16
    if own.ndim == 5:
        own_spec = pl.BlockSpec(
            (local, 1, 1, tile, lanes), lambda i, place: (0, slab + i, place[0], 0, 0)
        )
    else:
        own_spec = pl.BlockSpec((local, tile, lanes), lambda i, place: (0, i, 0))
    whole = lambda a: pl.BlockSpec(a.shape, lambda i, place: (0,) * a.ndim)
    by_image = lambda a: pl.BlockSpec((a.shape[0], tile, a.shape[2]), lambda i, place: (0, i, 0))
    grid_spec = pltpu.PrefetchScalarGridSpec(
        num_scalar_prefetch=1,
        grid=(images // tile,),
        in_specs=[own_spec]
        + [by_image(a) for a in received]
        + [by_image(edge_a), by_image(edge_b)]
        + [whole(a) for a in shared],
        out_specs=pl.BlockSpec((tile, out_lanes), lambda i, place: (i, 0)),
        scratch_shapes=[
            pltpu.VMEM((m_rows, space, 128 + lanes), BF16),
            pltpu.VMEM((m_rows + 1, space, 128 + lanes), BF16),
            pltpu.VMEM((m_rows, space, (width + 2) * CT_OUT), BF16),
        ],
    )
    return pl.pallas_call(
        functools.partial(teacher_kernel, p_rows, width, group, 4),
        grid_spec=grid_spec,
        out_shape=jax.ShapeDtypeStruct((images, out_lanes), F32),
        compiler_params=pltpu.CompilerParams(vmem_limit_bytes=VMEM_LIMIT),
        cost_estimate=cost(40 * images * p_rows * width / 10240),
    )(place, own, *received, edge_a, edge_b, *shared)


def entry_tables(tot_ref, norm_ref, w0, w1):
    means, scales = group_norms(tot_ref[...], entry_counts(tot_ref), CS_IN)
    scale = per_image(w0, w1, scales)
    shift = per_image(w0, w1, [-m * s for m, s in zip(means, scales)])
    gain, bias = norm_ref[0:1], norm_ref[1:2]
    present = w0 + w1
    return gain * scale, gain * shift + bias * present, scale, shift


def inner_tables(tot_ref, inner_ref, norm_ref, w0, w1):
    means, scales = group_norms(inner_ref[...], inner_counts(tot_ref), CS_OUT)
    scale = per_image(w0, w1, scales)
    shift = per_image(w0, w1, [-m * s for m, s in zip(means, scales)])
    gain, bias = norm_ref[0:1], norm_ref[1:2]
    present = w0 + w1
    return gain * scale, gain * shift + bias * present, scale, shift


def indicators(label_ref):
    label = label_ref[...]
    return (label == 0.0).astype(F32), (label == 1.0).astype(F32)


def keep_row(place, row, inside):
    z = place[1]
    outside = jnp.logical_or(
        jnp.logical_and(row < 0, z == 0), jnp.logical_and(row >= inside, z == SLABS - 1)
    )
    return jnp.where(outside, 0.0, 1.0)


def rows_of_neighbours(place, first, second, use):
    even = lax.rem(place[1], 2) == 0

    @pl.when(even)
    def _():
        use(second, first)

    @pl.when(jnp.logical_not(even))
    def _():
        use(first, second)


def add_rows(ref, value):
    first = pl.program_id(0) == 0

    @pl.when(first)
    def _():
        ref[...] = value

    @pl.when(jnp.logical_not(first))
    def _():
        ref[...] += value


def forward_kernel(
    p_rows, group, blocks, place, *refs
):
    pieces, refs = refs[:group], refs[group:]
    first, second, label_ref, tot, norm, weights = refs[:6]
    raw_ref, even_ref, odd_ref, out_ref, stats, raw, even, odd = refs[6:]
    images, lanes = raw.shape[1:]
    local = pieces[0].shape[0]
    w0, w1 = indicators(label_ref)
    gain, bias, _, _ = entry_tables(tot, norm, w0, w1)
    gain2, bias2 = twice(gain), twice(bias)
    zero = jnp.zeros((images, 128), BF16)

    def put_edges(above, below):
        raw[0:5] = above[1:6]
        raw[2 * p_rows + 5 : 2 * p_rows + 11] = below[...]

    rows_of_neighbours(place, first, second, put_edges)
    x = place[0]
    for s in range(group):
        distance = lax.rem(x - s + group, group)
        for d in range(group):

            @pl.when(distance == d)
            def _():
                raw[5 + s * local : 5 + (s + 1) * local] = pieces[d][...]

    def activate(row, target, index):
        keep = keep_row(place, row - 5, 2 * p_rows)
        target[index, :, 0:128] = zero
        for c in range(0, lanes, 256):
            z = raw[row, :, c : c + 256].astype(F32) * gain2 + bias2
            target[index, :, 128 + c : 384 + c] = (z * sigmoid(z) * keep).astype(BF16)

    def pair(i, carry):
        activate(2 * i, even, i)
        activate(2 * i + 1, odd, i)
        return carry

    f_rows = p_rows + 5
    lax.fori_loop(0, f_rows, pair, 0)
    activate(2 * f_rows, even, f_rows)
    raw_ref[...] = raw[5 : 2 * p_rows + 5]
    even_ref[...] = even[2 : p_rows + 3]
    odd_ref[...] = odd[1 : p_rows + 4]
    s = jnp.zeros((images, 128), F32)
    q = jnp.zeros((images, 128), F32)
    for j in range(0, lanes // 256, blocks):
        left = stacked(
            j, blocks, images, f_rows, [(even, 0, 0, 384), (odd, 0, 0, 384), (even, 1, 0, 384)]
        )
        y = matmul(left, weights[...]).reshape(blocks, f_rows, images, 256)
        for t in range(blocks):
            out_ref[:, :, (j + t) * 256 : (j + t + 1) * 256] = y[t]
            own = y[t, 2 : 2 + p_rows]
            u = jnp.sum(own, axis=0)
            v = jnp.sum(own * own, axis=0)
            s = s + u[:, 0:128] + u[:, 128:256]
            q = q + v[:, 0:128] + v[:, 128:256]
    add_rows(stats, grouped_rows(w0, w1, [s, q]))


def whole_spec(a):
    return pl.BlockSpec(a.shape, lambda i, *_: (0,) * len(a.shape))


def image_spec(a, tile):
    return pl.BlockSpec((a.shape[0], tile, a.shape[2]), lambda i, *_: (0, i, 0))


def table_spec(a, tile):
    return pl.BlockSpec((tile, a.shape[1]), lambda i, *_: (i, 0))


def shape_of(shape, dtype):
    return jax.ShapeDtypeStruct(shape, dtype)


def student_forward(place, pieces, first, second, label, tot, norm, weights, tile):
    group = len(pieces)
    local, images, lanes = pieces[0].shape
    p_rows = group * local // 2
    outs = [
        shape_of((2 * p_rows, images, lanes), BF16),
        shape_of((p_rows + 1, images, 128 + lanes), BF16),
        shape_of((p_rows + 3, images, 128 + lanes), BF16),
        shape_of((p_rows + 5, images, lanes), F32),
    ]
    stats = shape_of((8, 128), F32)
    big = (*pieces, first, second)
    shared = (tot, norm, weights)
    grid_spec = pltpu.PrefetchScalarGridSpec(
        num_scalar_prefetch=1,
        grid=(images // tile,),
        in_specs=[image_spec(a, tile) for a in big]
        + [table_spec(label, tile)]
        + [whole_spec(a) for a in shared],
        out_specs=[image_spec(o, tile) for o in outs] + [whole_spec(stats)],
        scratch_shapes=[
            pltpu.VMEM((2 * p_rows + 11, tile, lanes), BF16),
            pltpu.VMEM((p_rows + 6, tile, 128 + lanes), BF16),
            pltpu.VMEM((p_rows + 5, tile, 128 + lanes), BF16),
        ],
    )
    return pl.pallas_call(
        functools.partial(forward_kernel, p_rows, group, 4),
        grid_spec=grid_spec,
        out_shape=outs + [stats],
        compiler_params=pltpu.CompilerParams(vmem_limit_bytes=VMEM_LIMIT),
        cost_estimate=cost(15),
    )(place, *big, label, *shared)


def split_bf16(value):
    high = value.astype(BF16)
    return high, (value - high.astype(F32)).astype(BF16)


def block_kernel(
    p_rows,
    blocks,
    place,
    first_ref,
    odd,
    label_ref,
    tot,
    inner,
    norm,
    weights,
    spread,
    act_ref,
    own_ref,
    sum_ref,
    low_ref,
    energy,
    act,
):
    images, lanes = first_ref.shape[1:]
    w0, w1 = indicators(label_ref)
    gain, bias, _, _ = inner_tables(tot, inner, norm, w0, w1)
    gain2, bias2 = twice(gain), twice(bias)
    zero = jnp.zeros((images, 128), BF16)
    f_rows, b_rows = p_rows + 5, p_rows + 3

    def activate(f, carry):
        keep = keep_row(place, f - 2, p_rows)
        act[f, :, 0:128] = zero
        act[f, :, 128 + lanes : 256 + lanes] = zero
        for c in range(0, lanes, 256):
            z = first_ref[f, :, c : c + 256] * gain2 + bias2
            act[f, :, 128 + c : 384 + c] = (z * sigmoid(z) * keep).astype(BF16)
        return carry

    lax.fori_loop(0, f_rows, activate, 0)
    act_ref[...] = act[1 : p_rows + 3]
    own_ref[...] = first_ref[2 : p_rows + 3]

    per_chunk = 128 // (lanes // CS_OUT)
    chunks = energy.shape[1] // 128
    measured = [jnp.zeros((images, 128), F32) for _ in range(chunks)]
    for j in range(0, lanes // 256, blocks):
        parts = [(act, a, 0, 512) for a in range(3)] + [(odd, 0, 128, 256)]
        left = stacked(j, blocks, images, b_rows, parts)
        flat = matmul(left, weights[...])
        y = flat.reshape(blocks, b_rows, images, 256)
        high, low = split_bf16(flat * flat)
        e = matmul(jnp.concatenate([high, low], axis=1), spread[...])
        e = e.reshape(blocks, b_rows, images, 128)
        for t in range(blocks):
            here = slice((j + t) * 256, (j + t + 1) * 256)
            sum_ref[:, :, here] = y[t]
            low_ref[:, :, here] = y[t, 1 : p_rows + 1].astype(BF16)
            for b in range(b_rows):
                shift = b % per_chunk * (128 // per_chunk) + 4 * (j + t)
                part = pltpu.roll(e[t, b], shift, 1) if shift else e[t, b]
                measured[b // per_chunk] = measured[b // per_chunk] + part
    for c in range(chunks):
        energy[:, c * 128 : c * 128 + 128] = measured[c]


def student_block(place, first_out, odd, label, tot, inner, norm, weights, spread, tile):
    rows, images, lanes = first_out.shape
    p_rows = rows - 5
    width = lanes // CS_OUT
    energy_lanes = -(-(p_rows + 3) * width // 128) * 128
    outs = [
        shape_of((p_rows + 2, images, 256 + lanes), BF16),
        shape_of((p_rows + 1, images, lanes), F32),
        shape_of((p_rows + 3, images, lanes), F32),
        shape_of((p_rows, images, lanes), BF16),
    ]
    energy = shape_of((images, energy_lanes), F32)
    return pl.pallas_call(
        functools.partial(block_kernel, p_rows, 4),
        grid_spec=pltpu.PrefetchScalarGridSpec(
            num_scalar_prefetch=1,
            grid=(images // tile,),
            in_specs=[image_spec(first_out, tile), image_spec(odd, tile), table_spec(label, tile)]
            + [whole_spec(a) for a in (tot, inner, norm, weights, spread)],
            out_specs=[image_spec(o, tile) for o in outs] + [table_spec(energy, tile)],
            scratch_shapes=[pltpu.VMEM((p_rows + 5, tile, 256 + lanes), BF16)],
        ),
        out_shape=outs + [energy],
        compiler_params=pltpu.CompilerParams(vmem_limit_bytes=VMEM_LIMIT),
        cost_estimate=cost(18),
    )(place, first_out, odd, label, tot, inner, norm, weights, spread)


def map_kernel(slabs, group, widths, p_counts, pieces, *refs):
    student, present = refs[0:2], refs[2:4]
    given = refs[4 : 4 + sum(pieces)]
    refs = refs[4 + sum(pieces) :]
    outs, loss_ref = refs[0:2], refs[2]
    teacher, sums, boxes = refs[3:5], refs[5:7], refs[7:9]
    from_above, from_below = refs[9:11], refs[11:13]
    send, recv, send_halo, recv_halo, ready = refs[13:]
    for res in range(2):
        at = 0
        for part in given[res * pieces[0] : res * pieces[0] + pieces[res]]:
            teacher[res][at : at + part.shape[0]] = part[...]
            at += part.shape[0]
        rest = teacher[res].shape[0] - at
        if rest:
            teacher[res][at:] = jnp.zeros((rest, teacher[res].shape[1]), F32)
    me = lax.axis_index("space")
    z, x = lax.div(me, group), lax.rem(me, group)
    greet_barrier = pltpu.get_barrier_semaphore()
    for d in range(1, slabs):
        pl.semaphore_signal(
            greet_barrier,
            inc=1,
            device_id={"space": lax.rem(z + d, slabs) * group + x},
            device_id_type=MESH,
        )
    pl.semaphore_wait(greet_barrier, slabs - 1)

    def halo_copies(res, direction):
        width, p_rows = widths[res], p_counts[res]
        lane = (p_rows * width if direction == 0 else width) // 128 * 128
        target = (from_above, from_below)[direction][res]
        return pltpu.make_async_remote_copy(
            src_ref=teacher[res].at[:, pl.ds(lane, 128)],
            dst_ref=target,
            send_sem=send_halo.at[2 * res + direction],
            recv_sem=recv_halo.at[2 * res + direction],
            device_id={"space": me + (group if direction == 0 else -group)},
            device_id_type=MESH,
        )

    for res in range(2):
        from_above[res][...] = jnp.zeros(from_above[res].shape, F32)
        from_below[res][...] = jnp.zeros(from_below[res].shape, F32)

    @pl.when(z > 0)
    def _():
        pl.semaphore_signal(
            ready.at[0], inc=1, device_id={"space": me - group}, device_id_type=MESH
        )

    @pl.when(z < slabs - 1)
    def _():
        pl.semaphore_signal(
            ready.at[1], inc=1, device_id={"space": me + group}, device_id_type=MESH
        )
        pl.semaphore_wait(ready.at[0], 1)
        halo_copies(0, 0).start()
        halo_copies(1, 0).start()

    @pl.when(z > 0)
    def _():
        pl.semaphore_wait(ready.at[1], 1)
        halo_copies(0, 1).start()
        halo_copies(1, 1).start()

    copies = []
    for res in range(2):
        width, p_rows = widths[res], p_counts[res]
        images, lanes = student[res].shape
        lane = lax.broadcasted_iota(jnp.int32, (images, lanes), 1)
        own = jnp.logical_and(lane >= width, lane < (p_rows + 1) * width)
        es = jnp.where(own, student[res][...], 0.0)
        et = jnp.where(own, teacher[res][...], 0.0)
        columns = [
            jnp.sum(v, axis=1, keepdims=True) for v in (es * es, et * et, es * et)
        ]
        small_lane = lax.broadcasted_iota(jnp.int32, (images, 128), 1)
        packed = jnp.zeros((images, 128), F32)
        for k, column in enumerate(columns):
            packed = jnp.where(small_lane == k, column, packed)
        padded = sums[res].shape[1]
        packed = jnp.concatenate([packed, jnp.zeros((padded - images, 128), F32)], axis=0)
        sums[res][...] = packed.T[0:8]
        for d in range(1, slabs):
            copy = pltpu.make_async_remote_copy(
                src_ref=sums[res],
                dst_ref=boxes[res].at[d],
                send_sem=send.at[res * slabs + d],
                recv_sem=recv.at[res * slabs + d],
                device_id={"space": lax.rem(z + d, slabs) * group + x},
                device_id_type=MESH,
            )
            copy.start()
            copies.append(copy)
    for copy in copies:
        copy.wait()

    @pl.when(z < slabs - 1)
    def _():
        halo_copies(0, 0).wait_send()
        halo_copies(1, 0).wait_send()
        halo_copies(0, 1).wait_recv()
        halo_copies(1, 1).wait_recv()

    @pl.when(z > 0)
    def _():
        halo_copies(0, 1).wait_send()
        halo_copies(1, 1).wait_send()
        halo_copies(0, 0).wait_recv()
        halo_copies(1, 0).wait_recv()

    loss = jnp.zeros((1, 128), F32)
    for res in range(2):
        width, p_rows = widths[res], p_counts[res]
        images, lanes = student[res].shape
        total = sums[res][...]
        for d in range(1, slabs):
            total = total + boxes[res][d]
        padded = total.shape[1]
        total = jnp.concatenate([total, jnp.zeros((120, padded), F32)], axis=0).T[0:images]
        ss, tt, st = total[:, 0:1], total[:, 1:2], total[:, 2:3]
        scale_s = lax.rsqrt(ss + 1e-12)
        scale_t = lax.rsqrt(tt + 1e-12)
        pulled = TRANSFER_WEIGHT * scale_s * (scale_s * ss - scale_t * st)
        lane = lax.broadcasted_iota(jnp.int32, (images, lanes), 1)
        shift = p_rows * width
        chunks = lanes // 128
        first_rows = from_below[res][...]
        last_rows = from_above[res][...]
        if shift % 128:
            first_rows = pltpu.roll(first_rows, shift % 128, 1)
            last_rows = pltpu.roll(last_rows, 128 - shift % 128, 1)
        blank = jnp.zeros((images, 128), F32)
        before = [last_rows] + [blank] * (chunks - 1)
        after = [blank] * (chunks - 1) + [first_rows]
        before = jnp.concatenate(before, axis=1) if chunks > 1 else before[0]
        after = jnp.concatenate(after, axis=1) if chunks > 1 else after[0]
        et = jnp.where(lane < width, before, teacher[res][...])
        et = jnp.where(lane >= (p_rows + 1) * width, after, et)
        u = student[res][...] * scale_s
        difference = u - et * scale_t
        own = jnp.logical_and(lane >= width, lane < (p_rows + 1) * width)
        squares = jnp.where(own, difference * difference, 0.0)
        kept = (present[res][...] >= 0.0).astype(F32)
        for c in range(chunks):
            loss = loss + jnp.sum(squares[:, c * 128 : c * 128 + 128] * kept, axis=0, keepdims=True)
        factor = (TRANSFER_WEIGHT * difference - u * pulled) * (scale_s * (2.0 / CS_OUT))
        for c in range(chunks):
            here = slice(c * 128, c * 128 + 128)
            outs[res][:, here] = jnp.where(kept > 0.0, factor[:, here], 0.0)
    loss_ref[...] = jnp.concatenate(
        [loss * (TRANSFER_WEIGHT / 2), jnp.zeros((7, 128), F32)], axis=0
    )


def attention_maps(student, teacher, present, widths, p_counts, slabs, group, collective_id):
    padded = [-(-s.shape[0] // 128) * 128 for s in student]
    images = [s.shape[0] for s in student]
    vmem = pl.BlockSpec(memory_space=pltpu.VMEM)
    return pl.pallas_call(
        functools.partial(
            map_kernel, slabs, group, widths, p_counts, tuple(len(t) for t in teacher)
        ),
        out_shape=[shape_of(s.shape, F32) for s in student] + [shape_of((8, 128), F32)],
        in_specs=[vmem] * (4 + sum(len(t) for t in teacher)),
        out_specs=[vmem] * 3,
        scratch_shapes=[pltpu.VMEM(s.shape, F32) for s in student]
        + [pltpu.VMEM((8, n), F32) for n in padded]
        + [pltpu.VMEM((slabs, 8, n), F32) for n in padded]
        + [pltpu.VMEM((n, 128), F32) for n in images] * 2
        + [pltpu.SemaphoreType.DMA((2 * slabs,))] * 2
        + [pltpu.SemaphoreType.DMA((4,))] * 2
        + [pltpu.SemaphoreType.REGULAR((2,))],
        compiler_params=pltpu.CompilerParams(collective_id=collective_id, has_side_effects=True),
        cost_estimate=cost(11),
    )(*student, *present, *teacher[0], *teacher[1])


def back_kernel(
    p_rows,
    blocks,
    place,
    sum_ref,
    cot,
    factor,
    spread,
    first_ref,
    act,
    odd,
    label_ref,
    tot,
    inner,
    norm,
    weights,
    flow_ref,
    grad_ref,
    stats,
    second_ref,
    shortcut_ref,
    kernel_ref,
    grad,
):
    images, lanes = sum_ref.shape[1:]
    w0, w1 = indicators(label_ref)
    gain, bias, scale, shift = inner_tables(tot, inner, norm, w0, w1)
    gain2, bias2, scale2, shift2 = twice(gain), twice(bias), twice(scale), twice(shift)
    zero = jnp.zeros((images, 128), BF16)
    b_rows, k_rows = p_rows + 3, p_rows + 1
    width = lanes // CS_OUT
    per_chunk = 128 // width
    for b in range(b_rows):
        grad[b, :, 0:128] = zero
        grad[b, :, 128 + lanes : 256 + lanes] = zero
    halves = [split_bf16(factor[:, c * 128 : c * 128 + 128]) for c in range(factor.shape[1] // 128)]
    halves = [[h.astype(F32) for h in pair] for pair in halves]
    for j in range(0, lanes // 256, blocks):
        rows = []
        for t in range(blocks):
            for b in range(b_rows):
                shift = (128 - (b % per_chunk * width + 4 * (j + t))) % 128
                pair = halves[b // per_chunk]
                if shift:
                    pair = [pltpu.roll(h, shift, 1) for h in pair]
                rows.append(jnp.concatenate(pair, axis=1))
        wide = matmul(jnp.concatenate(rows, axis=0).astype(BF16), spread[...])
        wide = wide.reshape(blocks, b_rows, images, 256)
        for t in range(blocks):
            at = (j + t) * 256
            for b in range(b_rows):
                keep = keep_row(place, b - 1, p_rows)
                v = cot[b, :, at : at + 256].astype(F32) + wide[t, b] * sum_ref[b, :, at : at + 256]
                grad[b, :, 128 + at : 384 + at] = (v * keep).astype(BF16)

    grad_ref[...] = grad[1 : p_rows + 1, :, 128 : 128 + lanes]

    @pl.when(pl.program_id(0) == 0)
    def _():
        kernel_ref[...] = jnp.zeros(kernel_ref.shape, F32)

    ones = jnp.zeros((images, 128), F32)
    cross = jnp.zeros((images, 128), F32)
    for j in range(0, lanes // 256, blocks):
        left = stacked(j, blocks, images, k_rows, [(grad, d, 0, 512) for d in range(3)])
        y = matmul(left, weights[...]).reshape(blocks, k_rows, images, 256)
        for t in range(blocks):
            here = slice((j + t) * 256, (j + t + 1) * 256)
            for k in range(k_rows):
                x = first_ref[k, :, here]
                z = x * gain2 + bias2
                s = sigmoid(z)
                flow = y[t, k] * (s * (1.0 + z * (1.0 - s)))
                flow_ref[k, :, here] = flow
                if k < p_rows:
                    crossed = flow * (x * scale2 + shift2)
                    ones = ones + flow[:, 0:128] + flow[:, 128:256]
                    cross = cross + crossed[:, 0:128] + crossed[:, 128:256]
        right = stacked(
            j,
            blocks,
            images,
            p_rows,
            [(act, a, 0, 512) for a in range(3)] + [(odd, 1, 128, 256)],
        )
        own = stacked(j, blocks, images, p_rows, [(grad, 1, 128, 256)])
        kernel_ref[...] += lax.dot_general(
            own, right, (((0,), (0,)), ((), ())), preferred_element_type=F32
        )
    add_rows(stats, grouped_rows(w0, w1, [ones, cross]))

    @pl.when(pl.program_id(0) == pl.num_programs(0) - 1)
    def _():
        for a in range(3):
            for b in range(3):
                tap = jnp.zeros((CS_OUT, CS_OUT), F32)
                for q in range(4):
                    lane = a * 512 + (q + b + 1) * CS_OUT
                    tap = tap + kernel_ref[q * CS_OUT : (q + 1) * CS_OUT, lane : lane + CS_OUT]
                row = (3 * a + b) * CS_OUT
                second_ref[row : row + CS_OUT] = tap
        tap = jnp.zeros((CS_OUT, CS_IN), F32)
        for q in range(4):
            lane = 1536 + 2 * q * CS_IN
            tap = tap + kernel_ref[q * CS_OUT : (q + 1) * CS_OUT, lane : lane + CS_IN]
        shortcut_ref[...] = tap


def student_back(
    place, block_sum, cot, factor, spread, first_out, act, odd, label, tot, inner, norm, weights, tile
):
    rows, images, lanes = block_sum.shape
    p_rows = rows - 3
    outs = [
        shape_of((p_rows + 1, images, lanes), F32),
        shape_of((p_rows, images, lanes), BF16),
    ]
    stats = shape_of((8, 128), F32)
    second = shape_of((9 * CS_OUT, CS_OUT), F32)
    shortcut = shape_of((CS_OUT, CS_IN), F32)
    return pl.pallas_call(
        functools.partial(back_kernel, p_rows, 4),
        grid_spec=pltpu.PrefetchScalarGridSpec(
            num_scalar_prefetch=1,
            grid=(images // tile,),
            in_specs=[image_spec(block_sum, tile), image_spec(cot, tile), table_spec(factor, tile)]
            + [whole_spec(spread), image_spec(first_out, tile), image_spec(act, tile)]
            + [image_spec(odd, tile), table_spec(label, tile)]
            + [whole_spec(a) for a in (tot, inner, norm, weights)],
            out_specs=[image_spec(o, tile) for o in outs]
            + [whole_spec(a) for a in (stats, second, shortcut)],
            scratch_shapes=[
                pltpu.VMEM((256, 1792), F32),
                pltpu.VMEM((p_rows + 3, tile, 256 + lanes), BF16),
            ],
        ),
        out_shape=outs + [stats, second, shortcut],
        compiler_params=pltpu.CompilerParams(vmem_limit_bytes=VMEM_LIMIT),
        cost_estimate=cost(18),
    )(place, block_sum, cot, factor, spread, first_out, act, odd, label, tot, inner, norm, weights)


def entry_kernel(
    p_rows,
    blocks,
    place,
    flow_ref,
    first_ref,
    grad,
    even,
    odd,
    raw,
    label_ref,
    tot,
    inner,
    pulled,
    norm_in,
    norm,
    weights_even,
    weights_odd,
    *refs,
):
    outs, (taps_ref, stats, first_grad, kernel_ref, rows_ref) = refs[:-5], refs[-5:]
    images, lanes = first_ref.shape[1:]
    w0, w1 = indicators(label_ref)
    gain, _, scale, shift = inner_tables(tot, inner, norm, w0, w1)
    counts = inner_counts(tot)
    folded = fold(pulled[...], CS_OUT)
    ones_mean = per_image(w0, w1, [folded[g : g + 1] / counts[g] for g in range(2)])
    cross_mean = per_image(w0, w1, [folded[2 + g : 3 + g] / counts[g] for g in range(2)])
    gain2, scale2, shift2 = twice(gain), twice(scale), twice(shift)
    ones2, cross2 = twice(ones_mean), twice(cross_mean)
    zero = jnp.zeros((images, 128), BF16)

    def first_rows(k, carry):
        keep = keep_row(place, k, p_rows)
        first_grad[k, :, lanes : lanes + 128] = zero
        for c in range(0, lanes, 256):
            normed = first_ref[k, :, c : c + 256] * scale2 + shift2
            v = gain2 * (flow_ref[k, :, c : c + 256] - ones2 - normed * cross2)
            first_grad[k, :, c : c + 256] = (v * keep).astype(BF16)
        return carry

    lax.fori_loop(0, p_rows + 1, first_rows, 0)

    @pl.when(pl.program_id(0) == 0)
    def _():
        kernel_ref[...] = jnp.zeros(kernel_ref.shape, F32)

    gain, bias, scale, shift = entry_tables(tot, norm_in, w0, w1)
    gain2, bias2, scale2, shift2 = twice(gain), twice(bias), twice(scale), twice(shift)

    ones = jnp.zeros((images, 128), F32)
    cross = jnp.zeros((images, 128), F32)
    for j in range(0, lanes // 256, blocks):
        upper = (first_grad, 0, 0, 384)
        lower = (first_grad, 1, 0, 384)
        left = stacked(j, blocks, images, p_rows, [upper, (grad, 0, 0, 256)])
        rows_even = matmul(left, weights_even[...])
        rows_odd = matmul(stacked(j, blocks, images, p_rows, [upper, lower]), weights_odd[...])
        for parity, rows in enumerate((rows_even, rows_odd)):
            low = rows.astype(BF16).reshape(blocks, p_rows, images, 256)
            for t in range(blocks):
                here = slice((j + t) * 256, (j + t + 1) * 256)
                for p in range(p_rows):
                    rows_ref[2 * p + parity, :, here] = low[t, p]
                    x = raw[2 * p + parity, :, here].astype(F32)
                    z = x * gain2 + bias2
                    s = sigmoid(z)
                    flow = low[t, p].astype(F32) * (s * (1.0 + z * (1.0 - s)))
                    crossed = flow * (x * scale2 + shift2)
                    ones = ones + flow[:, 0:128] + flow[:, 128:256]
                    cross = cross + crossed[:, 0:128] + crossed[:, 128:256]
        right = stacked(
            j,
            blocks,
            images,
            p_rows,
            [(even, 0, 0, 384), (odd, 1, 0, 384), (even, 1, 0, 384)],
        )
        own = stacked(j, blocks, images, p_rows, [(first_grad, 0, 0, 256)])
        kernel_ref[...] += lax.dot_general(
            own, right, (((0,), (0,)), ((), ())), preferred_element_type=F32
        )
    group, local = len(outs), outs[0].shape[0]
    for s in range(group):
        distance = lax.rem(s - place[0] + group, group)
        for d in range(group):

            @pl.when(distance == d)
            def _():
                outs[d][...] = rows_ref[s * local : (s + 1) * local]

    add_rows(stats, grouped_rows(w0, w1, [ones, cross]))

    @pl.when(pl.program_id(0) == pl.num_programs(0) - 1)
    def _():
        for a in range(3):
            for b in range(3):
                tap = jnp.zeros((CS_OUT, CS_IN), F32)
                for q in range(4):
                    lane = a * 384 + (2 * q + b + 3) * CS_IN
                    tap = tap + kernel_ref[q * CS_OUT : (q + 1) * CS_OUT, lane : lane + CS_IN]
                row = (3 * a + b) * CS_OUT
                taps_ref[row : row + CS_OUT] = tap


def student_entry(
    place, flow, first_out, grad, even, odd, raw, label, tot, inner, pulled, norm_in, norm,
    weights_even, weights_odd, tile, group,
):
    rows, images, lanes = flow.shape
    p_rows = rows - 1
    outs = [shape_of((2 * p_rows // group, images, lanes), BF16)] * group
    taps = shape_of((9 * CS_OUT, CS_IN), F32)
    stats = shape_of((8, 128), F32)
    big = (flow, first_out, grad, even, odd, raw)
    shared = (tot, inner, pulled, norm_in, norm, weights_even, weights_odd)
    return pl.pallas_call(
        functools.partial(entry_kernel, p_rows, 4),
        grid_spec=pltpu.PrefetchScalarGridSpec(
            num_scalar_prefetch=1,
            grid=(images // tile,),
            in_specs=[image_spec(a, tile) for a in big]
            + [table_spec(label, tile)]
            + [whole_spec(a) for a in shared],
            out_specs=[image_spec(o, tile) for o in outs] + [whole_spec(taps), whole_spec(stats)],
            scratch_shapes=[
                pltpu.VMEM((p_rows + 1, tile, 128 + lanes), BF16),
                pltpu.VMEM((256, 1152), F32),
                pltpu.VMEM((2 * p_rows, tile, lanes), BF16),
            ],
        ),
        out_shape=outs + [taps, stats],
        compiler_params=pltpu.CompilerParams(vmem_limit_bytes=VMEM_LIMIT),
        cost_estimate=cost(16),
    )(place, *big, label, *shared)


def bands_kernel(first, first_t, second, second_t, short, short_t, *outs):
    one, two, back, even, odd, gather, scatter, wide = outs

    def fill(out, entries):
        rows = out.shape[0]
        wide[0:rows] = jnp.zeros((rows, 256), F32)
        for row, lane, tap in entries:
            wide[row : row + tap.shape[0], lane : lane + tap.shape[1]] = tap
        out[...] = wide[0:rows].astype(BF16)

    def tap_of(ref, a, b):
        size = ref.shape[0] // 9
        return ref[(3 * a + b) * size : (3 * a + b + 1) * size]

    taps = [(a, b) for a in range(3) for b in range(3)]
    fill(
        one,
        [
            (a * 384 + (2 * q + b + 3) * CS_IN, q * CS_OUT, tap_of(first, a, b))
            for a, b in taps
            for q in range(4)
        ],
    )
    fill(
        two,
        [
            (a * 512 + (q + b + 1) * CS_OUT, q * CS_OUT, tap_of(second, a, b))
            for a, b in taps
            for q in range(4)
        ]
        + [(1536 + 2 * q * CS_IN, q * CS_OUT, short[...]) for q in range(4)],
    )
    fill(
        back,
        [
            ((2 - a) * 512 + (s - b + 3) * CS_OUT, s * CS_OUT, tap_of(second_t, a, b))
            for a, b in taps
            for s in range(4)
        ],
    )

    def backward(a, row):
        entries = []
        for q in range(6):
            for b in range(3):
                s = 2 * q + b - 1
                if 0 <= s < 8:
                    entries.append((row + q * CS_OUT, s * CS_IN, tap_of(first_t, a, b)))
        return entries

    corner = [(384 + q * CS_OUT, 2 * q * CS_IN, short_t[...]) for q in range(4)]
    fill(even, backward(1, 0) + corner)
    fill(odd, backward(2, 0) + backward(0, 384))
    channel = lax.rem(lax.broadcasted_iota(jnp.int32, gather.shape, 0), 256)
    lane = lax.broadcasted_iota(jnp.int32, gather.shape, 1)
    gather[...] = jnp.where(lax.div(channel, CS_OUT) == lane, 1.0 / CS_OUT, 0.0).astype(BF16)
    lane = lax.rem(lax.broadcasted_iota(jnp.int32, scatter.shape, 0), 128)
    channel = lax.broadcasted_iota(jnp.int32, scatter.shape, 1)
    scatter[...] = jnp.where(lax.div(channel, CS_OUT) == lane, 1.0, 0.0).astype(BF16)


def banded_kernels(first, second, shortcut):
    turn = lambda k: jnp.swapaxes(k, 2, 3).reshape(-1, k.shape[2])
    rounded = lambda k: k.astype(BF16).astype(F32)
    first, second, shortcut = rounded(first), rounded(second), rounded(shortcut)
    args = (
        first.reshape(-1, CS_OUT),
        turn(first),
        second.reshape(-1, CS_OUT),
        turn(second),
        shortcut,
        shortcut.T,
    )
    shapes = [(1152, 256), (1792, 256), (1536, 256), (640, 256), (768, 256), (512, 128), (256, 256)]
    return pl.pallas_call(
        bands_kernel,
        in_specs=[pl.BlockSpec(memory_space=pltpu.VMEM)] * 6,
        out_specs=[pl.BlockSpec(memory_space=pltpu.VMEM)] * len(shapes),
        out_shape=[shape_of(shape, BF16) for shape in shapes],
        scratch_shapes=[pltpu.VMEM((1792, 256), F32)],
        compiler_params=pltpu.CompilerParams(vmem_limit_bytes=VMEM_LIMIT),
        cost_estimate=cost(8),
    )(*args)


def body(
    space,
    batch,
    small_in,
    large_in,
    small_teacher,
    large_teacher,
    small_groups,
    large_groups,
    small_cot,
    large_cot,
    teacher_gains,
    teacher_first,
    teacher_inner,
    teacher_second,
    teacher_bypass,
    entry_norm,
    first_conv,
    inner_norm,
    second_conv,
    shortcut,
    momentum_entry,
    momentum_first,
    momentum_inner,
    momentum_second,
    momentum_shortcut,
    average_entry,
    average_first,
    average_inner,
    average_second,
    average_shortcut,
):
    slabs = SLABS
    group = space // slabs
    axes = (("space", space), ("batch", batch))
    me = lax.axis_index("space")
    z, x = me // group, me % group
    place = jnp.stack([x, z]).astype(jnp.int32)
    total_positions = batch * (small_in.shape[0] * SIDE * SIDE // 4 + large_in.shape[0] * SIDE * SIDE)
    pixels = [small_in, large_in]
    teachers = [small_teacher, large_teacher]
    labels = [small_groups, large_groups]
    cots = [small_cot, large_cot]
    sides = [SIDE, 2 * SIDE]
    both = range(2)
    per_device = [p.shape[0] // space for p in pixels]
    local_rows = [p.shape[1] for p in pixels]
    images = [slabs * n for n in per_device]
    padded = [-(-n // 16) * 16 for n in images]
    tiles = [32 if padded[0] % 32 == 0 else 16, 16]
    p_counts = [s // (2 * slabs) for s in sides]
    widths = [s // 2 for s in sides]

    def to_sub(d):
        return [(k, k // group * group + (k % group + d) % group) for k in range(space)]

    def to_slab(d):
        return [(k, (k // group + d) % slabs * group + k % group) for k in range(space)]

    def send(array, pairs):
        return lax.ppermute(array, "space", pairs)

    def pick_images(array, res, sub):
        n, rows, lanes = array.shape
        parts = array.reshape(slabs, group, per_device[res], rows, lanes)
        part = lax.dynamic_index_in_dim(parts, sub, 1, False)
        return part.reshape(images[res], rows, lanes)

    def rows_first(array):
        return jnp.transpose(array, (1, 0, 2))

    def slab_rows(pieces, first, last):
        local = pieces[0].shape[0]
        out = []
        for s in range(first // local, (last - 1) // local + 1):
            lo, hi = max(first - s * local, 0), min(last - s * local, local)
            cut = [p[lo:hi] for p in pieces]
            out.append(lax.select_n((x - s) % group, *cut) if group > 1 else cut[0])
        return jnp.concatenate(out, axis=0) if len(out) > 1 else out[0]

    def partner(b, k, first):
        slab = k // group
        other = slab ^ 1 if first else ((slab + 1) ^ 1) - 1
        if 0 <= other < slabs:
            return b * space + other * group + k % group
        return (b ^ 1) * space + k

    pair_lists = [
        [(b * space + k, partner(b, k, first)) for b in range(batch) for k in range(space)]
        for first in (True, False)
    ]

    def edge_rows(pieces, count):
        rows = group * pieces[0].shape[0]
        last, first = slab_rows(pieces, rows - count, rows), slab_rows(pieces, 0, count)
        even = z % 2 == 0
        return lax.select(even, last, first), lax.select(even, first, last)

    def to_neighbours(rows):
        return [lax.ppermute(r, ("batch", "space"), pairs) for r, pairs in zip(rows, pair_lists)]

    def pad_to(array, size):
        extra = size - array.shape[1]
        return jnp.pad(array, ((0, 0), (0, extra), (0, 0))) if extra else array

    def pad_images(array, res):
        return pad_to(array, padded[res])

    def label_table(res, sub, size):
        mine = lax.dynamic_index_in_dim(
            labels[res].reshape(slabs, group, per_device[res]), sub, 1, False
        ).reshape(images[res])
        mine = jnp.pad(mine.astype(F32), (0, size - images[res]), constant_values=-1.0)
        return jnp.broadcast_to(mine[:, None], (size, 128))

    tables = [label_table(res, x, padded[res]) for res in both]
    norm_in = jnp.tile(entry_norm, (1, 128 // CS_IN))
    norm_mid = jnp.tile(inner_norm, (1, 128 // CS_OUT))
    by_slab = [[sub + group * k for k in range(slabs)] for sub in range(group)]

    def among_slabs(array, axis):
        if axis:
            array = jnp.moveaxis(array, axis, 0)
        return lax.all_to_all(array, "space", 0, 0, axis_index_groups=by_slab, tiled=True)

    subs = [(x + d) % group for d in range(group)]
    picked_small = [rows_first(pick_images(small_in, 0, sub)) for sub in subs]
    cots_here = after(cots, picked_small[1:])
    narrow = cots[0].shape[2]
    cot_stacks = []
    for res in both:
        c = jnp.pad(rows_first(cots_here[res]), ((1, 2), (0, 0), (0, 0)))
        count = p_counts[res]
        c = jnp.stack([c[k * count : (k + 1) * count + 3] for k in range(slabs)])
        if c.shape[3] > narrow:
            c = jnp.concatenate(
                [c[..., k : k + narrow] for k in range(0, c.shape[3], narrow)], axis=2
            )
        cot_stacks.append(c)
    flat = [c.reshape(slabs, -1, narrow) for c in cot_stacks]
    cot_flat = jnp.concatenate(flat, axis=1)
    cots_ready = cot_flat
    cot_flat = among_slabs(cot_flat, 0)
    large_source = after(large_in, cots_ready)
    picked_large = [rows_first(pick_images(large_source, 1, sub)) for sub in subs]
    picked = [picked_small, picked_large]
    arrived = [
        [picked[res][0]] + [send(picked[res][d], to_sub(d)) for d in range(1, group)]
        for res in both
    ]


    gains = jnp.tile(teacher_gains, (1, max(t.shape[2] for t in teachers) // CT_IN))

    def activated(array, size):
        lanes = array.shape[2]
        z_t = gains[0, :lanes] * array.astype(F32) + gains[1, :lanes]
        return pad_to(rows_first(jax.nn.silu(z_t).astype(BF16)), size)

    large_raw_in = after(large_teacher, [p[1:] for p in picked], cots_ready)
    own_large = pick_images(large_raw_in, 1, x)
    away_large = [pick_images(large_raw_in, 1, sub) for sub in subs[1:]]
    cut = min(16, images[1])
    sizes = [cut, images[1] - cut]
    ranges = [(0, cut), (cut, images[1])]

    def large_part(k, *others):
        lo, hi = ranges[k]
        return [
            send(after(away_large[d - 1][lo:hi], *others), to_sub(d)) for d in range(1, group)
        ]

    large_raw = [large_part(0)]

    stat_tables = [label_table(res, sub, images[res]) for res in both for sub in subs]
    entry_sums = input_stats(picked[0] + picked[1], stat_tables)
    (lo, hi), size = ranges[0], sizes[0]
    large_own = [activated(own_large[lo:hi], size)]
    raw_edges = [edge_rows(arrived[res], 6) for res in both]
    corners = lambda parts: [p[:1, :, :128] for p in parts]
    waits = ([p[1:] for p in arrived], cot_flat, corners(large_raw[0]), large_own, raw_edges)
    entry_total = total_over_devices([entry_sums], axes, 0, waits)

    raw_halos = [to_neighbours(after(raw_edges[res], entry_total)) for res in both]
    large_raw.append(large_part(1, entry_total))
    large_pieces = [
        [large_own[0]] + [activated(after(p, entry_total), sizes[0]) for p in large_raw[0]]
    ]

    def large_edges_of(k, *others):
        lo, hi = ranges[k]
        rows = [after(p[:, : hi - lo], *others) for p in large_pieces[k]]
        return to_neighbours(edge_rows(rows, 3))

    lanes = small_teacher.shape[2]
    z_t = after(small_teacher, large_raw_in).astype(F32) * gains[0, :lanes] + gains[1, :lanes]
    small_active = rows_first(jax.nn.silu(z_t).astype(BF16))
    small_active = small_active.reshape(local_rows[0], slabs, group, per_device[0], lanes)

    parts_of = [list(range(slabs // 2)), *([k] for k in range(slabs // 2, slabs))]

    def small_part(ks, sub):
        part = lax.dynamic_slice(
            small_active,
            (0, ks[0], sub, 0, 0),
            (local_rows[0], len(ks), 1, per_device[0], lanes),
        )
        return part.reshape(local_rows[0], len(ks) * per_device[0], lanes)

    small_away = [[small_part(ks, sub) for sub in subs[1:]] for ks in parts_of]
    bands = banded_kernels(*after((first_conv, second_conv, shortcut), entry_total))
    bands_first, bands_second, bands_second_back, bands_even, bands_odd, gather, scatter = bands
    raws, evens, odds, firsts, first_sums = ([None, None] for _ in range(5))
    for res in (1, 0):
        pieces = [pad_images(p, res) for p in arrived[res]]
        if res == 0:
            large_edges = [large_edges_of(0, sums)]
            cot_here = after(cot_flat, sums)
            cot_slabs = []
            at = 0
            for at_res, sent in zip(both, cot_stacks):
                size = sent.shape[1] * sent.shape[2]
                c = cot_here[:, at : at + size].reshape(sent.shape)
                at += size
                n = per_device[at_res]
                c = jnp.concatenate([c[:, :, k : k + n] for k in range(0, c.shape[2], n)], axis=3)
                c = jnp.moveaxis(c, 0, 1).reshape(c.shape[1], images[at_res], c.shape[3])
                cot_slabs.append(pad_images(c, at_res))
            pieces = after(pieces, cot_slabs)
        raw, even, odd, first, sums = student_forward(
            place,
            pieces,
            *[pad_images(p, res) for p in raw_halos[res]],
            tables[res],
            entry_total,
            norm_in,
            bands_first,
            tiles[res],
        )
        raws[res] = raw
        evens[res] = even
        odds[res] = odd
        firsts[res] = first
        first_sums[res] = sums
    inner_total = total_over_devices(first_sums, axes, 1, (corners(large_raw[1]), large_edges))

    (lo, hi), size = ranges[1], sizes[1]
    large_pieces.append(
        [activated(after(p, inner_total), size) for p in (own_large[lo:hi], *large_raw[1])]
    )
    large_edges.append(large_edges_of(1, inner_total))
    small_pieces = [
        [send(after(p, inner_total), to_sub(d + 1)) for d, p in enumerate(away)]
        for away in small_away[::-1]
    ][::-1]

    def small_rows(n, *others):
        own = small_part(parts_of[n], x)
        return edge_rows([own] + after(small_pieces[n], *others), 3)

    acts, own_firsts, sums_out, lows, energies = [], [], [], [], []
    for res in both:
        act, own_first, block_sum, low, energy = student_block(
            place,
            firsts[res],
            odds[res],
            tables[res],
            entry_total,
            inner_total,
            norm_mid,
            bands_second,
            gather,
            tiles[res],
        )
        acts.append(act)
        own_firsts.append(own_first)
        sums_out.append(block_sum)
        lows.append(low)
        energies.append(energy)

    shared = (
        teacher_first.reshape(9 * CT_IN, CT_OUT),
        teacher_second.reshape(9 * CT_OUT, CT_OUT),
        teacher_bypass,
        teacher_inner,
    )
    def large_map(k, *others):
        pieces = large_pieces[k]
        own = after(pieces[0], *others)
        edges = [pad_to(h, sizes[k]) for h in large_edges[k]]
        return teacher_energies(place, own, 0, pieces[1:], *edges, shared, sizes[k])

    def small_map(n, edges, *others):
        arrays = after((*small_pieces[n], *edges), *others)
        return [
            teacher_energies(
                place, small_active, parts_of[n][0], arrays[:-2], *arrays[-2:], shared, per_device[0]
            )
        ]

    large_maps = [large_map(0, inner_total)]
    rows = small_rows(0, large_maps[0], energies)
    edges = [to_neighbours(rows)]
    large_maps.append(large_map(1, rows))
    rows = small_rows(1, large_maps[1])
    edges.append(to_neighbours(rows))
    small_maps = small_map(0, edges[0], rows)
    for n in range(2, len(parts_of)):
        rows = small_rows(n, small_maps)
        edges.append(to_neighbours(rows))
        small_maps = small_maps + small_map(n - 1, edges[n - 1], rows)
    small_maps = small_maps + small_map(len(parts_of) - 1, edges[-1])
    factors = attention_maps(
        energies, [small_maps, large_maps], tables, widths, p_counts, slabs, group, 2
    )
    loss_sums = factors[2]

    def to_owners(res, *others):
        low = after(lows[res][:, : images[res]], *others)
        rows, _, lanes = low.shape
        return among_slabs(low.reshape(rows, slabs, per_device[res], lanes), 1)

    out_parts = [to_owners(0, factors[2])]

    flows, grads, flow_sums, second_parts, shortcut_parts = [], [], [], [], []
    for res in both:
        flow, grad, sums, second_part, shortcut_part = student_back(
            place,
            sums_out[res],
            cot_slabs[res],
            factors[res],
            scatter,
            own_firsts[res],
            acts[res],
            odds[res],
            tables[res],
            entry_total,
            inner_total,
            norm_mid,
            bands_second_back,
            tiles[res],
        )
        flows.append(flow)
        grads.append(grad)
        flow_sums.append(sums)
        second_parts.append(second_part)
        shortcut_parts.append(shortcut_part)
    flow_total = total_over_devices(flow_sums, axes, 3, out_parts)

    entry_parts, first_parts, entry_flow_sums = [], [], []
    held = None
    for res in both:
        flow = flows[res] if held is None else after(flows[res], held)
        *rows, first_part, sums = student_entry(
            place,
            flow,
            own_firsts[res],
            grads[res],
            evens[res],
            odds[res],
            raws[res],
            tables[res],
            entry_total,
            inner_total,
            flow_total,
            norm_in,
            norm_mid,
            bands_even,
            bands_odd,
            tiles[res],
            group,
        )
        if res == 0:
            held = rows[0]
        first_parts.append(first_part)
        entry_flow_sums.append(sums)
        rows = [r[:, : images[res]] for r in rows]
        if res == 0:
            rows[1:] = [send(r, to_sub(d + 1)) for d, r in enumerate(rows[1:])]
        entry_parts.append(rows)
    def native_rows(res):
        ordered = [lax.select_n((x - s) % group, *entry_parts[res]) for s in range(group)]
        n, rows, lanes = pixels[res].shape
        rows_in = jnp.stack(ordered).reshape(group, rows, slabs, per_device[res], lanes)
        return jnp.transpose(rows_in, (2, 0, 3, 1, 4)).reshape(n, rows, lanes)

    rate_scale = 1.0 / math.sqrt(total_positions)
    flat = lambda k: k.reshape(-1, k.shape[-1])
    kernel_states = [
        [flat(k) for k in (first_conv, momentum_first, average_first)],
        [flat(k) for k in (second_conv, momentum_second, average_second)],
        [shortcut, momentum_shortcut, average_shortcut],
    ]
    packed = gradient_sum(
        [first_parts, second_parts, shortcut_parts, entry_flow_sums, [loss_sums]],
        axes,
        4,
        (entry_parts[0][1:], entry_parts[1]),
    )
    first_state, second_state, bypass_state, entry_state, image_tables, total_loss = update(
        packed,
        kernel_states,
        [entry_norm, momentum_entry, average_entry],
        entry_total,
        norm_in,
        (CONV_RATE * rate_scale, NORM_RATE * rate_scale, 1.0 / total_positions),
    )
    rows = entry_parts[1]
    rows[1:] = [send(after(r, packed), to_sub(d + 1)) for d, r in enumerate(rows[1:])]
    out_parts.append(to_owners(1, packed))
    first_state = [k.reshape(first_conv.shape) for k in first_state]
    second_state = [k.reshape(second_conv.shape) for k in second_state]
    inner_folded = flow_total.reshape(8, 128 // CS_OUT, CS_OUT).sum(axis=1)
    ones_inner, cross_inner = inner_folded[0:2], inner_folded[2:4]
    block_outs = []
    for res in both:
        low = jnp.transpose(out_parts[res], (2, 0, 1, 3))
        block_outs.append(low.reshape(low.shape[0], -1, low.shape[3]))
    def wide_rows(lanes):
        wide = jnp.tile(image_tables, (1, lanes // 128))
        return [wide[k] for k in range(8)]

    wide = [wide_rows(p.shape[2]) for p in pixels]
    arrived_rows = [native_rows(0)]
    entry_parts[1] = after(entry_parts[1], block_outs, wide[1])
    arrived_rows.append(native_rows(1))
    input_grads = []
    for res in both:
        one = (labels[res] == 1)[:, None, None]
        gain, bias, slope, level = [
            jnp.where(one, wide[res][2 * k + 1], wide[res][2 * k]) for k in range(4)
        ]
        value = pixels[res].astype(F32)
        before = value * gain + bias
        s = jax.nn.sigmoid(before)
        flow = arrived_rows[res].astype(F32) * (s * (1.0 + before * (1.0 - s)))
        input_grads.append(gain * flow + (value * slope + level))

    inner_grads = jnp.stack([jnp.sum(cross_inner, axis=0), jnp.sum(ones_inner, axis=0)])
    inner_state = renew(inner_norm, inner_grads, momentum_inner, average_inner, NORM_RATE * rate_scale)
    return (
        *block_outs,
        input_grads[0],
        input_grads[1],
        total_loss.reshape(()),
        *entry_state,
        *first_state,
        *inner_state,
        *second_state,
        *bypass_state,
    )


def solution(mesh):
    rows = P("batch", "space", None)
    blocks = P(("batch", "space"), None, None)
    return jax.shard_map(
        functools.partial(body, mesh.shape["space"], mesh.shape["batch"]),
        mesh=mesh,
        in_specs=(rows,) * 4 + (P("batch"),) * 2 + (blocks,) * 2 + (P(),) * 20,
        out_specs=(blocks,) * 2 + (rows,) * 2 + (P(),) * 24,
        check_vma=False,
    )
```

```python
import functools
import math

import jax
import jax.numpy as jnp
import numpy as np
from jax import lax
from jax.experimental import pallas as pl
from jax.experimental.pallas import tpu as pltpu
from jax.sharding import PartitionSpec as P

CS_IN = 32
CS_OUT = 64
CT_IN = 128
CT_OUT = 256
SIDE = 32
SLABS = 4

EPSILON = 1e-05
TRANSFER_WEIGHT = 1000.0
MOMENTUM = 0.9
WEIGHT_DECAY = 0.0005
AVERAGING = 0.7
CONV_RATE = 0.06
NORM_RATE = 0.3

F32 = jnp.float32
BF16 = jnp.bfloat16
MESH = pl.DeviceIdType.MESH
VMEM_LIMIT = 56 << 20


def sigmoid(z):
    return 0.5 * jnp.tanh(0.5 * z) + 0.5


def matmul(a, b):
    return jnp.dot(a, b, preferred_element_type=F32)


def after(value, *others):
    return lax.optimization_barrier((value, others))[0]


def cost(microseconds):
    return pl.CostEstimate(
        flops=int(microseconds * 1e9), bytes_accessed=1 << 20, transcendentals=0
    )


def stacked(first, count, images, rows, parts):
    blocks = []
    for t in range(count):
        at = (first + t) * 256
        pieces = [ref[lo : lo + rows, :, at + off : at + off + size] for ref, lo, off, size in parts]
        block = jnp.concatenate(pieces, axis=2) if len(pieces) > 1 else pieces[0]
        blocks.append(block.reshape(rows * images, block.shape[2]))
    return jnp.concatenate(blocks, axis=0) if count > 1 else blocks[0]


def fold(rows, width):
    shift = width
    while shift < 128:
        rows = rows + pltpu.roll(rows, shift, 1)
        shift *= 2
    return rows


def group_norms(totals, counts, width):
    folded = fold(totals, width)
    means, scales = [], []
    for g in range(2):
        mean = folded[g : g + 1] / counts[g]
        variance = folded[2 + g : 3 + g] / counts[g] - mean * mean
        means.append(mean)
        scales.append(lax.rsqrt(variance + EPSILON))
    return means, scales


def per_image(w0, w1, pair):
    return w0 * pair[0] + w1 * pair[1]


def twice(table):
    return jnp.concatenate([table, table], axis=1)


def grouped_rows(w0, w1, values):
    rows = []
    for v in values:
        rows.append(jnp.sum(v * w0, axis=0, keepdims=True))
        rows.append(jnp.sum(v * w1, axis=0, keepdims=True))
    rows.append(jnp.zeros((8 - len(rows), 128), F32))
    return jnp.concatenate(rows, axis=0)


def entry_counts(tot_ref):
    return [tot_ref[4:5], tot_ref[5:6]]


def inner_counts(tot_ref):
    return [tot_ref[4:5] * 0.25, tot_ref[5:6] * 0.25]


def renew(weights, gradient, moment, average, factor):
    descent = gradient + WEIGHT_DECAY * weights
    velocity = MOMENTUM * moment + descent
    updated = weights - factor * (descent + MOMENTUM * velocity)
    smoothed = AVERAGING * average + (1.0 - AVERAGING) * updated
    return (gradient, velocity, smoothed, updated)


def stats_kernel(x_refs, label_refs, out_ref):
    step = pl.program_id(0)
    total = jnp.zeros((8, 128), F32)
    for x_ref, label_ref in zip(x_refs, label_refs):
        rows, images, lanes = x_ref.shape
        s = jnp.zeros((images, 128), F32)
        q = jnp.zeros((images, 128), F32)
        for r in range(rows):
            for c in range(0, lanes, 128):
                v = x_ref[r, :, c : c + 128].astype(F32)
                s = s + v
                q = q + v * v
        w0, w1 = indicators(label_ref)
        positions = jnp.full((images, 128), float(rows * lanes // CS_IN), F32)
        total = total + grouped_rows(w0, w1, [s, q, positions])

    @pl.when(step == 0)
    def _():
        out_ref[...] = total

    @pl.when(step > 0)
    def _():
        out_ref[...] += total


def input_stats(pieces, tables):
    steps = min(4, min(x.shape[0] for x in pieces))
    count = len(pieces)

    def kernel(*refs):
        stats_kernel(refs[:count], refs[count:-1], refs[-1])

    specs = [
        pl.BlockSpec((x.shape[0] // steps,) + x.shape[1:], lambda i: (i, 0, 0)) for x in pieces
    ]
    specs += [pl.BlockSpec(w.shape, lambda i: (0, 0)) for w in tables]
    return pl.pallas_call(
        kernel,
        grid=(steps,),
        in_specs=specs,
        out_specs=pl.BlockSpec((8, 128), lambda i: (0, 0)),
        out_shape=jax.ShapeDtypeStruct((8, 128), F32),
        compiler_params=pltpu.CompilerParams(vmem_limit_bytes=VMEM_LIMIT),
        cost_estimate=cost(5),
    )(*pieces, *tables)


def greet(axes):
    barrier = pltpu.get_barrier_semaphore()
    expected = 0
    for name, size in axes:
        me = lax.axis_index(name)
        for d in range(1, size):
            pl.semaphore_signal(
                barrier,
                inc=1,
                device_id={name: lax.rem(me + d, size)},
                device_id_type=MESH,
            )
            expected += 1
    pl.semaphore_wait(barrier, expected)


def total_kernel(axes, count, *refs):
    parts = refs[:count]
    out_ref, held, boxes_a, boxes_b, send_a, recv_a, send_b, recv_b = refs[-8:]
    value = parts[0][...]
    for part in parts[1:]:
        value = value + part[...]
    held[0] = value
    greet(axes)
    for level, ((name, size), boxes, send, recv) in enumerate(
        zip(axes, (boxes_a, boxes_b), (send_a, send_b), (recv_a, recv_b))
    ):
        me = lax.axis_index(name)
        copies = []
        for d in range(1, size):
            copy = pltpu.make_async_remote_copy(
                src_ref=held.at[level],
                dst_ref=boxes.at[d],
                send_sem=send.at[d],
                recv_sem=recv.at[d],
                device_id={name: lax.rem(me + d, size)},
                device_id_type=MESH,
            )
            copy.start()
            copies.append(copy)
        for copy in copies:
            copy.wait_recv()
        value = jnp.zeros(value.shape, F32)
        for source in range(size):
            back = lax.rem(me - source + size, size)
            value = value + jnp.where(
                back == 0, held[level], boxes[jnp.maximum(back, 1)]
            )
        for copy in copies:
            copy.wait_send()
        if level == 0:
            held[1] = value
        else:
            out_ref[...] = value


def total_over_devices(parts, axes, collective_id, waits):
    waits = jax.tree.leaves(waits)
    shape = parts[0].shape
    return pl.pallas_call(
        functools.partial(total_kernel, axes, len(parts)),
        out_shape=jax.ShapeDtypeStruct(shape, F32),
        in_specs=[pl.BlockSpec(memory_space=pltpu.VMEM)] * len(parts)
        + [pl.BlockSpec(memory_space=pl.ANY)] * len(waits),
        out_specs=pl.BlockSpec(memory_space=pltpu.VMEM),
        scratch_shapes=[
            pltpu.VMEM((2,) + shape, F32),
            pltpu.VMEM((axes[0][1],) + shape, F32),
            pltpu.VMEM((axes[1][1],) + shape, F32),
            pltpu.SemaphoreType.DMA((axes[0][1],)),
            pltpu.SemaphoreType.DMA((axes[0][1],)),
            pltpu.SemaphoreType.DMA((axes[1][1],)),
            pltpu.SemaphoreType.DMA((axes[1][1],)),
        ],
        compiler_params=pltpu.CompilerParams(collective_id=collective_id, has_side_effects=True),
        cost_estimate=cost(12),
    )(*parts, *waits)


def gradient_sum_kernel(axes, layout, waits, *refs):
    count = sum(len(parts) for parts in layout)
    inputs, refs = refs[:count], refs[count + waits :]
    out_ref, x_ref, boxes_a, boxes_b, held = refs[:5]
    send_a, recv_a, send_b, recv_b, send_c, recv_c = refs[5:]
    at = 0
    for parts in layout:
        value = inputs[parts[0]][...]
        for k in parts[1:]:
            value = value + inputs[k][...]
        parts = 128 // value.shape[1]
        if parts > 1:
            n = value.shape[0] // parts
            value = jnp.concatenate([value[k * n : k * n + n] for k in range(parts)], axis=1)
        x_ref[at : at + value.shape[0]] = value
        at += value.shape[0]
    if at < x_ref.shape[0]:
        x_ref[at:] = jnp.zeros((x_ref.shape[0] - at, 128), F32)
    (name_a, size_a), (name_b, size_b) = axes
    me_a, me_b = lax.axis_index(name_a), lax.axis_index(name_b)
    piece = x_ref.shape[0] // size_a
    greet(axes)

    def rows(index):
        return pl.ds(pl.multiple_of(index * piece, 8), piece)

    copies = []
    for d in range(1, size_a):
        peer = lax.rem(me_a + d, size_a)
        copy = pltpu.make_async_remote_copy(
            src_ref=x_ref.at[rows(peer)],
            dst_ref=boxes_a.at[d],
            send_sem=send_a.at[d],
            recv_sem=recv_a.at[d],
            device_id={name_a: peer},
            device_id_type=MESH,
        )
        copy.start()
        copies.append(copy)
    value = x_ref[rows(me_a)]
    for d in range(1, size_a):
        copies[d - 1].wait_recv()
        value = value + boxes_a[d]
    held[0] = value
    for copy in copies:
        copy.wait_send()
    copies = []
    for d in range(1, size_b):
        copy = pltpu.make_async_remote_copy(
            src_ref=held.at[0],
            dst_ref=boxes_b.at[d],
            send_sem=send_b.at[d],
            recv_sem=recv_b.at[d],
            device_id={name_b: lax.rem(me_b + d, size_b)},
            device_id_type=MESH,
        )
        copy.start()
        copies.append(copy)
    for copy in copies:
        copy.wait_recv()
    value = jnp.zeros(value.shape, F32)
    for source in range(size_b):
        back = lax.rem(me_b - source + size_b, size_b)
        value = value + jnp.where(back == 0, held[0], boxes_b[jnp.maximum(back, 1)])
    held[1] = value
    out_ref[rows(me_a)] = value
    for copy in copies:
        copy.wait_send()
    copies = []
    for d in range(1, size_a):
        copy = pltpu.make_async_remote_copy(
            src_ref=held.at[1],
            dst_ref=out_ref.at[rows(me_a)],
            send_sem=send_c.at[d],
            recv_sem=recv_c.at[d],
            device_id={name_a: lax.rem(me_a + d, size_a)},
            device_id_type=MESH,
        )
        copy.start()
        copies.append(copy)
    for copy in copies:
        copy.wait()


def update_kernel(rates, *refs):
    out_ref, tot, norm = refs[:3]
    states, entry, outs = refs[3:12], refs[12:15], refs[15:]
    conv_rate, norm_rate, per_position = rates
    at = 0
    for k in range(3):
        weights, moment, average = [ref[...] for ref in states[3 * k : 3 * k + 3]]
        width = (CS_IN, CS_OUT, CS_IN)[k]
        n = weights.shape[0] * weights.shape[1] // 128
        packed = out_ref[at : at + n]
        at += n
        parts = [packed[:, lane : lane + width] for lane in range(0, 128, width)]
        turned = jnp.concatenate(parts, axis=0)
        taps = turned.shape[0] // CS_OUT
        gradient = jnp.concatenate(
            [turned[t * CS_OUT : (t + 1) * CS_OUT].T for t in range(taps)], axis=0
        )
        state = renew(weights, gradient, moment, average, conv_rate)
        for ref, value in zip(outs[5 * k : 5 * k + 4], state):
            ref[...] = value
        outs[5 * k + 4][...] = state[3].astype(BF16)
    pulled = fold(out_ref[at : at + 8], CS_IN)
    ones, cross = [pulled[0:1], pulled[1:2]], [pulled[2:3], pulled[3:4]]
    gradient = jnp.concatenate([cross[0] + cross[1], ones[0] + ones[1]], axis=0)[:, 0:CS_IN]
    state = renew(entry[0][...], gradient, entry[1][...], entry[2][...], norm_rate)
    for ref, value in zip(outs[15:19], state):
        ref[...] = value
    counts = entry_counts(tot)
    means, scales = group_norms(tot[...], counts, CS_IN)
    gains, biases, slopes, levels = [], [], [], []
    for g in range(2):
        shift = -means[g] * scales[g]
        gain = norm[0:1] * scales[g]
        gains.append(gain)
        biases.append(norm[0:1] * shift + norm[1:2])
        slopes.append(-gain * (cross[g] / counts[g]) * scales[g])
        levels.append(-gain * ((ones[g] + cross[g] * shift) / counts[g]))
    outs[19][...] = jnp.concatenate(gains + biases + slopes + levels, axis=0)
    losses = out_ref[at + 8 : at + 9]
    outs[20][...] = jnp.sum(losses, axis=1, keepdims=True) * per_position


def gradient_sum(groups, axes, collective_id, waits):
    (_, size_a), (_, size_b) = axes
    arrays, layout, rows = [], [], []
    for members in groups:
        layout.append(tuple(range(len(arrays), len(arrays) + len(members))))
        arrays += members
        rows.append(members[0].shape[0] * members[0].shape[1] // 128)
    padded = -(-sum(rows) // (8 * size_a)) * 8 * size_a
    piece = padded // size_a
    sems = []
    for size in (size_a, size_b, size_a):
        sems += [pltpu.SemaphoreType.DMA((size,))] * 2
    waits = jax.tree.leaves(waits)
    vmem = pl.BlockSpec(memory_space=pltpu.VMEM)
    return pl.pallas_call(
        functools.partial(gradient_sum_kernel, axes, tuple(layout), len(waits)),
        out_shape=jax.ShapeDtypeStruct((padded, 128), F32),
        in_specs=[vmem] * len(arrays) + [pl.BlockSpec(memory_space=pl.ANY)] * len(waits),
        out_specs=vmem,
        scratch_shapes=[
            pltpu.VMEM((padded, 128), F32),
            pltpu.VMEM((size_a, piece, 128), F32),
            pltpu.VMEM((size_b, piece, 128), F32),
            pltpu.VMEM((2, piece, 128), F32),
        ]
        + sems,
        compiler_params=pltpu.CompilerParams(collective_id=collective_id, has_side_effects=True),
        cost_estimate=cost(20),
    )(*arrays, *waits)


def update(total, states, entry, tot, norm, rates):
    given = [total, tot, norm] + [a for state in states for a in state] + entry
    outs = []
    for state in states:
        outs += [shape_of(state[0].shape, F32)] * 4 + [shape_of(state[0].shape, BF16)]
    outs += [shape_of(entry[0].shape, F32)] * 4 + [shape_of((8, 128), F32), shape_of((1, 1), F32)]
    vmem = pl.BlockSpec(memory_space=pltpu.VMEM)
    got = pl.pallas_call(
        functools.partial(update_kernel, rates),
        out_shape=outs,
        in_specs=[vmem] * len(given),
        out_specs=[vmem] * len(outs),
        compiler_params=pltpu.CompilerParams(vmem_limit_bytes=VMEM_LIMIT),
        cost_estimate=cost(4),
    )(*given)
    return got[0:5], got[5:10], got[10:15], got[15:19], got[19], got[20]


def teacher_kernel(p_rows, width, group, columns, place, *refs):
    pieces, refs = refs[:group], refs[group:]
    edge_a, edge_b, first, second, bypass, inner, out_ref, even, odd, mid = refs
    local, lanes = pieces[0].shape[0], pieces[0].shape[-1]
    real, images = edge_a.shape[1], even.shape[1]
    m_rows = p_rows + 2
    zero = jnp.zeros((images, 128), BF16)

    def put(row, source, at):
        if row % 2 == 0:
            even[row // 2 + 1, 0:real, 128 : 128 + lanes] = source[at]
        else:
            odd[(row + 1) // 2 + 1, 0:real, 128 : 128 + lanes] = source[at]

    def put_edges(above, below):
        for k in range(3):
            put(k - 3, above, k)
        for k in range(2):
            put(2 * p_rows + k, below, k)

    rows_of_neighbours(place, edge_a, edge_b, put_edges)
    nothing = jnp.zeros((1, real, lanes), BF16)

    @pl.when(place[1] == 0)
    def _():
        for k in range(3):
            put(k - 3, nothing, 0)

    @pl.when(place[1] == SLABS - 1)
    def _():
        for k in range(2):
            put(2 * p_rows + k, nothing, 0)

    x = place[0]
    for s in range(group):
        distance = lax.rem(x - s + group, group)
        for d in range(group):

            @pl.when(distance == d)
            def _():
                for k in range(local):
                    at = (k, 0, 0) if len(pieces[d].shape) == 5 else k
                    put(s * local + k, pieces[d], at)

    for i in range(m_rows):
        even[i, :, 0:128] = zero
    for i in range(m_rows + 1):
        odd[i, :, 0:128] = zero
    wide_zero = jnp.zeros((images, CT_OUT), BF16)
    for i in range(m_rows):
        mid[i, :, 0:CT_OUT] = wide_zero
        mid[i, :, (width + 1) * CT_OUT : (width + 2) * CT_OUT] = wide_zero
    scale, shift = inner[0:1], inner[1:2]
    top, bottom = keep_row(place, -1, p_rows), keep_row(place, p_rows, p_rows)

    def first_step(g, carry):
        lefts = []
        for t in range(columns):
            window = pl.ds(pl.multiple_of((g * columns + t) * 256, 256), 384)
            parts = [odd[0:m_rows, :, window], even[0:m_rows, :, window]]
            parts.append(odd[1 : m_rows + 1, :, window])
            lefts.append(jnp.concatenate(parts, axis=2).reshape(m_rows * images, 9 * CT_IN))
        z = scale * matmul(jnp.concatenate(lefts, axis=0), first[...]) + shift
        act = (z * sigmoid(z)).reshape(columns, m_rows, images, CT_OUT)
        for t in range(columns):
            here = pl.ds(pl.multiple_of((g * columns + t + 1) * CT_OUT, 256), CT_OUT)
            mid[0, :, here] = (act[t, 0] * top).astype(BF16)
            mid[1 : p_rows + 1, :, here] = act[t, 1 : p_rows + 1].astype(BF16)
            mid[p_rows + 1, :, here] = (act[t, p_rows + 1] * bottom).astype(BF16)
        return carry

    lax.fori_loop(0, width // columns, first_step, 0)
    out_ref[...] = jnp.zeros(out_ref.shape, F32)
    lane = lax.broadcasted_iota(jnp.int32, (real, 128), 1)

    def second_step(g, carry):
        lefts, corners = [], []
        for t in range(columns):
            at = pl.multiple_of((g * columns + t) * 256, 256)
            window = pl.ds(at, 3 * CT_OUT)
            corner = pl.ds(pl.multiple_of(at + 128, 128), 128)
            parts = [mid[a : a + p_rows, :, window] for a in range(3)]
            lefts.append(jnp.concatenate(parts, axis=2).reshape(p_rows * images, 9 * CT_OUT))
            corners.append(even[1 : p_rows + 1, :, corner].reshape(p_rows * images, CT_IN))
        y = matmul(jnp.concatenate(lefts, axis=0), second[...])
        y = y + matmul(jnp.concatenate(corners, axis=0), bypass[...])
        square = y * y
        energy = jnp.sum(square[:, 0:128] + square[:, 128:256], axis=1, keepdims=True)
        energy = (energy * (1.0 / CT_OUT)).reshape(columns, p_rows, images, 1)
        for t in range(columns):
            for p in range(p_rows):
                chunk, start = divmod((p + 1) * width, 128)
                where = slice(chunk * 128, chunk * 128 + 128)
                here = lane == start + g * columns + t
                out_ref[:, where] = jnp.where(here, energy[t, p, 0:real], out_ref[:, where])
        return carry

    lax.fori_loop(0, width // columns, second_step, 0)


def teacher_energies(place, own, slab, received, edge_a, edge_b, shared, tile):
    group = len(received) + 1
    local, lanes = own.shape[0], own.shape[-1]
    images = edge_a.shape[1]
    p_rows, width = group * local // 2, lanes // (2 * CT_IN)
    out_lanes = -(-(p_rows + 3) * width // 128) * 128
    m_rows = p_rows + 2
    space = -(-tile // 16) * 16
    if own.ndim == 5:
        own_spec = pl.BlockSpec(
            (local, 1, 1, tile, lanes), lambda i, place: (0, slab + i, place[0], 0, 0)
        )
    else:
        own_spec = pl.BlockSpec((local, tile, lanes), lambda i, place: (0, i, 0))
    whole = lambda a: pl.BlockSpec(a.shape, lambda i, place: (0,) * a.ndim)
    by_image = lambda a: pl.BlockSpec((a.shape[0], tile, a.shape[2]), lambda i, place: (0, i, 0))
    grid_spec = pltpu.PrefetchScalarGridSpec(
        num_scalar_prefetch=1,
        grid=(images // tile,),
        in_specs=[own_spec]
        + [by_image(a) for a in received]
        + [by_image(edge_a), by_image(edge_b)]
        + [whole(a) for a in shared],
        out_specs=pl.BlockSpec((tile, out_lanes), lambda i, place: (i, 0)),
        scratch_shapes=[
            pltpu.VMEM((m_rows, space, 128 + lanes), BF16),
            pltpu.VMEM((m_rows + 1, space, 128 + lanes), BF16),
            pltpu.VMEM((m_rows, space, (width + 2) * CT_OUT), BF16),
        ],
    )
    return pl.pallas_call(
        functools.partial(teacher_kernel, p_rows, width, group, 4),
        grid_spec=grid_spec,
        out_shape=jax.ShapeDtypeStruct((images, out_lanes), F32),
        compiler_params=pltpu.CompilerParams(vmem_limit_bytes=VMEM_LIMIT),
        cost_estimate=cost(40 * images * p_rows * width / 10240),
    )(place, own, *received, edge_a, edge_b, *shared)


def entry_tables(tot_ref, norm_ref, w0, w1):
    means, scales = group_norms(tot_ref[...], entry_counts(tot_ref), CS_IN)
    scale = per_image(w0, w1, scales)
    shift = per_image(w0, w1, [-m * s for m, s in zip(means, scales)])
    gain, bias = norm_ref[0:1], norm_ref[1:2]
    present = w0 + w1
    return gain * scale, gain * shift + bias * present, scale, shift


def inner_tables(tot_ref, inner_ref, norm_ref, w0, w1):
    means, scales = group_norms(inner_ref[...], inner_counts(tot_ref), CS_OUT)
    scale = per_image(w0, w1, scales)
    shift = per_image(w0, w1, [-m * s for m, s in zip(means, scales)])
    gain, bias = norm_ref[0:1], norm_ref[1:2]
    present = w0 + w1
    return gain * scale, gain * shift + bias * present, scale, shift


def indicators(label_ref):
    label = label_ref[...]
    return (label == 0.0).astype(F32), (label == 1.0).astype(F32)


def keep_row(place, row, inside):
    z = place[1]
    outside = jnp.logical_or(
        jnp.logical_and(row < 0, z == 0), jnp.logical_and(row >= inside, z == SLABS - 1)
    )
    return jnp.where(outside, 0.0, 1.0)


def rows_of_neighbours(place, first, second, use):
    even = lax.rem(place[1], 2) == 0

    @pl.when(even)
    def _():
        use(second, first)

    @pl.when(jnp.logical_not(even))
    def _():
        use(first, second)


def add_rows(ref, value):
    first = pl.program_id(0) == 0

    @pl.when(first)
    def _():
        ref[...] = value

    @pl.when(jnp.logical_not(first))
    def _():
        ref[...] += value


def forward_kernel(
    p_rows, group, blocks, place, *refs
):
    pieces, refs = refs[:group], refs[group:]
    first, second, label_ref, tot, norm, weights = refs[:6]
    raw_ref, even_ref, odd_ref, out_ref, stats, raw, even, odd = refs[6:]
    images, lanes = raw.shape[1:]
    local = pieces[0].shape[0]
    w0, w1 = indicators(label_ref)
    gain, bias, _, _ = entry_tables(tot, norm, w0, w1)
    gain2, bias2 = twice(gain), twice(bias)
    zero = jnp.zeros((images, 128), BF16)

    def put_edges(above, below):
        raw[0:5] = above[1:6]
        raw[2 * p_rows + 5 : 2 * p_rows + 11] = below[...]

    rows_of_neighbours(place, first, second, put_edges)
    x = place[0]
    for s in range(group):
        distance = lax.rem(x - s + group, group)
        for d in range(group):

            @pl.when(distance == d)
            def _():
                raw[5 + s * local : 5 + (s + 1) * local] = pieces[d][...]

    def activate(row, target, index):
        keep = keep_row(place, row - 5, 2 * p_rows)
        target[index, :, 0:128] = zero
        for c in range(0, lanes, 256):
            z = raw[row, :, c : c + 256].astype(F32) * gain2 + bias2
            target[index, :, 128 + c : 384 + c] = (z * sigmoid(z) * keep).astype(BF16)

    def pair(i, carry):
        activate(2 * i, even, i)
        activate(2 * i + 1, odd, i)
        return carry

    f_rows = p_rows + 5
    lax.fori_loop(0, f_rows, pair, 0)
    activate(2 * f_rows, even, f_rows)
    raw_ref[...] = raw[5 : 2 * p_rows + 5]
    even_ref[...] = even[2 : p_rows + 3]
    odd_ref[...] = odd[1 : p_rows + 4]
    s = jnp.zeros((images, 128), F32)
    q = jnp.zeros((images, 128), F32)
    for j in range(0, lanes // 256, blocks):
        left = stacked(
            j, blocks, images, f_rows, [(even, 0, 0, 384), (odd, 0, 0, 384), (even, 1, 0, 384)]
        )
        y = matmul(left, weights[...]).reshape(blocks, f_rows, images, 256)
        for t in range(blocks):
            out_ref[:, :, (j + t) * 256 : (j + t + 1) * 256] = y[t]
            own = y[t, 2 : 2 + p_rows]
            u = jnp.sum(own, axis=0)
            v = jnp.sum(own * own, axis=0)
            s = s + u[:, 0:128] + u[:, 128:256]
            q = q + v[:, 0:128] + v[:, 128:256]
    add_rows(stats, grouped_rows(w0, w1, [s, q]))


def whole_spec(a):
    return pl.BlockSpec(a.shape, lambda i, *_: (0,) * len(a.shape))


def image_spec(a, tile):
    return pl.BlockSpec((a.shape[0], tile, a.shape[2]), lambda i, *_: (0, i, 0))


def table_spec(a, tile):
    return pl.BlockSpec((tile, a.shape[1]), lambda i, *_: (i, 0))


def shape_of(shape, dtype):
    return jax.ShapeDtypeStruct(shape, dtype)


def student_forward(place, pieces, first, second, label, tot, norm, weights, tile):
    group = len(pieces)
    local, images, lanes = pieces[0].shape
    p_rows = group * local // 2
    outs = [
        shape_of((2 * p_rows, images, lanes), BF16),
        shape_of((p_rows + 1, images, 128 + lanes), BF16),
        shape_of((p_rows + 3, images, 128 + lanes), BF16),
        shape_of((p_rows + 5, images, lanes), F32),
    ]
    stats = shape_of((8, 128), F32)
    big = (*pieces, first, second)
    shared = (tot, norm, weights)
    grid_spec = pltpu.PrefetchScalarGridSpec(
        num_scalar_prefetch=1,
        grid=(images // tile,),
        in_specs=[image_spec(a, tile) for a in big]
        + [table_spec(label, tile)]
        + [whole_spec(a) for a in shared],
        out_specs=[image_spec(o, tile) for o in outs] + [whole_spec(stats)],
        scratch_shapes=[
            pltpu.VMEM((2 * p_rows + 11, tile, lanes), BF16),
            pltpu.VMEM((p_rows + 6, tile, 128 + lanes), BF16),
            pltpu.VMEM((p_rows + 5, tile, 128 + lanes), BF16),
        ],
    )
    return pl.pallas_call(
        functools.partial(forward_kernel, p_rows, group, 4),
        grid_spec=grid_spec,
        out_shape=outs + [stats],
        compiler_params=pltpu.CompilerParams(vmem_limit_bytes=VMEM_LIMIT),
        cost_estimate=cost(15),
    )(place, *big, label, *shared)


def split_bf16(value):
    high = value.astype(BF16)
    return high, (value - high.astype(F32)).astype(BF16)


def block_kernel(
    p_rows,
    blocks,
    place,
    first_ref,
    odd,
    label_ref,
    tot,
    inner,
    norm,
    weights,
    spread,
    act_ref,
    own_ref,
    sum_ref,
    low_ref,
    energy,
    act,
):
    images, lanes = first_ref.shape[1:]
    w0, w1 = indicators(label_ref)
    gain, bias, _, _ = inner_tables(tot, inner, norm, w0, w1)
    gain2, bias2 = twice(gain), twice(bias)
    zero = jnp.zeros((images, 128), BF16)
    f_rows, b_rows = p_rows + 5, p_rows + 3

    def activate(f, carry):
        keep = keep_row(place, f - 2, p_rows)
        act[f, :, 0:128] = zero
        act[f, :, 128 + lanes : 256 + lanes] = zero
        for c in range(0, lanes, 256):
            z = first_ref[f, :, c : c + 256] * gain2 + bias2
            act[f, :, 128 + c : 384 + c] = (z * sigmoid(z) * keep).astype(BF16)
        return carry

    lax.fori_loop(0, f_rows, activate, 0)
    act_ref[...] = act[1 : p_rows + 3]
    own_ref[...] = first_ref[2 : p_rows + 3]

    per_chunk = 128 // (lanes // CS_OUT)
    chunks = energy.shape[1] // 128
    measured = [jnp.zeros((images, 128), F32) for _ in range(chunks)]
    for j in range(0, lanes // 256, blocks):
        parts = [(act, a, 0, 512) for a in range(3)] + [(odd, 0, 128, 256)]
        left = stacked(j, blocks, images, b_rows, parts)
        flat = matmul(left, weights[...])
        y = flat.reshape(blocks, b_rows, images, 256)
        high, low = split_bf16(flat * flat)
        e = matmul(jnp.concatenate([high, low], axis=1), spread[...])
        e = e.reshape(blocks, b_rows, images, 128)
        for t in range(blocks):
            here = slice((j + t) * 256, (j + t + 1) * 256)
            sum_ref[:, :, here] = y[t]
            low_ref[:, :, here] = y[t, 1 : p_rows + 1].astype(BF16)
            for b in range(b_rows):
                shift = b % per_chunk * (128 // per_chunk) + 4 * (j + t)
                part = pltpu.roll(e[t, b], shift, 1) if shift else e[t, b]
                measured[b // per_chunk] = measured[b // per_chunk] + part
    for c in range(chunks):
        energy[:, c * 128 : c * 128 + 128] = measured[c]


def student_block(place, first_out, odd, label, tot, inner, norm, weights, spread, tile):
    rows, images, lanes = first_out.shape
    p_rows = rows - 5
    width = lanes // CS_OUT
    energy_lanes = -(-(p_rows + 3) * width // 128) * 128
    outs = [
        shape_of((p_rows + 2, images, 256 + lanes), BF16),
        shape_of((p_rows + 1, images, lanes), F32),
        shape_of((p_rows + 3, images, lanes), F32),
        shape_of((p_rows, images, lanes), BF16),
    ]
    energy = shape_of((images, energy_lanes), F32)
    return pl.pallas_call(
        functools.partial(block_kernel, p_rows, 4),
        grid_spec=pltpu.PrefetchScalarGridSpec(
            num_scalar_prefetch=1,
            grid=(images // tile,),
            in_specs=[image_spec(first_out, tile), image_spec(odd, tile), table_spec(label, tile)]
            + [whole_spec(a) for a in (tot, inner, norm, weights, spread)],
            out_specs=[image_spec(o, tile) for o in outs] + [table_spec(energy, tile)],
            scratch_shapes=[pltpu.VMEM((p_rows + 5, tile, 256 + lanes), BF16)],
        ),
        out_shape=outs + [energy],
        compiler_params=pltpu.CompilerParams(vmem_limit_bytes=VMEM_LIMIT),
        cost_estimate=cost(18),
    )(place, first_out, odd, label, tot, inner, norm, weights, spread)


def map_kernel(slabs, group, widths, p_counts, pieces, *refs):
    student, present = refs[0:2], refs[2:4]
    given = refs[4 : 4 + sum(pieces)]
    refs = refs[4 + sum(pieces) :]
    outs, loss_ref = refs[0:2], refs[2]
    teacher, sums, boxes = refs[3:5], refs[5:7], refs[7:9]
    from_above, from_below = refs[9:11], refs[11:13]
    send, recv, send_halo, recv_halo, ready = refs[13:]
    for res in range(2):
        at = 0
        for part in given[res * pieces[0] : res * pieces[0] + pieces[res]]:
            teacher[res][at : at + part.shape[0]] = part[...]
            at += part.shape[0]
        rest = teacher[res].shape[0] - at
        if rest:
            teacher[res][at:] = jnp.zeros((rest, teacher[res].shape[1]), F32)
    me = lax.axis_index("space")
    z, x = lax.div(me, group), lax.rem(me, group)
    greet_barrier = pltpu.get_barrier_semaphore()
    for d in range(1, slabs):
        pl.semaphore_signal(
            greet_barrier,
            inc=1,
            device_id={"space": lax.rem(z + d, slabs) * group + x},
            device_id_type=MESH,
        )
    pl.semaphore_wait(greet_barrier, slabs - 1)

    def halo_copies(res, direction):
        width, p_rows = widths[res], p_counts[res]
        lane = (p_rows * width if direction == 0 else width) // 128 * 128
        target = (from_above, from_below)[direction][res]
        return pltpu.make_async_remote_copy(
            src_ref=teacher[res].at[:, pl.ds(lane, 128)],
            dst_ref=target,
            send_sem=send_halo.at[2 * res + direction],
            recv_sem=recv_halo.at[2 * res + direction],
            device_id={"space": me + (group if direction == 0 else -group)},
            device_id_type=MESH,
        )

    for res in range(2):
        from_above[res][...] = jnp.zeros(from_above[res].shape, F32)
        from_below[res][...] = jnp.zeros(from_below[res].shape, F32)

    @pl.when(z > 0)
    def _():
        pl.semaphore_signal(
            ready.at[0], inc=1, device_id={"space": me - group}, device_id_type=MESH
        )

    @pl.when(z < slabs - 1)
    def _():
        pl.semaphore_signal(
            ready.at[1], inc=1, device_id={"space": me + group}, device_id_type=MESH
        )
        pl.semaphore_wait(ready.at[0], 1)
        halo_copies(0, 0).start()
        halo_copies(1, 0).start()

    @pl.when(z > 0)
    def _():
        pl.semaphore_wait(ready.at[1], 1)
        halo_copies(0, 1).start()
        halo_copies(1, 1).start()

    copies = []
    for res in range(2):
        width, p_rows = widths[res], p_counts[res]
        images, lanes = student[res].shape
        lane = lax.broadcasted_iota(jnp.int32, (images, lanes), 1)
        own = jnp.logical_and(lane >= width, lane < (p_rows + 1) * width)
        es = jnp.where(own, student[res][...], 0.0)
        et = jnp.where(own, teacher[res][...], 0.0)
        columns = [
            jnp.sum(v, axis=1, keepdims=True) for v in (es * es, et * et, es * et)
        ]
        small_lane = lax.broadcasted_iota(jnp.int32, (images, 128), 1)
        packed = jnp.zeros((images, 128), F32)
        for k, column in enumerate(columns):
            packed = jnp.where(small_lane == k, column, packed)
        padded = sums[res].shape[1]
        packed = jnp.concatenate([packed, jnp.zeros((padded - images, 128), F32)], axis=0)
        sums[res][...] = packed.T[0:8]
        for d in range(1, slabs):
            copy = pltpu.make_async_remote_copy(
                src_ref=sums[res],
                dst_ref=boxes[res].at[d],
                send_sem=send.at[res * slabs + d],
                recv_sem=recv.at[res * slabs + d],
                device_id={"space": lax.rem(z + d, slabs) * group + x},
                device_id_type=MESH,
            )
            copy.start()
            copies.append(copy)
    for copy in copies:
        copy.wait()

    @pl.when(z < slabs - 1)
    def _():
        halo_copies(0, 0).wait_send()
        halo_copies(1, 0).wait_send()
        halo_copies(0, 1).wait_recv()
        halo_copies(1, 1).wait_recv()

    @pl.when(z > 0)
    def _():
        halo_copies(0, 1).wait_send()
        halo_copies(1, 1).wait_send()
        halo_copies(0, 0).wait_recv()
        halo_copies(1, 0).wait_recv()

    loss = jnp.zeros((1, 128), F32)
    for res in range(2):
        width, p_rows = widths[res], p_counts[res]
        images, lanes = student[res].shape
        total = sums[res][...]
        for d in range(1, slabs):
            total = total + boxes[res][d]
        padded = total.shape[1]
        total = jnp.concatenate([total, jnp.zeros((120, padded), F32)], axis=0).T[0:images]
        ss, tt, st = total[:, 0:1], total[:, 1:2], total[:, 2:3]
        scale_s = lax.rsqrt(ss + 1e-12)
        scale_t = lax.rsqrt(tt + 1e-12)
        pulled = TRANSFER_WEIGHT * scale_s * (scale_s * ss - scale_t * st)
        lane = lax.broadcasted_iota(jnp.int32, (images, lanes), 1)
        shift = p_rows * width
        chunks = lanes // 128
        first_rows = from_below[res][...]
        last_rows = from_above[res][...]
        if shift % 128:
            first_rows = pltpu.roll(first_rows, shift % 128, 1)
            last_rows = pltpu.roll(last_rows, 128 - shift % 128, 1)
        blank = jnp.zeros((images, 128), F32)
        before = [last_rows] + [blank] * (chunks - 1)
        after = [blank] * (chunks - 1) + [first_rows]
        before = jnp.concatenate(before, axis=1) if chunks > 1 else before[0]
        after = jnp.concatenate(after, axis=1) if chunks > 1 else after[0]
        et = jnp.where(lane < width, before, teacher[res][...])
        et = jnp.where(lane >= (p_rows + 1) * width, after, et)
        u = student[res][...] * scale_s
        difference = u - et * scale_t
        own = jnp.logical_and(lane >= width, lane < (p_rows + 1) * width)
        squares = jnp.where(own, difference * difference, 0.0)
        kept = (present[res][...] >= 0.0).astype(F32)
        for c in range(chunks):
            loss = loss + jnp.sum(squares[:, c * 128 : c * 128 + 128] * kept, axis=0, keepdims=True)
        factor = (TRANSFER_WEIGHT * difference - u * pulled) * (scale_s * (2.0 / CS_OUT))
        for c in range(chunks):
            here = slice(c * 128, c * 128 + 128)
            outs[res][:, here] = jnp.where(kept > 0.0, factor[:, here], 0.0)
    loss_ref[...] = jnp.concatenate(
        [loss * (TRANSFER_WEIGHT / 2), jnp.zeros((7, 128), F32)], axis=0
    )


def attention_maps(student, teacher, present, widths, p_counts, slabs, group, collective_id):
    padded = [-(-s.shape[0] // 128) * 128 for s in student]
    images = [s.shape[0] for s in student]
    vmem = pl.BlockSpec(memory_space=pltpu.VMEM)
    return pl.pallas_call(
        functools.partial(
            map_kernel, slabs, group, widths, p_counts, tuple(len(t) for t in teacher)
        ),
        out_shape=[shape_of(s.shape, F32) for s in student] + [shape_of((8, 128), F32)],
        in_specs=[vmem] * (4 + sum(len(t) for t in teacher)),
        out_specs=[vmem] * 3,
        scratch_shapes=[pltpu.VMEM(s.shape, F32) for s in student]
        + [pltpu.VMEM((8, n), F32) for n in padded]
        + [pltpu.VMEM((slabs, 8, n), F32) for n in padded]
        + [pltpu.VMEM((n, 128), F32) for n in images] * 2
        + [pltpu.SemaphoreType.DMA((2 * slabs,))] * 2
        + [pltpu.SemaphoreType.DMA((4,))] * 2
        + [pltpu.SemaphoreType.REGULAR((2,))],
        compiler_params=pltpu.CompilerParams(collective_id=collective_id, has_side_effects=True),
        cost_estimate=cost(11),
    )(*student, *present, *teacher[0], *teacher[1])


def back_kernel(
    p_rows,
    blocks,
    place,
    sum_ref,
    cot,
    factor,
    spread,
    first_ref,
    act,
    odd,
    label_ref,
    tot,
    inner,
    norm,
    weights,
    flow_ref,
    grad_ref,
    stats,
    second_ref,
    shortcut_ref,
    kernel_ref,
    grad,
):
    images, lanes = sum_ref.shape[1:]
    w0, w1 = indicators(label_ref)
    gain, bias, scale, shift = inner_tables(tot, inner, norm, w0, w1)
    gain2, bias2, scale2, shift2 = twice(gain), twice(bias), twice(scale), twice(shift)
    zero = jnp.zeros((images, 128), BF16)
    b_rows, k_rows = p_rows + 3, p_rows + 1
    width = lanes // CS_OUT
    per_chunk = 128 // width
    for b in range(b_rows):
        grad[b, :, 0:128] = zero
        grad[b, :, 128 + lanes : 256 + lanes] = zero
    halves = [split_bf16(factor[:, c * 128 : c * 128 + 128]) for c in range(factor.shape[1] // 128)]
    halves = [[h.astype(F32) for h in pair] for pair in halves]
    for j in range(0, lanes // 256, blocks):
        rows = []
        for t in range(blocks):
            for b in range(b_rows):
                shift = (128 - (b % per_chunk * width + 4 * (j + t))) % 128
                pair = halves[b // per_chunk]
                if shift:
                    pair = [pltpu.roll(h, shift, 1) for h in pair]
                rows.append(jnp.concatenate(pair, axis=1))
        wide = matmul(jnp.concatenate(rows, axis=0).astype(BF16), spread[...])
        wide = wide.reshape(blocks, b_rows, images, 256)
        for t in range(blocks):
            at = (j + t) * 256
            for b in range(b_rows):
                keep = keep_row(place, b - 1, p_rows)
                v = cot[b, :, at : at + 256].astype(F32) + wide[t, b] * sum_ref[b, :, at : at + 256]
                grad[b, :, 128 + at : 384 + at] = (v * keep).astype(BF16)

    grad_ref[...] = grad[1 : p_rows + 1, :, 128 : 128 + lanes]

    @pl.when(pl.program_id(0) == 0)
    def _():
        kernel_ref[...] = jnp.zeros(kernel_ref.shape, F32)

    ones = jnp.zeros((images, 128), F32)
    cross = jnp.zeros((images, 128), F32)
    for j in range(0, lanes // 256, blocks):
        left = stacked(j, blocks, images, k_rows, [(grad, d, 0, 512) for d in range(3)])
        y = matmul(left, weights[...]).reshape(blocks, k_rows, images, 256)
        for t in range(blocks):
            here = slice((j + t) * 256, (j + t + 1) * 256)
            for k in range(k_rows):
                x = first_ref[k, :, here]
                z = x * gain2 + bias2
                s = sigmoid(z)
                flow = y[t, k] * (s * (1.0 + z * (1.0 - s)))
                flow_ref[k, :, here] = flow
                if k < p_rows:
                    crossed = flow * (x * scale2 + shift2)
                    ones = ones + flow[:, 0:128] + flow[:, 128:256]
                    cross = cross + crossed[:, 0:128] + crossed[:, 128:256]
        right = stacked(
            j,
            blocks,
            images,
            p_rows,
            [(act, a, 0, 512) for a in range(3)] + [(odd, 1, 128, 256)],
        )
        own = stacked(j, blocks, images, p_rows, [(grad, 1, 128, 256)])
        kernel_ref[...] += lax.dot_general(
            own, right, (((0,), (0,)), ((), ())), preferred_element_type=F32
        )
    add_rows(stats, grouped_rows(w0, w1, [ones, cross]))

    @pl.when(pl.program_id(0) == pl.num_programs(0) - 1)
    def _():
        for a in range(3):
            for b in range(3):
                tap = jnp.zeros((CS_OUT, CS_OUT), F32)
                for q in range(4):
                    lane = a * 512 + (q + b + 1) * CS_OUT
                    tap = tap + kernel_ref[q * CS_OUT : (q + 1) * CS_OUT, lane : lane + CS_OUT]
                row = (3 * a + b) * CS_OUT
                second_ref[row : row + CS_OUT] = tap
        tap = jnp.zeros((CS_OUT, CS_IN), F32)
        for q in range(4):
            lane = 1536 + 2 * q * CS_IN
            tap = tap + kernel_ref[q * CS_OUT : (q + 1) * CS_OUT, lane : lane + CS_IN]
        shortcut_ref[...] = tap


def student_back(
    place, block_sum, cot, factor, spread, first_out, act, odd, label, tot, inner, norm, weights, tile
):
    rows, images, lanes = block_sum.shape
    p_rows = rows - 3
    outs = [
        shape_of((p_rows + 1, images, lanes), F32),
        shape_of((p_rows, images, lanes), BF16),
    ]
    stats = shape_of((8, 128), F32)
    second = shape_of((9 * CS_OUT, CS_OUT), F32)
    shortcut = shape_of((CS_OUT, CS_IN), F32)
    return pl.pallas_call(
        functools.partial(back_kernel, p_rows, 4),
        grid_spec=pltpu.PrefetchScalarGridSpec(
            num_scalar_prefetch=1,
            grid=(images // tile,),
            in_specs=[image_spec(block_sum, tile), image_spec(cot, tile), table_spec(factor, tile)]
            + [whole_spec(spread), image_spec(first_out, tile), image_spec(act, tile)]
            + [image_spec(odd, tile), table_spec(label, tile)]
            + [whole_spec(a) for a in (tot, inner, norm, weights)],
            out_specs=[image_spec(o, tile) for o in outs]
            + [whole_spec(a) for a in (stats, second, shortcut)],
            scratch_shapes=[
                pltpu.VMEM((256, 1792), F32),
                pltpu.VMEM((p_rows + 3, tile, 256 + lanes), BF16),
            ],
        ),
        out_shape=outs + [stats, second, shortcut],
        compiler_params=pltpu.CompilerParams(vmem_limit_bytes=VMEM_LIMIT),
        cost_estimate=cost(18),
    )(place, block_sum, cot, factor, spread, first_out, act, odd, label, tot, inner, norm, weights)


def entry_kernel(
    p_rows,
    blocks,
    place,
    flow_ref,
    first_ref,
    grad,
    even,
    odd,
    raw,
    label_ref,
    tot,
    inner,
    pulled,
    norm_in,
    norm,
    weights_even,
    weights_odd,
    *refs,
):
    outs, (taps_ref, stats, first_grad, kernel_ref, rows_ref) = refs[:-5], refs[-5:]
    images, lanes = first_ref.shape[1:]
    w0, w1 = indicators(label_ref)
    gain, _, scale, shift = inner_tables(tot, inner, norm, w0, w1)
    counts = inner_counts(tot)
    folded = fold(pulled[...], CS_OUT)
    ones_mean = per_image(w0, w1, [folded[g : g + 1] / counts[g] for g in range(2)])
    cross_mean = per_image(w0, w1, [folded[2 + g : 3 + g] / counts[g] for g in range(2)])
    gain2, scale2, shift2 = twice(gain), twice(scale), twice(shift)
    ones2, cross2 = twice(ones_mean), twice(cross_mean)
    zero = jnp.zeros((images, 128), BF16)

    def first_rows(k, carry):
        keep = keep_row(place, k, p_rows)
        first_grad[k, :, lanes : lanes + 128] = zero
        for c in range(0, lanes, 256):
            normed = first_ref[k, :, c : c + 256] * scale2 + shift2
            v = gain2 * (flow_ref[k, :, c : c + 256] - ones2 - normed * cross2)
            first_grad[k, :, c : c + 256] = (v * keep).astype(BF16)
        return carry

    lax.fori_loop(0, p_rows + 1, first_rows, 0)

    @pl.when(pl.program_id(0) == 0)
    def _():
        kernel_ref[...] = jnp.zeros(kernel_ref.shape, F32)

    gain, bias, scale, shift = entry_tables(tot, norm_in, w0, w1)
    gain2, bias2, scale2, shift2 = twice(gain), twice(bias), twice(scale), twice(shift)

    ones = jnp.zeros((images, 128), F32)
    cross = jnp.zeros((images, 128), F32)
    for j in range(0, lanes // 256, blocks):
        upper = (first_grad, 0, 0, 384)
        lower = (first_grad, 1, 0, 384)
        left = stacked(j, blocks, images, p_rows, [upper, (grad, 0, 0, 256)])
        rows_even = matmul(left, weights_even[...])
        rows_odd = matmul(stacked(j, blocks, images, p_rows, [upper, lower]), weights_odd[...])
        for parity, rows in enumerate((rows_even, rows_odd)):
            low = rows.astype(BF16).reshape(blocks, p_rows, images, 256)
            for t in range(blocks):
                here = slice((j + t) * 256, (j + t + 1) * 256)
                for p in range(p_rows):
                    rows_ref[2 * p + parity, :, here] = low[t, p]
                    x = raw[2 * p + parity, :, here].astype(F32)
                    z = x * gain2 + bias2
                    s = sigmoid(z)
                    flow = low[t, p].astype(F32) * (s * (1.0 + z * (1.0 - s)))
                    crossed = flow * (x * scale2 + shift2)
                    ones = ones + flow[:, 0:128] + flow[:, 128:256]
                    cross = cross + crossed[:, 0:128] + crossed[:, 128:256]
        right = stacked(
            j,
            blocks,
            images,
            p_rows,
            [(even, 0, 0, 384), (odd, 1, 0, 384), (even, 1, 0, 384)],
        )
        own = stacked(j, blocks, images, p_rows, [(first_grad, 0, 0, 256)])
        kernel_ref[...] += lax.dot_general(
            own, right, (((0,), (0,)), ((), ())), preferred_element_type=F32
        )
    group, local = len(outs), outs[0].shape[0]
    for s in range(group):
        distance = lax.rem(s - place[0] + group, group)
        for d in range(group):

            @pl.when(distance == d)
            def _():
                outs[d][...] = rows_ref[s * local : (s + 1) * local]

    add_rows(stats, grouped_rows(w0, w1, [ones, cross]))

    @pl.when(pl.program_id(0) == pl.num_programs(0) - 1)
    def _():
        for a in range(3):
            for b in range(3):
                tap = jnp.zeros((CS_OUT, CS_IN), F32)
                for q in range(4):
                    lane = a * 384 + (2 * q + b + 3) * CS_IN
                    tap = tap + kernel_ref[q * CS_OUT : (q + 1) * CS_OUT, lane : lane + CS_IN]
                row = (3 * a + b) * CS_OUT
                taps_ref[row : row + CS_OUT] = tap


def student_entry(
    place, flow, first_out, grad, even, odd, raw, label, tot, inner, pulled, norm_in, norm,
    weights_even, weights_odd, tile, group,
):
    rows, images, lanes = flow.shape
    p_rows = rows - 1
    outs = [shape_of((2 * p_rows // group, images, lanes), BF16)] * group
    taps = shape_of((9 * CS_OUT, CS_IN), F32)
    stats = shape_of((8, 128), F32)
    big = (flow, first_out, grad, even, odd, raw)
    shared = (tot, inner, pulled, norm_in, norm, weights_even, weights_odd)
    return pl.pallas_call(
        functools.partial(entry_kernel, p_rows, 4),
        grid_spec=pltpu.PrefetchScalarGridSpec(
            num_scalar_prefetch=1,
            grid=(images // tile,),
            in_specs=[image_spec(a, tile) for a in big]
            + [table_spec(label, tile)]
            + [whole_spec(a) for a in shared],
            out_specs=[image_spec(o, tile) for o in outs] + [whole_spec(taps), whole_spec(stats)],
            scratch_shapes=[
                pltpu.VMEM((p_rows + 1, tile, 128 + lanes), BF16),
                pltpu.VMEM((256, 1152), F32),
                pltpu.VMEM((2 * p_rows, tile, lanes), BF16),
            ],
        ),
        out_shape=outs + [taps, stats],
        compiler_params=pltpu.CompilerParams(vmem_limit_bytes=VMEM_LIMIT),
        cost_estimate=cost(16),
    )(place, *big, label, *shared)


def bands_kernel(first, first_t, second, second_t, short, short_t, *outs):
    one, two, back, even, odd, gather, scatter, wide = outs

    def fill(out, entries):
        rows = out.shape[0]
        wide[0:rows] = jnp.zeros((rows, 256), F32)
        for row, lane, tap in entries:
            wide[row : row + tap.shape[0], lane : lane + tap.shape[1]] = tap
        out[...] = wide[0:rows].astype(BF16)

    def tap_of(ref, a, b):
        size = ref.shape[0] // 9
        return ref[(3 * a + b) * size : (3 * a + b + 1) * size]

    taps = [(a, b) for a in range(3) for b in range(3)]
    fill(
        one,
        [
            (a * 384 + (2 * q + b + 3) * CS_IN, q * CS_OUT, tap_of(first, a, b))
            for a, b in taps
            for q in range(4)
        ],
    )
    fill(
        two,
        [
            (a * 512 + (q + b + 1) * CS_OUT, q * CS_OUT, tap_of(second, a, b))
            for a, b in taps
            for q in range(4)
        ]
        + [(1536 + 2 * q * CS_IN, q * CS_OUT, short[...]) for q in range(4)],
    )
    fill(
        back,
        [
            ((2 - a) * 512 + (s - b + 3) * CS_OUT, s * CS_OUT, tap_of(second_t, a, b))
            for a, b in taps
            for s in range(4)
        ],
    )

    def backward(a, row):
        entries = []
        for q in range(6):
            for b in range(3):
                s = 2 * q + b - 1
                if 0 <= s < 8:
                    entries.append((row + q * CS_OUT, s * CS_IN, tap_of(first_t, a, b)))
        return entries

    corner = [(384 + q * CS_OUT, 2 * q * CS_IN, short_t[...]) for q in range(4)]
    fill(even, backward(1, 0) + corner)
    fill(odd, backward(2, 0) + backward(0, 384))
    channel = lax.rem(lax.broadcasted_iota(jnp.int32, gather.shape, 0), 256)
    lane = lax.broadcasted_iota(jnp.int32, gather.shape, 1)
    gather[...] = jnp.where(lax.div(channel, CS_OUT) == lane, 1.0 / CS_OUT, 0.0).astype(BF16)
    lane = lax.rem(lax.broadcasted_iota(jnp.int32, scatter.shape, 0), 128)
    channel = lax.broadcasted_iota(jnp.int32, scatter.shape, 1)
    scatter[...] = jnp.where(lax.div(channel, CS_OUT) == lane, 1.0, 0.0).astype(BF16)


def banded_kernels(first, second, shortcut):
    turn = lambda k: jnp.swapaxes(k, 2, 3).reshape(-1, k.shape[2])
    rounded = lambda k: k.astype(BF16).astype(F32)
    first, second, shortcut = rounded(first), rounded(second), rounded(shortcut)
    args = (
        first.reshape(-1, CS_OUT),
        turn(first),
        second.reshape(-1, CS_OUT),
        turn(second),
        shortcut,
        shortcut.T,
    )
    shapes = [(1152, 256), (1792, 256), (1536, 256), (640, 256), (768, 256), (512, 128), (256, 256)]
    return pl.pallas_call(
        bands_kernel,
        in_specs=[pl.BlockSpec(memory_space=pltpu.VMEM)] * 6,
        out_specs=[pl.BlockSpec(memory_space=pltpu.VMEM)] * len(shapes),
        out_shape=[shape_of(shape, BF16) for shape in shapes],
        scratch_shapes=[pltpu.VMEM((1792, 256), F32)],
        compiler_params=pltpu.CompilerParams(vmem_limit_bytes=VMEM_LIMIT),
        cost_estimate=cost(8),
    )(*args)


def body(
    space,
    batch,
    small_in,
    large_in,
    small_teacher,
    large_teacher,
    small_groups,
    large_groups,
    small_cot,
    large_cot,
    teacher_gains,
    teacher_first,
    teacher_inner,
    teacher_second,
    teacher_bypass,
    entry_norm,
    first_conv,
    inner_norm,
    second_conv,
    shortcut,
    momentum_entry,
    momentum_first,
    momentum_inner,
    momentum_second,
    momentum_shortcut,
    average_entry,
    average_first,
    average_inner,
    average_second,
    average_shortcut,
):
    slabs = SLABS
    group = space // slabs
    axes = (("space", space), ("batch", batch))
    me = lax.axis_index("space")
    z, x = me // group, me % group
    place = jnp.stack([x, z]).astype(jnp.int32)
    total_positions = batch * (small_in.shape[0] * SIDE * SIDE // 4 + large_in.shape[0] * SIDE * SIDE)
    pixels = [small_in, large_in]
    teachers = [small_teacher, large_teacher]
    labels = [small_groups, large_groups]
    cots = [small_cot, large_cot]
    sides = [SIDE, 2 * SIDE]
    both = range(2)
    per_device = [p.shape[0] // space for p in pixels]
    local_rows = [p.shape[1] for p in pixels]
    images = [slabs * n for n in per_device]
    padded = [-(-n // 16) * 16 for n in images]
    tiles = [32 if padded[0] % 32 == 0 else 16, 16]
    p_counts = [s // (2 * slabs) for s in sides]
    widths = [s // 2 for s in sides]

    def to_sub(d):
        return [(k, k // group * group + (k % group + d) % group) for k in range(space)]

    def to_slab(d):
        return [(k, (k // group + d) % slabs * group + k % group) for k in range(space)]

    def send(array, pairs):
        return lax.ppermute(array, "space", pairs)

    def pick_images(array, res, sub):
        n, rows, lanes = array.shape
        parts = array.reshape(slabs, group, per_device[res], rows, lanes)
        part = lax.dynamic_index_in_dim(parts, sub, 1, False)
        return part.reshape(images[res], rows, lanes)

    def rows_first(array):
        return jnp.transpose(array, (1, 0, 2))

    def slab_rows(pieces, first, last):
        local = pieces[0].shape[0]
        out = []
        for s in range(first // local, (last - 1) // local + 1):
            lo, hi = max(first - s * local, 0), min(last - s * local, local)
            cut = [p[lo:hi] for p in pieces]
            out.append(lax.select_n((x - s) % group, *cut) if group > 1 else cut[0])
        return jnp.concatenate(out, axis=0) if len(out) > 1 else out[0]

    def partner(b, k, first):
        slab = k // group
        other = slab ^ 1 if first else ((slab + 1) ^ 1) - 1
        if 0 <= other < slabs:
            return b * space + other * group + k % group
        return (b ^ 1) * space + k

    pair_lists = [
        [(b * space + k, partner(b, k, first)) for b in range(batch) for k in range(space)]
        for first in (True, False)
    ]

    def edge_rows(pieces, count):
        rows = group * pieces[0].shape[0]
        last, first = slab_rows(pieces, rows - count, rows), slab_rows(pieces, 0, count)
        even = z % 2 == 0
        return lax.select(even, last, first), lax.select(even, first, last)

    def to_neighbours(rows):
        return [lax.ppermute(r, ("batch", "space"), pairs) for r, pairs in zip(rows, pair_lists)]

    def pad_to(array, size):
        extra = size - array.shape[1]
        return jnp.pad(array, ((0, 0), (0, extra), (0, 0))) if extra else array

    def pad_images(array, res):
        return pad_to(array, padded[res])

    def label_table(res, sub, size):
        mine = lax.dynamic_index_in_dim(
            labels[res].reshape(slabs, group, per_device[res]), sub, 1, False
        ).reshape(images[res])
        mine = jnp.pad(mine.astype(F32), (0, size - images[res]), constant_values=-1.0)
        return jnp.broadcast_to(mine[:, None], (size, 128))

    tables = [label_table(res, x, padded[res]) for res in both]
    norm_in = jnp.tile(entry_norm, (1, 128 // CS_IN))
    norm_mid = jnp.tile(inner_norm, (1, 128 // CS_OUT))
    by_slab = [[sub + group * k for k in range(slabs)] for sub in range(group)]

    def among_slabs(array, axis):
        if axis:
            array = jnp.moveaxis(array, axis, 0)
        return lax.all_to_all(array, "space", 0, 0, axis_index_groups=by_slab, tiled=True)

    subs = [(x + d) % group for d in range(group)]
    picked_small = [rows_first(pick_images(small_in, 0, sub)) for sub in subs]
    cots_here = after(cots, picked_small[1:])
    narrow = cots[0].shape[2]
    cot_stacks = []
    for res in both:
        c = jnp.pad(rows_first(cots_here[res]), ((1, 2), (0, 0), (0, 0)))
        count = p_counts[res]
        c = jnp.stack([c[k * count : (k + 1) * count + 3] for k in range(slabs)])
        if c.shape[3] > narrow:
            c = jnp.concatenate(
                [c[..., k : k + narrow] for k in range(0, c.shape[3], narrow)], axis=2
            )
        cot_stacks.append(c)
    flat = [c.reshape(slabs, -1, narrow) for c in cot_stacks]
    cot_flat = jnp.concatenate(flat, axis=1)
    cots_ready = cot_flat
    cot_flat = among_slabs(cot_flat, 0)
    large_source = after(large_in, cots_ready)
    picked_large = [rows_first(pick_images(large_source, 1, sub)) for sub in subs]
    picked = [picked_small, picked_large]
    arrived = [
        [picked[res][0]] + [send(picked[res][d], to_sub(d)) for d in range(1, group)]
        for res in both
    ]


    gains = jnp.tile(teacher_gains, (1, max(t.shape[2] for t in teachers) // CT_IN))

    def activated(array, size):
        lanes = array.shape[2]
        z_t = gains[0, :lanes] * array.astype(F32) + gains[1, :lanes]
        return pad_to(rows_first(jax.nn.silu(z_t).astype(BF16)), size)

    large_raw_in = after(large_teacher, [p[1:] for p in picked], cots_ready)
    own_large = pick_images(large_raw_in, 1, x)
    away_large = [pick_images(large_raw_in, 1, sub) for sub in subs[1:]]
    cut = min(16, images[1])
    sizes = [cut, images[1] - cut]
    ranges = [(0, cut), (cut, images[1])]

    def large_part(k, *others):
        lo, hi = ranges[k]
        return [
            send(after(away_large[d - 1][lo:hi], *others), to_sub(d)) for d in range(1, group)
        ]

    large_raw = [large_part(0)]

    stat_tables = [label_table(res, sub, images[res]) for res in both for sub in subs]
    entry_sums = input_stats(picked[0] + picked[1], stat_tables)
    (lo, hi), size = ranges[0], sizes[0]
    large_own = [activated(own_large[lo:hi], size)]
    raw_edges = [edge_rows(arrived[res], 6) for res in both]
    corners = lambda parts: [p[:1, :, :128] for p in parts]
    waits = ([p[1:] for p in arrived], cot_flat, corners(large_raw[0]), large_own, raw_edges)
    entry_total = total_over_devices([entry_sums], axes, 0, waits)

    raw_halos = [to_neighbours(after(raw_edges[res], entry_total)) for res in both]
    large_raw.append(large_part(1, entry_total))
    large_pieces = [
        [large_own[0]] + [activated(after(p, entry_total), sizes[0]) for p in large_raw[0]]
    ]

    def large_edges_of(k, *others):
        lo, hi = ranges[k]
        rows = [after(p[:, : hi - lo], *others) for p in large_pieces[k]]
        return to_neighbours(edge_rows(rows, 3))

    lanes = small_teacher.shape[2]
    z_t = after(small_teacher, large_raw_in).astype(F32) * gains[0, :lanes] + gains[1, :lanes]
    small_active = rows_first(jax.nn.silu(z_t).astype(BF16))
    small_active = small_active.reshape(local_rows[0], slabs, group, per_device[0], lanes)

    parts_of = [list(range(slabs // 2)), *([k] for k in range(slabs // 2, slabs))]

    def small_part(ks, sub):
        part = lax.dynamic_slice(
            small_active,
            (0, ks[0], sub, 0, 0),
            (local_rows[0], len(ks), 1, per_device[0], lanes),
        )
        return part.reshape(local_rows[0], len(ks) * per_device[0], lanes)

    small_away = [[small_part(ks, sub) for sub in subs[1:]] for ks in parts_of]
    bands = banded_kernels(*after((first_conv, second_conv, shortcut), entry_total))
    bands_first, bands_second, bands_second_back, bands_even, bands_odd, gather, scatter = bands
    raws, evens, odds, firsts, first_sums = ([None, None] for _ in range(5))
    for res in (1, 0):
        pieces = [pad_images(p, res) for p in arrived[res]]
        if res == 0:
            large_edges = [large_edges_of(0, sums)]
            cot_here = after(cot_flat, sums)
            cot_slabs = []
            at = 0
            for at_res, sent in zip(both, cot_stacks):
                size = sent.shape[1] * sent.shape[2]
                c = cot_here[:, at : at + size].reshape(sent.shape)
                at += size
                n = per_device[at_res]
                c = jnp.concatenate([c[:, :, k : k + n] for k in range(0, c.shape[2], n)], axis=3)
                c = jnp.moveaxis(c, 0, 1).reshape(c.shape[1], images[at_res], c.shape[3])
                cot_slabs.append(pad_images(c, at_res))
            pieces = after(pieces, cot_slabs)
        raw, even, odd, first, sums = student_forward(
            place,
            pieces,
            *[pad_images(p, res) for p in raw_halos[res]],
            tables[res],
            entry_total,
            norm_in,
            bands_first,
            tiles[res],
        )
        raws[res] = raw
        evens[res] = even
        odds[res] = odd
        firsts[res] = first
        first_sums[res] = sums
    inner_total = total_over_devices(first_sums, axes, 1, (corners(large_raw[1]), large_edges))

    (lo, hi), size = ranges[1], sizes[1]
    large_pieces.append(
        [activated(after(p, inner_total), size) for p in (own_large[lo:hi], *large_raw[1])]
    )
    large_edges.append(large_edges_of(1, inner_total))
    small_pieces = [
        [send(after(p, inner_total), to_sub(d + 1)) for d, p in enumerate(away)]
        for away in small_away[::-1]
    ][::-1]

    def small_rows(n, *others):
        own = small_part(parts_of[n], x)
        return edge_rows([own] + after(small_pieces[n], *others), 3)

    acts, own_firsts, sums_out, lows, energies = [], [], [], [], []
    for res in both:
        act, own_first, block_sum, low, energy = student_block(
            place,
            firsts[res],
            odds[res],
            tables[res],
            entry_total,
            inner_total,
            norm_mid,
            bands_second,
            gather,
            tiles[res],
        )
        acts.append(act)
        own_firsts.append(own_first)
        sums_out.append(block_sum)
        lows.append(low)
        energies.append(energy)

    shared = (
        teacher_first.reshape(9 * CT_IN, CT_OUT),
        teacher_second.reshape(9 * CT_OUT, CT_OUT),
        teacher_bypass,
        teacher_inner,
    )
    def large_map(k, *others):
        pieces = large_pieces[k]
        own = after(pieces[0], *others)
        edges = [pad_to(h, sizes[k]) for h in large_edges[k]]
        return teacher_energies(place, own, 0, pieces[1:], *edges, shared, sizes[k])

    def small_map(n, edges, *others):
        arrays = after((*small_pieces[n], *edges), *others)
        return [
            teacher_energies(
                place, small_active, parts_of[n][0], arrays[:-2], *arrays[-2:], shared, per_device[0]
            )
        ]

    large_maps = [large_map(0, inner_total)]
    rows = small_rows(0, large_maps[0], energies)
    edges = [to_neighbours(rows)]
    large_maps.append(large_map(1, rows))
    rows = small_rows(1, large_maps[1])
    edges.append(to_neighbours(rows))
    small_maps = small_map(0, edges[0], rows)
    for n in range(2, len(parts_of)):
        rows = small_rows(n, small_maps)
        edges.append(to_neighbours(rows))
        small_maps = small_maps + small_map(n - 1, edges[n - 1], rows)
    small_maps = small_maps + small_map(len(parts_of) - 1, edges[-1])
    factors = attention_maps(
        energies, [small_maps, large_maps], tables, widths, p_counts, slabs, group, 2
    )
    loss_sums = factors[2]

    def to_owners(res, first, last, *others):
        low = after(lows[res][first:last, : images[res]], *others)
        rows, _, lanes = low.shape
        return among_slabs(low.reshape(rows, slabs, per_device[res], lanes), 1)

    out_parts = [to_owners(0, 0, p_counts[0], factors[2])]

    flows, grads, flow_sums, second_parts, shortcut_parts = [], [], [], [], []
    for res in both:
        flow, grad, sums, second_part, shortcut_part = student_back(
            place,
            sums_out[res],
            cot_slabs[res],
            factors[res],
            scatter,
            own_firsts[res],
            acts[res],
            odds[res],
            tables[res],
            entry_total,
            inner_total,
            norm_mid,
            bands_second_back,
            tiles[res],
        )
        flows.append(flow)
        grads.append(grad)
        flow_sums.append(sums)
        second_parts.append(second_part)
        shortcut_parts.append(shortcut_part)
    flow_total = total_over_devices(flow_sums, axes, 3, out_parts)

    entry_parts, first_parts, entry_flow_sums = [], [], []
    held = None
    for res in both:
        flow = flows[res] if held is None else after(flows[res], held)
        *rows, first_part, sums = student_entry(
            place,
            flow,
            own_firsts[res],
            grads[res],
            evens[res],
            odds[res],
            raws[res],
            tables[res],
            entry_total,
            inner_total,
            flow_total,
            norm_in,
            norm_mid,
            bands_even,
            bands_odd,
            tiles[res],
            group,
        )
        if res == 0:
            held = rows[0]
            half_out = to_owners(1, 0, p_counts[1] // 2, held)
        first_parts.append(first_part)
        entry_flow_sums.append(sums)
        rows = [r[:, : images[res]] for r in rows]
        if res == 0:
            rows[1:] = [send(r, to_sub(d + 1)) for d, r in enumerate(rows[1:])]
        entry_parts.append(rows)
    def native_rows(res):
        ordered = [lax.select_n((x - s) % group, *entry_parts[res]) for s in range(group)]
        n, rows, lanes = pixels[res].shape
        rows_in = jnp.stack(ordered).reshape(group, rows, slabs, per_device[res], lanes)
        return jnp.transpose(rows_in, (2, 0, 3, 1, 4)).reshape(n, rows, lanes)

    rate_scale = 1.0 / math.sqrt(total_positions)
    flat = lambda k: k.reshape(-1, k.shape[-1])
    kernel_states = [
        [flat(k) for k in (first_conv, momentum_first, average_first)],
        [flat(k) for k in (second_conv, momentum_second, average_second)],
        [shortcut, momentum_shortcut, average_shortcut],
    ]
    packed = gradient_sum(
        [first_parts, second_parts, shortcut_parts, entry_flow_sums, [loss_sums]],
        axes,
        4,
        (entry_parts[0][1:], entry_parts[1], half_out),
    )
    first_state, second_state, bypass_state, entry_state, image_tables, total_loss = update(
        packed,
        kernel_states,
        [entry_norm, momentum_entry, average_entry],
        entry_total,
        norm_in,
        (CONV_RATE * rate_scale, NORM_RATE * rate_scale, 1.0 / total_positions),
    )
    rows = entry_parts[1]
    rows[1:] = [send(after(r, packed), to_sub(d + 1)) for d, r in enumerate(rows[1:])]
    out_parts.append(jnp.concatenate([half_out, to_owners(1, p_counts[1] // 2, p_counts[1], packed)], axis=1))
    first_state = [k.reshape(first_conv.shape) for k in first_state]
    second_state = [k.reshape(second_conv.shape) for k in second_state]
    inner_folded = flow_total.reshape(8, 128 // CS_OUT, CS_OUT).sum(axis=1)
    ones_inner, cross_inner = inner_folded[0:2], inner_folded[2:4]
    block_outs = []
    for res in both:
        low = jnp.transpose(out_parts[res], (2, 0, 1, 3))
        block_outs.append(low.reshape(low.shape[0], -1, low.shape[3]))
    def wide_rows(lanes):
        wide = jnp.tile(image_tables, (1, lanes // 128))
        return [wide[k] for k in range(8)]

    wide = [wide_rows(p.shape[2]) for p in pixels]
    arrived_rows = [native_rows(0)]
    entry_parts[1] = after(entry_parts[1], block_outs, wide[1])
    arrived_rows.append(native_rows(1))
    input_grads = []
    for res in both:
        one = (labels[res] == 1)[:, None, None]
        gain, bias, slope, level = [
            jnp.where(one, wide[res][2 * k + 1], wide[res][2 * k]) for k in range(4)
        ]
        value = pixels[res].astype(F32)
        before = value * gain + bias
        s = jax.nn.sigmoid(before)
        flow = arrived_rows[res].astype(F32) * (s * (1.0 + before * (1.0 - s)))
        input_grads.append(gain * flow + (value * slope + level))

    inner_grads = jnp.stack([jnp.sum(cross_inner, axis=0), jnp.sum(ones_inner, axis=0)])
    inner_state = renew(inner_norm, inner_grads, momentum_inner, average_inner, NORM_RATE * rate_scale)
    return (
        *block_outs,
        input_grads[0],
        input_grads[1],
        total_loss.reshape(()),
        *entry_state,
        *first_state,
        *inner_state,
        *second_state,
        *bypass_state,
    )


def solution(mesh):
    rows = P("batch", "space", None)
    blocks = P(("batch", "space"), None, None)
    return jax.shard_map(
        functools.partial(body, mesh.shape["space"], mesh.shape["batch"]),
        mesh=mesh,
        in_specs=(rows,) * 4 + (P("batch"),) * 2 + (blocks,) * 2 + (P(),) * 20,
        out_specs=(blocks,) * 2 + (rows,) * 2 + (P(),) * 24,
        check_vma=False,
    )
```

```python
import functools
import math

import jax
import jax.numpy as jnp
import numpy as np
from jax import lax
from jax.experimental import pallas as pl
from jax.experimental.pallas import tpu as pltpu
from jax.sharding import PartitionSpec as P

CS_IN = 32
CS_OUT = 64
CT_IN = 128
CT_OUT = 256
SIDE = 32
SLABS = 4

EPSILON = 1e-05
TRANSFER_WEIGHT = 1000.0
MOMENTUM = 0.9
WEIGHT_DECAY = 0.0005
AVERAGING = 0.7
CONV_RATE = 0.06
NORM_RATE = 0.3

F32 = jnp.float32
BF16 = jnp.bfloat16
MESH = pl.DeviceIdType.MESH
VMEM_LIMIT = 56 << 20


def sigmoid(z):
    return 0.5 * jnp.tanh(0.5 * z) + 0.5


def matmul(a, b):
    return jnp.dot(a, b, preferred_element_type=F32)


def after(value, *others):
    return lax.optimization_barrier((value, others))[0]


def cost(microseconds):
    return pl.CostEstimate(
        flops=int(microseconds * 1e9), bytes_accessed=1 << 20, transcendentals=0
    )


def stacked(first, count, images, rows, parts):
    blocks = []
    for t in range(count):
        at = (first + t) * 256
        pieces = [ref[lo : lo + rows, :, at + off : at + off + size] for ref, lo, off, size in parts]
        block = jnp.concatenate(pieces, axis=2) if len(pieces) > 1 else pieces[0]
        blocks.append(block.reshape(rows * images, block.shape[2]))
    return jnp.concatenate(blocks, axis=0) if count > 1 else blocks[0]


def fold(rows, width):
    shift = width
    while shift < 128:
        rows = rows + pltpu.roll(rows, shift, 1)
        shift *= 2
    return rows


def group_norms(totals, counts, width):
    folded = fold(totals, width)
    means, scales = [], []
    for g in range(2):
        mean = folded[g : g + 1] / counts[g]
        variance = folded[2 + g : 3 + g] / counts[g] - mean * mean
        means.append(mean)
        scales.append(lax.rsqrt(variance + EPSILON))
    return means, scales


def per_image(w0, w1, pair):
    return w0 * pair[0] + w1 * pair[1]


def twice(table):
    return jnp.concatenate([table, table], axis=1)


def grouped_rows(w0, w1, values):
    rows = []
    for v in values:
        rows.append(jnp.sum(v * w0, axis=0, keepdims=True))
        rows.append(jnp.sum(v * w1, axis=0, keepdims=True))
    rows.append(jnp.zeros((8 - len(rows), 128), F32))
    return jnp.concatenate(rows, axis=0)


def entry_counts(tot_ref):
    return [tot_ref[4:5], tot_ref[5:6]]


def inner_counts(tot_ref):
    return [tot_ref[4:5] * 0.25, tot_ref[5:6] * 0.25]


def renew(weights, gradient, moment, average, factor):
    descent = gradient + WEIGHT_DECAY * weights
    velocity = MOMENTUM * moment + descent
    updated = weights - factor * (descent + MOMENTUM * velocity)
    smoothed = AVERAGING * average + (1.0 - AVERAGING) * updated
    return (gradient, velocity, smoothed, updated)


def stats_kernel(x_refs, label_refs, out_ref):
    step = pl.program_id(0)
    total = jnp.zeros((8, 128), F32)
    for x_ref, label_ref in zip(x_refs, label_refs):
        rows, images, lanes = x_ref.shape
        s = jnp.zeros((images, 128), F32)
        q = jnp.zeros((images, 128), F32)
        for r in range(rows):
            for c in range(0, lanes, 128):
                v = x_ref[r, :, c : c + 128].astype(F32)
                s = s + v
                q = q + v * v
        w0, w1 = indicators(label_ref)
        positions = jnp.full((images, 128), float(rows * lanes // CS_IN), F32)
        total = total + grouped_rows(w0, w1, [s, q, positions])

    @pl.when(step == 0)
    def _():
        out_ref[...] = total

    @pl.when(step > 0)
    def _():
        out_ref[...] += total


def input_stats(pieces, tables):
    steps = min(4, min(x.shape[0] for x in pieces))
    count = len(pieces)

    def kernel(*refs):
        stats_kernel(refs[:count], refs[count:-1], refs[-1])

    specs = [
        pl.BlockSpec((x.shape[0] // steps,) + x.shape[1:], lambda i: (i, 0, 0)) for x in pieces
    ]
    specs += [pl.BlockSpec(w.shape, lambda i: (0, 0)) for w in tables]
    return pl.pallas_call(
        kernel,
        grid=(steps,),
        in_specs=specs,
        out_specs=pl.BlockSpec((8, 128), lambda i: (0, 0)),
        out_shape=jax.ShapeDtypeStruct((8, 128), F32),
        compiler_params=pltpu.CompilerParams(vmem_limit_bytes=VMEM_LIMIT),
        cost_estimate=cost(5),
    )(*pieces, *tables)


def greet(axes):
    barrier = pltpu.get_barrier_semaphore()
    expected = 0
    for name, size in axes:
        me = lax.axis_index(name)
        for d in range(1, size):
            pl.semaphore_signal(
                barrier,
                inc=1,
                device_id={name: lax.rem(me + d, size)},
                device_id_type=MESH,
            )
            expected += 1
    pl.semaphore_wait(barrier, expected)


def total_kernel(axes, count, *refs):
    parts = refs[:count]
    out_ref, held, boxes_a, boxes_b, send_a, recv_a, send_b, recv_b = refs[-8:]
    value = parts[0][...]
    for part in parts[1:]:
        value = value + part[...]
    held[0] = value
    greet(axes)
    for level, ((name, size), boxes, send, recv) in enumerate(
        zip(axes, (boxes_a, boxes_b), (send_a, send_b), (recv_a, recv_b))
    ):
        me = lax.axis_index(name)
        copies = []
        for d in range(1, size):
            copy = pltpu.make_async_remote_copy(
                src_ref=held.at[level],
                dst_ref=boxes.at[d],
                send_sem=send.at[d],
                recv_sem=recv.at[d],
                device_id={name: lax.rem(me + d, size)},
                device_id_type=MESH,
            )
            copy.start()
            copies.append(copy)
        for copy in copies:
            copy.wait_recv()
        value = jnp.zeros(value.shape, F32)
        for source in range(size):
            back = lax.rem(me - source + size, size)
            value = value + jnp.where(
                back == 0, held[level], boxes[jnp.maximum(back, 1)]
            )
        for copy in copies:
            copy.wait_send()
        if level == 0:
            held[1] = value
        else:
            out_ref[...] = value


def total_over_devices(parts, axes, collective_id, waits):
    waits = jax.tree.leaves(waits)
    shape = parts[0].shape
    return pl.pallas_call(
        functools.partial(total_kernel, axes, len(parts)),
        out_shape=jax.ShapeDtypeStruct(shape, F32),
        in_specs=[pl.BlockSpec(memory_space=pltpu.VMEM)] * len(parts)
        + [pl.BlockSpec(memory_space=pl.ANY)] * len(waits),
        out_specs=pl.BlockSpec(memory_space=pltpu.VMEM),
        scratch_shapes=[
            pltpu.VMEM((2,) + shape, F32),
            pltpu.VMEM((axes[0][1],) + shape, F32),
            pltpu.VMEM((axes[1][1],) + shape, F32),
            pltpu.SemaphoreType.DMA((axes[0][1],)),
            pltpu.SemaphoreType.DMA((axes[0][1],)),
            pltpu.SemaphoreType.DMA((axes[1][1],)),
            pltpu.SemaphoreType.DMA((axes[1][1],)),
        ],
        compiler_params=pltpu.CompilerParams(collective_id=collective_id, has_side_effects=True),
        cost_estimate=cost(12),
    )(*parts, *waits)


def gradient_sum_kernel(axes, layout, waits, *refs):
    count = sum(len(parts) for parts in layout)
    inputs, refs = refs[:count], refs[count + waits :]
    out_ref, x_ref, boxes_a, boxes_b, held = refs[:5]
    send_a, recv_a, send_b, recv_b, send_c, recv_c = refs[5:]
    at = 0
    for parts in layout:
        value = inputs[parts[0]][...]
        for k in parts[1:]:
            value = value + inputs[k][...]
        parts = 128 // value.shape[1]
        if parts > 1:
            n = value.shape[0] // parts
            value = jnp.concatenate([value[k * n : k * n + n] for k in range(parts)], axis=1)
        x_ref[at : at + value.shape[0]] = value
        at += value.shape[0]
    if at < x_ref.shape[0]:
        x_ref[at:] = jnp.zeros((x_ref.shape[0] - at, 128), F32)
    (name_a, size_a), (name_b, size_b) = axes
    me_a, me_b = lax.axis_index(name_a), lax.axis_index(name_b)
    piece = x_ref.shape[0] // size_a
    greet(axes)

    def rows(index):
        return pl.ds(pl.multiple_of(index * piece, 8), piece)

    copies = []
    for d in range(1, size_a):
        peer = lax.rem(me_a + d, size_a)
        copy = pltpu.make_async_remote_copy(
            src_ref=x_ref.at[rows(peer)],
            dst_ref=boxes_a.at[d],
            send_sem=send_a.at[d],
            recv_sem=recv_a.at[d],
            device_id={name_a: peer},
            device_id_type=MESH,
        )
        copy.start()
        copies.append(copy)
    value = x_ref[rows(me_a)]
    for d in range(1, size_a):
        copies[d - 1].wait_recv()
        value = value + boxes_a[d]
    held[0] = value
    for copy in copies:
        copy.wait_send()
    copies = []
    for d in range(1, size_b):
        copy = pltpu.make_async_remote_copy(
            src_ref=held.at[0],
            dst_ref=boxes_b.at[d],
            send_sem=send_b.at[d],
            recv_sem=recv_b.at[d],
            device_id={name_b: lax.rem(me_b + d, size_b)},
            device_id_type=MESH,
        )
        copy.start()
        copies.append(copy)
    for copy in copies:
        copy.wait_recv()
    value = jnp.zeros(value.shape, F32)
    for source in range(size_b):
        back = lax.rem(me_b - source + size_b, size_b)
        value = value + jnp.where(back == 0, held[0], boxes_b[jnp.maximum(back, 1)])
    held[1] = value
    out_ref[rows(me_a)] = value
    for copy in copies:
        copy.wait_send()
    copies = []
    for d in range(1, size_a):
        copy = pltpu.make_async_remote_copy(
            src_ref=held.at[1],
            dst_ref=out_ref.at[rows(me_a)],
            send_sem=send_c.at[d],
            recv_sem=recv_c.at[d],
            device_id={name_a: lax.rem(me_a + d, size_a)},
            device_id_type=MESH,
        )
        copy.start()
        copies.append(copy)
    for copy in copies:
        copy.wait()


def update_kernel(rates, *refs):
    out_ref, tot, norm = refs[:3]
    states, entry, outs = refs[3:12], refs[12:15], refs[15:]
    conv_rate, norm_rate, per_position = rates
    at = 0
    for k in range(3):
        weights, moment, average = [ref[...] for ref in states[3 * k : 3 * k + 3]]
        width = (CS_IN, CS_OUT, CS_IN)[k]
        n = weights.shape[0] * weights.shape[1] // 128
        packed = out_ref[at : at + n]
        at += n
        parts = [packed[:, lane : lane + width] for lane in range(0, 128, width)]
        turned = jnp.concatenate(parts, axis=0)
        taps = turned.shape[0] // CS_OUT
        gradient = jnp.concatenate(
            [turned[t * CS_OUT : (t + 1) * CS_OUT].T for t in range(taps)], axis=0
        )
        state = renew(weights, gradient, moment, average, conv_rate)
        for ref, value in zip(outs[5 * k : 5 * k + 4], state):
            ref[...] = value
        outs[5 * k + 4][...] = state[3].astype(BF16)
    pulled = fold(out_ref[at : at + 8], CS_IN)
    ones, cross = [pulled[0:1], pulled[1:2]], [pulled[2:3], pulled[3:4]]
    gradient = jnp.concatenate([cross[0] + cross[1], ones[0] + ones[1]], axis=0)[:, 0:CS_IN]
    state = renew(entry[0][...], gradient, entry[1][...], entry[2][...], norm_rate)
    for ref, value in zip(outs[15:19], state):
        ref[...] = value
    counts = entry_counts(tot)
    means, scales = group_norms(tot[...], counts, CS_IN)
    gains, biases, slopes, levels = [], [], [], []
    for g in range(2):
        shift = -means[g] * scales[g]
        gain = norm[0:1] * scales[g]
        gains.append(gain)
        biases.append(norm[0:1] * shift + norm[1:2])
        slopes.append(-gain * (cross[g] / counts[g]) * scales[g])
        levels.append(-gain * ((ones[g] + cross[g] * shift) / counts[g]))
    outs[19][...] = jnp.concatenate(gains + biases + slopes + levels, axis=0)
    losses = out_ref[at + 8 : at + 9]
    outs[20][...] = jnp.sum(losses, axis=1, keepdims=True) * per_position


def gradient_sum(groups, axes, collective_id, waits):
    (_, size_a), (_, size_b) = axes
    arrays, layout, rows = [], [], []
    for members in groups:
        layout.append(tuple(range(len(arrays), len(arrays) + len(members))))
        arrays += members
        rows.append(members[0].shape[0] * members[0].shape[1] // 128)
    padded = -(-sum(rows) // (8 * size_a)) * 8 * size_a
    piece = padded // size_a
    sems = []
    for size in (size_a, size_b, size_a):
        sems += [pltpu.SemaphoreType.DMA((size,))] * 2
    waits = jax.tree.leaves(waits)
    vmem = pl.BlockSpec(memory_space=pltpu.VMEM)
    return pl.pallas_call(
        functools.partial(gradient_sum_kernel, axes, tuple(layout), len(waits)),
        out_shape=jax.ShapeDtypeStruct((padded, 128), F32),
        in_specs=[vmem] * len(arrays) + [pl.BlockSpec(memory_space=pl.ANY)] * len(waits),
        out_specs=vmem,
        scratch_shapes=[
            pltpu.VMEM((padded, 128), F32),
            pltpu.VMEM((size_a, piece, 128), F32),
            pltpu.VMEM((size_b, piece, 128), F32),
            pltpu.VMEM((2, piece, 128), F32),
        ]
        + sems,
        compiler_params=pltpu.CompilerParams(collective_id=collective_id, has_side_effects=True),
        cost_estimate=cost(20),
    )(*arrays, *waits)


def update(total, states, entry, tot, norm, rates):
    given = [total, tot, norm] + [a for state in states for a in state] + entry
    outs = []
    for state in states:
        outs += [shape_of(state[0].shape, F32)] * 4 + [shape_of(state[0].shape, BF16)]
    outs += [shape_of(entry[0].shape, F32)] * 4 + [shape_of((8, 128), F32), shape_of((1, 1), F32)]
    vmem = pl.BlockSpec(memory_space=pltpu.VMEM)
    got = pl.pallas_call(
        functools.partial(update_kernel, rates),
        out_shape=outs,
        in_specs=[vmem] * len(given),
        out_specs=[vmem] * len(outs),
        compiler_params=pltpu.CompilerParams(vmem_limit_bytes=VMEM_LIMIT),
        cost_estimate=cost(4),
    )(*given)
    return got[0:5], got[5:10], got[10:15], got[15:19], got[19], got[20]


def teacher_kernel(p_rows, width, group, columns, place, *refs):
    pieces, refs = refs[:group], refs[group:]
    edge_a, edge_b, first, second, bypass, inner, out_ref, even, odd, mid = refs
    local, lanes = pieces[0].shape[0], pieces[0].shape[-1]
    real, images = edge_a.shape[1], even.shape[1]
    m_rows = p_rows + 2
    zero = jnp.zeros((images, 128), BF16)

    def put(row, source, at):
        if row % 2 == 0:
            even[row // 2 + 1, 0:real, 128 : 128 + lanes] = source[at]
        else:
            odd[(row + 1) // 2 + 1, 0:real, 128 : 128 + lanes] = source[at]

    def put_edges(above, below):
        for k in range(3):
            put(k - 3, above, k)
        for k in range(2):
            put(2 * p_rows + k, below, k)

    rows_of_neighbours(place, edge_a, edge_b, put_edges)
    nothing = jnp.zeros((1, real, lanes), BF16)

    @pl.when(place[1] == 0)
    def _():
        for k in range(3):
            put(k - 3, nothing, 0)

    @pl.when(place[1] == SLABS - 1)
    def _():
        for k in range(2):
            put(2 * p_rows + k, nothing, 0)

    x = place[0]
    for s in range(group):
        distance = lax.rem(x - s + group, group)
        for d in range(group):

            @pl.when(distance == d)
            def _():
                for k in range(local):
                    at = (k, 0, 0) if len(pieces[d].shape) == 5 else k
                    put(s * local + k, pieces[d], at)

    for i in range(m_rows):
        even[i, :, 0:128] = zero
    for i in range(m_rows + 1):
        odd[i, :, 0:128] = zero
    wide_zero = jnp.zeros((images, CT_OUT), BF16)
    for i in range(m_rows):
        mid[i, :, 0:CT_OUT] = wide_zero
        mid[i, :, (width + 1) * CT_OUT : (width + 2) * CT_OUT] = wide_zero
    scale, shift = inner[0:1], inner[1:2]
    top, bottom = keep_row(place, -1, p_rows), keep_row(place, p_rows, p_rows)

    def first_step(g, carry):
        lefts = []
        for t in range(columns):
            window = pl.ds(pl.multiple_of((g * columns + t) * 256, 256), 384)
            parts = [odd[0:m_rows, :, window], even[0:m_rows, :, window]]
            parts.append(odd[1 : m_rows + 1, :, window])
            lefts.append(jnp.concatenate(parts, axis=2).reshape(m_rows * images, 9 * CT_IN))
        z = scale * matmul(jnp.concatenate(lefts, axis=0), first[...]) + shift
        act = (z * sigmoid(z)).reshape(columns, m_rows, images, CT_OUT)
        for t in range(columns):
            here = pl.ds(pl.multiple_of((g * columns + t + 1) * CT_OUT, 256), CT_OUT)
            mid[0, :, here] = (act[t, 0] * top).astype(BF16)
            mid[1 : p_rows + 1, :, here] = act[t, 1 : p_rows + 1].astype(BF16)
            mid[p_rows + 1, :, here] = (act[t, p_rows + 1] * bottom).astype(BF16)
        return carry

    lax.fori_loop(0, width // columns, first_step, 0)
    out_ref[...] = jnp.zeros(out_ref.shape, F32)
    lane = lax.broadcasted_iota(jnp.int32, (real, 128), 1)

    def second_step(g, carry):
        lefts, corners = [], []
        for t in range(columns):
            at = pl.multiple_of((g * columns + t) * 256, 256)
            window = pl.ds(at, 3 * CT_OUT)
            corner = pl.ds(pl.multiple_of(at + 128, 128), 128)
            parts = [mid[a : a + p_rows, :, window] for a in range(3)]
            lefts.append(jnp.concatenate(parts, axis=2).reshape(p_rows * images, 9 * CT_OUT))
            corners.append(even[1 : p_rows + 1, :, corner].reshape(p_rows * images, CT_IN))
        y = matmul(jnp.concatenate(lefts, axis=0), second[...])
        y = y + matmul(jnp.concatenate(corners, axis=0), bypass[...])
        square = y * y
        energy = jnp.sum(square[:, 0:128] + square[:, 128:256], axis=1, keepdims=True)
        energy = (energy * (1.0 / CT_OUT)).reshape(columns, p_rows, images, 1)
        for t in range(columns):
            for p in range(p_rows):
                chunk, start = divmod((p + 1) * width, 128)
                where = slice(chunk * 128, chunk * 128 + 128)
                here = lane == start + g * columns + t
                out_ref[:, where] = jnp.where(here, energy[t, p, 0:real], out_ref[:, where])
        return carry

    lax.fori_loop(0, width // columns, second_step, 0)


def teacher_energies(place, own, slab, received, edge_a, edge_b, shared, tile):
    group = len(received) + 1
    local, lanes = own.shape[0], own.shape[-1]
    images = edge_a.shape[1]
    p_rows, width = group * local // 2, lanes // (2 * CT_IN)
    out_lanes = -(-(p_rows + 3) * width // 128) * 128
    m_rows = p_rows + 2
    space = -(-tile // 16) * 16
    if own.ndim == 5:
        own_spec = pl.BlockSpec(
            (local, 1, 1, tile, lanes), lambda i, place: (0, slab + i, place[0], 0, 0)
        )
    else:
        own_spec = pl.BlockSpec((local, tile, lanes), lambda i, place: (0, i, 0))
    whole = lambda a: pl.BlockSpec(a.shape, lambda i, place: (0,) * a.ndim)
    by_image = lambda a: pl.BlockSpec((a.shape[0], tile, a.shape[2]), lambda i, place: (0, i, 0))
    grid_spec = pltpu.PrefetchScalarGridSpec(
        num_scalar_prefetch=1,
        grid=(images // tile,),
        in_specs=[own_spec]
        + [by_image(a) for a in received]
        + [by_image(edge_a), by_image(edge_b)]
        + [whole(a) for a in shared],
        out_specs=pl.BlockSpec((tile, out_lanes), lambda i, place: (i, 0)),
        scratch_shapes=[
            pltpu.VMEM((m_rows, space, 128 + lanes), BF16),
            pltpu.VMEM((m_rows + 1, space, 128 + lanes), BF16),
            pltpu.VMEM((m_rows, space, (width + 2) * CT_OUT), BF16),
        ],
    )
    return pl.pallas_call(
        functools.partial(teacher_kernel, p_rows, width, group, 4),
        grid_spec=grid_spec,
        out_shape=jax.ShapeDtypeStruct((images, out_lanes), F32),
        compiler_params=pltpu.CompilerParams(vmem_limit_bytes=VMEM_LIMIT),
        cost_estimate=cost(40 * images * p_rows * width / 10240),
    )(place, own, *received, edge_a, edge_b, *shared)


def entry_tables(tot_ref, norm_ref, w0, w1):
    means, scales = group_norms(tot_ref[...], entry_counts(tot_ref), CS_IN)
    scale = per_image(w0, w1, scales)
    shift = per_image(w0, w1, [-m * s for m, s in zip(means, scales)])
    gain, bias = norm_ref[0:1], norm_ref[1:2]
    present = w0 + w1
    return gain * scale, gain * shift + bias * present, scale, shift


def inner_tables(tot_ref, inner_ref, norm_ref, w0, w1):
    means, scales = group_norms(inner_ref[...], inner_counts(tot_ref), CS_OUT)
    scale = per_image(w0, w1, scales)
    shift = per_image(w0, w1, [-m * s for m, s in zip(means, scales)])
    gain, bias = norm_ref[0:1], norm_ref[1:2]
    present = w0 + w1
    return gain * scale, gain * shift + bias * present, scale, shift


def indicators(label_ref):
    label = label_ref[...]
    return (label == 0.0).astype(F32), (label == 1.0).astype(F32)


def keep_row(place, row, inside):
    z = place[1]
    outside = jnp.logical_or(
        jnp.logical_and(row < 0, z == 0), jnp.logical_and(row >= inside, z == SLABS - 1)
    )
    return jnp.where(outside, 0.0, 1.0)


def rows_of_neighbours(place, first, second, use):
    even = lax.rem(place[1], 2) == 0

    @pl.when(even)
    def _():
        use(second, first)

    @pl.when(jnp.logical_not(even))
    def _():
        use(first, second)


def add_rows(ref, value):
    first = pl.program_id(0) == 0

    @pl.when(first)
    def _():
        ref[...] = value

    @pl.when(jnp.logical_not(first))
    def _():
        ref[...] += value


def forward_kernel(
    p_rows, group, blocks, place, *refs
):
    pieces, refs = refs[:group], refs[group:]
    first, second, label_ref, tot, norm, weights = refs[:6]
    raw_ref, even_ref, odd_ref, out_ref, stats, raw, even, odd = refs[6:]
    images, lanes = raw.shape[1:]
    local = pieces[0].shape[0]
    w0, w1 = indicators(label_ref)
    gain, bias, _, _ = entry_tables(tot, norm, w0, w1)
    gain2, bias2 = twice(gain), twice(bias)
    zero = jnp.zeros((images, 128), BF16)

    def put_edges(above, below):
        raw[0:5] = above[1:6]
        raw[2 * p_rows + 5 : 2 * p_rows + 11] = below[...]

    rows_of_neighbours(place, first, second, put_edges)
    x = place[0]
    for s in range(group):
        distance = lax.rem(x - s + group, group)
        for d in range(group):

            @pl.when(distance == d)
            def _():
                raw[5 + s * local : 5 + (s + 1) * local] = pieces[d][...]

    def activate(row, target, index):
        keep = keep_row(place, row - 5, 2 * p_rows)
        target[index, :, 0:128] = zero
        for c in range(0, lanes, 256):
            z = raw[row, :, c : c + 256].astype(F32) * gain2 + bias2
            target[index, :, 128 + c : 384 + c] = (z * sigmoid(z) * keep).astype(BF16)

    def pair(i, carry):
        activate(2 * i, even, i)
        activate(2 * i + 1, odd, i)
        return carry

    f_rows = p_rows + 5
    lax.fori_loop(0, f_rows, pair, 0)
    activate(2 * f_rows, even, f_rows)
    raw_ref[...] = raw[5 : 2 * p_rows + 5]
    even_ref[...] = even[2 : p_rows + 3]
    odd_ref[...] = odd[1 : p_rows + 4]
    s = jnp.zeros((images, 128), F32)
    q = jnp.zeros((images, 128), F32)
    for j in range(0, lanes // 256, blocks):
        left = stacked(
            j, blocks, images, f_rows, [(even, 0, 0, 384), (odd, 0, 0, 384), (even, 1, 0, 384)]
        )
        y = matmul(left, weights[...]).reshape(blocks, f_rows, images, 256)
        for t in range(blocks):
            out_ref[:, :, (j + t) * 256 : (j + t + 1) * 256] = y[t]
            own = y[t, 2 : 2 + p_rows]
            u = jnp.sum(own, axis=0)
            v = jnp.sum(own * own, axis=0)
            s = s + u[:, 0:128] + u[:, 128:256]
            q = q + v[:, 0:128] + v[:, 128:256]
    add_rows(stats, grouped_rows(w0, w1, [s, q]))


def whole_spec(a):
    return pl.BlockSpec(a.shape, lambda i, *_: (0,) * len(a.shape))


def image_spec(a, tile):
    return pl.BlockSpec((a.shape[0], tile, a.shape[2]), lambda i, *_: (0, i, 0))


def table_spec(a, tile):
    return pl.BlockSpec((tile, a.shape[1]), lambda i, *_: (i, 0))


def shape_of(shape, dtype):
    return jax.ShapeDtypeStruct(shape, dtype)


def student_forward(place, pieces, first, second, label, tot, norm, weights, tile):
    group = len(pieces)
    local, images, lanes = pieces[0].shape
    p_rows = group * local // 2
    outs = [
        shape_of((2 * p_rows, images, lanes), BF16),
        shape_of((p_rows + 1, images, 128 + lanes), BF16),
        shape_of((p_rows + 3, images, 128 + lanes), BF16),
        shape_of((p_rows + 5, images, lanes), F32),
    ]
    stats = shape_of((8, 128), F32)
    big = (*pieces, first, second)
    shared = (tot, norm, weights)
    grid_spec = pltpu.PrefetchScalarGridSpec(
        num_scalar_prefetch=1,
        grid=(images // tile,),
        in_specs=[image_spec(a, tile) for a in big]
        + [table_spec(label, tile)]
        + [whole_spec(a) for a in shared],
        out_specs=[image_spec(o, tile) for o in outs] + [whole_spec(stats)],
        scratch_shapes=[
            pltpu.VMEM((2 * p_rows + 11, tile, lanes), BF16),
            pltpu.VMEM((p_rows + 6, tile, 128 + lanes), BF16),
            pltpu.VMEM((p_rows + 5, tile, 128 + lanes), BF16),
        ],
    )
    return pl.pallas_call(
        functools.partial(forward_kernel, p_rows, group, 4),
        grid_spec=grid_spec,
        out_shape=outs + [stats],
        compiler_params=pltpu.CompilerParams(vmem_limit_bytes=VMEM_LIMIT),
        cost_estimate=cost(15),
    )(place, *big, label, *shared)


def split_bf16(value):
    high = value.astype(BF16)
    return high, (value - high.astype(F32)).astype(BF16)


def block_kernel(
    p_rows,
    blocks,
    place,
    first_ref,
    odd,
    label_ref,
    tot,
    inner,
    norm,
    weights,
    spread,
    act_ref,
    own_ref,
    sum_ref,
    low_ref,
    energy,
    act,
):
    images, lanes = first_ref.shape[1:]
    w0, w1 = indicators(label_ref)
    gain, bias, _, _ = inner_tables(tot, inner, norm, w0, w1)
    gain2, bias2 = twice(gain), twice(bias)
    zero = jnp.zeros((images, 128), BF16)
    f_rows, b_rows = p_rows + 5, p_rows + 3

    def activate(f, carry):
        keep = keep_row(place, f - 2, p_rows)
        act[f, :, 0:128] = zero
        act[f, :, 128 + lanes : 256 + lanes] = zero
        for c in range(0, lanes, 256):
            z = first_ref[f, :, c : c + 256] * gain2 + bias2
            act[f, :, 128 + c : 384 + c] = (z * sigmoid(z) * keep).astype(BF16)
        return carry

    lax.fori_loop(0, f_rows, activate, 0)
    act_ref[...] = act[1 : p_rows + 3]
    own_ref[...] = first_ref[2 : p_rows + 3]

    per_chunk = 128 // (lanes // CS_OUT)
    chunks = energy.shape[1] // 128
    measured = [jnp.zeros((images, 128), F32) for _ in range(chunks)]
    for j in range(0, lanes // 256, blocks):
        parts = [(act, a, 0, 512) for a in range(3)] + [(odd, 0, 128, 256)]
        left = stacked(j, blocks, images, b_rows, parts)
        flat = matmul(left, weights[...])
        y = flat.reshape(blocks, b_rows, images, 256)
        high, low = split_bf16(flat * flat)
        e = matmul(jnp.concatenate([high, low], axis=1), spread[...])
        e = e.reshape(blocks, b_rows, images, 128)
        for t in range(blocks):
            here = slice((j + t) * 256, (j + t + 1) * 256)
            sum_ref[:, :, here] = y[t]
            low_ref[:, :, here] = y[t, 1 : p_rows + 1].astype(BF16)
            for b in range(b_rows):
                shift = b % per_chunk * (128 // per_chunk) + 4 * (j + t)
                part = pltpu.roll(e[t, b], shift, 1) if shift else e[t, b]
                measured[b // per_chunk] = measured[b // per_chunk] + part
    for c in range(chunks):
        energy[:, c * 128 : c * 128 + 128] = measured[c]


def student_block(place, first_out, odd, label, tot, inner, norm, weights, spread, tile):
    rows, images, lanes = first_out.shape
    p_rows = rows - 5
    width = lanes // CS_OUT
    energy_lanes = -(-(p_rows + 3) * width // 128) * 128
    outs = [
        shape_of((p_rows + 2, images, 256 + lanes), BF16),
        shape_of((p_rows + 1, images, lanes), F32),
        shape_of((p_rows + 3, images, lanes), F32),
        shape_of((p_rows, images, lanes), BF16),
    ]
    energy = shape_of((images, energy_lanes), F32)
    return pl.pallas_call(
        functools.partial(block_kernel, p_rows, 4),
        grid_spec=pltpu.PrefetchScalarGridSpec(
            num_scalar_prefetch=1,
            grid=(images // tile,),
            in_specs=[image_spec(first_out, tile), image_spec(odd, tile), table_spec(label, tile)]
            + [whole_spec(a) for a in (tot, inner, norm, weights, spread)],
            out_specs=[image_spec(o, tile) for o in outs] + [table_spec(energy, tile)],
            scratch_shapes=[pltpu.VMEM((p_rows + 5, tile, 256 + lanes), BF16)],
        ),
        out_shape=outs + [energy],
        compiler_params=pltpu.CompilerParams(vmem_limit_bytes=VMEM_LIMIT),
        cost_estimate=cost(18),
    )(place, first_out, odd, label, tot, inner, norm, weights, spread)


def map_kernel(slabs, group, widths, p_counts, pieces, *refs):
    student, present = refs[0:2], refs[2:4]
    given = refs[4 : 4 + sum(pieces)]
    refs = refs[4 + sum(pieces) :]
    outs, loss_ref = refs[0:2], refs[2]
    teacher, sums, boxes = refs[3:5], refs[5:7], refs[7:9]
    from_above, from_below = refs[9:11], refs[11:13]
    send, recv, send_halo, recv_halo, ready = refs[13:]
    for res in range(2):
        at = 0
        for part in given[res * pieces[0] : res * pieces[0] + pieces[res]]:
            teacher[res][at : at + part.shape[0]] = part[...]
            at += part.shape[0]
        rest = teacher[res].shape[0] - at
        if rest:
            teacher[res][at:] = jnp.zeros((rest, teacher[res].shape[1]), F32)
    me = lax.axis_index("space")
    z, x = lax.div(me, group), lax.rem(me, group)
    greet_barrier = pltpu.get_barrier_semaphore()
    for d in range(1, slabs):
        pl.semaphore_signal(
            greet_barrier,
            inc=1,
            device_id={"space": lax.rem(z + d, slabs) * group + x},
            device_id_type=MESH,
        )
    pl.semaphore_wait(greet_barrier, slabs - 1)

    def halo_copies(res, direction):
        width, p_rows = widths[res], p_counts[res]
        lane = (p_rows * width if direction == 0 else width) // 128 * 128
        target = (from_above, from_below)[direction][res]
        return pltpu.make_async_remote_copy(
            src_ref=teacher[res].at[:, pl.ds(lane, 128)],
            dst_ref=target,
            send_sem=send_halo.at[2 * res + direction],
            recv_sem=recv_halo.at[2 * res + direction],
            device_id={"space": me + (group if direction == 0 else -group)},
            device_id_type=MESH,
        )

    for res in range(2):
        from_above[res][...] = jnp.zeros(from_above[res].shape, F32)
        from_below[res][...] = jnp.zeros(from_below[res].shape, F32)

    @pl.when(z > 0)
    def _():
        pl.semaphore_signal(
            ready.at[0], inc=1, device_id={"space": me - group}, device_id_type=MESH
        )

    @pl.when(z < slabs - 1)
    def _():
        pl.semaphore_signal(
            ready.at[1], inc=1, device_id={"space": me + group}, device_id_type=MESH
        )
        pl.semaphore_wait(ready.at[0], 1)
        halo_copies(0, 0).start()
        halo_copies(1, 0).start()

    @pl.when(z > 0)
    def _():
        pl.semaphore_wait(ready.at[1], 1)
        halo_copies(0, 1).start()
        halo_copies(1, 1).start()

    copies = []
    for res in range(2):
        width, p_rows = widths[res], p_counts[res]
        images, lanes = student[res].shape
        lane = lax.broadcasted_iota(jnp.int32, (images, lanes), 1)
        own = jnp.logical_and(lane >= width, lane < (p_rows + 1) * width)
        es = jnp.where(own, student[res][...], 0.0)
        et = jnp.where(own, teacher[res][...], 0.0)
        columns = [
            jnp.sum(v, axis=1, keepdims=True) for v in (es * es, et * et, es * et)
        ]
        small_lane = lax.broadcasted_iota(jnp.int32, (images, 128), 1)
        packed = jnp.zeros((images, 128), F32)
        for k, column in enumerate(columns):
            packed = jnp.where(small_lane == k, column, packed)
        padded = sums[res].shape[1]
        packed = jnp.concatenate([packed, jnp.zeros((padded - images, 128), F32)], axis=0)
        sums[res][...] = packed.T[0:8]
        for d in range(1, slabs):
            copy = pltpu.make_async_remote_copy(
                src_ref=sums[res],
                dst_ref=boxes[res].at[d],
                send_sem=send.at[res * slabs + d],
                recv_sem=recv.at[res * slabs + d],
                device_id={"space": lax.rem(z + d, slabs) * group + x},
                device_id_type=MESH,
            )
            copy.start()
            copies.append(copy)
    for copy in copies:
        copy.wait()

    @pl.when(z < slabs - 1)
    def _():
        halo_copies(0, 0).wait_send()
        halo_copies(1, 0).wait_send()
        halo_copies(0, 1).wait_recv()
        halo_copies(1, 1).wait_recv()

    @pl.when(z > 0)
    def _():
        halo_copies(0, 1).wait_send()
        halo_copies(1, 1).wait_send()
        halo_copies(0, 0).wait_recv()
        halo_copies(1, 0).wait_recv()

    loss = jnp.zeros((1, 128), F32)
    for res in range(2):
        width, p_rows = widths[res], p_counts[res]
        images, lanes = student[res].shape
        total = sums[res][...]
        for d in range(1, slabs):
            total = total + boxes[res][d]
        padded = total.shape[1]
        total = jnp.concatenate([total, jnp.zeros((120, padded), F32)], axis=0).T[0:images]
        ss, tt, st = total[:, 0:1], total[:, 1:2], total[:, 2:3]
        scale_s = lax.rsqrt(ss + 1e-12)
        scale_t = lax.rsqrt(tt + 1e-12)
        pulled = TRANSFER_WEIGHT * scale_s * (scale_s * ss - scale_t * st)
        lane = lax.broadcasted_iota(jnp.int32, (images, lanes), 1)
        shift = p_rows * width
        chunks = lanes // 128
        first_rows = from_below[res][...]
        last_rows = from_above[res][...]
        if shift % 128:
            first_rows = pltpu.roll(first_rows, shift % 128, 1)
            last_rows = pltpu.roll(last_rows, 128 - shift % 128, 1)
        blank = jnp.zeros((images, 128), F32)
        before = [last_rows] + [blank] * (chunks - 1)
        after = [blank] * (chunks - 1) + [first_rows]
        before = jnp.concatenate(before, axis=1) if chunks > 1 else before[0]
        after = jnp.concatenate(after, axis=1) if chunks > 1 else after[0]
        et = jnp.where(lane < width, before, teacher[res][...])
        et = jnp.where(lane >= (p_rows + 1) * width, after, et)
        u = student[res][...] * scale_s
        difference = u - et * scale_t
        own = jnp.logical_and(lane >= width, lane < (p_rows + 1) * width)
        squares = jnp.where(own, difference * difference, 0.0)
        kept = (present[res][...] >= 0.0).astype(F32)
        for c in range(chunks):
            loss = loss + jnp.sum(squares[:, c * 128 : c * 128 + 128] * kept, axis=0, keepdims=True)
        factor = (TRANSFER_WEIGHT * difference - u * pulled) * (scale_s * (2.0 / CS_OUT))
        for c in range(chunks):
            here = slice(c * 128, c * 128 + 128)
            outs[res][:, here] = jnp.where(kept > 0.0, factor[:, here], 0.0)
    loss_ref[...] = jnp.concatenate(
        [loss * (TRANSFER_WEIGHT / 2), jnp.zeros((7, 128), F32)], axis=0
    )


def attention_maps(student, teacher, present, widths, p_counts, slabs, group, collective_id):
    padded = [-(-s.shape[0] // 128) * 128 for s in student]
    images = [s.shape[0] for s in student]
    vmem = pl.BlockSpec(memory_space=pltpu.VMEM)
    return pl.pallas_call(
        functools.partial(
            map_kernel, slabs, group, widths, p_counts, tuple(len(t) for t in teacher)
        ),
        out_shape=[shape_of(s.shape, F32) for s in student] + [shape_of((8, 128), F32)],
        in_specs=[vmem] * (4 + sum(len(t) for t in teacher)),
        out_specs=[vmem] * 3,
        scratch_shapes=[pltpu.VMEM(s.shape, F32) for s in student]
        + [pltpu.VMEM((8, n), F32) for n in padded]
        + [pltpu.VMEM((slabs, 8, n), F32) for n in padded]
        + [pltpu.VMEM((n, 128), F32) for n in images] * 2
        + [pltpu.SemaphoreType.DMA((2 * slabs,))] * 2
        + [pltpu.SemaphoreType.DMA((4,))] * 2
        + [pltpu.SemaphoreType.REGULAR((2,))],
        compiler_params=pltpu.CompilerParams(collective_id=collective_id, has_side_effects=True),
        cost_estimate=cost(11),
    )(*student, *present, *teacher[0], *teacher[1])


def back_kernel(
    p_rows,
    blocks,
    place,
    sum_ref,
    cot,
    factor,
    spread,
    first_ref,
    act,
    odd,
    label_ref,
    tot,
    inner,
    norm,
    weights,
    flow_ref,
    grad_ref,
    stats,
    second_ref,
    shortcut_ref,
    kernel_ref,
    grad,
):
    images, lanes = sum_ref.shape[1:]
    w0, w1 = indicators(label_ref)
    gain, bias, scale, shift = inner_tables(tot, inner, norm, w0, w1)
    gain2, bias2, scale2, shift2 = twice(gain), twice(bias), twice(scale), twice(shift)
    zero = jnp.zeros((images, 128), BF16)
    b_rows, k_rows = p_rows + 3, p_rows + 1
    width = lanes // CS_OUT
    per_chunk = 128 // width
    for b in range(b_rows):
        grad[b, :, 0:128] = zero
        grad[b, :, 128 + lanes : 256 + lanes] = zero
    halves = [split_bf16(factor[:, c * 128 : c * 128 + 128]) for c in range(factor.shape[1] // 128)]
    halves = [[h.astype(F32) for h in pair] for pair in halves]
    for j in range(0, lanes // 256, blocks):
        rows = []
        for t in range(blocks):
            for b in range(b_rows):
                shift = (128 - (b % per_chunk * width + 4 * (j + t))) % 128
                pair = halves[b // per_chunk]
                if shift:
                    pair = [pltpu.roll(h, shift, 1) for h in pair]
                rows.append(jnp.concatenate(pair, axis=1))
        wide = matmul(jnp.concatenate(rows, axis=0).astype(BF16), spread[...])
        wide = wide.reshape(blocks, b_rows, images, 256)
        for t in range(blocks):
            at = (j + t) * 256
            for b in range(b_rows):
                keep = keep_row(place, b - 1, p_rows)
                v = cot[b, :, at : at + 256].astype(F32) + wide[t, b] * sum_ref[b, :, at : at + 256]
                grad[b, :, 128 + at : 384 + at] = (v * keep).astype(BF16)

    grad_ref[...] = grad[1 : p_rows + 1, :, 128 : 128 + lanes]

    @pl.when(pl.program_id(0) == 0)
    def _():
        kernel_ref[...] = jnp.zeros(kernel_ref.shape, F32)

    ones = jnp.zeros((images, 128), F32)
    cross = jnp.zeros((images, 128), F32)
    for j in range(0, lanes // 256, blocks):
        left = stacked(j, blocks, images, k_rows, [(grad, d, 0, 512) for d in range(3)])
        y = matmul(left, weights[...]).reshape(blocks, k_rows, images, 256)
        for t in range(blocks):
            here = slice((j + t) * 256, (j + t + 1) * 256)
            for k in range(k_rows):
                x = first_ref[k, :, here]
                z = x * gain2 + bias2
                s = sigmoid(z)
                flow = y[t, k] * (s * (1.0 + z * (1.0 - s)))
                flow_ref[k, :, here] = flow
                if k < p_rows:
                    crossed = flow * (x * scale2 + shift2)
                    ones = ones + flow[:, 0:128] + flow[:, 128:256]
                    cross = cross + crossed[:, 0:128] + crossed[:, 128:256]
        right = stacked(
            j,
            blocks,
            images,
            p_rows,
            [(act, a, 0, 512) for a in range(3)] + [(odd, 1, 128, 256)],
        )
        own = stacked(j, blocks, images, p_rows, [(grad, 1, 128, 256)])
        kernel_ref[...] += lax.dot_general(
            own, right, (((0,), (0,)), ((), ())), preferred_element_type=F32
        )
    add_rows(stats, grouped_rows(w0, w1, [ones, cross]))

    @pl.when(pl.program_id(0) == pl.num_programs(0) - 1)
    def _():
        for a in range(3):
            for b in range(3):
                tap = jnp.zeros((CS_OUT, CS_OUT), F32)
                for q in range(4):
                    lane = a * 512 + (q + b + 1) * CS_OUT
                    tap = tap + kernel_ref[q * CS_OUT : (q + 1) * CS_OUT, lane : lane + CS_OUT]
                row = (3 * a + b) * CS_OUT
                second_ref[row : row + CS_OUT] = tap
        tap = jnp.zeros((CS_OUT, CS_IN), F32)
        for q in range(4):
            lane = 1536 + 2 * q * CS_IN
            tap = tap + kernel_ref[q * CS_OUT : (q + 1) * CS_OUT, lane : lane + CS_IN]
        shortcut_ref[...] = tap


def student_back(
    place, block_sum, cot, factor, spread, first_out, act, odd, label, tot, inner, norm, weights, tile
):
    rows, images, lanes = block_sum.shape
    p_rows = rows - 3
    outs = [
        shape_of((p_rows + 1, images, lanes), F32),
        shape_of((p_rows, images, lanes), BF16),
    ]
    stats = shape_of((8, 128), F32)
    second = shape_of((9 * CS_OUT, CS_OUT), F32)
    shortcut = shape_of((CS_OUT, CS_IN), F32)
    return pl.pallas_call(
        functools.partial(back_kernel, p_rows, 4),
        grid_spec=pltpu.PrefetchScalarGridSpec(
            num_scalar_prefetch=1,
            grid=(images // tile,),
            in_specs=[image_spec(block_sum, tile), image_spec(cot, tile), table_spec(factor, tile)]
            + [whole_spec(spread), image_spec(first_out, tile), image_spec(act, tile)]
            + [image_spec(odd, tile), table_spec(label, tile)]
            + [whole_spec(a) for a in (tot, inner, norm, weights)],
            out_specs=[image_spec(o, tile) for o in outs]
            + [whole_spec(a) for a in (stats, second, shortcut)],
            scratch_shapes=[
                pltpu.VMEM((256, 1792), F32),
                pltpu.VMEM((p_rows + 3, tile, 256 + lanes), BF16),
            ],
        ),
        out_shape=outs + [stats, second, shortcut],
        compiler_params=pltpu.CompilerParams(vmem_limit_bytes=VMEM_LIMIT),
        cost_estimate=cost(18),
    )(place, block_sum, cot, factor, spread, first_out, act, odd, label, tot, inner, norm, weights)


def entry_kernel(
    p_rows,
    blocks,
    place,
    flow_ref,
    first_ref,
    grad,
    even,
    odd,
    raw,
    label_ref,
    tot,
    inner,
    pulled,
    norm_in,
    norm,
    weights_even,
    weights_odd,
    *refs,
):
    outs, (taps_ref, stats, first_grad, kernel_ref, rows_ref) = refs[:-5], refs[-5:]
    images, lanes = first_ref.shape[1:]
    w0, w1 = indicators(label_ref)
    gain, _, scale, shift = inner_tables(tot, inner, norm, w0, w1)
    counts = inner_counts(tot)
    folded = fold(pulled[...], CS_OUT)
    ones_mean = per_image(w0, w1, [folded[g : g + 1] / counts[g] for g in range(2)])
    cross_mean = per_image(w0, w1, [folded[2 + g : 3 + g] / counts[g] for g in range(2)])
    gain2, scale2, shift2 = twice(gain), twice(scale), twice(shift)
    ones2, cross2 = twice(ones_mean), twice(cross_mean)
    zero = jnp.zeros((images, 128), BF16)

    def first_rows(k, carry):
        keep = keep_row(place, k, p_rows)
        first_grad[k, :, lanes : lanes + 128] = zero
        for c in range(0, lanes, 256):
            normed = first_ref[k, :, c : c + 256] * scale2 + shift2
            v = gain2 * (flow_ref[k, :, c : c + 256] - ones2 - normed * cross2)
            first_grad[k, :, c : c + 256] = (v * keep).astype(BF16)
        return carry

    lax.fori_loop(0, p_rows + 1, first_rows, 0)

    @pl.when(pl.program_id(0) == 0)
    def _():
        kernel_ref[...] = jnp.zeros(kernel_ref.shape, F32)

    gain, bias, scale, shift = entry_tables(tot, norm_in, w0, w1)
    gain2, bias2, scale2, shift2 = twice(gain), twice(bias), twice(scale), twice(shift)

    ones = jnp.zeros((images, 128), F32)
    cross = jnp.zeros((images, 128), F32)
    for j in range(0, lanes // 256, blocks):
        upper = (first_grad, 0, 0, 384)
        lower = (first_grad, 1, 0, 384)
        left = stacked(j, blocks, images, p_rows, [upper, (grad, 0, 0, 256)])
        rows_even = matmul(left, weights_even[...])
        rows_odd = matmul(stacked(j, blocks, images, p_rows, [upper, lower]), weights_odd[...])
        for parity, rows in enumerate((rows_even, rows_odd)):
            low = rows.astype(BF16).reshape(blocks, p_rows, images, 256)
            for t in range(blocks):
                here = slice((j + t) * 256, (j + t + 1) * 256)
                for p in range(p_rows):
                    rows_ref[2 * p + parity, :, here] = low[t, p]
                    x = raw[2 * p + parity, :, here].astype(F32)
                    z = x * gain2 + bias2
                    s = sigmoid(z)
                    flow = low[t, p].astype(F32) * (s * (1.0 + z * (1.0 - s)))
                    crossed = flow * (x * scale2 + shift2)
                    ones = ones + flow[:, 0:128] + flow[:, 128:256]
                    cross = cross + crossed[:, 0:128] + crossed[:, 128:256]
        right = stacked(
            j,
            blocks,
            images,
            p_rows,
            [(even, 0, 0, 384), (odd, 1, 0, 384), (even, 1, 0, 384)],
        )
        own = stacked(j, blocks, images, p_rows, [(first_grad, 0, 0, 256)])
        kernel_ref[...] += lax.dot_general(
            own, right, (((0,), (0,)), ((), ())), preferred_element_type=F32
        )
    group, local = len(outs), outs[0].shape[0]
    for s in range(group):
        distance = lax.rem(s - place[0] + group, group)
        for d in range(group):

            @pl.when(distance == d)
            def _():
                outs[d][...] = rows_ref[s * local : (s + 1) * local]

    add_rows(stats, grouped_rows(w0, w1, [ones, cross]))

    @pl.when(pl.program_id(0) == pl.num_programs(0) - 1)
    def _():
        for a in range(3):
            for b in range(3):
                tap = jnp.zeros((CS_OUT, CS_IN), F32)
                for q in range(4):
                    lane = a * 384 + (2 * q + b + 3) * CS_IN
                    tap = tap + kernel_ref[q * CS_OUT : (q + 1) * CS_OUT, lane : lane + CS_IN]
                row = (3 * a + b) * CS_OUT
                taps_ref[row : row + CS_OUT] = tap


def student_entry(
    place, flow, first_out, grad, even, odd, raw, label, tot, inner, pulled, norm_in, norm,
    weights_even, weights_odd, tile, group,
):
    rows, images, lanes = flow.shape
    p_rows = rows - 1
    outs = [shape_of((2 * p_rows // group, images, lanes), BF16)] * group
    taps = shape_of((9 * CS_OUT, CS_IN), F32)
    stats = shape_of((8, 128), F32)
    big = (flow, first_out, grad, even, odd, raw)
    shared = (tot, inner, pulled, norm_in, norm, weights_even, weights_odd)
    return pl.pallas_call(
        functools.partial(entry_kernel, p_rows, 4),
        grid_spec=pltpu.PrefetchScalarGridSpec(
            num_scalar_prefetch=1,
            grid=(images // tile,),
            in_specs=[image_spec(a, tile) for a in big]
            + [table_spec(label, tile)]
            + [whole_spec(a) for a in shared],
            out_specs=[image_spec(o, tile) for o in outs] + [whole_spec(taps), whole_spec(stats)],
            scratch_shapes=[
                pltpu.VMEM((p_rows + 1, tile, 128 + lanes), BF16),
                pltpu.VMEM((256, 1152), F32),
                pltpu.VMEM((2 * p_rows, tile, lanes), BF16),
            ],
        ),
        out_shape=outs + [taps, stats],
        compiler_params=pltpu.CompilerParams(vmem_limit_bytes=VMEM_LIMIT),
        cost_estimate=cost(16),
    )(place, *big, label, *shared)


def bands_kernel(first, first_t, second, second_t, short, short_t, *outs):
    one, two, back, even, odd, gather, scatter, wide = outs

    def fill(out, entries):
        rows = out.shape[0]
        wide[0:rows] = jnp.zeros((rows, 256), F32)
        for row, lane, tap in entries:
            wide[row : row + tap.shape[0], lane : lane + tap.shape[1]] = tap
        out[...] = wide[0:rows].astype(BF16)

    def tap_of(ref, a, b):
        size = ref.shape[0] // 9
        return ref[(3 * a + b) * size : (3 * a + b + 1) * size]

    taps = [(a, b) for a in range(3) for b in range(3)]
    fill(
        one,
        [
            (a * 384 + (2 * q + b + 3) * CS_IN, q * CS_OUT, tap_of(first, a, b))
            for a, b in taps
            for q in range(4)
        ],
    )
    fill(
        two,
        [
            (a * 512 + (q + b + 1) * CS_OUT, q * CS_OUT, tap_of(second, a, b))
            for a, b in taps
            for q in range(4)
        ]
        + [(1536 + 2 * q * CS_IN, q * CS_OUT, short[...]) for q in range(4)],
    )
    fill(
        back,
        [
            ((2 - a) * 512 + (s - b + 3) * CS_OUT, s * CS_OUT, tap_of(second_t, a, b))
            for a, b in taps
            for s in range(4)
        ],
    )

    def backward(a, row):
        entries = []
        for q in range(6):
            for b in range(3):
                s = 2 * q + b - 1
                if 0 <= s < 8:
                    entries.append((row + q * CS_OUT, s * CS_IN, tap_of(first_t, a, b)))
        return entries

    corner = [(384 + q * CS_OUT, 2 * q * CS_IN, short_t[...]) for q in range(4)]
    fill(even, backward(1, 0) + corner)
    fill(odd, backward(2, 0) + backward(0, 384))
    channel = lax.rem(lax.broadcasted_iota(jnp.int32, gather.shape, 0), 256)
    lane = lax.broadcasted_iota(jnp.int32, gather.shape, 1)
    gather[...] = jnp.where(lax.div(channel, CS_OUT) == lane, 1.0 / CS_OUT, 0.0).astype(BF16)
    lane = lax.rem(lax.broadcasted_iota(jnp.int32, scatter.shape, 0), 128)
    channel = lax.broadcasted_iota(jnp.int32, scatter.shape, 1)
    scatter[...] = jnp.where(lax.div(channel, CS_OUT) == lane, 1.0, 0.0).astype(BF16)


def banded_kernels(first, second, shortcut):
    turn = lambda k: jnp.swapaxes(k, 2, 3).reshape(-1, k.shape[2])
    rounded = lambda k: k.astype(BF16).astype(F32)
    first, second, shortcut = rounded(first), rounded(second), rounded(shortcut)
    args = (
        first.reshape(-1, CS_OUT),
        turn(first),
        second.reshape(-1, CS_OUT),
        turn(second),
        shortcut,
        shortcut.T,
    )
    shapes = [(1152, 256), (1792, 256), (1536, 256), (640, 256), (768, 256), (512, 128), (256, 256)]
    return pl.pallas_call(
        bands_kernel,
        in_specs=[pl.BlockSpec(memory_space=pltpu.VMEM)] * 6,
        out_specs=[pl.BlockSpec(memory_space=pltpu.VMEM)] * len(shapes),
        out_shape=[shape_of(shape, BF16) for shape in shapes],
        scratch_shapes=[pltpu.VMEM((1792, 256), F32)],
        compiler_params=pltpu.CompilerParams(vmem_limit_bytes=VMEM_LIMIT),
        cost_estimate=cost(8),
    )(*args)


def body(
    space,
    batch,
    small_in,
    large_in,
    small_teacher,
    large_teacher,
    small_groups,
    large_groups,
    small_cot,
    large_cot,
    teacher_gains,
    teacher_first,
    teacher_inner,
    teacher_second,
    teacher_bypass,
    entry_norm,
    first_conv,
    inner_norm,
    second_conv,
    shortcut,
    momentum_entry,
    momentum_first,
    momentum_inner,
    momentum_second,
    momentum_shortcut,
    average_entry,
    average_first,
    average_inner,
    average_second,
    average_shortcut,
):
    slabs = SLABS
    group = space // slabs
    axes = (("space", space), ("batch", batch))
    me = lax.axis_index("space")
    z, x = me // group, me % group
    place = jnp.stack([x, z]).astype(jnp.int32)
    total_positions = batch * (small_in.shape[0] * SIDE * SIDE // 4 + large_in.shape[0] * SIDE * SIDE)
    pixels = [small_in, large_in]
    teachers = [small_teacher, large_teacher]
    labels = [small_groups, large_groups]
    cots = [small_cot, large_cot]
    sides = [SIDE, 2 * SIDE]
    both = range(2)
    per_device = [p.shape[0] // space for p in pixels]
    local_rows = [p.shape[1] for p in pixels]
    images = [slabs * n for n in per_device]
    padded = [-(-n // 16) * 16 for n in images]
    tiles = [32 if padded[0] % 32 == 0 else 16, 16]
    p_counts = [s // (2 * slabs) for s in sides]
    widths = [s // 2 for s in sides]

    def to_sub(d):
        return [(k, k // group * group + (k % group + d) % group) for k in range(space)]

    def to_slab(d):
        return [(k, (k // group + d) % slabs * group + k % group) for k in range(space)]

    def send(array, pairs):
        return lax.ppermute(array, "space", pairs)

    def pick_images(array, res, sub):
        n, rows, lanes = array.shape
        parts = array.reshape(slabs, group, per_device[res], rows, lanes)
        part = lax.dynamic_index_in_dim(parts, sub, 1, False)
        return part.reshape(images[res], rows, lanes)

    def rows_first(array):
        return jnp.transpose(array, (1, 0, 2))

    def slab_rows(pieces, first, last):
        local = pieces[0].shape[0]
        out = []
        for s in range(first // local, (last - 1) // local + 1):
            lo, hi = max(first - s * local, 0), min(last - s * local, local)
            cut = [p[lo:hi] for p in pieces]
            out.append(lax.select_n((x - s) % group, *cut) if group > 1 else cut[0])
        return jnp.concatenate(out, axis=0) if len(out) > 1 else out[0]

    def partner(b, k, first):
        slab = k // group
        other = slab ^ 1 if first else ((slab + 1) ^ 1) - 1
        if 0 <= other < slabs:
            return b * space + other * group + k % group
        return (b ^ 1) * space + k

    pair_lists = [
        [(b * space + k, partner(b, k, first)) for b in range(batch) for k in range(space)]
        for first in (True, False)
    ]

    def edge_rows(pieces, count):
        rows = group * pieces[0].shape[0]
        last, first = slab_rows(pieces, rows - count, rows), slab_rows(pieces, 0, count)
        even = z % 2 == 0
        return lax.select(even, last, first), lax.select(even, first, last)

    def to_neighbours(rows):
        return [lax.ppermute(r, ("batch", "space"), pairs) for r, pairs in zip(rows, pair_lists)]

    def pad_to(array, size):
        extra = size - array.shape[1]
        return jnp.pad(array, ((0, 0), (0, extra), (0, 0))) if extra else array

    def pad_images(array, res):
        return pad_to(array, padded[res])

    def label_table(res, sub, size):
        mine = lax.dynamic_index_in_dim(
            labels[res].reshape(slabs, group, per_device[res]), sub, 1, False
        ).reshape(images[res])
        mine = jnp.pad(mine.astype(F32), (0, size - images[res]), constant_values=-1.0)
        return jnp.broadcast_to(mine[:, None], (size, 128))

    tables = [label_table(res, x, padded[res]) for res in both]
    norm_in = jnp.tile(entry_norm, (1, 128 // CS_IN))
    norm_mid = jnp.tile(inner_norm, (1, 128 // CS_OUT))
    by_slab = [[sub + group * k for k in range(slabs)] for sub in range(group)]

    def among_slabs(array, axis):
        if axis:
            array = jnp.moveaxis(array, axis, 0)
        return lax.all_to_all(array, "space", 0, 0, axis_index_groups=by_slab, tiled=True)

    subs = [(x + d) % group for d in range(group)]
    picked_small = [rows_first(pick_images(small_in, 0, sub)) for sub in subs]
    cots_here = after(cots, picked_small[1:])
    narrow = cots[0].shape[2]
    cot_stacks = []
    for res in both:
        c = jnp.pad(rows_first(cots_here[res]), ((1, 2), (0, 0), (0, 0)))
        count = p_counts[res]
        c = jnp.stack([c[k * count : (k + 1) * count + 3] for k in range(slabs)])
        if c.shape[3] > narrow:
            c = jnp.concatenate(
                [c[..., k : k + narrow] for k in range(0, c.shape[3], narrow)], axis=2
            )
        cot_stacks.append(c)
    flat = [c.reshape(slabs, -1, narrow) for c in cot_stacks]
    cot_flat = jnp.concatenate(flat, axis=1)
    cots_ready = cot_flat
    cot_flat = among_slabs(cot_flat, 0)
    large_source = after(large_in, cots_ready)
    picked_large = [rows_first(pick_images(large_source, 1, sub)) for sub in subs]
    picked = [picked_small, picked_large]
    arrived = [
        [picked[res][0]] + [send(picked[res][d], to_sub(d)) for d in range(1, group)]
        for res in both
    ]


    gains = jnp.tile(teacher_gains, (1, max(t.shape[2] for t in teachers) // CT_IN))

    def activated(array, size):
        lanes = array.shape[2]
        z_t = gains[0, :lanes] * array.astype(F32) + gains[1, :lanes]
        return pad_to(rows_first(jax.nn.silu(z_t).astype(BF16)), size)

    large_raw_in = after(large_teacher, [p[1:] for p in picked], cots_ready)
    own_large = pick_images(large_raw_in, 1, x)
    away_large = [pick_images(large_raw_in, 1, sub) for sub in subs[1:]]
    cut = min(16, images[1])
    sizes = [cut, images[1] - cut]
    ranges = [(0, cut), (cut, images[1])]

    def large_part(k, *others):
        lo, hi = ranges[k]
        return [
            send(after(away_large[d - 1][lo:hi], *others), to_sub(d)) for d in range(1, group)
        ]

    large_raw = [large_part(0)]

    stat_tables = [label_table(res, sub, images[res]) for res in both for sub in subs]
    entry_sums = input_stats(picked[0] + picked[1], stat_tables)
    (lo, hi), size = ranges[0], sizes[0]
    large_own = [activated(own_large[lo:hi], size)]
    raw_edges = [edge_rows(arrived[res], 6) for res in both]
    corners = lambda parts: [p[:1, :, :128] for p in parts]
    waits = ([p[1:] for p in arrived], cot_flat, corners(large_raw[0]), large_own, raw_edges)
    entry_total = total_over_devices([entry_sums], axes, 0, waits)

    raw_halos = [to_neighbours(after(raw_edges[res], entry_total)) for res in both]
    large_raw.append(large_part(1, entry_total))
    large_pieces = [
        [large_own[0]] + [activated(after(p, entry_total), sizes[0]) for p in large_raw[0]]
    ]

    def large_edges_of(k, *others):
        lo, hi = ranges[k]
        rows = [after(p[:, : hi - lo], *others) for p in large_pieces[k]]
        return to_neighbours(edge_rows(rows, 3))

    lanes = small_teacher.shape[2]
    z_t = after(small_teacher, large_raw_in).astype(F32) * gains[0, :lanes] + gains[1, :lanes]
    small_active = rows_first(jax.nn.silu(z_t).astype(BF16))
    small_active = small_active.reshape(local_rows[0], slabs, group, per_device[0], lanes)

    parts_of = [list(range(slabs // 2)), *([k] for k in range(slabs // 2, slabs))]

    def small_part(ks, sub):
        part = lax.dynamic_slice(
            small_active,
            (0, ks[0], sub, 0, 0),
            (local_rows[0], len(ks), 1, per_device[0], lanes),
        )
        return part.reshape(local_rows[0], len(ks) * per_device[0], lanes)

    small_away = [[small_part(ks, sub) for sub in subs[1:]] for ks in parts_of]
    bands = banded_kernels(*after((first_conv, second_conv, shortcut), entry_total))
    bands_first, bands_second, bands_second_back, bands_even, bands_odd, gather, scatter = bands
    raws, evens, odds, firsts, first_sums = ([None, None] for _ in range(5))
    for res in (1, 0):
        pieces = [pad_images(p, res) for p in arrived[res]]
        if res == 0:
            large_edges = [large_edges_of(0, sums)]
            cot_here = after(cot_flat, sums)
            cot_slabs = []
            at = 0
            for at_res, sent in zip(both, cot_stacks):
                size = sent.shape[1] * sent.shape[2]
                c = cot_here[:, at : at + size].reshape(sent.shape)
                at += size
                n = per_device[at_res]
                c = jnp.concatenate([c[:, :, k : k + n] for k in range(0, c.shape[2], n)], axis=3)
                c = jnp.moveaxis(c, 0, 1).reshape(c.shape[1], images[at_res], c.shape[3])
                cot_slabs.append(pad_images(c, at_res))
            pieces = after(pieces, cot_slabs)
        raw, even, odd, first, sums = student_forward(
            place,
            pieces,
            *[pad_images(p, res) for p in raw_halos[res]],
            tables[res],
            entry_total,
            norm_in,
            bands_first,
            tiles[res],
        )
        raws[res] = raw
        evens[res] = even
        odds[res] = odd
        firsts[res] = first
        first_sums[res] = sums
    inner_total = total_over_devices(first_sums, axes, 1, (corners(large_raw[1]), large_edges))

    (lo, hi), size = ranges[1], sizes[1]
    large_pieces.append(
        [activated(after(p, inner_total), size) for p in (own_large[lo:hi], *large_raw[1])]
    )
    large_edges.append(large_edges_of(1, inner_total))
    small_pieces = [
        [send(after(p, inner_total), to_sub(d + 1)) for d, p in enumerate(away)]
        for away in small_away[::-1]
    ][::-1]

    def small_rows(n, *others):
        own = small_part(parts_of[n], x)
        return edge_rows([own] + after(small_pieces[n], *others), 3)

    acts, own_firsts, sums_out, lows, energies = [], [], [], [], []
    for res in both:
        act, own_first, block_sum, low, energy = student_block(
            place,
            firsts[res],
            odds[res],
            tables[res],
            entry_total,
            inner_total,
            norm_mid,
            bands_second,
            gather,
            tiles[res],
        )
        acts.append(act)
        own_firsts.append(own_first)
        sums_out.append(block_sum)
        lows.append(low)
        energies.append(energy)

    shared = (
        teacher_first.reshape(9 * CT_IN, CT_OUT),
        teacher_second.reshape(9 * CT_OUT, CT_OUT),
        teacher_bypass,
        teacher_inner,
    )
    def large_map(k, *others):
        pieces = large_pieces[k]
        own = after(pieces[0], *others)
        edges = [pad_to(h, sizes[k]) for h in large_edges[k]]
        return teacher_energies(place, own, 0, pieces[1:], *edges, shared, sizes[k])

    def small_map(n, edges, *others):
        arrays = after((*small_pieces[n], *edges), *others)
        return [
            teacher_energies(
                place, small_active, parts_of[n][0], arrays[:-2], *arrays[-2:], shared, per_device[0]
            )
        ]

    large_maps = [large_map(0, inner_total)]
    rows = small_rows(0, large_maps[0], energies)
    edges = [to_neighbours(rows)]
    large_maps.append(large_map(1, rows))
    rows = small_rows(1, large_maps[1])
    edges.append(to_neighbours(rows))
    small_maps = small_map(0, edges[0], rows)
    for n in range(2, len(parts_of)):
        rows = small_rows(n, small_maps)
        edges.append(to_neighbours(rows))
        small_maps = small_maps + small_map(n - 1, edges[n - 1], rows)
    small_maps = small_maps + small_map(len(parts_of) - 1, edges[-1])
    factors = attention_maps(
        energies, [small_maps, large_maps], tables, widths, p_counts, slabs, group, 2
    )
    loss_sums = factors[2]

    def to_owners(res, first, last, *others):
        low = lows[res][first:last, : images[res]]
        rows, _, lanes = low.shape
        low = jnp.moveaxis(low.reshape(rows, slabs, per_device[res], lanes), 1, 0)
        return among_slabs(after(low, *others), 0)

    out_parts = [to_owners(0, 0, p_counts[0], factors[2])]

    flows, grads, flow_sums, second_parts, shortcut_parts = [], [], [], [], []
    for res in both:
        flow, grad, sums, second_part, shortcut_part = student_back(
            place,
            sums_out[res],
            cot_slabs[res],
            factors[res],
            scatter,
            own_firsts[res],
            acts[res],
            odds[res],
            tables[res],
            entry_total,
            inner_total,
            norm_mid,
            bands_second_back,
            tiles[res],
        )
        flows.append(flow)
        grads.append(grad)
        flow_sums.append(sums)
        second_parts.append(second_part)
        shortcut_parts.append(shortcut_part)
    flow_total = total_over_devices(flow_sums, axes, 3, out_parts)

    entry_parts, first_parts, entry_flow_sums = [], [], []
    held = None
    for res in both:
        flow = flows[res] if held is None else after(flows[res], held)
        *rows, first_part, sums = student_entry(
            place,
            flow,
            own_firsts[res],
            grads[res],
            evens[res],
            odds[res],
            raws[res],
            tables[res],
            entry_total,
            inner_total,
            flow_total,
            norm_in,
            norm_mid,
            bands_even,
            bands_odd,
            tiles[res],
            group,
        )
        if res == 0:
            held = rows[0]
            half_out = to_owners(1, 0, p_counts[1] // 2, held)
        first_parts.append(first_part)
        entry_flow_sums.append(sums)
        rows = [r[:, : images[res]] for r in rows]
        if res == 0:
            rows[1:] = [send(r, to_sub(d + 1)) for d, r in enumerate(rows[1:])]
        entry_parts.append(rows)
    def native_rows(res):
        ordered = [lax.select_n((x - s) % group, *entry_parts[res]) for s in range(group)]
        n, rows, lanes = pixels[res].shape
        rows_in = jnp.stack(ordered).reshape(group, rows, slabs, per_device[res], lanes)
        return jnp.transpose(rows_in, (2, 0, 3, 1, 4)).reshape(n, rows, lanes)

    rate_scale = 1.0 / math.sqrt(total_positions)
    flat = lambda k: k.reshape(-1, k.shape[-1])
    kernel_states = [
        [flat(k) for k in (first_conv, momentum_first, average_first)],
        [flat(k) for k in (second_conv, momentum_second, average_second)],
        [shortcut, momentum_shortcut, average_shortcut],
    ]
    packed = gradient_sum(
        [first_parts, second_parts, shortcut_parts, entry_flow_sums, [loss_sums]],
        axes,
        4,
        (entry_parts[0][1:], entry_parts[1], half_out),
    )
    first_state, second_state, bypass_state, entry_state, image_tables, total_loss = update(
        packed,
        kernel_states,
        [entry_norm, momentum_entry, average_entry],
        entry_total,
        norm_in,
        (CONV_RATE * rate_scale, NORM_RATE * rate_scale, 1.0 / total_positions),
    )
    rows = entry_parts[1]
    rows[1:] = [send(after(r, packed), to_sub(d + 1)) for d, r in enumerate(rows[1:])]
    out_parts.append(jnp.concatenate([half_out, to_owners(1, p_counts[1] // 2, p_counts[1], packed)], axis=1))
    first_state = [k.reshape(first_conv.shape) for k in first_state]
    second_state = [k.reshape(second_conv.shape) for k in second_state]
    inner_folded = flow_total.reshape(8, 128 // CS_OUT, CS_OUT).sum(axis=1)
    ones_inner, cross_inner = inner_folded[0:2], inner_folded[2:4]
    block_outs = []
    for res in both:
        low = jnp.transpose(out_parts[res], (2, 0, 1, 3))
        block_outs.append(low.reshape(low.shape[0], -1, low.shape[3]))
    def wide_rows(lanes):
        wide = jnp.tile(image_tables, (1, lanes // 128))
        return [wide[k] for k in range(8)]

    wide = [wide_rows(p.shape[2]) for p in pixels]
    arrived_rows = [native_rows(0)]
    entry_parts[1] = after(entry_parts[1], block_outs, wide[1])
    arrived_rows.append(native_rows(1))
    input_grads = []
    for res in both:
        one = (labels[res] == 1)[:, None, None]
        gain, bias, slope, level = [
            jnp.where(one, wide[res][2 * k + 1], wide[res][2 * k]) for k in range(4)
        ]
        value = pixels[res].astype(F32)
        before = value * gain + bias
        s = jax.nn.sigmoid(before)
        flow = arrived_rows[res].astype(F32) * (s * (1.0 + before * (1.0 - s)))
        input_grads.append(gain * flow + (value * slope + level))

    inner_grads = jnp.stack([jnp.sum(cross_inner, axis=0), jnp.sum(ones_inner, axis=0)])
    inner_state = renew(inner_norm, inner_grads, momentum_inner, average_inner, NORM_RATE * rate_scale)
    return (
        *block_outs,
        input_grads[0],
        input_grads[1],
        total_loss.reshape(()),
        *entry_state,
        *first_state,
        *inner_state,
        *second_state,
        *bypass_state,
    )


def solution(mesh):
    rows = P("batch", "space", None)
    blocks = P(("batch", "space"), None, None)
    return jax.shard_map(
        functools.partial(body, mesh.shape["space"], mesh.shape["batch"]),
        mesh=mesh,
        in_specs=(rows,) * 4 + (P("batch"),) * 2 + (blocks,) * 2 + (P(),) * 20,
        out_specs=(blocks,) * 2 + (rows,) * 2 + (P(),) * 24,
        check_vma=False,
    )
```
